32 devices in a mesh: expert: 4 (over x, core), shard: 8 (over z, y).
Axes of the slice: x: 2, y: 2, z: 4, core: 2. Of those that a mesh axis runs over, the one named last changes fastest.
Arguments:
- tokens: bfloat16 [32768, 768], P(('expert', 'shard')), may hold values from -6 to 6
- segments: int32 [32, 1024], P(('expert', 'shard')), may hold values from 0 to 12, never falling along the last dimension, each value on 1 to 256 neighbouring positions
- parents: int32 [32, 13], P(('expert', 'shard')), may hold values from 0 to 11, as said below
- adapter_of: int32 [32], P(('expert', 'shard')), may hold values from 0 to 7
- routes: int32 [32768, 2], P(('expert', 'shard')), may hold values from 0 to 11, all different within a row; in each aligned block of 1024 rows (0 to 1023, 1024 to 2047, ...) at most 192 rows name the same one
- norm_gain: float32 [2, 2, 768], replicated, may hold values from 0.5 to 1.5
- query_key_value_weight: bfloat16 [2, 768, 2304], P(None, 'shard'), may hold values from -0.21875 to 0.21875
- output_weight: bfloat16 [2, 768, 768], P(None, 'shard'), may hold values from -1.75 to 1.75
- adapter_down: bfloat16 [2, 4, 8, 768, 16], replicated, may hold values from -0.21875 to 0.21875
- adapter_up: bfloat16 [2, 4, 8, 768, 16], replicated, may hold values from -0.29882812 to 0.29882812
- router: float32 [2, 768, 12], replicated, may hold values from -0.15625 to 0.15625
- router_residual: float32 [12, 12], replicated, may hold values from -1.5 to 1.5
- const_proj: float32 [2, 2, 768, 2], replicated, may hold values from -0.21875 to 0.21875
- const_vec: float32 [2, 2, 768], replicated, may hold values from -6 to 6
- w_gate_up: bfloat16 [2, 8, 768, 4096], P(None, 'expert', 'shard'), may hold values from -0.21875 to 0.21875
- w_down: bfloat16 [2, 8, 2048, 768], P(None, 'expert', 'shard'), may hold values from -0.125 to 0.125
- out_grad: bfloat16 [32768, 768], P(('expert', 'shard')), may hold values from -6 to 6
Outputs:
- block_out: float32 [32768, 768], P(('expert', 'shard'))
- grad_tokens: float32 [32768, 768], P(('expert', 'shard'))
- grad_adapter_down: float32 [2, 4, 8, 768, 16], P(None, None, 'expert', 'shard')
- grad_adapter_up: float32 [2, 4, 8, 768, 16], P(None, None, 'expert', 'shard')
The draws below stay inside these ranges and needn't reach their ends.
Inputs may be any that keep to these rules, and one draw needn't show every extreme that they name: Within a tree segment numbers never fall, and each of the 13 segments holds 1 to 256 tokens. parents[t, s] < s for s >= 1 and parents[t, 0] = 0. `routes`: each row names two different experts: 0 to 7 feed-forward, 8 zero, 9 copy, the last two constant. In the rows of one device no expert is named by more than 192 rows, a bound that some block reaches.
All inputs are finite; a program needn't handle non-finite values.
Results may differ from the reference program's by a relative error of at most 0.024.
Values may be sent and summed in bfloat16 or wider, within the bound.
A program may use at most 320 MiB of HBM per device.

```python
import math
import jax
import jax.numpy as jnp
import numpy as np
from jax import lax

D = 768
HEADS = 12
HD = 64
FF = 2048
NFFN = 8
NEXP = 12
R = 16
NA = 8
NSEG = 13
LAYERS = 2
TREE_LEN = 1024
TOK_DEV = 1024
TREES = 32
TOKENS = 32768
CAP = 192


def draw_parents(key, part):
    key = jax.random.fold_in(key, 11)
    raw = jax.random.randint(key, (TREES, NSEG), 0, 1048576, dtype=jnp.int32)
    limits = jnp.maximum(jnp.arange(NSEG, dtype=jnp.int32), 1)
    parent_table = raw % limits[None, :]
    return parent_table.at[0, NSEG - 1].set(NSEG - 2)


def plant(result, own_key, low, top_value):
    place = [jax.random.randint(jax.random.fold_in(own_key, axis), (), 0, length) for axis, length in enumerate(result.shape)]
    main_axis = result.shape.index(max(result.shape))
    next_to = place[:main_axis] + [(place[main_axis] + 1) % result.shape[main_axis]] + place[main_axis + 1:]
    return result.at[tuple(place)].set(low).at[tuple(next_to)].set(top_value)


def level_of(rng, shape, split, smallest, high):
    factor_of = 1.0
    for axis_at, shards_of in split:
        draws = jax.random.uniform(jax.random.fold_in(jax.random.fold_in(rng, 6), axis_at), (shards_of,), jnp.float32, smallest / len(split), high / len(split))
        factor_of = factor_of * jnp.repeat(jnp.exp(draws), shape[axis_at] // shards_of).reshape((-1,) + (1,) * (len(shape) - 1 - axis_at))
    return factor_of


def split_up(number_of, total, most, skew):
    portions = [(1 << 20) // math.isqrt(standing ** skew) + 1 for standing in range(2, number_of + 1)]
    spare, given = total - most - (number_of - 1), [1] * (number_of - 1)
    while spare > 0:
        movable = [i for i in range(number_of - 1) if given[i] < most]
        pool, budget = sum([portions[i] for i in movable]), spare
        for i in movable:
            extra = min(most - given[i], max(1, budget * portions[i] // pool), spare)
            given[i] = given[i] + extra
            spare = spare - extra
    return np.array([most] + given)


def uneven_parts(stream_key, count, total, most, lean):
    if count == 2:
        one = jax.random.randint(stream_key, (), max(1, total - most), min(most, total - 1) + 1)
        return jnp.stack([one, total - one])
    sizes = jnp.asarray(split_up(count, total, most, lean), jnp.int32)
    pairs = (count - 1) // 2
    giver, sink = sizes[1:1 + 2 * pairs:2], sizes[2:2 + 2 * pairs:2]
    room = jnp.minimum(giver - 1, most - sink)
    shifted = jax.random.randint(jax.random.fold_in(stream_key, 1), (pairs,), 0, 1 << 20) % (room + 1)
    sizes = sizes.at[1:1 + 2 * pairs:2].set(giver - shifted).at[2:2 + 2 * pairs:2].set(sink + shifted)
    return sizes[jax.random.permutation(jax.random.fold_in(stream_key, 2), count)]


def assign_block(stream_key, own, number, rows, number_of, top, bound, slope):
    order = jax.random.permutation(stream_key, number_of)
    crowded, usual = portions_of(number_of, rows * top, bound, slope, True), portions_of(number_of, rows * top, bound, slope, False)
    places = jnp.arange(number_of)

    def named(sizes, rotation):
        used = int((sizes > 0).sum())
        fixed = max(1, used // 4)
        passed = fixed + (places - fixed + rotation * (used - fixed)) % max(1, number_of - fixed)
        return jnp.zeros((number_of,), jnp.int32).at[order[jnp.where(places < fixed, places, passed)]].set(jnp.asarray(sizes, jnp.int32))

    sizes = jnp.where(number % 4 == 0, named(crowded, number // 4), named(usual, number - number // 4 - 1))
    mixed = jax.random.permutation(jax.random.fold_in(own, 3), number_of)
    donor, sink = mixed[0:number_of // 2 * 2:2], mixed[1:number_of // 2 * 2:2]
    slack = jnp.minimum(sizes[donor] - 1, bound - sizes[sink]) // 2
    slack = jnp.where((donor == order[0]) | (sink == order[0]) | (sizes[sink] == 0), 0, jnp.maximum(slack, 0))
    passed = jax.random.randint(jax.random.fold_in(own, 4), (number_of // 2,), 0, 1 << 20) % (slack + 1)
    sizes = sizes.at[donor].add(-passed).at[sink].add(passed)
    labels = jnp.searchsorted(jnp.cumsum(sizes), jnp.arange(rows * top), side="right").astype(jnp.int32)
    grid = labels.reshape(top, rows).T
    grid = grid[jax.random.permutation(jax.random.fold_in(own, 1), rows)]
    rotation = jax.random.randint(jax.random.fold_in(own, 2), (rows, 1), 0, top)
    return jnp.take_along_axis(grid, (jnp.arange(top)[None, :] + rotation) % top, axis=1)


def portions_of(count, total, most, skew, full):
    portions = [(1 << 20) // math.isqrt(standing ** skew) + 1 for standing in range(1, count + 1)]
    largest = most if full else min(most, max(-(-total // count), total * portions[0] // sum(portions)))
    least = 1 if total - largest >= count - 1 else 0
    counts, spare = [largest] + [least] * (count - 1), total - largest - least * (count - 1)
    while spare > 0:
        free = [i for i in range(1, count) if counts[i] < largest] or [i for i in range(1, count) if counts[i] < most]
        pool, budget = sum([portions[i] for i in free]), spare
        for i in free:
            extra = min(most - counts[i], max(1, budget * portions[i] // pool), spare)
            counts[i] = counts[i] + extra
            spare = spare - extra
    return np.array(counts)


def scatter_about(rng, extent, deviation, most, split=(), held_as=jnp.bfloat16):
    result = deviation * jax.random.normal(rng, extent, jnp.float32)
    if split:
        result = result * level_of(rng, extent, split, -0.22, 0.18)
    return jnp.clip(result, -most, most).astype(held_as)


def setup_inputs(seed: int = 0) -> dict:
    arg_keys = jax.random.split(jax.random.key(seed), 18)
    tokens = scatter_about(arg_keys[0], (TOKENS, D), 1.0, 6.0, ((0, 32),))
    segments = jax.vmap(lambda own: jnp.searchsorted(jnp.cumsum(uneven_parts(own, NSEG, TREE_LEN, TREE_LEN // 4, 1)), jnp.arange(TREE_LEN), side="right"))(jax.random.split(arg_keys[1], TREES)).reshape((TREES, TREE_LEN)).astype(jnp.int32)
    parents = draw_parents(jax.random.fold_in(arg_keys[17], 71), 0)
    adapter_of = plant(jax.random.randint(arg_keys[3], (TREES,), 0, NA), jax.random.fold_in(arg_keys[3], 1), 0, NA - 1).astype(jnp.int32)
    routes_keys = jax.random.split(jax.random.fold_in(arg_keys[4], 1), TOKENS // TOK_DEV)
    routes_turns = jax.random.permutation(jax.random.fold_in(arg_keys[4], 3), TOKENS // TOK_DEV)
    routes = jax.vmap(lambda own, number: assign_block(jax.random.fold_in(arg_keys[4], 2), own, number, TOK_DEV, NEXP, 2, CAP, 2))(routes_keys, routes_turns).reshape((TOKENS, 2))
    norm_gain = jnp.clip(1.0 + 0.1 * jax.random.normal(arg_keys[5], (LAYERS, 2, D), jnp.float32), 0.5, 1.5)
    query_key_value_weight = scatter_about(arg_keys[6], (LAYERS, D, 3 * D), D ** -0.5, 0.21875, ((1, 8),))
    output_weight = scatter_about(arg_keys[7], (LAYERS, D, D), (D // 64) ** -0.5, 1.75, ((1, 8),))
    adapter_down = scatter_about(arg_keys[8], (LAYERS, 4, NA, D, R), D ** -0.5, 0.21875)
    adapter_up = scatter_about(arg_keys[9], (LAYERS, 4, NA, D, R), 0.05, 0.29882812)
    router = scatter_about(arg_keys[10], (LAYERS, D, NEXP), (2 * D) ** -0.5, 0.15625, (), jnp.float32)
    router_residual = scatter_about(arg_keys[11], (NEXP, NEXP), 0.25, 1.5, (), jnp.float32)
    const_proj = scatter_about(arg_keys[12], (LAYERS, 2, D, 2), D ** -0.5, 0.21875, (), jnp.float32)
    const_vec = scatter_about(arg_keys[13], (LAYERS, 2, D), 1.0, 6.0, (), jnp.float32)
    w_gate_up = scatter_about(arg_keys[14], (LAYERS, NFFN, D, 2 * FF), D ** -0.5, 0.21875, ((1, 4), (2, 8)))
    w_down = scatter_about(arg_keys[15], (LAYERS, NFFN, FF, D), FF ** -0.5, 0.125, ((1, 4), (2, 8)))
    out_grad = scatter_about(arg_keys[16], (TOKENS, D), 1.0, 6.0, ((0, 32),))
    return dict(tokens=tokens, segments=segments, parents=parents, adapter_of=adapter_of, routes=routes, norm_gain=norm_gain, query_key_value_weight=query_key_value_weight, output_weight=output_weight, adapter_down=adapter_down, adapter_up=adapter_up, router=router, router_residual=router_residual, const_proj=const_proj, const_vec=const_vec, w_gate_up=w_gate_up, w_down=w_down, out_grad=out_grad)


@jax.custom_vjp
def low(v):
    return lax.optimization_barrier(v.astype(jnp.bfloat16)).astype(jnp.float32)

@jax.custom_vjp
def low_back(v):
    return v

def low_keep(v):
    return (low(v), None)

def low_pass(kept, grad):
    return (grad,)

def back_keep(v):
    return (v, None)

def back_low(kept, grad):
    return (low(grad),)
low.defvjp(low_keep, low_pass)
low_back.defvjp(back_keep, back_low)
HIGH_ACCURACY = lax.Precision.HIGHEST
ADAPTER_SCALE = 2.0
EPSILON = 1e-06

def rounded_both(value):
    return low_back(low(value))

def rms_norm(value, gain):
    return value * lax.rsqrt(lax.optimization_barrier(jnp.mean(value * value, axis=-1, keepdims=True)) + EPSILON) * gain

def ancestry(parents):
    indices = jnp.arange(NSEG, dtype=jnp.int32)
    table_rows = [(indices == 0).astype(jnp.float32)]
    for segment in range(1, NSEG):
        inherit = jnp.zeros((NSEG,), jnp.float32)
        for earlier in range(segment):
            inherit = inherit + jnp.where(parents[segment] == earlier, table_rows[earlier], 0.0)
        table_rows.append(jnp.maximum(inherit, (indices == segment).astype(jnp.float32)))
    return jnp.stack(table_rows)

def tree_mask(segments, parents):
    length = segments.shape[0]
    ancestors = ancestry(parents)
    member = (segments[:, None] == jnp.arange(NSEG, dtype=jnp.int32)[None, :]).astype(jnp.float32)
    reach = jnp.dot(jnp.dot(member, ancestors, precision=HIGH_ACCURACY), member.T, precision=HIGH_ACCURACY)
    places = jnp.arange(length, dtype=jnp.int32)
    allowed = (reach > 0.5) & (places[:, None] >= places[None, :])
    depth = lax.optimization_barrier(jnp.sum(allowed.astype(jnp.int32), axis=1)) - 1
    return (allowed, depth)

def rotate(values, depth):
    half = values.shape[-1] // 2
    inverse = jnp.exp(-math.log(10000.0) * jnp.arange(half, dtype=jnp.float32) / half)
    angles = depth.astype(jnp.float32)[:, None] * inverse[None, :]
    cosine = jnp.cos(angles)[:, None, :]
    sine = jnp.sin(angles)[:, None, :]
    first = values[..., :half]
    second = values[..., half:]
    return jnp.concatenate([first * cosine - second * sine, first * sine + second * cosine], axis=-1)

def dispatch_index(routes):
    flat = routes.reshape(-1)
    pairs = flat.shape[0]
    hits = (flat[:, None] == jnp.arange(NEXP, dtype=jnp.int32)[None, :]).astype(jnp.int32)
    slots = lax.optimization_barrier(jnp.sum((jnp.cumsum(hits, axis=0) - hits) * hits, axis=1))
    target = jnp.where(flat < NFFN, flat * CAP + slots, NFFN * CAP).astype(jnp.int32)
    holder = jnp.full((NFFN * CAP + 1,), pairs, jnp.int32).at[target].set(jnp.arange(pairs, dtype=jnp.int32))
    return (holder[:NFFN * CAP], target)

def mixture(normalized_rows, earlier, chosen, routes, router, residual_map, const_proj, const_vec):
    logits = jnp.dot(normalized_rows, router, precision=HIGH_ACCURACY) + jnp.dot(earlier, residual_map, precision=HIGH_ACCURACY)
    member = (routes[:, :, None] == jnp.arange(NEXP, dtype=jnp.int32)[None, None, :]).astype(jnp.float32)
    picked = jnp.einsum('tke,te->tk', member, logits, precision=HIGH_ACCURACY)
    gates = jax.nn.softmax(picked, axis=1)
    value = chosen + jnp.where((routes == NFFN + 1)[:, :, None], normalized_rows[:, None, :], 0.0)
    for which in range(2):
        share = jax.nn.softmax(jnp.dot(normalized_rows, const_proj[which], precision=HIGH_ACCURACY), axis=-1)
        constant = share[:, :1] * normalized_rows + share[:, 1:] * const_vec[which][None, :]
        value = value + jnp.where((routes == NFFN + 2 + which)[:, :, None], constant[:, None, :], 0.0)
    return (lax.optimization_barrier(jnp.sum(gates[:, :, None] * value, axis=1)), logits)

def tree_attention(normalized_rows, tree_segments, tree_parents, which, query_key_value_weight, output_weight, down_layer, up_layer):
    length = normalized_rows.shape[0]
    scale = 1.0 / math.sqrt(HD)
    allowed, depth = tree_mask(tree_segments, tree_parents)
    down = down_layer[:, which]
    upper_result = up_layer[:, which]
    narrow = rounded_both(jnp.einsum('ld,pdr->lpr', normalized_rows, down[:3], precision=HIGH_ACCURACY))
    additional_term = jnp.einsum('lpr,pdr->lpd', narrow, upper_result[:3], precision=HIGH_ACCURACY).reshape(length, 3 * D)
    projected_output = low_back(jnp.dot(normalized_rows, query_key_value_weight, precision=HIGH_ACCURACY) + ADAPTER_SCALE * additional_term)
    query = rounded_both(rotate(projected_output[:, :D].reshape(length, HEADS, HD), depth))
    keys = rounded_both(rotate(projected_output[:, D:2 * D].reshape(length, HEADS, HD), depth))
    values = rounded_both(projected_output[:, 2 * D:].reshape(length, HEADS, HD))
    scores = low_back(jnp.einsum('qhd,khd->hqk', query, keys, precision=HIGH_ACCURACY) * scale)
    masked = jnp.where(allowed[None], scores, -1e+30)
    top = lax.optimization_barrier(jnp.max(masked, axis=-1, keepdims=True))
    weights = jnp.exp(masked - top)
    probs = weights / lax.optimization_barrier(jnp.sum(weights, axis=-1, keepdims=True))
    blended_heads = jnp.einsum('hqk,khd->qhd', low(probs), values, precision=HIGH_ACCURACY).reshape(length, D)
    blended_heads = rounded_both(blended_heads)
    reduced_output = rounded_both(jnp.dot(blended_heads, down[3], precision=HIGH_ACCURACY))
    return low_back(jnp.dot(blended_heads, output_weight, precision=HIGH_ACCURACY) + ADAPTER_SCALE * jnp.dot(reduced_output, upper_result[3].T, precision=HIGH_ACCURACY))

def expert_block(rows, gate_up, down_w):
    parts = low_back(jnp.dot(rows, gate_up, precision=HIGH_ACCURACY))
    active = low(jax.nn.silu(parts[:, :FF]) * parts[:, FF:])
    return rounded_both(jnp.dot(active, down_w, precision=HIGH_ACCURACY))

def expert_path(sent, token_table, target, gate_up, down_w):
    block_count = token_table.shape[0]
    blocks = sent.reshape(block_count, TOK_DEV, D)
    padded = jnp.concatenate([blocks, jnp.zeros((block_count, 1, D), jnp.float32)], axis=1)
    buffer = low_back(jax.vmap(lambda rows, picks: rows[picks])(padded, token_table))
    grouped = buffer.reshape(block_count, NFFN, CAP, D).transpose(1, 0, 2, 3).reshape(NFFN, block_count * CAP, D)
    produced = lax.map(jax.checkpoint(lambda items: expert_block(items[0], items[1], items[2])), (grouped, gate_up, down_w))
    spread = produced.reshape(NFFN, block_count, CAP, D).transpose(1, 0, 2, 3).reshape(block_count, NFFN * CAP, D)
    spread = jnp.concatenate([spread, jnp.zeros((block_count, 1, D), jnp.float32)], axis=1)
    chosen = jax.vmap(lambda rows, picks: rows[picks])(spread, target)
    return chosen.reshape(block_count * TOK_DEV, 2, D)

def reference(tokens, segments, parents, adapter_of, routes, norm_gain, query_key_value_weight, output_weight, adapter_down, adapter_up, router, router_residual, const_proj, const_vec, w_gate_up, w_down, out_grad):
    qkv_all = query_key_value_weight.astype(jnp.float32)
    out_all = output_weight.astype(jnp.float32)
    gate_up_all = w_gate_up.astype(jnp.float32)
    down_all_w = w_down.astype(jnp.float32)
    block_count = TOKENS // TOK_DEV
    pair_table, target = jax.vmap(dispatch_index)(routes.reshape(block_count, TOK_DEV, 2))
    token_table = pair_table // 2

    def forward(stream, down_all, up_all):
        earlier = jnp.zeros((TOKENS, NEXP), jnp.float32)
        for layer in range(LAYERS):
            normalized_rows = low(rms_norm(stream, norm_gain[layer, 0]))

            def one_tree(items):
                return tree_attention(items[0], items[1], items[2], items[3], qkv_all[layer], out_all[layer], down_all[layer], up_all[layer])
            attended = lax.map(jax.checkpoint(one_tree), (normalized_rows.reshape(TREES, TREE_LEN, D), segments, parents, adapter_of))
            middle = stream + attended.reshape(TOKENS, D)
            normed_two = rms_norm(middle, norm_gain[layer, 1])
            chosen = expert_path(low(normed_two), token_table, target, gate_up_all[layer], down_all_w[layer])
            mixed_out, earlier = mixture(normed_two, earlier, chosen, routes, router[layer], router_residual, const_proj[layer], const_vec[layer])
            stream = middle + mixed_out
        return stream
    block_out, pull_back = jax.vjp(forward, tokens.astype(jnp.float32), adapter_down.astype(jnp.float32), adapter_up.astype(jnp.float32))
    grad_tokens, grad_down, grad_up = pull_back(out_grad.astype(jnp.float32))
    return (block_out, grad_tokens, grad_down, grad_up)
```

```python
import math

import jax
import jax.numpy as jnp
from jax import lax
from jax.experimental import pallas as pl
from jax.experimental.pallas import tpu as pltpu
from jax.sharding import PartitionSpec as P

D = 768
HEADS = 12
HD = 64
FF = 2048
NFFN = 8
NEXP = 12
R = 16
NA = 8
NSEG = 13
LAYERS = 2
CAP = 192
T = 1024
SLOTS = NFFN * CAP
RB = 256
NB = T // RB
PAIRS = HEADS // 2
FC = 512
EPSILON = 1e-06
BIG = 2.0**100
LOG_SCALE = math.log2(math.e) / math.sqrt(HD)
F32 = jnp.float32
BF = jnp.bfloat16
HIGHEST = lax.Precision.HIGHEST
VMEM_BYTES = 56 * 1024 * 1024


def mm(a, b):
    return lax.dot_general(a, b, (((1,), (0,)), ((), ())), preferred_element_type=F32)


def mm_nt(a, b):
    return lax.dot_general(a, b, (((1,), (1,)), ((), ())), preferred_element_type=F32)


def mm_tn(a, b):
    return lax.dot_general(a, b, (((0,), (0,)), ((), ())), preferred_element_type=F32)


def mm_exact(a, b):
    return lax.dot_general(
        a, b, (((1,), (0,)), ((), ())), preferred_element_type=F32, precision=HIGHEST
    )


def iota(shape, axis):
    return lax.broadcasted_iota(jnp.int32, shape, axis)


def sigmoid(v):
    return 1.0 / (1.0 + jnp.exp(-v))


def call(body, grid, ins, outs, scratch=(), name=None, flops=0, nbytes=0):
    def spec(entry):
        if entry[1] == "smem":
            return pl.BlockSpec(memory_space=pltpu.SMEM)
        if entry[1] is None:
            shape = entry[0].shape
            return pl.BlockSpec(shape, lambda *_: (0,) * len(shape))
        return pl.BlockSpec(entry[1], entry[2])

    return pl.pallas_call(
        body,
        grid=grid,
        in_specs=[spec(e) for e in ins],
        out_specs=[spec(e) for e in outs],
        out_shape=[jax.ShapeDtypeStruct(e[0].shape, e[0].dtype) for e in outs],
        scratch_shapes=list(scratch),
        compiler_params=pltpu.CompilerParams(
            dimension_semantics=("arbitrary",) * len(grid), vmem_limit_bytes=VMEM_BYTES
        ),
        cost_estimate=pl.CostEstimate(
            flops=int(flops), bytes_accessed=int(nbytes), transcendentals=0
        ),
        name=name,
    )(*[e[0] for e in ins])


def out(shape, dtype):
    return jax.ShapeDtypeStruct(shape, dtype)


def rows(i):
    return (i, 0)


def prep_body(par_ref, seg_ref, rt_ref, qf_ref, kf_ref, cos_ref, sin_ref, tcol_ref, trow_ref, anc):
    first = iota((1, 128), 1) & 63
    anc[...] = jnp.zeros_like(anc)
    anc[0:1, :] = (first == 0).astype(F32)
    for s in range(1, NSEG):
        above = anc[pl.ds(par_ref[0, s], 1), :]
        anc[s : s + 1, :] = jnp.maximum(above, (first == s).astype(F32))
    lane = iota((T, 128), 1)
    lane6 = lane & 63
    low = lane < 64
    member = (seg_ref[...] == lane6).astype(F32)
    ways = mm(jnp.where(low, member, 0.0).astype(BF), anc[...].astype(BF))
    qf_ref[...] = jnp.where(lane6 < NSEG, (ways - 1.0) * BIG, 0.0).astype(BF)
    ones = ((lane6 >= 16) & (lane6 < 19)).astype(F32)
    kf_ref[...] = (member + ones).astype(BF)
    hit0 = (rt_ref[:, 0:1] == lane).astype(F32)
    hit1 = (rt_ref[:, 1:2] == lane).astype(F32)
    hits = hit0 + hit1
    upto = (iota((T, T), 0) >= iota((T, T), 1)).astype(F32).astype(BF)
    seen = mm(upto, jnp.concatenate([member.astype(BF), hits.astype(BF)], axis=1))
    depth = jnp.sum(jnp.where(low, ways * seen[:, :128], 0.0), axis=1, keepdims=True) - 1.0
    before = seen[:, 128:] - hits

    def target(hit, route):
        slot = jnp.sum(hit * before, axis=1, keepdims=True)
        place = route.astype(F32) * CAP + slot
        return jnp.where(route < NFFN, place, 4.0 * SLOTS)

    t0 = target(hit0, rt_ref[:, 0:1])
    t1 = target(hit1, rt_ref[:, 1:2])
    both = jnp.where(lane == 0, t0, jnp.where(lane == 1, t1, 0.0))
    tcol_ref[...] = both.astype(jnp.int32)
    trow_ref[...] = both.T[0:8, :].astype(jnp.int32)
    inverse = jnp.exp((lane & 31).astype(F32) * (-math.log(10000.0) / 32.0))
    angle = depth * inverse
    cos_ref[...] = jnp.cos(angle)
    sine = jnp.sin(angle)
    sin_ref[...] = jnp.where((lane & 32) == 0, -sine, sine)


def prep(parents, seg_col, routes):
    return call(
        prep_body,
        (1,),
        [(parents, "smem"), (seg_col, None), (routes, None)],
        [
            (out((T, 128), BF), None),
            (out((T, 128), BF), None),
            (out((T, 128), F32), None),
            (out((T, 128), F32), None),
            (out((T, 128), jnp.int32), None),
            (out((8, T), jnp.int32), None),
        ],
        [pltpu.VMEM((128, 128), F32)],
        name="prep",
        flops=2 * T * T * 256,
        nbytes=3e6,
    )


def turn(v, cos, sin):
    first = (iota(v.shape, 1) & 32) == 0
    other = jnp.where(first, pltpu.roll(v, 96, 1), pltpu.roll(v, 32, 1))
    return v * cos + other * sin


def project_rows(x, gain, w_ref, d_ref, u_ref, cos, sin, n_ref, nar_ref, qkv_ref):
    scale = lax.rsqrt(jnp.mean(x * x, axis=1, keepdims=True) + EPSILON)
    normed = (x * scale * gain).astype(BF)
    n_ref[...] = normed
    narrow = mm(normed, d_ref[...]).astype(BF)
    nar_ref[...] = narrow
    for block in range(3):
        cols = slice(block * D, (block + 1) * D)
        part = mm(normed, w_ref[:, cols]) + mm(narrow, u_ref[:, cols])
        for j in range(PAIRS):
            piece = part[:, j * 128 : (j + 1) * 128]
            if block < 2:
                piece = turn(piece, cos, sin)
            at = block * D + j * 128
            qkv_ref[:, at : at + 128] = piece.astype(BF)


def project_body(x_ref, g_ref, w_ref, d_ref, u_ref, cos_ref, sin_ref, n_ref, nar_ref, qkv_ref):
    project_rows(
        x_ref[...].astype(F32),
        g_ref[...],
        w_ref,
        d_ref,
        u_ref,
        cos_ref[...],
        sin_ref[...],
        n_ref,
        nar_ref,
        qkv_ref,
    )


def project(x, gain, w, down, up, cos, sin):
    return call(
        project_body,
        (NB,),
        [
            (x, (RB, D), rows),
            (gain, None),
            (w, None),
            (down, None),
            (up, None),
            (cos, (RB, 128), rows),
            (sin, (RB, 128), rows),
        ],
        [
            (out((T, D), BF), (RB, D), rows),
            (out((T, 128), BF), (RB, 128), rows),
            (out((T, 3 * D), BF), (RB, 3 * D), rows),
        ],
        name="project",
        flops=2 * T * D * 3 * D,
        nbytes=12e6,
    )


def three(v):
    high = v.astype(BF)
    rest = v - high.astype(F32)
    middle = rest.astype(BF)
    return high, middle, (rest - middle.astype(F32)).astype(BF)


def attend_body(q_ref, k_ref, v_ref, qf_ref, kf_ref, mixed_ref, aug_ref):
    low = iota((T, 128), 1) < 64
    k = k_ref[...]
    kf = kf_ref[...]
    v = v_ref[...]
    one = jnp.ones((T, 128), BF)
    keys = (jnp.where(low, k, kf), jnp.where(low, kf, k))
    values = (jnp.where(low, v, one), jnp.where(low, one, v))
    low = low[:RB]
    tri = iota((RB, RB), 0) >= iota((RB, RB), 1)
    lane6 = iota((RB, 128), 1) & 63
    for i in range(NB):
        here = slice(i * RB, (i + 1) * RB)
        q = q_ref[here, :]
        qf = qf_ref[here, :]
        tops = []
        outs = []
        for h in range(2):
            qa = jnp.where(low, q, qf) if h == 0 else jnp.where(low, qf, q)
            diag = jnp.where(tri, mm_nt(qa, keys[h][here]), -BIG)
            top = jnp.max(diag, axis=1, keepdims=True)
            if i:
                off = mm_nt(qa, keys[h][: i * RB])
                top = jnp.maximum(top, jnp.max(off, axis=1, keepdims=True))
            result = mm(jnp.exp2((diag - top) * LOG_SCALE).astype(BF), values[h][here])
            if i:
                weights = jnp.exp2((off - top) * LOG_SCALE).astype(BF)
                result = result + mm(weights, values[h][: i * RB])
            tops.append(top)
            outs.append(result)
        total = jnp.where(low, outs[1], outs[0])
        mixed = jnp.where(low, outs[0], outs[1]) / pltpu.roll(total, 64, 1)
        mixed_ref[here, :] = mixed.astype(BF)
        level = -(jnp.where(low, tops[1], tops[0]) + math.sqrt(HD) * jnp.log(total))
        a, b, c = three(level)
        aug_ref[0, here, :] = jnp.where(
            lane6 == 16, a, jnp.where(lane6 == 17, b, jnp.where(lane6 == 18, c, qf))
        )


def attend(qkv, qf, kf):
    return call(
        attend_body,
        (PAIRS,),
        [
            (qkv, (T, 128), lambda j: (0, j)),
            (qkv, (T, 128), lambda j: (0, PAIRS + j)),
            (qkv, (T, 128), lambda j: (0, 2 * PAIRS + j)),
            (qf, None),
            (kf, None),
        ],
        [
            (out((T, D), BF), (T, 128), lambda j: (0, j)),
            (out((PAIRS, T, 128), BF), (1, T, 128), lambda j: (j, 0, 0)),
        ],
        name="attend",
        flops=12 * 4 * T * T * 128,
        nbytes=8e6,
    )


def settle_body(
    x_ref, mixed_ref, w_ref, d_ref, u_ref, g_ref, rt_ref, earlier_ref, res_ref,
    mid_ref, sent_ref, lg_ref, nar_ref,
):
    mixed = mixed_ref[...]
    narrow = mm(mixed, d_ref[...]).astype(BF)
    nar_ref[...] = narrow
    mid = x_ref[...].astype(F32) + mm(mixed, w_ref[...]) + mm(narrow, u_ref[...])
    mid_ref[...] = mid
    scale = lax.rsqrt(jnp.mean(mid * mid, axis=1, keepdims=True) + EPSILON)
    normed = mid * scale * g_ref[...]
    sent_ref[...] = normed.astype(BF)
    lg_ref[...] = mm_exact(normed, rt_ref[...]) + mm_exact(earlier_ref[...], res_ref[...])


def settle(x, mixed, w, down, up, gain, router, earlier, residual):
    return call(
        settle_body,
        (NB,),
        [
            (x, (RB, D), rows),
            (mixed, (RB, D), rows),
            (w, None),
            (down, None),
            (up, None),
            (gain, None),
            (router, None),
            (earlier, (RB, 128), rows),
            (residual, None),
        ],
        [
            (out((T, D), F32), (RB, D), rows),
            (out((T, D), BF), (RB, D), rows),
            (out((T, 128), F32), (RB, 128), rows),
            (out((T, 128), BF), (RB, 128), rows),
        ],
        name="settle",
        flops=2 * T * D * D * 2,
        nbytes=10e6,
    )


def dispatch_body(trow_ref, s_ref, o_ref):
    place = pl.program_id(0) * CAP + iota((CAP, T), 0)
    hit = (trow_ref[0:1, :] == place) | (trow_ref[1:2, :] == place)
    o_ref[0] = mm(hit.astype(F32).astype(BF), s_ref[...]).astype(BF)


def dispatch(trow, sent):
    return call(
        dispatch_body,
        (NFFN,),
        [(trow, None), (sent, None)],
        [(out((NFFN, CAP, D), BF), (1, CAP, D), lambda j: (j, 0, 0))],
        name="dispatch",
        flops=2 * T * SLOTS * D,
        nbytes=4e6,
    )[0]


def dispatch_grad_body(trow_ref, a_ref, b_ref, o_ref):
    place = pl.program_id(0) * CAP + iota((CAP, T), 0)
    hit0 = (trow_ref[0:1, :] == place).astype(F32).astype(BF)
    hit1 = (trow_ref[1:2, :] == place).astype(F32).astype(BF)
    o_ref[0] = (mm(hit0, a_ref[...]) + mm(hit1, b_ref[...])).astype(BF)


def dispatch_grad(trow, a, b):
    return call(
        dispatch_grad_body,
        (NFFN,),
        [(trow, None), (a, None), (b, None)],
        [(out((NFFN, CAP, D), BF), (1, CAP, D), lambda j: (j, 0, 0))],
        name="dispatch_grad",
        flops=4 * T * SLOTS * D,
        nbytes=6e6,
    )[0]


MB = 512


def expert_body(r_ref, wg_ref, wu_ref, wd_ref, p_ref, gate_ref, up_ref, acc):
    step = pl.program_id(0)

    @pl.when(step == 0)
    def _():
        acc[...] = jnp.zeros_like(acc)

    for m in range(SLOTS // MB):
        at = slice(m * MB, (m + 1) * MB)
        r = r_ref[at, :]
        gate = mm(r, wg_ref[...])
        up = mm(r, wu_ref[...])
        gate_ref[at, :] = gate.astype(BF)
        up_ref[at, :] = up.astype(BF)
        active = (gate * sigmoid(gate) * up).astype(BF)
        acc[at, :] += mm(active, wd_ref[...])

    @pl.when(step == pl.num_programs(0) - 1)
    def _():
        p_ref[...] = acc[...].astype(BF)


def expert_forward(received, gate_up, down):
    steps = FF // FC
    return call(
        expert_body,
        (steps,),
        [
            (received, None),
            (gate_up, (D, FC), lambda j: (0, j)),
            (gate_up, (D, FC), lambda j: (0, steps + j)),
            (down, (FC, D), lambda j: (j, 0)),
        ],
        [
            (out((SLOTS, D), BF), None),
            (out((SLOTS, FF), BF), (SLOTS, FC), lambda j: (0, j)),
            (out((SLOTS, FF), BF), (SLOTS, FC), lambda j: (0, j)),
        ],
        [pltpu.VMEM((SLOTS, D), F32)],
        name="expert_forward",
        flops=2 * SLOTS * D * FF * 3,
        nbytes=26e6,
    )


def expert_grad_body(g_ref, gate_ref, up_ref, wg_ref, wu_ref, wd_ref, o_ref, acc):
    step = pl.program_id(0)

    @pl.when(step == 0)
    def _():
        acc[...] = jnp.zeros_like(acc)

    for m in range(SLOTS // MB):
        at = slice(m * MB, (m + 1) * MB)
        grad = mm_nt(g_ref[at, :], wd_ref[...])
        gate = gate_ref[at, :].astype(F32)
        up = up_ref[at, :].astype(F32)
        s = sigmoid(gate)
        grad_s = grad * s
        grad_gate = (grad_s * up * (1.0 + gate * (1.0 - s))).astype(BF)
        grad_up = (grad_s * gate).astype(BF)
        acc[at, :] += mm_nt(grad_gate, wg_ref[...]) + mm_nt(grad_up, wu_ref[...])

    @pl.when(step == pl.num_programs(0) - 1)
    def _():
        o_ref[...] = acc[...].astype(BF)


def expert_backward(grads, gate, up, gate_up, down):
    steps = FF // FC
    return call(
        expert_grad_body,
        (steps,),
        [
            (grads, None),
            (gate, (SLOTS, FC), lambda j: (0, j)),
            (up, (SLOTS, FC), lambda j: (0, j)),
            (gate_up, (D, FC), lambda j: (0, j)),
            (gate_up, (D, FC), lambda j: (0, steps + j)),
            (down, (FC, D), lambda j: (j, 0)),
        ],
        [(out((SLOTS, D), BF), None)],
        [pltpu.VMEM((SLOTS, D), F32)],
        name="expert_backward",
        flops=2 * SLOTS * D * FF * 3,
        nbytes=26e6,
    )[0]


def mix_terms(logits, routes):
    lane = iota(logits.shape, 1)

    def at(place):
        return jnp.sum(jnp.where(lane == place, logits, 0.0), axis=1, keepdims=True)

    r0, r1 = routes[:, 0:1], routes[:, 1:2]
    gap = at(r0) - at(r1)
    gates = (sigmoid(gap), sigmoid(-gap))

    def weight(e):
        return jnp.where(r0 == e, gates[0], 0.0) + jnp.where(r1 == e, gates[1], 0.0)

    shares = []
    for c in range(2):
        apart = logits[:, 12 + 2 * c : 13 + 2 * c] - logits[:, 13 + 2 * c : 14 + 2 * c]
        shares.append((sigmoid(apart), sigmoid(-apart)))
    weights = [weight(NFFN + 1), weight(NFFN + 2), weight(NFFN + 3)]
    return gates, weights, shares


def rms_scale(v):
    return lax.rsqrt(jnp.mean(v * v, axis=1, keepdims=True) + EPSILON)


def combine_body(tcol_ref, ret_ref, mid_ref, lg_ref, rt_ref, g_ref, cv_ref, x_ref, c0_ref, c1_ref):
    place = iota((RB, SLOTS), 1)
    back = ret_ref[...]
    chosen = []
    for k, c_ref in enumerate((c0_ref, c1_ref)):
        hit = (tcol_ref[:, k : k + 1] == place).astype(F32).astype(BF)
        value = mm(hit, back)
        c_ref[...] = value.astype(BF)
        chosen.append(value)
    mid = mid_ref[...]
    normed = mid * rms_scale(mid) * g_ref[...]
    gates, weights, shares = mix_terms(lg_ref[...], rt_ref[...])
    same = weights[0] + weights[1] * shares[0][0] + weights[2] * shares[1][0]
    moe = gates[0] * chosen[0] + gates[1] * chosen[1] + same * normed
    moe = moe + (weights[1] * shares[0][1]) * cv_ref[0:1, :]
    moe = moe + (weights[2] * shares[1][1]) * cv_ref[1:2, :]
    x_ref[...] = mid + moe


def combine(tcol, returned, mid, logits, routes, gain, const_vec):
    return call(
        combine_body,
        (NB,),
        [
            (tcol, (RB, 128), rows),
            (returned, None),
            (mid, (RB, D), rows),
            (logits, (RB, 128), rows),
            (routes, (RB, 2), rows),
            (gain, None),
            (const_vec, None),
        ],
        [
            (out((T, D), F32), (RB, D), rows),
            (out((T, D), BF), (RB, D), rows),
            (out((T, D), BF), (RB, D), rows),
        ],
        name="combine",
        flops=4 * T * SLOTS * D,
        nbytes=12e6,
    )


def mix_grad_body(
    g_ref, mid_ref, c0_ref, c1_ref, lg_ref, rt_ref, gl_ref, gain_ref, cv_ref, wt_ref, res_ref,
    a_ref, b_ref, gn_ref, gle_ref,
):
    g = g_ref[...].astype(F32)
    mid = mid_ref[...]
    normed = mid * rms_scale(mid) * gain_ref[...]
    routes = rt_ref[...]
    gates, weights, shares = mix_terms(lg_ref[...], routes)
    a_ref[...] = (gates[0] * g).astype(BF)
    b_ref[...] = (gates[1] * g).astype(BF)

    def along(v):
        return jnp.sum(g * v, axis=1, keepdims=True)

    same = along(normed)
    const = [along(cv_ref[c : c + 1, :]) for c in range(2)]
    gate_grads = []
    for k, c_ref in enumerate((c0_ref, c1_ref)):
        r = routes[:, k : k + 1]
        value = along(c_ref[...].astype(F32)) + jnp.where(r == NFFN + 1, same, 0.0)
        for c in range(2):
            mixed = shares[c][0] * same + shares[c][1] * const[c]
            value = value + jnp.where(r == NFFN + 2 + c, mixed, 0.0)
        gate_grads.append(value)
    slope = gates[0] * gates[1] * (gate_grads[0] - gate_grads[1])
    lane = iota((RB, 128), 1)
    grad = gl_ref[...]
    grad = grad + jnp.where(lane == routes[:, 0:1], slope, 0.0)
    grad = grad - jnp.where(lane == routes[:, 1:2], slope, 0.0)
    for c in range(2):
        tilt = weights[1 + c] * shares[c][0] * shares[c][1] * (same - const[c])
        grad = grad + jnp.where(lane == 12 + 2 * c, tilt, 0.0)
        grad = grad - jnp.where(lane == 13 + 2 * c, tilt, 0.0)
    keep = weights[0] + weights[1] * shares[0][0] + weights[2] * shares[1][0]
    gn_ref[...] = mm_exact(grad, wt_ref[...]) + keep * g
    gle_ref[...] = mm_exact(grad, res_ref[...])


def mix_grad(g, mid, c0, c1, logits, routes, gl, gain, const_vec, router_t, residual_t):
    return call(
        mix_grad_body,
        (NB,),
        [
            (g, (RB, D), rows),
            (mid, (RB, D), rows),
            (c0, (RB, D), rows),
            (c1, (RB, D), rows),
            (logits, (RB, 128), rows),
            (routes, (RB, 2), rows),
            (gl, (RB, 128), rows),
            (gain, None),
            (const_vec, None),
            (router_t, None),
            (residual_t, None),
        ],
        [
            (out((T, D), BF), (RB, D), rows),
            (out((T, D), BF), (RB, D), rows),
            (out((T, D), F32), (RB, D), rows),
            (out((T, 128), F32), (RB, 128), rows),
        ],
        name="mix_grad",
        flops=2 * T * 128 * D * 6,
        nbytes=16e6,
    )


def rms_back(grad, v, gain):
    scale = rms_scale(v)
    inner = grad * gain
    return scale * inner - v * (scale**3 * jnp.mean(v * inner, axis=1, keepdims=True))


def settle_grad_body(
    tcol_ref, back_ref, gn_ref, mid_ref, g_ref, gain_ref, mixed_ref, nar_ref, w_ref, d_ref, u_ref,
    gm_ref, gx_ref, gu_ref, gd_ref,
):
    @pl.when(pl.program_id(0) == 0)
    def _():
        gu_ref[...] = jnp.zeros_like(gu_ref)
        gd_ref[...] = jnp.zeros_like(gd_ref)

    place = iota((RB, SLOTS), 1)
    hit = (tcol_ref[:, 0:1] == place) | (tcol_ref[:, 1:2] == place)
    grad = gn_ref[...] + mm(hit.astype(F32).astype(BF), back_ref[...])
    grad_mid = g_ref[...].astype(F32) + rms_back(grad, mid_ref[...], gain_ref[...])
    gm_ref[...] = grad_mid
    out_grad = grad_mid.astype(BF)
    grad_narrow = mm_nt(out_grad, u_ref[...]).astype(BF)
    mixed = mixed_ref[...]
    gu_ref[...] += 2.0 * mm_tn(nar_ref[...], out_grad)
    gd_ref[...] += mm_tn(grad_narrow, mixed)
    gx_ref[...] = (mm_nt(out_grad, w_ref[...]) + mm_nt(grad_narrow, d_ref[...])).astype(BF)


def settle_grad(tcol, back, gn, mid, g, gain, mixed, narrow, w, down, up):
    return call(
        settle_grad_body,
        (NB,),
        [
            (tcol, (RB, 128), rows),
            (back, None),
            (gn, (RB, D), rows),
            (mid, (RB, D), rows),
            (g, (RB, D), rows),
            (gain, None),
            (mixed, (RB, D), rows),
            (narrow, (RB, 128), rows),
            (w, None),
            (down, None),
            (up, None),
        ],
        [
            (out((T, D), F32), (RB, D), rows),
            (out((T, D), BF), (RB, D), rows),
            (out((128, D), F32), None),
            (out((128, D), F32), None),
        ],
        name="settle_grad",
        flops=2 * T * SLOTS * D + 2 * T * D * D * 2,
        nbytes=16e6,
    )


def attend_grad_body(
    q_ref, k_ref, v_ref, aug_ref, kf_ref, g_ref, mixed_ref, cos_ref, sin_ref,
    gq_ref, gk_ref, gv_ref, dqt,
):
    lane = iota((T, 128), 1)
    low = lane < 64
    lane6 = lane & 63
    q, k, v, kf, g = q_ref[...], k_ref[...], v_ref[...], kf_ref[...], g_ref[...]
    aug = aug_ref[0]
    product = g.astype(F32) * mixed_ref[...].astype(F32)
    d0 = jnp.sum(jnp.where(low, product, 0.0), axis=1, keepdims=True)
    d1 = jnp.sum(jnp.where(low, 0.0, product), axis=1, keepdims=True)
    a, b, c = three(-jnp.where(low, d1, d0))
    zero = jnp.zeros((T, 128), BF)
    ga = jnp.where(lane6 == 0, a, jnp.where(lane6 == 1, b, jnp.where(lane6 == 2, c, zero)))
    va = (lane6 < 3).astype(F32).astype(BF)
    qs = (jnp.where(low, q, aug), jnp.where(low, aug, q))
    ks = (jnp.where(low, k, kf), jnp.where(low, kf, k))
    vs = (jnp.where(low, v, va), jnp.where(low, va, v))
    gs = (jnp.where(low, g, ga), jnp.where(low, ga, g))
    kt = k.T
    tri = iota((RB, RB), 0) <= iota((RB, RB), 1)
    dqt[...] = jnp.zeros_like(dqt)
    low = low[:RB]
    for i in range(NB):
        here = slice(i * RB, (i + 1) * RB)
        dks = []
        dvs = []
        for h in range(2):
            dk = None
            for j in range(i, NB):
                there = slice(j * RB, (j + 1) * RB)
                p = jnp.exp2(mm_nt(ks[h][here], qs[h][there]) * LOG_SCALE)
                if i == j:
                    p = jnp.where(tri, p, 0.0)
                ds = (p * mm_nt(vs[h][here], gs[h][there])).astype(BF)
                p = p.astype(BF)
                dv_part = mm(p, g[there])
                dk_part = mm(ds, q[there])
                dk = dk_part if dk is None else dk + dk_part
                dv = dv_part if j == i else dv + dv_part
                half = slice(h * 64, (h + 1) * 64)
                dqt[half, there] += mm(kt[half, here], ds)
            dks.append(dk)
            dvs.append(dv)
        gv_ref[here, :] = jnp.where(low, dvs[0], dvs[1]).astype(BF)
        dk = (jnp.where(low, dks[0], dks[1]) * (1.0 / math.sqrt(HD))).astype(BF).astype(F32)
        gk_ref[here, :] = turn(dk, cos_ref[here, :], -sin_ref[here, :]).astype(BF)
    dq = (dqt[...].T * (1.0 / math.sqrt(HD))).astype(BF).astype(F32)
    gq_ref[...] = turn(dq, cos_ref[...], -sin_ref[...]).astype(BF)


def attend_grad(qkv, aug, kf, g, mixed, cos, sin):
    def col(j):
        return (0, j)

    return call(
        attend_grad_body,
        (PAIRS,),
        [
            (qkv, (T, 128), col),
            (qkv, (T, 128), lambda j: (0, PAIRS + j)),
            (qkv, (T, 128), lambda j: (0, 2 * PAIRS + j)),
            (aug, (1, T, 128), lambda j: (j, 0, 0)),
            (kf, None),
            (g, (T, 128), col),
            (mixed, (T, 128), col),
            (cos, None),
            (sin, None),
        ],
        [(out((T, D), BF), (T, 128), col)] * 3,
        [pltpu.VMEM((128, T), F32)],
        name="attend_grad",
        flops=12 * 10 * T * T * 128,
        nbytes=14e6,
    )


def project_grad_body(
    gq_ref, gk_ref, gv_ref, w_ref, d_ref, u_ref, n_ref, nar_ref, x_ref, gain_ref, gm_ref,
    gx_ref, gu_ref, gd_ref,
):
    @pl.when(pl.program_id(0) == 0)
    def _():
        gu_ref[...] = jnp.zeros_like(gu_ref)
        gd_ref[...] = jnp.zeros_like(gd_ref)

    grad = jnp.zeros((RB, D), F32)
    slim = jnp.zeros((RB, 128), F32)
    narrow = nar_ref[...]
    for block, ref in enumerate((gq_ref, gk_ref, gv_ref)):
        cols = slice(block * D, (block + 1) * D)
        g = ref[...]
        grad = grad + mm_nt(g, w_ref[:, cols])
        slim = slim + mm_nt(g, u_ref[:, cols])
        gu_ref[:, cols] += 2.0 * mm_tn(narrow, g)
    slim = slim.astype(BF)
    gd_ref[...] += mm_tn(slim, n_ref[...])
    grad = grad + mm_nt(slim, d_ref[...])
    gx_ref[...] = gm_ref[...] + rms_back(grad, x_ref[...].astype(F32), gain_ref[...])


def project_grad(gq, gk, gv, w, down, up, normed, narrow, x, gain, gm):
    return call(
        project_grad_body,
        (NB,),
        [
            (gq, (RB, D), rows),
            (gk, (RB, D), rows),
            (gv, (RB, D), rows),
            (w, None),
            (down, None),
            (up, None),
            (normed, (RB, D), rows),
            (narrow, (RB, 128), rows),
            (x, (RB, D), rows),
            (gain, None),
            (gm, (RB, D), rows),
        ],
        [
            (out((T, D), F32), (RB, D), rows),
            (out((128, 3 * D), F32), None),
            (out((128, D), F32), None),
        ],
        name="project_grad",
        flops=2 * T * D * 3 * D * 1.3,
        nbytes=22e6,
    )


def swap_pairs(axis):
    return [(0, 1), (1, 0)]


def gather_shared(w):
    half = w.shape[1] // 2
    core = lax.axis_index("c")
    mine = lax.dynamic_slice_in_dim(w, core * half, half, axis=1)
    mine = lax.all_gather(mine, ("z", "y"), axis=0, tiled=True)
    other = lax.ppermute(mine, "c", swap_pairs("c"))
    first = jnp.where(core == 0, mine, other)
    second = jnp.where(core == 0, other, mine)
    return jnp.concatenate([first, second], axis=1)


def gather_expert(w):
    count = w.shape[0]
    if count == 2:
        y = lax.axis_index("y")
        mine = lax.dynamic_index_in_dim(w, y, axis=0, keepdims=False)
        other = lax.ppermute(
            lax.dynamic_index_in_dim(w, 1 - y, axis=0, keepdims=False), "y", swap_pairs("y")
        )
        w = jnp.where(y == 0, jnp.stack([mine, other]), jnp.stack([other, mine]))
    elif count > 2:
        w = lax.all_to_all(w, "y", 0, 0, tiled=True)
    w = lax.all_gather(w, "z", axis=0, tiled=True)
    return w.reshape(-1, w.shape[-1])


def exchange(v):
    return lax.all_to_all(v, ("x", "c", "y"), split_axis=0, concat_axis=0, tiled=True)


def pad_to(v, shape):
    return jnp.pad(v, [(0, n - m) for m, n in zip(v.shape, shape)])


def per_device(
    tokens,
    segments,
    parents,
    adapter_of,
    routes,
    norm_gain,
    query_key_value_weight,
    output_weight,
    adapter_down,
    adapter_up,
    router,
    router_residual,
    const_proj,
    const_vec,
    w_gate_up,
    w_down,
    out_grad,
):
    qkv_full = []
    out_full = []
    gate_up_full = []
    down_full = []
    for layer in range(LAYERS):
        qkv_full.append(gather_shared(query_key_value_weight[layer]))
        out_full.append(gather_shared(output_weight[layer]))
        gate_up_full.append(gather_expert(w_gate_up[layer]))
        down_full.append(gather_expert(w_down[layer]))

    which = adapter_of[0]
    down_sel = lax.dynamic_index_in_dim(adapter_down, which, axis=2, keepdims=False)
    up_sel = lax.dynamic_index_in_dim(adapter_up, which, axis=2, keepdims=False)
    down_in = jnp.pad(
        down_sel[:, :3].transpose(0, 2, 1, 3).reshape(LAYERS, D, 3 * R), ((0, 0), (0, 0), (0, 80))
    )
    down_out = jnp.pad(down_sel[:, 3], ((0, 0), (0, 0), (0, 112)))
    up_t = 2.0 * up_sel.transpose(0, 1, 3, 2)
    up_in = jnp.zeros((LAYERS, 128, 3 * D), BF)
    for p in range(3):
        up_in = up_in.at[:, p * R : (p + 1) * R, p * D : (p + 1) * D].set(up_t[:, p])
    up_out = jnp.pad(up_t[:, 3], ((0, 0), (0, 112), (0, 0)))
    rcat = jnp.concatenate([router, const_proj[:, 0], const_proj[:, 1]], axis=2)
    rcat = jnp.pad(rcat, ((0, 0), (0, 0), (0, 112)))
    rcat_t = rcat.transpose(0, 2, 1)
    residual = pad_to(router_residual, (128, 128))
    residual_t = residual.T

    qf, kf, cos, sin, tcol, trow = prep(parents, segments.reshape(T, 1), routes)

    stream = tokens
    earlier = jnp.zeros((T, 128), F32)
    saved = []
    for layer in range(LAYERS):
        gain0 = norm_gain[layer, 0:1]
        gain1 = norm_gain[layer, 1:2]
        normed, narrow, qkv = project(
            stream, gain0, qkv_full[layer], down_in[layer], up_in[layer], cos, sin
        )
        mixed, aug = attend(qkv, qf, kf)
        mid, sent, logits, narrow_out = settle(
            stream, mixed, out_full[layer], down_out[layer], up_out[layer], gain1, rcat[layer],
            earlier, residual,
        )
        received = exchange(dispatch(trow, sent)).reshape(SLOTS, D)
        produced, gate, up = expert_forward(received, gate_up_full[layer], down_full[layer])
        returned = exchange(produced.reshape(NFFN, CAP, D)).reshape(SLOTS, D)
        following, c0, c1 = combine(tcol, returned, mid, logits, routes, gain1, const_vec[layer])
        saved.append((stream, normed, narrow, qkv, mixed, aug, mid, logits, narrow_out, gate, up, c0, c1))
        stream = following
        earlier = logits

    grad = out_grad
    grad_logits = jnp.zeros((T, 128), F32)
    tree_grads = [None] * LAYERS
    for layer in reversed(range(LAYERS)):
        x_in, normed, narrow, qkv, mixed, aug, mid, logits, narrow_out, gate, up, c0, c1 = saved[layer]
        gain0 = norm_gain[layer, 0:1]
        gain1 = norm_gain[layer, 1:2]
        a, b, grad_normed, grad_earlier = mix_grad(
            grad, mid, c0, c1, logits, routes, grad_logits, gain1, const_vec[layer], rcat_t[layer],
            residual_t,
        )
        slot_grads = exchange(dispatch_grad(trow, a, b)).reshape(SLOTS, D)
        grad_rows = expert_backward(slot_grads, gate, up, gate_up_full[layer], down_full[layer])
        back = exchange(grad_rows.reshape(NFFN, CAP, D)).reshape(SLOTS, D)
        grad_mid, grad_mixed, gu_out, gd_out = settle_grad(
            tcol, back, grad_normed, mid, grad, gain1, mixed, narrow_out, out_full[layer],
            down_out[layer], up_out[layer],
        )
        gq, gk, gv = attend_grad(qkv, aug, kf, grad_mixed, mixed, cos, sin)
        grad, gu_in, gd_in = project_grad(
            gq, gk, gv, qkv_full[layer], down_in[layer], up_in[layer], normed, narrow, x_in, gain0,
            grad_mid,
        )
        grad_logits = grad_earlier
        downs = [gd_in[p * R : (p + 1) * R] for p in range(3)] + [gd_out[:R]]
        ups = [gu_in[p * R : (p + 1) * R, p * D : (p + 1) * D] for p in range(3)] + [gu_out[:R]]
        tree_grads[layer] = jnp.stack([jnp.stack(downs), jnp.stack(ups)])

    compact = jnp.stack(tree_grads).astype(BF)
    ranks = lax.axis_size("z") * lax.axis_size("y")
    span = D // ranks
    pieces = compact.reshape(LAYERS, 2, 4, R, ranks, span).transpose(4, 0, 1, 2, 3, 5)
    pieces = lax.all_to_all(pieces, ("z", "y"), split_axis=0, concat_axis=0, tiled=True)
    owners = lax.all_gather(adapter_of, ("z", "y"), axis=0, tiled=True)
    pick = (owners[None, :] == jnp.arange(NA, dtype=jnp.int32)[:, None]).astype(F32)
    summed = jnp.dot(
        pick, pieces.reshape(ranks, -1).astype(F32), precision=HIGHEST
    ).astype(BF)
    groups = lax.axis_size("x") * lax.axis_size("c")
    each = NA // groups
    summed = lax.all_to_all(
        summed.reshape(groups, each, -1), ("x", "c"), split_axis=0, concat_axis=0, tiled=True
    )
    final = jnp.sum(summed.astype(F32), axis=0).reshape(each, LAYERS, 2, 4, R, span)
    final = final.transpose(2, 1, 3, 0, 5, 4)
    return (stream, grad, final[0], final[1])


def solution(mesh):
    owners, shards = mesh.shape["expert"], mesh.shape["shard"]
    each = NFFN // owners
    fine = jax.sharding.Mesh(
        mesh.devices.reshape(owners // 2, 2, shards // each, each), ("x", "c", "z", "y")
    )
    expert, shard = ("x", "c"), ("z", "y")
    both = expert + shard
    in_specs = (
        P(both, None),
        P(both, None),
        P(both, None),
        P(both),
        P(both, None),
        P(),
        P(None, shard, None),
        P(None, shard, None),
        P(),
        P(),
        P(),
        P(),
        P(),
        P(),
        P(None, expert, shard, None),
        P(None, expert, shard, None),
        P(both, None),
    )
    out_specs = (
        P(both, None),
        P(both, None),
        P(None, None, expert, shard, None),
        P(None, None, expert, shard, None),
    )
    return jax.shard_map(
        per_device, mesh=fine, in_specs=in_specs, out_specs=out_specs, check_vma=False
    )
```

```python
import math

import jax
import jax.numpy as jnp
from jax import lax
from jax.experimental import pallas as pl
from jax.experimental.pallas import tpu as pltpu
from jax.sharding import PartitionSpec as P

D = 768
HEADS = 12
HD = 64
FF = 2048
NFFN = 8
NEXP = 12
R = 16
NA = 8
NSEG = 13
LAYERS = 2
CAP = 192
T = 1024
SLOTS = NFFN * CAP
RB = 256
NB = T // RB
PAIRS = HEADS // 2
FC = 512
EPSILON = 1e-06
BIG = 2.0**100
LOG_SCALE = math.log2(math.e) / math.sqrt(HD)
F32 = jnp.float32
BF = jnp.bfloat16
HIGHEST = lax.Precision.HIGHEST
VMEM_BYTES = 56 * 1024 * 1024


def mm(a, b):
    return lax.dot_general(a, b, (((1,), (0,)), ((), ())), preferred_element_type=F32)


def mm_nt(a, b):
    return lax.dot_general(a, b, (((1,), (1,)), ((), ())), preferred_element_type=F32)


def mm_tn(a, b):
    return lax.dot_general(a, b, (((0,), (0,)), ((), ())), preferred_element_type=F32)


def mm_exact(a, b):
    return lax.dot_general(
        a, b, (((1,), (0,)), ((), ())), preferred_element_type=F32, precision=HIGHEST
    )


def iota(shape, axis):
    return lax.broadcasted_iota(jnp.int32, shape, axis)


def sigmoid(v):
    return 1.0 / (1.0 + jnp.exp(-v))


def call(body, grid, ins, outs, scratch=(), name=None, flops=0, nbytes=0):
    def spec(entry):
        if entry[1] == "smem":
            return pl.BlockSpec(memory_space=pltpu.SMEM)
        if entry[1] is None:
            shape = entry[0].shape
            return pl.BlockSpec(shape, lambda *_: (0,) * len(shape))
        return pl.BlockSpec(entry[1], entry[2])

    return pl.pallas_call(
        body,
        grid=grid,
        in_specs=[spec(e) for e in ins],
        out_specs=[spec(e) for e in outs],
        out_shape=[jax.ShapeDtypeStruct(e[0].shape, e[0].dtype) for e in outs],
        scratch_shapes=list(scratch),
        compiler_params=pltpu.CompilerParams(
            dimension_semantics=("arbitrary",) * len(grid), vmem_limit_bytes=VMEM_BYTES
        ),
        cost_estimate=pl.CostEstimate(
            flops=int(flops), bytes_accessed=int(nbytes), transcendentals=0
        ),
        name=name,
    )(*[e[0] for e in ins])


def out(shape, dtype):
    return jax.ShapeDtypeStruct(shape, dtype)


def rows(i):
    return (i, 0)


def three(v):
    high = v.astype(BF)
    rest = v - high.astype(F32)
    middle = rest.astype(BF)
    return high, middle, (rest - middle.astype(F32)).astype(BF)


def spread_lanes(v):
    a, b, c = (part.astype(F32) for part in three(v))
    total = a + pltpu.roll(b, 16, 1) + pltpu.roll(c, 32, 1)
    total = total + pltpu.roll(a, 48, 1) + pltpu.roll(b, 64, 1) + pltpu.roll(a, 80, 1)
    return total.astype(BF)


def stack_rows(w):
    a, b, c = three(w)
    return jnp.concatenate([a, a, a, b, b, c, jnp.zeros((32, w.shape[1]), BF)], axis=0)


def prep_body(
    par_ref, seg_ref, rt_ref, rc_ref, rct_ref, res_ref, rest_ref,
    qf_ref, kf_ref, cos_ref, sin_ref, tcol_ref, trow_ref, rs_ref, rts_ref, ress_ref, rests_ref, anc,
):
    for layer in range(LAYERS):
        a, b, c = (part.astype(F32) for part in three(rc_ref[layer]))
        rs_ref[layer] = (a + pltpu.roll(b, 16, 1) + pltpu.roll(c, 32, 1)).astype(BF)
        rts_ref[layer] = stack_rows(rct_ref[layer])
    ress_ref[...] = stack_rows(res_ref[...])
    rests_ref[...] = stack_rows(rest_ref[...])
    first = iota((1, 128), 1) & 63
    anc[...] = jnp.zeros_like(anc)
    anc[0:1, :] = (first == 0).astype(F32)
    for s in range(1, NSEG):
        above = anc[pl.ds(par_ref[0, s], 1), :]
        anc[s : s + 1, :] = jnp.maximum(above, (first == s).astype(F32))
    lane = iota((T, 128), 1)
    lane6 = lane & 63
    low = lane < 64
    member = (seg_ref[...] == lane6).astype(F32)
    ways = mm(jnp.where(low, member, 0.0).astype(BF), anc[...].astype(BF))
    qf_ref[...] = jnp.where(lane6 < NSEG, (ways - 1.0) * BIG, 0.0).astype(BF)
    ones = ((lane6 >= 16) & (lane6 < 19)).astype(F32)
    kf_ref[...] = (member + ones).astype(BF)
    hit0 = (rt_ref[:, 0:1] == lane).astype(F32)
    hit1 = (rt_ref[:, 1:2] == lane).astype(F32)
    hits = hit0 + hit1
    upto = (iota((T, T), 0) >= iota((T, T), 1)).astype(F32).astype(BF)
    seen = mm(upto, jnp.concatenate([member.astype(BF), hits.astype(BF)], axis=1))
    depth = jnp.sum(jnp.where(low, ways * seen[:, :128], 0.0), axis=1, keepdims=True) - 1.0
    before = seen[:, 128:] - hits

    def target(hit, route):
        slot = jnp.sum(hit * before, axis=1, keepdims=True)
        place = route.astype(F32) * CAP + slot
        return jnp.where(route < NFFN, place, 4.0 * SLOTS)

    t0 = target(hit0, rt_ref[:, 0:1])
    t1 = target(hit1, rt_ref[:, 1:2])
    both = jnp.where(lane == 0, t0, jnp.where(lane == 1, t1, 0.0))
    tcol_ref[...] = both.astype(jnp.int32)
    trow_ref[...] = both.T[0:8, :].astype(jnp.int32)
    inverse = jnp.exp((lane & 31).astype(F32) * (-math.log(10000.0) / 32.0))
    angle = depth * inverse
    cos_ref[...] = jnp.cos(angle)
    sine = jnp.sin(angle)
    sin_ref[...] = jnp.where((lane & 32) == 0, -sine, sine)


def prep(parents, seg_col, routes, rcat, rcat_t, residual, residual_t):
    return call(
        prep_body,
        (1,),
        [
            (parents, "smem"),
            (seg_col, None),
            (routes, None),
            (rcat, None),
            (rcat_t, None),
            (residual, None),
            (residual_t, None),
        ],
        [
            (out((T, 128), BF), None),
            (out((T, 128), BF), None),
            (out((T, 128), F32), None),
            (out((T, 128), F32), None),
            (out((T, 128), jnp.int32), None),
            (out((8, T), jnp.int32), None),
            (out((LAYERS, D, 128), BF), None),
            (out((LAYERS, 128, D), BF), None),
            (out((128, 128), BF), None),
            (out((128, 128), BF), None),
        ],
        [pltpu.VMEM((128, 128), F32)],
        name="prep",
        flops=2 * T * T * 256,
        nbytes=3e6,
    )


def turn(v, cos, sin):
    first = (iota(v.shape, 1) & 32) == 0
    other = jnp.where(first, pltpu.roll(v, 96, 1), pltpu.roll(v, 32, 1))
    return v * cos + other * sin


def project_rows(x, gain, w_ref, d_ref, u_ref, cos, sin, n_ref, nar_ref, qkv_ref):
    scale = lax.rsqrt(jnp.mean(x * x, axis=1, keepdims=True) + EPSILON)
    normed = (x * scale * gain).astype(BF)
    n_ref[...] = normed
    narrow = mm(normed, d_ref[...]).astype(BF)
    nar_ref[...] = narrow
    for block in range(3):
        cols = slice(block * D, (block + 1) * D)
        part = mm(normed, w_ref[block]) + mm(narrow, u_ref[:, cols])
        for j in range(PAIRS):
            piece = part[:, j * 128 : (j + 1) * 128]
            if block < 2:
                piece = turn(piece, cos, sin)
            at = block * D + j * 128
            qkv_ref[:, at : at + 128] = piece.astype(BF)


def project_body(x_ref, g_ref, w_ref, d_ref, u_ref, cos_ref, sin_ref, n_ref, nar_ref, qkv_ref):
    project_rows(
        x_ref[...].astype(F32),
        g_ref[...],
        w_ref,
        d_ref,
        u_ref,
        cos_ref[...],
        sin_ref[...],
        n_ref,
        nar_ref,
        qkv_ref,
    )


def project(x, gain, w, down, up, cos, sin):
    return call(
        project_body,
        (NB,),
        [
            (x, (RB, D), rows),
            (gain, None),
            (w, (3, D, D), lambda i: (0, 0, 0)),
            (down, None),
            (up, None),
            (cos, (RB, 128), rows),
            (sin, (RB, 128), rows),
        ],
        [
            (out((T, D), BF), (RB, D), rows),
            (out((T, 128), BF), (RB, 128), rows),
            (out((T, 3 * D), BF), (RB, 3 * D), rows),
        ],
        name="project",
        flops=2 * T * D * 3 * D,
        nbytes=12e6,
    )


def attend_body(q_ref, k_ref, v_ref, qf_ref, kf_ref, mixed_ref, aug_ref):
    low = iota((T, 128), 1) < 64
    k = k_ref[...]
    kf = kf_ref[...]
    v = v_ref[...]
    one = jnp.ones((T, 128), BF)
    keys = (jnp.where(low, k, kf), jnp.where(low, kf, k))
    values = (jnp.where(low, v, one), jnp.where(low, one, v))
    low = low[:RB]
    tri = iota((RB, RB), 0) >= iota((RB, RB), 1)
    lane6 = iota((RB, 128), 1) & 63
    for i in range(NB):
        here = slice(i * RB, (i + 1) * RB)
        q = q_ref[here, :]
        qf = qf_ref[here, :]
        tops = []
        outs = []
        for h in range(2):
            qa = jnp.where(low, q, qf) if h == 0 else jnp.where(low, qf, q)
            diag = jnp.where(tri, mm_nt(qa, keys[h][here]), -BIG)
            top = jnp.max(diag, axis=1, keepdims=True)
            if i:
                off = mm_nt(qa, keys[h][: i * RB])
                top = jnp.maximum(top, jnp.max(off, axis=1, keepdims=True))
            result = mm(jnp.exp2((diag - top) * LOG_SCALE).astype(BF), values[h][here])
            if i:
                weights = jnp.exp2((off - top) * LOG_SCALE).astype(BF)
                result = result + mm(weights, values[h][: i * RB])
            tops.append(top)
            outs.append(result)
        total = jnp.where(low, outs[1], outs[0])
        mixed = jnp.where(low, outs[0], outs[1]) / pltpu.roll(total, 64, 1)
        mixed_ref[here, :] = mixed.astype(BF)
        level = -(jnp.where(low, tops[1], tops[0]) + math.sqrt(HD) * jnp.log(total))
        a, b, c = three(level)
        aug_ref[0, here, :] = jnp.where(
            lane6 == 16, a, jnp.where(lane6 == 17, b, jnp.where(lane6 == 18, c, qf))
        )


def attend(qkv, qf, kf):
    return call(
        attend_body,
        (PAIRS,),
        [
            (qkv, (T, 128), lambda j: (0, j)),
            (qkv, (T, 128), lambda j: (0, PAIRS + j)),
            (qkv, (T, 128), lambda j: (0, 2 * PAIRS + j)),
            (qf, None),
            (kf, None),
        ],
        [
            (out((T, D), BF), (T, 128), lambda j: (0, j)),
            (out((PAIRS, T, 128), BF), (1, T, 128), lambda j: (j, 0, 0)),
        ],
        name="attend",
        flops=12 * 4 * T * T * 128,
        nbytes=8e6,
    )


def settle_body(
    x_ref, mixed_ref, w_ref, d_ref, u_ref, g_ref, rt_ref, earlier_ref, res_ref,
    mid_ref, sent_ref, lg_ref, nar_ref,
):
    mixed = mixed_ref[...]
    narrow = mm(mixed, d_ref[...]).astype(BF)
    nar_ref[...] = narrow
    mid = x_ref[...].astype(F32) + mm(mixed, w_ref[0]) + mm(narrow, u_ref[...])
    mid_ref[...] = mid
    scale = lax.rsqrt(jnp.mean(mid * mid, axis=1, keepdims=True) + EPSILON)
    normed = mid * scale * g_ref[...]
    sent_ref[...] = normed.astype(BF)
    a, b, c = three(normed)
    one, two, last = mm(a, rt_ref[...]), mm(b, rt_ref[...]), mm(c, rt_ref[...])
    total = one + two + last + pltpu.roll(one + two, 112, 1) + pltpu.roll(one, 96, 1)
    lane = iota((RB, 128), 1)
    earlier = jnp.where(lane < NEXP, earlier_ref[...], 0.0)
    extra = mm(spread_lanes(earlier), res_ref[...])
    lg_ref[...] = jnp.where(lane < 16, total + extra, 0.0)


def settle(x, mixed, w, down, up, gain, router, earlier, residual):
    return call(
        settle_body,
        (NB,),
        [
            (x, (RB, D), rows),
            (mixed, (RB, D), rows),
            (w, (1, D, D), lambda i: (3, 0, 0)),
            (down, None),
            (up, None),
            (gain, None),
            (router, None),
            (earlier, (RB, 128), rows),
            (residual, None),
        ],
        [
            (out((T, D), F32), (RB, D), rows),
            (out((T, D), BF), (RB, D), rows),
            (out((T, 128), F32), (RB, 128), rows),
            (out((T, 128), BF), (RB, 128), rows),
        ],
        name="settle",
        flops=2 * T * D * D * 2,
        nbytes=10e6,
    )


def dispatch_body(trow_ref, s_ref, o_ref):
    place = pl.program_id(0) * CAP + iota((CAP, T), 0)
    hit = (trow_ref[0:1, :] == place) | (trow_ref[1:2, :] == place)
    o_ref[0] = mm(hit.astype(F32).astype(BF), s_ref[...]).astype(BF)


def dispatch(trow, sent):
    return call(
        dispatch_body,
        (NFFN,),
        [(trow, None), (sent, None)],
        [(out((NFFN, CAP, D), BF), (1, CAP, D), lambda j: (j, 0, 0))],
        name="dispatch",
        flops=2 * T * SLOTS * D,
        nbytes=4e6,
    )[0]


def dispatch_grad_body(trow_ref, g_ref, lg_ref, rt_ref, o_ref, first, second):
    @pl.when(pl.program_id(0) == 0)
    def _():
        for i in range(NB):
            at = slice(i * RB, (i + 1) * RB)
            gates = mix_terms(lg_ref[at, :], rt_ref[at, :])[0]
            g = g_ref[at, :].astype(F32)
            first[at, :] = (gates[0] * g).astype(BF)
            second[at, :] = (gates[1] * g).astype(BF)

    place = pl.program_id(0) * CAP + iota((CAP, T), 0)
    hit0 = (trow_ref[0:1, :] == place).astype(F32).astype(BF)
    hit1 = (trow_ref[1:2, :] == place).astype(F32).astype(BF)
    o_ref[0] = (mm(hit0, first[...]) + mm(hit1, second[...])).astype(BF)


def dispatch_grad(trow, g, logits, routes):
    return call(
        dispatch_grad_body,
        (NFFN,),
        [(trow, None), (g, None), (logits, None), (routes, None)],
        [(out((NFFN, CAP, D), BF), (1, CAP, D), lambda j: (j, 0, 0))],
        [pltpu.VMEM((T, D), BF), pltpu.VMEM((T, D), BF)],
        name="dispatch_grad",
        flops=4 * T * SLOTS * D,
        nbytes=6e6,
    )[0]


PR = 2 * CAP
NP = NFFN // 2


def flip(bit, change):
    return bit + change - 2 * bit * change


def owner_at(p, h, each):
    x, c, y = (lax.axis_index(name) for name in ("x", "c", "y"))
    far, near = 1 - p // 2, 1 - p % 2
    c = flip(c, h)
    if each == 2:
        x, y = flip(x, far), flip(y, near)
    else:
        x = 2 * flip(x // 2, far) + flip(x % 2, near)
    return {"x": x, "c": c, "y": y}, (x * 2 + c) * each + y


PLACES = [(p, h) for p in range(NP) for h in range(2)]


def greet(each):
    barrier = pltpu.get_barrier_semaphore()
    for p, h in PLACES[:-2] + PLACES[-1:]:
        pl.semaphore_signal(
            barrier, inc=1, device_id=owner_at(p, h, each)[0], device_id_type=pl.DeviceIdType.MESH
        )
    pl.semaphore_wait(barrier, NFFN - 1)


def block_of(ref, p, h):
    return ref.at[p, h * CAP : (h + 1) * CAP, :]


def fetch_weights(split, gate_ups, down_ref, w1, w2, sems):
    copies = []
    if split:
        y = lax.axis_index("y")
        for side, ref in enumerate(gate_ups):
            mine = flip(y, side)
            count, size = ref.shape[0], ref.shape[1]
            for k in range(count):
                at = pl.multiple_of((2 * k + mine) * size, size)
                copies.append(
                    pltpu.make_async_copy(
                        ref.at[k], w1.at[pl.ds(at, size), :], sems.at[side * count + k]
                    )
                )
    else:
        copies.append(pltpu.make_async_copy(gate_ups[0], w1, sems.at[0]))
    copies.append(pltpu.make_async_copy(down_ref, w2, sems.at[8]))
    for copy in copies:
        copy.start()
    return copies


def fetch_blocks(source, rv, sems, each):
    copies = []
    for n, (p, h) in enumerate(PLACES):
        number = owner_at(p, h, each)[1]
        copies.append(pltpu.make_async_copy(source.at[number], block_of(rv, p, h), sems.at[n]))
    for copy in copies:
        copy.start()
    return copies


def give_back(pv, p, target, send, recv, each):
    me = owner_at(NP - 1, 0, each)[1]
    copies = []
    for h in range(2):
        n = 2 * p + h
        if (p, h) == (NP - 1, 0):
            copy = pltpu.make_async_copy(block_of(pv, p, h), target.at[me], send.at[n])
        else:
            copy = pltpu.make_async_remote_copy(
                src_ref=block_of(pv, p, h),
                dst_ref=target.at[me],
                send_sem=send.at[n],
                recv_sem=recv.at[n],
                device_id=owner_at(p, h, each)[0],
                device_id_type=pl.DeviceIdType.MESH,
            )
        copy.start()
        copies.append(copy)
    return copies


def chunk_at(f):
    return pl.multiple_of(f * FC, FC)


def forward_chunk(r, w1, w2, f):
    at = chunk_at(f)
    gate = mm(r, w1[:, pl.ds(at, FC)])
    up = mm(r, w1[:, pl.ds(pl.multiple_of(FF + f * FC, FC), FC)])
    active = (gate * sigmoid(gate) * up).astype(BF)
    return gate, up, mm(active, w2[pl.ds(at, FC), :])


def backward_chunk(g, gate, up, w1, w2, f):
    at = chunk_at(f)
    grad = mm_nt(g, w2[pl.ds(at, FC), :])
    s = sigmoid(gate)
    grad_s = grad * s
    grad_gate = (grad_s * up * (1.0 + gate * (1.0 - s))).astype(BF)
    grad_up = (grad_s * gate).astype(BF)
    return mm_nt(grad_gate, w1[:, pl.ds(at, FC)]) + mm_nt(
        grad_up, w1[:, pl.ds(pl.multiple_of(FF + f * FC, FC), FC)]
    )


def expert_body(split, each, *refs):
    count = 2 if split else 1
    gate_ups = refs[:count]
    down_ref, rec_ref, ret_ref, gate_ref, up_ref = refs[count : count + 5]
    w1, w2, rv, pv, gv, uv, acc, wsem, rsem, gsem, usem, send, recv = refs[count + 5 :]
    weights = fetch_weights(split, gate_ups, down_ref, w1, w2, wsem)
    blocks = fetch_blocks(rec_ref, rv, rsem, each)
    greet(each)
    for copy in weights + blocks:
        copy.wait()
    stores = []
    moves = []
    for p in range(NP):
        r = rv[p]
        acc[...] = jnp.zeros_like(acc)

        def step(f, carry):
            gate, up, part = forward_chunk(r, w1, w2, f)
            gv[p, :, pl.ds(chunk_at(f), FC)] = gate.astype(BF)
            uv[p, :, pl.ds(chunk_at(f), FC)] = up.astype(BF)
            acc[...] += part
            return carry

        lax.fori_loop(0, FF // FC, step, 0)
        pv[p] = acc[...].astype(BF)
        moves += give_back(pv, p, ret_ref, send, recv, each)
        for values, ref, sems in ((gv, gate_ref, gsem), (uv, up_ref, usem)):
            copy = pltpu.make_async_copy(values.at[p], ref.at[p], sems.at[p])
            copy.start()
            stores.append(copy)
    for copy in moves + stores:
        copy.wait()


def comm_call(body, ins, outs, scratch, name, number, flops, nbytes):
    return pl.pallas_call(
        body,
        in_specs=[pl.BlockSpec(memory_space=pl.ANY)] * len(ins),
        out_specs=[pl.BlockSpec(memory_space=pl.ANY)] * len(outs),
        out_shape=outs,
        scratch_shapes=scratch,
        compiler_params=pltpu.CompilerParams(
            vmem_limit_bytes=VMEM_BYTES, collective_id=number, has_side_effects=True
        ),
        cost_estimate=pl.CostEstimate(
            flops=int(flops), bytes_accessed=int(nbytes), transcendentals=0
        ),
        name=name,
    )(*ins)


DMA = pltpu.SemaphoreType.DMA
WEIGHTS = [pltpu.VMEM((D, 2 * FF), BF), pltpu.VMEM((FF, D), BF)]
ROWS = pltpu.VMEM((NP, PR, D), BF)
WIDE = pltpu.VMEM((NP, PR, FF), BF)
SUM = pltpu.VMEM((PR, D), F32)
BLOCKS = jax.ShapeDtypeStruct((NFFN, CAP, D), BF)
KEPT = jax.ShapeDtypeStruct((NP, PR, FF), BF)


def expert_forward(received, gate_ups, down, each):
    split = len(gate_ups) == 2

    def body(*refs):
        expert_body(split, each, *refs)

    return comm_call(
        body,
        [*gate_ups, down, received],
        [BLOCKS, KEPT, KEPT],
        WEIGHTS + [ROWS, ROWS, WIDE, WIDE, SUM]
        + [DMA((9,)), DMA((8,)), DMA((NP,)), DMA((NP,)), DMA((8,)), DMA((8,))],
        "expert_forward",
        1,
        2 * SLOTS * D * FF * 3,
        26e6,
    )


def expert_both_body(each, gate_up_ref, down_ref, rec_ref, sg_ref, ret_ref, gret_ref, *scratch):
    w1, w2, rv, sv, pv, qv, acc, gacc, wsem, rsem, ssem, send, recv, gsend, grecv = scratch
    weights = fetch_weights(False, [gate_up_ref], down_ref, w1, w2, wsem)
    blocks = fetch_blocks(rec_ref, rv, rsem, each) + fetch_blocks(sg_ref, sv, ssem, each)
    greet(each)
    for copy in weights + blocks:
        copy.wait()
    moves = []
    for p in range(NP):
        r = rv[p]
        g = sv[p]
        acc[...] = jnp.zeros_like(acc)
        gacc[...] = jnp.zeros_like(gacc)

        def step(f, carry):
            gate, up, part = forward_chunk(r, w1, w2, f)
            acc[...] += part
            gacc[...] += backward_chunk(g, gate, up, w1, w2, f)
            return carry

        lax.fori_loop(0, FF // FC, step, 0)
        pv[p] = acc[...].astype(BF)
        qv[p] = gacc[...].astype(BF)
        moves += give_back(pv, p, ret_ref, send, recv, each)
        moves += give_back(qv, p, gret_ref, gsend, grecv, each)
    for copy in moves:
        copy.wait()


def expert_both(received, slot_grads, gate_up, down, each):
    def body(*refs):
        expert_both_body(each, *refs)

    return comm_call(
        body,
        [gate_up, down, received, slot_grads],
        [BLOCKS, BLOCKS],
        WEIGHTS + [ROWS, ROWS, ROWS, ROWS, SUM, SUM]
        + [DMA((9,)), DMA((8,)), DMA((8,)), DMA((8,)), DMA((8,)), DMA((8,)), DMA((8,))],
        "expert_both",
        2,
        2 * SLOTS * D * FF * 6,
        26e6,
    )


def expert_back_body(split, each, *refs):
    count = 2 if split else 1
    gate_ups = refs[:count]
    down_ref, sg_ref, gate_ref, up_ref, ret_ref = refs[count : count + 5]
    w1, w2, rv, pv, gv, uv, acc, wsem, gsem, usem, dsend, drecv, send, recv = refs[count + 5 :]
    weights = fetch_weights(split, gate_ups, down_ref, w1, w2, wsem)
    for values, ref, sems in ((gv, gate_ref, gsem), (uv, up_ref, usem)):
        for p in range(NP):
            copy = pltpu.make_async_copy(ref.at[p], values.at[p], sems.at[p])
            copy.start()
            weights.append(copy)
    greet(each)
    arrivals = {}
    for p in (3, 1, 2, 0):
        for h in range(2):
            where, number = owner_at(p, h, each)
            n = 2 * p + h
            if (p, h) == (NP - 1, 0):
                copy = pltpu.make_async_copy(sg_ref.at[number], block_of(rv, p, h), dsend.at[n])
            else:
                copy = pltpu.make_async_remote_copy(
                    src_ref=sg_ref.at[number],
                    dst_ref=block_of(rv, p, h),
                    send_sem=dsend.at[n],
                    recv_sem=drecv.at[n],
                    device_id=where,
                    device_id_type=pl.DeviceIdType.MESH,
                )
            copy.start()
            arrivals[p, h] = copy
    for copy in weights:
        copy.wait()
    moves = []
    for p in (3, 1, 2, 0):
        for h in range(2):
            arrivals[p, h].wait()
        g = rv[p]
        acc[...] = jnp.zeros_like(acc)

        def step(f, carry):
            at = pl.ds(chunk_at(f), FC)
            gate = gv[p, :, at].astype(F32)
            up = uv[p, :, at].astype(F32)
            acc[...] += backward_chunk(g, gate, up, w1, w2, f)
            return carry

        lax.fori_loop(0, FF // FC, step, 0)
        pv[p] = acc[...].astype(BF)
        moves += give_back(pv, p, ret_ref, send, recv, each)
    for copy in moves:
        copy.wait()


def expert_backward(slot_grads, gate, up, gate_ups, down, each):
    split = len(gate_ups) == 2

    def body(*refs):
        expert_back_body(split, each, *refs)

    return comm_call(
        body,
        [*gate_ups, down, slot_grads, gate, up],
        [BLOCKS],
        WEIGHTS + [ROWS, ROWS, WIDE, WIDE, SUM]
        + [DMA((9,)), DMA((NP,)), DMA((NP,)), DMA((8,)), DMA((8,)), DMA((8,)), DMA((8,))],
        "expert_backward",
        3,
        2 * SLOTS * D * FF * 3,
        26e6,
    )[0]


def mix_terms(logits, routes):
    lane = iota(logits.shape, 1)

    def at(place):
        return jnp.sum(jnp.where(lane == place, logits, 0.0), axis=1, keepdims=True)

    r0, r1 = routes[:, 0:1], routes[:, 1:2]
    gap = at(r0) - at(r1)
    gates = (sigmoid(gap), sigmoid(-gap))

    def weight(e):
        return jnp.where(r0 == e, gates[0], 0.0) + jnp.where(r1 == e, gates[1], 0.0)

    shares = []
    for c in range(2):
        apart = logits[:, 12 + 2 * c : 13 + 2 * c] - logits[:, 13 + 2 * c : 14 + 2 * c]
        shares.append((sigmoid(apart), sigmoid(-apart)))
    weights = [weight(NFFN + 1), weight(NFFN + 2), weight(NFFN + 3)]
    return gates, weights, shares


def rms_scale(v):
    return lax.rsqrt(jnp.mean(v * v, axis=1, keepdims=True) + EPSILON)


def combine_body(tcol_ref, ret_ref, mid_ref, lg_ref, rt_ref, g_ref, cv_ref, x_ref, c0_ref, c1_ref):
    place = iota((RB, SLOTS), 1)
    back = ret_ref[...]
    chosen = []
    for k, c_ref in enumerate((c0_ref, c1_ref)):
        hit = (tcol_ref[:, k : k + 1] == place).astype(F32).astype(BF)
        value = mm(hit, back)
        c_ref[...] = value.astype(BF)
        chosen.append(value)
    mid = mid_ref[...]
    normed = mid * rms_scale(mid) * g_ref[...]
    gates, weights, shares = mix_terms(lg_ref[...], rt_ref[...])
    same = weights[0] + weights[1] * shares[0][0] + weights[2] * shares[1][0]
    moe = gates[0] * chosen[0] + gates[1] * chosen[1] + same * normed
    moe = moe + (weights[1] * shares[0][1]) * cv_ref[0:1, :]
    moe = moe + (weights[2] * shares[1][1]) * cv_ref[1:2, :]
    x_ref[...] = mid + moe


def combine(tcol, returned, mid, logits, routes, gain, const_vec):
    return call(
        combine_body,
        (NB,),
        [
            (tcol, (RB, 128), rows),
            (returned, None),
            (mid, (RB, D), rows),
            (logits, (RB, 128), rows),
            (routes, (RB, 2), rows),
            (gain, None),
            (const_vec, None),
        ],
        [
            (out((T, D), F32), (RB, D), rows),
            (out((T, D), BF), (RB, D), rows),
            (out((T, D), BF), (RB, D), rows),
        ],
        name="combine",
        flops=4 * T * SLOTS * D,
        nbytes=12e6,
    )


def mix_grad(g, mid, chosen, logits, routes, grad, gain, cv_ref, wt, res):
    normed = mid * rms_scale(mid) * gain
    gates, weights, shares = mix_terms(logits, routes)

    def along(v):
        return jnp.sum(g * v, axis=1, keepdims=True)

    same = along(normed)
    const = [along(cv_ref[c : c + 1, :]) for c in range(2)]
    gate_grads = []
    for k in range(2):
        r = routes[:, k : k + 1]
        value = along(chosen[k].astype(F32)) + jnp.where(r == NFFN + 1, same, 0.0)
        for c in range(2):
            mixed = shares[c][0] * same + shares[c][1] * const[c]
            value = value + jnp.where(r == NFFN + 2 + c, mixed, 0.0)
        gate_grads.append(value)
    slope = gates[0] * gates[1] * (gate_grads[0] - gate_grads[1])
    lane = iota((RB, 128), 1)
    grad = grad + jnp.where(lane == routes[:, 0:1], slope, 0.0)
    grad = grad - jnp.where(lane == routes[:, 1:2], slope, 0.0)
    only = grad
    for c in range(2):
        tilt = weights[1 + c] * shares[c][0] * shares[c][1] * (same - const[c])
        grad = grad + jnp.where(lane == 12 + 2 * c, tilt, 0.0)
        grad = grad - jnp.where(lane == 13 + 2 * c, tilt, 0.0)
    keep = weights[0] + weights[1] * shares[0][0] + weights[2] * shares[1][0]
    return mm(spread_lanes(grad), wt) + keep * g, mm(spread_lanes(only), res)


def rms_back(grad, v, gain):
    scale = rms_scale(v)
    inner = grad * gain
    return scale * inner - v * (scale**3 * jnp.mean(v * inner, axis=1, keepdims=True))


def settle_grad_body(
    tcol_ref, back_ref, mid_ref, g_ref, c0_ref, c1_ref, lg_ref, rt_ref, gl_ref, gain_ref, cv_ref,
    wt_ref, res_ref, mixed_ref, nar_ref, w_ref, d_ref, u_ref,
    gm_ref, gx_ref, gle_ref, gu_ref, gd_ref,
):
    @pl.when(pl.program_id(0) == 0)
    def _():
        gu_ref[...] = jnp.zeros_like(gu_ref)
        gd_ref[...] = jnp.zeros_like(gd_ref)

    mid = mid_ref[...]
    g = g_ref[...].astype(F32)
    gain = gain_ref[...]
    grad, gle_ref[...] = mix_grad(
        g, mid, (c0_ref[...], c1_ref[...]), lg_ref[...], rt_ref[...], gl_ref[...], gain, cv_ref,
        wt_ref[...], res_ref[...],
    )
    place = iota((RB, SLOTS), 1)
    hit = (tcol_ref[:, 0:1] == place) | (tcol_ref[:, 1:2] == place)
    grad = grad + mm(hit.astype(F32).astype(BF), back_ref[...])
    grad_mid = g + rms_back(grad, mid, gain)
    gm_ref[...] = grad_mid
    out_grad = grad_mid.astype(BF)
    grad_narrow = mm_nt(out_grad, u_ref[...]).astype(BF)
    mixed = mixed_ref[...]
    gu_ref[...] += 2.0 * mm_tn(nar_ref[...], out_grad)
    gd_ref[...] += mm_tn(grad_narrow, mixed)
    gx_ref[...] = (mm_nt(out_grad, w_ref[0]) + mm_nt(grad_narrow, d_ref[...])).astype(BF)


def settle_grad(
    tcol, back, mid, g, c0, c1, logits, routes, gl, gain, const_vec, router_t, residual_t,
    mixed, narrow, w, down, up,
):
    return call(
        settle_grad_body,
        (NB,),
        [
            (tcol, (RB, 128), rows),
            (back, None),
            (mid, (RB, D), rows),
            (g, (RB, D), rows),
            (c0, (RB, D), rows),
            (c1, (RB, D), rows),
            (logits, (RB, 128), rows),
            (routes, (RB, 2), rows),
            (gl, (RB, 128), rows),
            (gain, None),
            (const_vec, None),
            (router_t, None),
            (residual_t, None),
            (mixed, (RB, D), rows),
            (narrow, (RB, 128), rows),
            (w, (1, D, D), lambda i: (3, 0, 0)),
            (down, None),
            (up, None),
        ],
        [
            (out((T, D), F32), (RB, D), rows),
            (out((T, D), BF), (RB, D), rows),
            (out((T, 128), F32), (RB, 128), rows),
            (out((128, D), F32), None),
            (out((128, D), F32), None),
        ],
        name="settle_grad",
        flops=2 * T * SLOTS * D + 2 * T * D * D * 2,
        nbytes=22e6,
    )


def attend_grad_body(
    q_ref, k_ref, v_ref, aug_ref, kf_ref, g_ref, mixed_ref, cos_ref, sin_ref,
    gq_ref, gk_ref, gv_ref, dqt,
):
    lane = iota((T, 128), 1)
    low = lane < 64
    lane6 = lane & 63
    q, k, v, kf, g = q_ref[...], k_ref[...], v_ref[...], kf_ref[...], g_ref[...]
    aug = aug_ref[0]
    product = g.astype(F32) * mixed_ref[...].astype(F32)
    d0 = jnp.sum(jnp.where(low, product, 0.0), axis=1, keepdims=True)
    d1 = jnp.sum(jnp.where(low, 0.0, product), axis=1, keepdims=True)
    a, b, c = three(-jnp.where(low, d1, d0))
    zero = jnp.zeros((T, 128), BF)
    ga = jnp.where(lane6 == 0, a, jnp.where(lane6 == 1, b, jnp.where(lane6 == 2, c, zero)))
    va = (lane6 < 3).astype(F32).astype(BF)
    qs = (jnp.where(low, q, aug), jnp.where(low, aug, q))
    ks = (jnp.where(low, k, kf), jnp.where(low, kf, k))
    vs = (jnp.where(low, v, va), jnp.where(low, va, v))
    gs = (jnp.where(low, g, ga), jnp.where(low, ga, g))
    kt = k.T
    tri = iota((RB, RB), 0) <= iota((RB, RB), 1)
    dqt[...] = jnp.zeros_like(dqt)
    low = low[:RB]
    for i in range(NB):
        here = slice(i * RB, (i + 1) * RB)
        dks = []
        dvs = []
        for h in range(2):
            dk = None
            for j in range(i, NB):
                there = slice(j * RB, (j + 1) * RB)
                p = jnp.exp2(mm_nt(ks[h][here], qs[h][there]) * LOG_SCALE)
                if i == j:
                    p = jnp.where(tri, p, 0.0)
                ds = (p * mm_nt(vs[h][here], gs[h][there])).astype(BF)
                p = p.astype(BF)
                dv_part = mm(p, g[there])
                dk_part = mm(ds, q[there])
                dk = dk_part if dk is None else dk + dk_part
                dv = dv_part if j == i else dv + dv_part
                half = slice(h * 64, (h + 1) * 64)
                dqt[half, there] += mm(kt[half, here], ds)
            dks.append(dk)
            dvs.append(dv)
        gv_ref[here, :] = jnp.where(low, dvs[0], dvs[1]).astype(BF)
        dk = (jnp.where(low, dks[0], dks[1]) * (1.0 / math.sqrt(HD))).astype(BF).astype(F32)
        gk_ref[here, :] = turn(dk, cos_ref[here, :], -sin_ref[here, :]).astype(BF)
    dq = (dqt[...].T * (1.0 / math.sqrt(HD))).astype(BF).astype(F32)
    gq_ref[...] = turn(dq, cos_ref[...], -sin_ref[...]).astype(BF)


def attend_grad(qkv, aug, kf, g, mixed, cos, sin):
    def col(j):
        return (0, j)

    return call(
        attend_grad_body,
        (PAIRS,),
        [
            (qkv, (T, 128), col),
            (qkv, (T, 128), lambda j: (0, PAIRS + j)),
            (qkv, (T, 128), lambda j: (0, 2 * PAIRS + j)),
            (aug, (1, T, 128), lambda j: (j, 0, 0)),
            (kf, None),
            (g, (T, 128), col),
            (mixed, (T, 128), col),
            (cos, None),
            (sin, None),
        ],
        [(out((T, D), BF), (T, 128), col)] * 3,
        [pltpu.VMEM((128, T), F32)],
        name="attend_grad",
        flops=12 * 10 * T * T * 128,
        nbytes=14e6,
    )


def project_grad_body(
    gq_ref, gk_ref, gv_ref, w_ref, d_ref, u_ref, n_ref, nar_ref, x_ref, gain_ref, gm_ref,
    gx_ref, gu_ref, gd_ref,
):
    @pl.when(pl.program_id(0) == 0)
    def _():
        gu_ref[...] = jnp.zeros_like(gu_ref)
        gd_ref[...] = jnp.zeros_like(gd_ref)

    grad = jnp.zeros((RB, D), F32)
    slim = jnp.zeros((RB, 128), F32)
    narrow = nar_ref[...]
    for block, ref in enumerate((gq_ref, gk_ref, gv_ref)):
        cols = slice(block * D, (block + 1) * D)
        g = ref[...]
        grad = grad + mm_nt(g, w_ref[block])
        slim = slim + mm_nt(g, u_ref[:, cols])
        gu_ref[:, cols] += 2.0 * mm_tn(narrow, g)
    slim = slim.astype(BF)
    gd_ref[...] += mm_tn(slim, n_ref[...])
    grad = grad + mm_nt(slim, d_ref[...])
    gx_ref[...] = gm_ref[...] + rms_back(grad, x_ref[...].astype(F32), gain_ref[...])


def project_grad(gq, gk, gv, w, down, up, normed, narrow, x, gain, gm):
    return call(
        project_grad_body,
        (NB,),
        [
            (gq, (RB, D), rows),
            (gk, (RB, D), rows),
            (gv, (RB, D), rows),
            (w, (3, D, D), lambda i: (0, 0, 0)),
            (down, None),
            (up, None),
            (normed, (RB, D), rows),
            (narrow, (RB, 128), rows),
            (x, (RB, D), rows),
            (gain, None),
            (gm, (RB, D), rows),
        ],
        [
            (out((T, D), F32), (RB, D), rows),
            (out((128, 3 * D), F32), None),
            (out((128, D), F32), None),
        ],
        name="project_grad",
        flops=2 * T * D * 3 * D * 1.3,
        nbytes=22e6,
    )


PIECE = 96


def shared_body(p_ref, o_ref, local, zs, zr, ys, yr, xs, xr, cs, cr):
    x, c, z, y = (lax.axis_index(name) for name in ("x", "c", "z", "y"))
    mine, theirs = 2 * x + c, 2 * (1 - x) + c

    def spot(quarter, column, j):
        at = (2 * ((z + 4 - j) % 4) + column) * PIECE
        return o_ref.at[quarter, pl.ds(pl.multiple_of(at, PIECE), PIECE), :]

    others = [{"z": (z + d) % 4} for d in range(1, 4)]
    others += [{"y": 1 - y}, {"x": 1 - x}, {"c": 1 - c}]
    barrier = pltpu.get_barrier_semaphore()
    for who in others:
        pl.semaphore_signal(barrier, inc=1, device_id=who, device_id_type=pl.DeviceIdType.MESH)
    pl.semaphore_wait(barrier, len(others))

    started = []

    def send(source, target, who, send_sem, recv_sem):
        copy = pltpu.make_async_remote_copy(
            src_ref=source,
            dst_ref=target,
            send_sem=send_sem,
            recv_sem=recv_sem,
            device_id=who,
            device_id_type=pl.DeviceIdType.MESH,
        )
        copy.start()
        started.append(copy)
        return copy

    core_copies = []

    def to_core(source, target):
        n = len(core_copies)
        core_copies.append(send(source, target, others[5], cs.at[n], cr.at[n]))

    own = pltpu.make_async_copy(p_ref, spot(mine, y, 0), local.at[0])
    own.start()
    z_copies = [
        send(p_ref, spot(mine, y, 0), others[d], zs.at[d], zr.at[d]) for d in range(3)
    ]
    y_copies = [None] * 6
    x_copies = [None] * 6

    def along_y(n, source, target):
        y_copies[n] = send(source, target, others[3], ys.at[n], yr.at[n])

    def along_x(n, source, target):
        x_copies[n] = send(source, target, others[4], xs.at[n], xr.at[n])

    along_y(0, p_ref, spot(mine, y, 0))
    along_x(0, p_ref, spot(mine, y, 0))
    to_core(p_ref, spot(mine, y, 0))
    for j in range(1, 4):
        z_copies[j - 1].wait_recv()
        piece = spot(mine, y, j)
        along_y(j, piece, piece)
        along_x(j, piece, piece)
        to_core(piece, piece)
    for j in range(4):
        y_copies[j].wait_recv()
        piece = spot(mine, 1 - y, j)
        if j < 2:
            along_x(4 + j, piece, piece)
        to_core(piece, piece)
        x_copies[j].wait_recv()
        piece = spot(theirs, y, j)
        if j >= 2:
            along_y(2 + j, piece, piece)
        to_core(piece, piece)
    for j in range(4):
        (x_copies[4 + j] if j < 2 else y_copies[2 + j]).wait_recv()
        piece = spot(theirs, 1 - y, j)
        to_core(piece, piece)
    for copy in core_copies:
        copy.wait_recv()
    own.wait()
    for copy in started:
        copy.wait_send()


def gather_shared(qkv, output):
    rows_here = qkv.shape[0]
    parts = jnp.concatenate([qkv.reshape(rows_here, 3, D).transpose(1, 0, 2), output[None]])
    sizes = tuple(lax.axis_size(name) for name in ("x", "c", "z", "y"))
    if sizes != (2, 2, 4, 2):
        whole = lax.all_gather(parts, ("z", "y"), axis=1, tiled=True)
        return whole
    quarter = 2 * lax.axis_index("x") + lax.axis_index("c")
    piece = lax.dynamic_index_in_dim(parts, quarter, axis=0, keepdims=False)
    return comm_call(
        shared_body,
        [piece],
        [jax.ShapeDtypeStruct((4, D, D), BF)],
        [DMA((1,)), DMA((3,)), DMA((3,)), DMA((6,)), DMA((6,)), DMA((6,)), DMA((6,)), DMA((16,)), DMA((16,))],
        "gather_shared",
        0,
        0,
        5e7,
    )[0]


def gather_expert(w, split):
    count = w.shape[0]
    if count == 2:
        y = lax.axis_index("y")
        mine = lax.dynamic_index_in_dim(w, y, axis=0, keepdims=False)
        other = lax.ppermute(
            lax.dynamic_index_in_dim(w, 1 - y, axis=0, keepdims=False), "y", [(0, 1), (1, 0)]
        )
        if split:
            return [lax.all_gather(part, "z", axis=0) for part in (mine, other)]
        w = jnp.where(y == 0, jnp.stack([mine, other]), jnp.stack([other, mine]))
    w = lax.all_gather(w, "z", axis=0, tiled=True)
    return [w.reshape(-1, w.shape[-1])]


def exchange(v):
    return lax.all_to_all(v, ("x", "c", "y"), split_axis=0, concat_axis=0, tiled=True)


def pad_to(v, shape):
    return jnp.pad(v, [(0, n - m) for m, n in zip(v.shape, shape)])


def per_device(
    tokens,
    segments,
    parents,
    adapter_of,
    routes,
    norm_gain,
    query_key_value_weight,
    output_weight,
    adapter_down,
    adapter_up,
    router,
    router_residual,
    const_proj,
    const_vec,
    w_gate_up,
    w_down,
    out_grad,
):
    each = w_gate_up.shape[1]
    gate_up_full = []
    down_full = []
    for layer in range(LAYERS):
        gate_up_full.append(gather_expert(w_gate_up[layer], layer == 0))
        down_full.append(gather_expert(w_down[layer], False)[0])
    shared = [gather_shared(query_key_value_weight[0], output_weight[0])]

    which = adapter_of[0]
    down_sel = lax.dynamic_index_in_dim(adapter_down, which, axis=2, keepdims=False)
    up_sel = lax.dynamic_index_in_dim(adapter_up, which, axis=2, keepdims=False)
    down_in = jnp.pad(
        down_sel[:, :3].transpose(0, 2, 1, 3).reshape(LAYERS, D, 3 * R), ((0, 0), (0, 0), (0, 80))
    )
    down_out = jnp.pad(down_sel[:, 3], ((0, 0), (0, 0), (0, 112)))
    up_t = 2.0 * up_sel.transpose(0, 1, 3, 2)
    up_in = jnp.zeros((LAYERS, 128, 3 * D), BF)
    for p in range(3):
        up_in = up_in.at[:, p * R : (p + 1) * R, p * D : (p + 1) * D].set(up_t[:, p])
    up_out = jnp.pad(up_t[:, 3], ((0, 0), (0, 112), (0, 0)))
    rcat = jnp.concatenate([router, const_proj[:, 0], const_proj[:, 1]], axis=2)
    rcat = jnp.pad(rcat, ((0, 0), (0, 0), (0, 112)))
    rcat_t = rcat[:, :, :16].transpose(0, 2, 1)
    residual = pad_to(router_residual, (16, 128))
    residual_t = pad_to(router_residual.T, (16, 128))

    qf, kf, cos, sin, tcol, trow, router_s, router_ts, residual_s, residual_ts = prep(
        parents, segments.reshape(T, 1), routes, rcat, rcat_t, residual, residual_t
    )

    stream = tokens
    earlier = jnp.zeros((T, 128), F32)
    saved = []
    for layer in range(LAYERS):
        gain0 = norm_gain[layer, 0:1]
        gain1 = norm_gain[layer, 1:2]
        normed, narrow, qkv = project(
            stream, gain0, shared[layer], down_in[layer], up_in[layer], cos, sin
        )
        mixed, aug = attend(qkv, qf, kf)
        mid, sent, logits, narrow_out = settle(
            stream, mixed, shared[layer], down_out[layer], up_out[layer], gain1, router_s[layer],
            earlier, residual_s,
        )
        received = exchange(dispatch(trow, sent))
        if layer == 0:
            later = lax.optimization_barrier(
                (query_key_value_weight[1], output_weight[1], logits)
            )
            shared.append(gather_shared(later[0], later[1]))
            returned, gate, up = expert_forward(received, gate_up_full[0], down_full[0], each)
        else:
            slot_grads = exchange(dispatch_grad(trow, out_grad, logits, routes))
            returned, back = expert_both(
                received, slot_grads, gate_up_full[1][0], down_full[1], each
            )
        following, c0, c1 = combine(
            tcol, returned.reshape(SLOTS, D), mid, logits, routes, gain1, const_vec[layer]
        )
        saved.append((stream, normed, narrow, qkv, mixed, aug, mid, logits, narrow_out, c0, c1))
        stream = following
        earlier = logits

    grad = out_grad
    grad_logits = jnp.zeros((T, 128), F32)
    tree_grads = [None] * LAYERS
    for layer in reversed(range(LAYERS)):
        x_in, normed, narrow, qkv, mixed, aug, mid, logits, narrow_out, c0, c1 = saved[layer]
        gain0 = norm_gain[layer, 0:1]
        gain1 = norm_gain[layer, 1:2]
        if layer == 0:
            back = expert_backward(
                dispatch_grad(trow, grad, logits, routes), gate, up, gate_up_full[0], down_full[0],
                each,
            )
        grad_mid, grad_mixed, grad_earlier, gu_out, gd_out = settle_grad(
            tcol, back.reshape(SLOTS, D), mid, grad, c0, c1, logits, routes, grad_logits, gain1,
            const_vec[layer], router_ts[layer], residual_ts, mixed, narrow_out, shared[layer],
            down_out[layer], up_out[layer],
        )
        gq, gk, gv = attend_grad(qkv, aug, kf, grad_mixed, mixed, cos, sin)
        grad, gu_in, gd_in = project_grad(
            gq, gk, gv, shared[layer], down_in[layer], up_in[layer], normed, narrow, x_in, gain0,
            grad_mid,
        )
        grad_logits = grad_earlier
        downs = [gd_in[p * R : (p + 1) * R] for p in range(3)] + [gd_out[:R]]
        ups = [gu_in[p * R : (p + 1) * R, p * D : (p + 1) * D] for p in range(3)] + [gu_out[:R]]
        tree_grads[layer] = jnp.stack([jnp.stack(downs), jnp.stack(ups)])

    compact = jnp.stack(tree_grads).astype(BF)
    ranks = lax.axis_size("z") * lax.axis_size("y")
    span = D // ranks
    pieces = compact.reshape(LAYERS, 2, 4, R, ranks, span).transpose(4, 0, 1, 2, 3, 5)
    pieces = lax.all_to_all(pieces, ("z", "y"), split_axis=0, concat_axis=0, tiled=True)
    owners = lax.all_gather(adapter_of, ("z", "y"), axis=0, tiled=True)
    pick = (owners[None, :] == jnp.arange(NA, dtype=jnp.int32)[:, None]).astype(F32)
    summed = jnp.dot(
        pick, pieces.reshape(ranks, -1).astype(F32), precision=HIGHEST
    ).astype(BF)
    groups = lax.axis_size("x") * lax.axis_size("c")
    each = NA // groups
    summed = lax.all_to_all(
        summed.reshape(groups, each, -1), ("x", "c"), split_axis=0, concat_axis=0, tiled=True
    )
    final = jnp.sum(summed.astype(F32), axis=0).reshape(each, LAYERS, 2, 4, R, span)
    final = final.transpose(2, 1, 3, 0, 5, 4)
    return (stream, grad, final[0], final[1])


def solution(mesh):
    owners, shards = mesh.shape["expert"], mesh.shape["shard"]
    each = NFFN // owners
    fine = jax.sharding.Mesh(
        mesh.devices.reshape(owners // 2, 2, shards // each, each), ("x", "c", "z", "y")
    )
    expert, shard = ("x", "c"), ("z", "y")
    both = expert + shard
    in_specs = (
        P(both, None),
        P(both, None),
        P(both, None),
        P(both),
        P(both, None),
        P(),
        P(None, shard, None),
        P(None, shard, None),
        P(),
        P(),
        P(),
        P(),
        P(),
        P(),
        P(None, expert, shard, None),
        P(None, expert, shard, None),
        P(both, None),
    )
    out_specs = (
        P(both, None),
        P(both, None),
        P(None, None, expert, shard, None),
        P(None, None, expert, shard, None),
    )
    return jax.shard_map(
        per_device, mesh=fine, in_specs=in_specs, out_specs=out_specs, check_vma=False
    )
```

```python
import math

import jax
import jax.numpy as jnp
from jax import lax
from jax.experimental import pallas as pl
from jax.experimental.pallas import tpu as pltpu
from jax.sharding import PartitionSpec as P

D = 768
HEADS = 12
HD = 64
FF = 2048
NFFN = 8
NEXP = 12
R = 16
NA = 8
NSEG = 13
LAYERS = 2
CAP = 192
T = 1024
SLOTS = NFFN * CAP
RB = 256
NB = T // RB
PAIRS = HEADS // 2
FC = 512
EPSILON = 1e-06
BIG = 2.0**100
LOG_SCALE = math.log2(math.e) / math.sqrt(HD)
F32 = jnp.float32
BF = jnp.bfloat16
HIGHEST = lax.Precision.HIGHEST
VMEM_BYTES = 56 * 1024 * 1024


def mm(a, b):
    return lax.dot_general(a, b, (((1,), (0,)), ((), ())), preferred_element_type=F32)


def mm_nt(a, b):
    return lax.dot_general(a, b, (((1,), (1,)), ((), ())), preferred_element_type=F32)


def mm_tn(a, b):
    return lax.dot_general(a, b, (((0,), (0,)), ((), ())), preferred_element_type=F32)


def mm_exact(a, b):
    return lax.dot_general(
        a, b, (((1,), (0,)), ((), ())), preferred_element_type=F32, precision=HIGHEST
    )


def iota(shape, axis):
    return lax.broadcasted_iota(jnp.int32, shape, axis)


def sigmoid(v):
    return 1.0 / (1.0 + jnp.exp(-v))


def call(body, grid, ins, outs, scratch=(), name=None, flops=0, nbytes=0):
    def spec(entry):
        if entry[1] == "smem":
            return pl.BlockSpec(memory_space=pltpu.SMEM)
        if entry[1] is None:
            shape = entry[0].shape
            return pl.BlockSpec(shape, lambda *_: (0,) * len(shape))
        return pl.BlockSpec(entry[1], entry[2])

    return pl.pallas_call(
        body,
        grid=grid,
        in_specs=[spec(e) for e in ins],
        out_specs=[spec(e) for e in outs],
        out_shape=[jax.ShapeDtypeStruct(e[0].shape, e[0].dtype) for e in outs],
        scratch_shapes=list(scratch),
        compiler_params=pltpu.CompilerParams(
            dimension_semantics=("arbitrary",) * len(grid), vmem_limit_bytes=VMEM_BYTES
        ),
        cost_estimate=pl.CostEstimate(
            flops=int(flops), bytes_accessed=int(nbytes), transcendentals=0
        ),
        name=name,
    )(*[e[0] for e in ins])


def out(shape, dtype):
    return jax.ShapeDtypeStruct(shape, dtype)


def rows(i):
    return (i, 0)


def three(v):
    high = v.astype(BF)
    rest = v - high.astype(F32)
    middle = rest.astype(BF)
    return high, middle, (rest - middle.astype(F32)).astype(BF)


def spread_lanes(v):
    a, b, c = (part.astype(F32) for part in three(v))
    total = a + pltpu.roll(b, 16, 1) + pltpu.roll(c, 32, 1)
    total = total + pltpu.roll(a, 48, 1) + pltpu.roll(b, 64, 1) + pltpu.roll(a, 80, 1)
    return total.astype(BF)


def stack_rows(w):
    a, b, c = three(w)
    return jnp.concatenate([a, a, a, b, b, c, jnp.zeros((32, w.shape[1]), BF)], axis=0)


def prep_body(
    par_ref, seg_ref, rt_ref, rc_ref, rct_ref, res_ref, rest_ref,
    qf_ref, kf_ref, cos_ref, sin_ref, tcol_ref, trow_ref, rs_ref, rts_ref, ress_ref, rests_ref, anc,
):
    for layer in range(LAYERS):
        a, b, c = (part.astype(F32) for part in three(rc_ref[layer]))
        rs_ref[layer] = (a + pltpu.roll(b, 16, 1) + pltpu.roll(c, 32, 1)).astype(BF)
        rts_ref[layer] = stack_rows(rct_ref[layer])
    ress_ref[...] = stack_rows(res_ref[...])
    rests_ref[...] = stack_rows(rest_ref[...])
    first = iota((1, 128), 1) & 63
    anc[...] = jnp.zeros_like(anc)
    anc[0:1, :] = (first == 0).astype(F32)
    for s in range(1, NSEG):
        above = anc[pl.ds(par_ref[0, s], 1), :]
        anc[s : s + 1, :] = jnp.maximum(above, (first == s).astype(F32))
    lane = iota((T, 128), 1)
    lane6 = lane & 63
    low = lane < 64
    member = (seg_ref[...] == lane6).astype(F32)
    ways = mm(jnp.where(low, member, 0.0).astype(BF), anc[...].astype(BF))
    qf_ref[...] = jnp.where(lane6 < NSEG, (ways - 1.0) * BIG, 0.0).astype(BF)
    ones = ((lane6 >= 16) & (lane6 < 19)).astype(F32)
    kf_ref[...] = (member + ones).astype(BF)
    hit0 = (rt_ref[:, 0:1] == lane).astype(F32)
    hit1 = (rt_ref[:, 1:2] == lane).astype(F32)
    hits = hit0 + hit1
    upto = (iota((T, T), 0) >= iota((T, T), 1)).astype(F32).astype(BF)
    seen = mm(upto, jnp.concatenate([member.astype(BF), hits.astype(BF)], axis=1))
    depth = jnp.sum(jnp.where(low, ways * seen[:, :128], 0.0), axis=1, keepdims=True) - 1.0
    before = seen[:, 128:] - hits

    def target(hit, route):
        slot = jnp.sum(hit * before, axis=1, keepdims=True)
        place = route.astype(F32) * CAP + slot
        return jnp.where(route < NFFN, place, 4.0 * SLOTS)

    t0 = target(hit0, rt_ref[:, 0:1])
    t1 = target(hit1, rt_ref[:, 1:2])
    both = jnp.where(lane == 0, t0, jnp.where(lane == 1, t1, 0.0))
    tcol_ref[...] = both.astype(jnp.int32)
    trow_ref[...] = both.T[0:8, :].astype(jnp.int32)
    inverse = jnp.exp((lane & 31).astype(F32) * (-math.log(10000.0) / 32.0))
    angle = depth * inverse
    cos_ref[...] = jnp.cos(angle)
    sine = jnp.sin(angle)
    sin_ref[...] = jnp.where((lane & 32) == 0, -sine, sine)


def prep(parents, seg_col, routes, rcat, rcat_t, residual, residual_t):
    return call(
        prep_body,
        (1,),
        [
            (parents, "smem"),
            (seg_col, None),
            (routes, None),
            (rcat, None),
            (rcat_t, None),
            (residual, None),
            (residual_t, None),
        ],
        [
            (out((T, 128), BF), None),
            (out((T, 128), BF), None),
            (out((T, 128), F32), None),
            (out((T, 128), F32), None),
            (out((T, 128), jnp.int32), None),
            (out((8, T), jnp.int32), None),
            (out((LAYERS, D, 128), BF), None),
            (out((LAYERS, 128, D), BF), None),
            (out((128, 128), BF), None),
            (out((128, 128), BF), None),
        ],
        [pltpu.VMEM((128, 128), F32)],
        name="prep",
        flops=2 * T * T * 256,
        nbytes=3e6,
    )


def turn(v, cos, sin):
    first = (iota(v.shape, 1) & 32) == 0
    other = jnp.where(first, pltpu.roll(v, 96, 1), pltpu.roll(v, 32, 1))
    return v * cos + other * sin


def project_rows(x, gain, w_ref, d_ref, u_ref, cos, sin, n_ref, nar_ref, qkv_ref):
    scale = lax.rsqrt(jnp.mean(x * x, axis=1, keepdims=True) + EPSILON)
    normed = (x * scale * gain).astype(BF)
    n_ref[...] = normed
    narrow = mm(normed, d_ref[...]).astype(BF)
    nar_ref[...] = narrow
    for block in range(3):
        cols = slice(block * D, (block + 1) * D)
        part = mm(normed, w_ref[block]) + mm(narrow, u_ref[:, cols])
        for j in range(PAIRS):
            piece = part[:, j * 128 : (j + 1) * 128]
            if block < 2:
                piece = turn(piece, cos, sin)
            at = block * D + j * 128
            qkv_ref[:, at : at + 128] = piece.astype(BF)


def project_body(x_ref, g_ref, w_ref, d_ref, u_ref, cos_ref, sin_ref, n_ref, nar_ref, qkv_ref):
    project_rows(
        x_ref[...].astype(F32),
        g_ref[...],
        w_ref,
        d_ref,
        u_ref,
        cos_ref[...],
        sin_ref[...],
        n_ref,
        nar_ref,
        qkv_ref,
    )


def project(x, gain, w, down, up, cos, sin):
    return call(
        project_body,
        (NB,),
        [
            (x, (RB, D), rows),
            (gain, None),
            (w, (3, D, D), lambda i: (0, 0, 0)),
            (down, None),
            (up, None),
            (cos, (RB, 128), rows),
            (sin, (RB, 128), rows),
        ],
        [
            (out((T, D), BF), (RB, D), rows),
            (out((T, 128), BF), (RB, 128), rows),
            (out((T, 3 * D), BF), (RB, 3 * D), rows),
        ],
        name="project",
        flops=2 * T * D * 3 * D,
        nbytes=12e6,
    )


def attend_body(q_ref, k_ref, v_ref, qf_ref, kf_ref, mixed_ref, aug_ref):
    low = iota((T, 128), 1) < 64
    k = k_ref[...]
    kf = kf_ref[...]
    v = v_ref[...]
    one = jnp.ones((T, 128), BF)
    keys = (jnp.where(low, k, kf), jnp.where(low, kf, k))
    values = (jnp.where(low, v, one), jnp.where(low, one, v))
    low = low[:RB]
    tri = iota((RB, RB), 0) >= iota((RB, RB), 1)
    lane6 = iota((RB, 128), 1) & 63
    for i in range(NB):
        here = slice(i * RB, (i + 1) * RB)
        q = q_ref[here, :]
        qf = qf_ref[here, :]
        tops = []
        outs = []
        for h in range(2):
            qa = jnp.where(low, q, qf) if h == 0 else jnp.where(low, qf, q)
            diag = jnp.where(tri, mm_nt(qa, keys[h][here]), -BIG)
            top = jnp.max(diag, axis=1, keepdims=True)
            if i:
                off = mm_nt(qa, keys[h][: i * RB])
                top = jnp.maximum(top, jnp.max(off, axis=1, keepdims=True))
            result = mm(jnp.exp2((diag - top) * LOG_SCALE).astype(BF), values[h][here])
            if i:
                weights = jnp.exp2((off - top) * LOG_SCALE).astype(BF)
                result = result + mm(weights, values[h][: i * RB])
            tops.append(top)
            outs.append(result)
        total = jnp.where(low, outs[1], outs[0])
        mixed = jnp.where(low, outs[0], outs[1]) / pltpu.roll(total, 64, 1)
        mixed_ref[here, :] = mixed.astype(BF)
        level = -(jnp.where(low, tops[1], tops[0]) + math.sqrt(HD) * jnp.log(total))
        a, b, c = three(level)
        aug_ref[0, here, :] = jnp.where(
            lane6 == 16, a, jnp.where(lane6 == 17, b, jnp.where(lane6 == 18, c, qf))
        )


def attend(qkv, qf, kf):
    return call(
        attend_body,
        (PAIRS,),
        [
            (qkv, (T, 128), lambda j: (0, j)),
            (qkv, (T, 128), lambda j: (0, PAIRS + j)),
            (qkv, (T, 128), lambda j: (0, 2 * PAIRS + j)),
            (qf, None),
            (kf, None),
        ],
        [
            (out((T, D), BF), (T, 128), lambda j: (0, j)),
            (out((PAIRS, T, 128), BF), (1, T, 128), lambda j: (j, 0, 0)),
        ],
        name="attend",
        flops=12 * 4 * T * T * 128,
        nbytes=8e6,
    )


def settle_body(
    x_ref, mixed_ref, w_ref, d_ref, u_ref, g_ref, rt_ref, earlier_ref, res_ref,
    mid_ref, sent_ref, lg_ref, nar_ref,
):
    mixed = mixed_ref[...]
    narrow = mm(mixed, d_ref[...]).astype(BF)
    nar_ref[...] = narrow
    mid = x_ref[...].astype(F32) + mm(mixed, w_ref[0]) + mm(narrow, u_ref[...])
    mid_ref[...] = mid
    scale = lax.rsqrt(jnp.mean(mid * mid, axis=1, keepdims=True) + EPSILON)
    normed = mid * scale * g_ref[...]
    sent_ref[...] = normed.astype(BF)
    a, b, c = three(normed)
    one, two, last = mm(a, rt_ref[...]), mm(b, rt_ref[...]), mm(c, rt_ref[...])
    total = one + two + last + pltpu.roll(one + two, 112, 1) + pltpu.roll(one, 96, 1)
    lane = iota((RB, 128), 1)
    earlier = jnp.where(lane < NEXP, earlier_ref[...], 0.0)
    extra = mm(spread_lanes(earlier), res_ref[...])
    lg_ref[...] = jnp.where(lane < 16, total + extra, 0.0)


def settle(x, mixed, w, down, up, gain, router, earlier, residual):
    return call(
        settle_body,
        (NB,),
        [
            (x, (RB, D), rows),
            (mixed, (RB, D), rows),
            (w, (1, D, D), lambda i: (3, 0, 0)),
            (down, None),
            (up, None),
            (gain, None),
            (router, None),
            (earlier, (RB, 128), rows),
            (residual, None),
        ],
        [
            (out((T, D), F32), (RB, D), rows),
            (out((T, D), BF), (RB, D), rows),
            (out((T, 128), F32), (RB, 128), rows),
            (out((T, 128), BF), (RB, 128), rows),
        ],
        name="settle",
        flops=2 * T * D * D * 2,
        nbytes=10e6,
    )


def dispatch_body(trow_ref, s_ref, o_ref):
    place = pl.program_id(0) * CAP + iota((CAP, T), 0)
    hit = (trow_ref[0:1, :] == place) | (trow_ref[1:2, :] == place)
    o_ref[0] = mm(hit.astype(F32).astype(BF), s_ref[...]).astype(BF)


def dispatch(trow, sent):
    return call(
        dispatch_body,
        (NFFN,),
        [(trow, None), (sent, None)],
        [(out((NFFN, CAP, D), BF), (1, CAP, D), lambda j: (j, 0, 0))],
        name="dispatch",
        flops=2 * T * SLOTS * D,
        nbytes=4e6,
    )[0]


def dispatch_grad_body(trow_ref, g_ref, lg_ref, rt_ref, o_ref, first, second):
    @pl.when(pl.program_id(0) == 0)
    def _():
        for i in range(NB):
            at = slice(i * RB, (i + 1) * RB)
            gates = mix_terms(lg_ref[at, :], rt_ref[at, :])[0]
            g = g_ref[at, :].astype(F32)
            first[at, :] = (gates[0] * g).astype(BF)
            second[at, :] = (gates[1] * g).astype(BF)

    place = pl.program_id(0) * CAP + iota((CAP, T), 0)
    hit0 = (trow_ref[0:1, :] == place).astype(F32).astype(BF)
    hit1 = (trow_ref[1:2, :] == place).astype(F32).astype(BF)
    o_ref[0] = (mm(hit0, first[...]) + mm(hit1, second[...])).astype(BF)


def dispatch_grad(trow, g, logits, routes):
    return call(
        dispatch_grad_body,
        (NFFN,),
        [(trow, None), (g, None), (logits, None), (routes, None)],
        [(out((NFFN, CAP, D), BF), (1, CAP, D), lambda j: (j, 0, 0))],
        [pltpu.VMEM((T, D), BF), pltpu.VMEM((T, D), BF)],
        name="dispatch_grad",
        flops=4 * T * SLOTS * D,
        nbytes=6e6,
    )[0]


PR = 2 * CAP
NP = NFFN // 2


def flip(bit, change):
    return bit + change - 2 * bit * change


PLANE, WIDE_SLICE = 0, 1
OWNERS = (("x", "c", "y"), ("x", "c"))


def owner_at(p, h, kind):
    x = lax.axis_index("x")
    far, near = 1 - p // 2, 1 - p % 2
    if kind == WIDE_SLICE:
        x = 2 * flip(x // 2, far) + flip(x % 2, near)
        c = flip(lax.axis_index("c"), h)
        return {"x": x, "c": c}, x * 2 + c
    x, c, y = flip(x, far), flip(lax.axis_index("c"), h), flip(lax.axis_index("y"), near)
    return {"x": x, "c": c, "y": y}, (x * 2 + c) * 2 + y


PLACES = [(p, h) for p in range(NP) for h in range(2)]


def greet(kind):
    barrier = pltpu.get_barrier_semaphore()
    for p, h in PLACES[:-2] + PLACES[-1:]:
        pl.semaphore_signal(
            barrier, inc=1, device_id=owner_at(p, h, kind)[0], device_id_type=pl.DeviceIdType.MESH
        )
    pl.semaphore_wait(barrier, NFFN - 1)


def block_of(ref, p, h):
    return ref.at[p, h * CAP : (h + 1) * CAP, :]


def fetch_weights(split, gate_ups, down_ref, w1, w2, sems):
    copies = []
    if split:
        y = lax.axis_index("y")
        for side, ref in enumerate(gate_ups):
            mine = flip(y, side)
            count, size = ref.shape[0], ref.shape[1]
            for k in range(count):
                at = pl.multiple_of((2 * k + mine) * size, size)
                copies.append(
                    pltpu.make_async_copy(
                        ref.at[k], w1.at[pl.ds(at, size), :], sems.at[side * count + k]
                    )
                )
    else:
        copies.append(pltpu.make_async_copy(gate_ups[0], w1, sems.at[0]))
    copies.append(pltpu.make_async_copy(down_ref, w2, sems.at[8]))
    for copy in copies:
        copy.start()
    return copies


def fetch_blocks(source, rv, sems, kind):
    copies = []
    for n, (p, h) in enumerate(PLACES):
        number = owner_at(p, h, kind)[1]
        copies.append(pltpu.make_async_copy(source.at[number], block_of(rv, p, h), sems.at[n]))
    for copy in copies:
        copy.start()
    return copies


def give_back(pv, p, target, send, recv, kind):
    me = owner_at(NP - 1, 0, kind)[1]
    copies = []
    for h in range(2):
        n = 2 * p + h
        if (p, h) == (NP - 1, 0):
            copy = pltpu.make_async_copy(block_of(pv, p, h), target.at[me], send.at[n])
        else:
            copy = pltpu.make_async_remote_copy(
                src_ref=block_of(pv, p, h),
                dst_ref=target.at[me],
                send_sem=send.at[n],
                recv_sem=recv.at[n],
                device_id=owner_at(p, h, kind)[0],
                device_id_type=pl.DeviceIdType.MESH,
            )
        copy.start()
        copies.append(copy)
    return copies


def chunk_at(f):
    return pl.multiple_of(f * FC, FC)


def forward_chunk(r, w1, w2, f):
    at = chunk_at(f)
    gate = mm(r, w1[:, pl.ds(at, FC)])
    up = mm(r, w1[:, pl.ds(pl.multiple_of(FF + f * FC, FC), FC)])
    active = (gate * sigmoid(gate) * up).astype(BF)
    return gate, up, mm(active, w2[pl.ds(at, FC), :])


def backward_chunk(g, gate, up, w1, w2, f):
    at = chunk_at(f)
    grad = mm_nt(g, w2[pl.ds(at, FC), :])
    s = sigmoid(gate)
    grad_s = grad * s
    grad_gate = (grad_s * up * (1.0 + gate * (1.0 - s))).astype(BF)
    grad_up = (grad_s * gate).astype(BF)
    return mm_nt(grad_gate, w1[:, pl.ds(at, FC)]) + mm_nt(
        grad_up, w1[:, pl.ds(pl.multiple_of(FF + f * FC, FC), FC)]
    )


def expert_body(split, kind, *refs):
    count = 2 if split else 1
    gate_ups = refs[:count]
    down_ref, rec_ref, ret_ref, gate_ref, up_ref = refs[count : count + 5]
    w1, w2, rv, pv, gv, uv, acc, wsem, rsem, gsem, usem, send, recv = refs[count + 5 :]
    weights = fetch_weights(split, gate_ups, down_ref, w1, w2, wsem)
    blocks = fetch_blocks(rec_ref, rv, rsem, kind)
    greet(kind)
    for copy in weights + blocks:
        copy.wait()
    stores = []
    moves = []
    for p in range(NP):
        r = rv[p]
        acc[...] = jnp.zeros_like(acc)

        def step(f, carry):
            gate, up, part = forward_chunk(r, w1, w2, f)
            gv[p, :, pl.ds(chunk_at(f), FC)] = gate.astype(BF)
            uv[p, :, pl.ds(chunk_at(f), FC)] = up.astype(BF)
            acc[...] += part
            return carry

        lax.fori_loop(0, FF // FC, step, 0)
        pv[p] = acc[...].astype(BF)
        moves += give_back(pv, p, ret_ref, send, recv, kind)
        for values, ref, sems in ((gv, gate_ref, gsem), (uv, up_ref, usem)):
            copy = pltpu.make_async_copy(values.at[p], ref.at[p], sems.at[p])
            copy.start()
            stores.append(copy)
    for copy in moves + stores:
        copy.wait()


def comm_call(body, ins, outs, scratch, name, number, flops, nbytes, near=(), near_outs=()):
    def specs(far, close):
        return [pl.BlockSpec(memory_space=pl.ANY)] * len(far) + [
            pl.BlockSpec(memory_space=pltpu.VMEM)
        ] * len(close)

    ins, outs, ins_specs, outs_specs = (
        [*ins, *near], [*outs, *near_outs], specs(ins, near), specs(outs, near_outs)
    )
    return pl.pallas_call(
        body,
        in_specs=ins_specs,
        out_specs=outs_specs,
        out_shape=outs,
        scratch_shapes=scratch,
        compiler_params=pltpu.CompilerParams(
            vmem_limit_bytes=VMEM_BYTES, collective_id=number, has_side_effects=True
        ),
        cost_estimate=pl.CostEstimate(
            flops=int(flops), bytes_accessed=int(nbytes), transcendentals=0
        ),
        name=name,
    )(*ins)


DMA = pltpu.SemaphoreType.DMA
WEIGHTS = [pltpu.VMEM((D, 2 * FF), BF), pltpu.VMEM((FF, D), BF)]
ROWS = pltpu.VMEM((NP, PR, D), BF)
WIDE = pltpu.VMEM((NP, PR, FF), BF)
SUM = pltpu.VMEM((PR, D), F32)
BLOCKS = jax.ShapeDtypeStruct((NFFN, CAP, D), BF)
KEPT = jax.ShapeDtypeStruct((NP, PR, FF), BF)


def expert_forward(received, gate_ups, down, kind):
    split = len(gate_ups) == 2

    def body(*refs):
        expert_body(split, kind, *refs)

    return comm_call(
        body,
        [*gate_ups, down, received],
        [BLOCKS, KEPT, KEPT],
        WEIGHTS + [ROWS, ROWS, WIDE, WIDE, SUM]
        + [DMA((9,)), DMA((8,)), DMA((NP,)), DMA((NP,)), DMA((8,)), DMA((8,))],
        "expert_forward",
        1,
        2 * SLOTS * D * FF * 3,
        26e6,
    )


def expert_both_body(
    kind, gate_up_ref, down_ref, rec_ref, sg_ref, mid_ref, g_ref, gret_ref, out_ref, gn_ref,
    gle_ref, tcol_ref, lg_ref, rt_ref, gain_ref, cv_ref, wt_ref, res_ref, *scratch,
):
    (
        w1, w2, rv, sv, pv, qv, gv, uv, back, mid, g, acc,
        wsem, rsem, ssem, msem, send, recv, gsend, grecv,
    ) = scratch
    weights = fetch_weights(False, [gate_up_ref], down_ref, w1, w2, wsem)
    blocks = fetch_blocks(rec_ref, rv, rsem, kind) + fetch_blocks(sg_ref, sv, ssem, kind)
    extra = [
        pltpu.make_async_copy(mid_ref, mid, msem.at[0]),
        pltpu.make_async_copy(g_ref, g, msem.at[1]),
    ]
    for copy in extra:
        copy.start()
    greet(kind)
    for copy in weights + blocks:
        copy.wait()
    moves = []
    for p in range(NP):
        r = rv[p]
        acc[...] = jnp.zeros_like(acc)

        def step(f, carry):
            gate, up, part = forward_chunk(r, w1, w2, f)
            gv[p, :, pl.ds(chunk_at(f), FC)] = gate.astype(BF)
            uv[p, :, pl.ds(chunk_at(f), FC)] = up.astype(BF)
            acc[...] += part
            return carry

        lax.fori_loop(0, FF // FC, step, 0)
        pv[p] = acc[...].astype(BF)
        moves += give_back(pv, p, back, send, recv, kind)
    later = []
    for p in range(NP):
        grads = sv[p]
        acc[...] = jnp.zeros_like(acc)

        def step(f, carry):
            at = pl.ds(chunk_at(f), FC)
            gate = gv[p, :, at].astype(F32)
            up = uv[p, :, at].astype(F32)
            acc[...] += backward_chunk(grads, gate, up, w1, w2, f)
            return carry

        lax.fori_loop(0, FF // FC, step, 0)
        qv[p] = acc[...].astype(BF)
        later += give_back(qv, p, gret_ref, gsend, grecv, kind)
    for copy in moves + extra:
        copy.wait()

    def finish(i, carry):
        at = pl.ds(pl.multiple_of(i * RB, RB), RB)
        logits, routes, middle = lg_ref[at, :], rt_ref[at, :], mid[at, :]
        following, chosen = combine_rows(
            tcol_ref[at, :], back, middle, logits, routes, gain_ref[...], cv_ref
        )
        out_ref[at, :] = following
        gn_ref[at, :], gle_ref[at, :] = mix_grad(
            g[at, :].astype(F32), middle, chosen, logits, routes, 0.0, gain_ref[...], cv_ref,
            wt_ref[...], res_ref[...],
        )
        return carry

    lax.fori_loop(0, NB, finish, 0)
    for copy in later:
        copy.wait()


def expert_both(
    received, slot_grads, gate_up, down, mid, g, tcol, logits, routes, gain, const_vec, router_t,
    residual_t, kind,
):
    def body(*refs):
        far, near, outs, scratch = refs[:6], refs[6:13], refs[13:17], refs[17:]
        expert_both_body(kind, *far, *outs, *near, *scratch)

    return comm_call(
        body,
        [gate_up, down, received, slot_grads, mid, g],
        [BLOCKS],
        WEIGHTS
        + [ROWS, ROWS, ROWS, ROWS, WIDE, WIDE, pltpu.VMEM((NFFN, CAP, D), BF)]
        + [pltpu.VMEM((T, D), F32), pltpu.VMEM((T, D), g.dtype), SUM]
        + [DMA((9,)), DMA((8,)), DMA((8,)), DMA((2,))]
        + [DMA((8,)), DMA((8,)), DMA((8,)), DMA((8,))],
        "expert_both",
        2,
        2 * SLOTS * D * FF * 6,
        26e6,
        [tcol, logits, routes, gain, const_vec, router_t, residual_t],
        [out((T, D), F32), out((T, D), F32), out((T, 128), F32)],
    )


def expert_back_body(split, kind, *refs):
    count = 2 if split else 1
    gate_ups = refs[:count]
    down_ref, gate_ref, up_ref, g_ref, mid_ref, c0_ref, c1_ref = refs[count : count + 7]
    trow_ref, lg_ref, rt_ref, gl_ref, gain_ref, cv_ref, wt_ref = refs[count + 7 : count + 14]
    ret_ref, gn_ref = refs[count + 14 : count + 16]
    (
        w1, w2, sgv, rv, pv, gv, uv, first, second, g, mid, c0, c1, acc,
        wsem, gsem, usem, msem, dsend, drecv, send, recv,
    ) = refs[count + 16 :]
    extra = [
        pltpu.make_async_copy(ref, values, msem.at[n])
        for n, (ref, values) in enumerate(
            ((g_ref, g), (mid_ref, mid), (c0_ref, c0), (c1_ref, c1))
        )
    ]
    for copy in extra:
        copy.start()
    weights = fetch_weights(split, gate_ups, down_ref, w1, w2, wsem)
    for values, ref, sems in ((gv, gate_ref, gsem), (uv, up_ref, usem)):
        for p in range(NP):
            copy = pltpu.make_async_copy(ref.at[p], values.at[p], sems.at[p])
            copy.start()
            weights.append(copy)
    extra[0].wait()

    def gated(i, carry):
        at = pl.ds(pl.multiple_of(i * RB, RB), RB)
        gates = mix_terms(lg_ref[at, :], rt_ref[at, :])[0]
        first[at, :] = (gates[0] * g[at, :]).astype(BF)
        second[at, :] = (gates[1] * g[at, :]).astype(BF)
        return carry

    lax.fori_loop(0, NB, gated, 0)
    greet(kind)
    arrivals = {}
    for p, h in [(1, 0), (2, 0), (1, 1), (2, 1), (0, 0), (0, 1), (3, 1), (3, 0)]:
        where, number = owner_at(p, h, kind)
        place = number * CAP + iota((CAP, T), 0)
        hit0 = (trow_ref[0:1, :] == place).astype(F32).astype(BF)
        hit1 = (trow_ref[1:2, :] == place).astype(F32).astype(BF)
        values = (mm(hit0, first[...]) + mm(hit1, second[...])).astype(BF)
        n = 2 * p + h
        if (p, h) == (NP - 1, 0):
            rv[p, h * CAP : (h + 1) * CAP, :] = values
            continue
        sgv[p, h * CAP : (h + 1) * CAP, :] = values
        copy = pltpu.make_async_remote_copy(
            src_ref=block_of(sgv, p, h),
            dst_ref=block_of(rv, p, h),
            send_sem=dsend.at[n],
            recv_sem=drecv.at[n],
            device_id=where,
            device_id_type=pl.DeviceIdType.MESH,
        )
        copy.start()
        arrivals[p, h] = copy
    for copy in weights + extra[1:]:
        copy.wait()
    moves = []

    for p in (3, 1, 2, 0):
        for h in range(2):
            if (p, h) in arrivals:
                arrivals[p, h].wait()
        grads = rv[p]
        acc[...] = jnp.zeros_like(acc)

        def step(f, carry):
            at = pl.ds(chunk_at(f), FC)
            gate = gv[p, :, at].astype(F32)
            up = uv[p, :, at].astype(F32)
            acc[...] += backward_chunk(grads, gate, up, w1, w2, f)
            return carry

        lax.fori_loop(0, FF // FC, step, 0)
        pv[p] = acc[...].astype(BF)
        moves += give_back(pv, p, ret_ref, send, recv, kind)

    def tidy(i, carry):
        at = pl.ds(pl.multiple_of(i * RB, RB), RB)
        gn_ref[at, :] = mix_grad(
            g[at, :], mid[at, :], (c0[at, :], c1[at, :]), lg_ref[at, :], rt_ref[at, :],
            gl_ref[at, :], gain_ref[...], cv_ref, wt_ref[...], None,
        )[0]
        return carry

    lax.fori_loop(0, NB, tidy, 0)
    for copy in moves:
        copy.wait()


def expert_backward(
    gate, up, gate_ups, down, g, mid, c0, c1, trow, logits, routes, gl, gain, const_vec, router_t, kind
):
    split = len(gate_ups) == 2

    def body(*refs):
        expert_back_body(split, kind, *refs)

    half, full = pltpu.VMEM((T, D), BF), pltpu.VMEM((T, D), F32)
    return comm_call(
        body,
        [*gate_ups, down, gate, up, g, mid, c0, c1],
        [BLOCKS],
        WEIGHTS
        + [ROWS, ROWS, ROWS, WIDE, WIDE, half, half, full, full, half, half, SUM]
        + [DMA((9,)), DMA((NP,)), DMA((NP,)), DMA((4,)), DMA((8,)), DMA((8,)), DMA((8,)), DMA((8,))],
        "expert_backward",
        3,
        2 * SLOTS * D * FF * 3,
        26e6,
        [trow, logits, routes, gl, gain, const_vec, router_t],
        [out((T, D), F32)],
    )


def mix_terms(logits, routes):
    lane = iota(logits.shape, 1)

    def at(place):
        return jnp.sum(jnp.where(lane == place, logits, 0.0), axis=1, keepdims=True)

    r0, r1 = routes[:, 0:1], routes[:, 1:2]
    gap = at(r0) - at(r1)
    gates = (sigmoid(gap), sigmoid(-gap))

    def weight(e):
        return jnp.where(r0 == e, gates[0], 0.0) + jnp.where(r1 == e, gates[1], 0.0)

    shares = []
    for c in range(2):
        apart = logits[:, 12 + 2 * c : 13 + 2 * c] - logits[:, 13 + 2 * c : 14 + 2 * c]
        shares.append((sigmoid(apart), sigmoid(-apart)))
    weights = [weight(NFFN + 1), weight(NFFN + 2), weight(NFFN + 3)]
    return gates, weights, shares


def rms_scale(v):
    return lax.rsqrt(jnp.mean(v * v, axis=1, keepdims=True) + EPSILON)


def combine_rows(tcol, back_ref, mid, logits, routes, gain, cv_ref):
    place = iota((RB, SLOTS), 1)
    back = back_ref[...].reshape(SLOTS, D)
    chosen = []
    for k in range(2):
        hit = (tcol[:, k : k + 1] == place).astype(F32).astype(BF)
        chosen.append(mm(hit, back))
    normed = mid * rms_scale(mid) * gain
    gates, weights, shares = mix_terms(logits, routes)
    same = weights[0] + weights[1] * shares[0][0] + weights[2] * shares[1][0]
    moe = gates[0] * chosen[0] + gates[1] * chosen[1] + same * normed
    moe = moe + (weights[1] * shares[0][1]) * cv_ref[0:1, :]
    moe = moe + (weights[2] * shares[1][1]) * cv_ref[1:2, :]
    return mid + moe, chosen


def combine_body(tcol_ref, ret_ref, mid_ref, lg_ref, rt_ref, g_ref, cv_ref, x_ref, c0_ref, c1_ref):
    x_ref[...], chosen = combine_rows(
        tcol_ref[...], ret_ref, mid_ref[...], lg_ref[...], rt_ref[...], g_ref[...], cv_ref
    )
    c0_ref[...] = chosen[0].astype(BF)
    c1_ref[...] = chosen[1].astype(BF)


def combine(tcol, returned, mid, logits, routes, gain, const_vec):
    return call(
        combine_body,
        (NB,),
        [
            (tcol, (RB, 128), rows),
            (returned, None),
            (mid, (RB, D), rows),
            (logits, (RB, 128), rows),
            (routes, (RB, 2), rows),
            (gain, None),
            (const_vec, None),
        ],
        [
            (out((T, D), F32), (RB, D), rows),
            (out((T, D), BF), (RB, D), rows),
            (out((T, D), BF), (RB, D), rows),
        ],
        name="combine",
        flops=4 * T * SLOTS * D,
        nbytes=12e6,
    )


def mix_grad(g, mid, chosen, logits, routes, grad, gain, cv_ref, wt, res):
    normed = mid * rms_scale(mid) * gain
    gates, weights, shares = mix_terms(logits, routes)

    def along(v):
        return jnp.sum(g * v, axis=1, keepdims=True)

    same = along(normed)
    const = [along(cv_ref[c : c + 1, :]) for c in range(2)]
    gate_grads = []
    for k in range(2):
        r = routes[:, k : k + 1]
        value = along(chosen[k].astype(F32)) + jnp.where(r == NFFN + 1, same, 0.0)
        for c in range(2):
            mixed = shares[c][0] * same + shares[c][1] * const[c]
            value = value + jnp.where(r == NFFN + 2 + c, mixed, 0.0)
        gate_grads.append(value)
    slope = gates[0] * gates[1] * (gate_grads[0] - gate_grads[1])
    lane = iota((RB, 128), 1)
    grad = grad + jnp.where(lane == routes[:, 0:1], slope, 0.0)
    grad = grad - jnp.where(lane == routes[:, 1:2], slope, 0.0)
    only = grad
    for c in range(2):
        tilt = weights[1 + c] * shares[c][0] * shares[c][1] * (same - const[c])
        grad = grad + jnp.where(lane == 12 + 2 * c, tilt, 0.0)
        grad = grad - jnp.where(lane == 13 + 2 * c, tilt, 0.0)
    keep = weights[0] + weights[1] * shares[0][0] + weights[2] * shares[1][0]
    residual = None if res is None else mm(spread_lanes(only), res)
    return mm(spread_lanes(grad), wt) + keep * g, residual


def rms_back(grad, v, gain):
    scale = rms_scale(v)
    inner = grad * gain
    return scale * inner - v * (scale**3 * jnp.mean(v * inner, axis=1, keepdims=True))


def attend_back(q, k, v, aug, kf, g, mixed, dqt):
    lane = iota((T, 128), 1)
    low = lane < 64
    lane6 = lane & 63
    product = g.astype(F32) * mixed.astype(F32)
    d0 = jnp.sum(jnp.where(low, product, 0.0), axis=1, keepdims=True)
    d1 = jnp.sum(jnp.where(low, 0.0, product), axis=1, keepdims=True)
    a, b, c = three(-jnp.where(low, d1, d0))
    zero = jnp.zeros((T, 128), BF)
    ga = jnp.where(lane6 == 0, a, jnp.where(lane6 == 1, b, jnp.where(lane6 == 2, c, zero)))
    va = (lane6 < 3).astype(F32).astype(BF)
    qs = (jnp.where(low, q, aug), jnp.where(low, aug, q))
    ks = (jnp.where(low, k, kf), jnp.where(low, kf, k))
    vs = (jnp.where(low, v, va), jnp.where(low, va, v))
    gs = (jnp.where(low, g, ga), jnp.where(low, ga, g))
    kt = k.T
    tri = iota((RB, RB), 0) <= iota((RB, RB), 1)
    low = low[:RB]
    dks = []
    dvs = []
    for i in range(NB):
        here = slice(i * RB, (i + 1) * RB)
        dk = [None, None]
        dv = [None, None]
        for h in range(2):
            half = slice(h * 64, (h + 1) * 64)
            for start, stop in ((i * RB, (i + 1) * RB), ((i + 1) * RB, T)):
                if start == stop:
                    continue
                there = slice(start, stop)
                p = jnp.exp2(mm_nt(ks[h][here], qs[h][there]) * LOG_SCALE)
                if stop == (i + 1) * RB:
                    p = jnp.where(tri, p, 0.0)
                ds = (p * mm_nt(vs[h][here], gs[h][there])).astype(BF)
                p = p.astype(BF)
                dv_part = mm(p, g[there])
                dk_part = mm(ds, q[there])
                dk[h] = dk_part if dk[h] is None else dk[h] + dk_part
                dv[h] = dv_part if dv[h] is None else dv[h] + dv_part
                part = mm(kt[half, here], ds)
                if i == 0:
                    dqt[half, there] = part
                else:
                    dqt[half, there] += part
        dvs.append(jnp.where(low, dv[0], dv[1]))
        dks.append(jnp.where(low, dk[0], dk[1]))
    return dqt[...].T, jnp.concatenate(dks), jnp.concatenate(dvs)


def layer_back_body(
    back_ref, gn_ref, mid_ref, g_ref, mixed_ref, w_ref, qkv_ref, aug_ref, n_ref, x_ref,
    tcol_ref, gain1_ref, gain0_ref, nar_out_ref, nar_ref, d_out_ref, u_out_ref, d_ref, u_ref,
    kf_ref, cos_ref, sin_ref,
    gx_ref, gu_out_ref, gd_out_ref, gu_ref, gd_ref,
    back, gn, mid, g, mixed, w, qkv, aug, n, x, gmix, gproj, dqt, sems, row_sems, out_sems,
):
    def block(i):
        return slice(i * RB, (i + 1) * RB)

    def start(source, target, sem):
        copy = pltpu.make_async_copy(source, target, sem)
        copy.start()
        return copy

    by_row = [(gn_ref, gn), (mid_ref, mid), (g_ref, g), (mixed_ref, mixed)]
    first = [start(back_ref, back, sems.at[0]), start(w_ref.at[3], w.at[3], sems.at[1])]
    strips = [
        [start(a.at[block(i), :], b.at[block(i), :], row_sems.at[i, m]) for m, (a, b) in enumerate(by_row)]
        for i in range(NB)
    ]
    second = [start(qkv_ref, qkv, sems.at[2]), start(aug_ref, aug, sems.at[3])]
    third = [start(w_ref.at[k], w.at[k], sems.at[4 + k]) for k in range(3)]
    third += [start(n_ref, n, sems.at[7]), start(x_ref, x, sems.at[8])]
    for copy in first:
        copy.wait()
    place = iota((RB, SLOTS), 1)
    gu = jnp.zeros((128, D), F32)
    gd = jnp.zeros((128, D), F32)
    for i in range(NB):
        at = block(i)
        for copy in strips[i]:
            copy.wait()
        hit = (tcol_ref[at, 0:1] == place) | (tcol_ref[at, 1:2] == place)
        grad = gn[at, :] + mm(hit.astype(F32).astype(BF), back[...])
        grad_mid = g[at, :].astype(F32) + rms_back(grad, mid[at, :], gain1_ref[...])
        gn[at, :] = grad_mid
        out_grad = grad_mid.astype(BF)
        grad_narrow = mm_nt(out_grad, u_out_ref[...]).astype(BF)
        gu = gu + 2.0 * mm_tn(nar_out_ref[at, :], out_grad)
        gd = gd + mm_tn(grad_narrow, mixed[at, :])
        gmix[at, :] = (mm_nt(out_grad, w[3]) + mm_nt(grad_narrow, d_out_ref[...])).astype(BF)
    gu_out_ref[...] = gu
    gd_out_ref[...] = gd
    for copy in second:
        copy.wait()

    def pair(j, carry):
        def cols(part):
            return pl.ds(pl.multiple_of(part * D + j * 128, 128), 128)

        dq, dk, dv = attend_back(
            qkv[:, cols(0)], qkv[:, cols(1)], qkv[:, cols(2)], aug[j], kf_ref[...],
            gmix[:, cols(0)], mixed[:, cols(0)], dqt,
        )
        for part, value in enumerate((dq, dk)):
            value = (value * (1.0 / math.sqrt(HD))).astype(BF).astype(F32)
            gproj[:, cols(part)] = turn(value, cos_ref[...], -sin_ref[...]).astype(BF)
        gproj[:, cols(2)] = dv.astype(BF)
        return carry

    lax.fori_loop(0, PAIRS, pair, 0)
    for copy in third:
        copy.wait()
    gu_ref[...] = jnp.zeros_like(gu_ref)
    gd_ref[...] = jnp.zeros_like(gd_ref)
    stores = []
    for i in range(NB):
        at = block(i)
        grad = jnp.zeros((RB, D), F32)
        slim = jnp.zeros((RB, 128), F32)
        narrow = nar_ref[at, :]
        for part in range(3):
            cols = slice(part * D, (part + 1) * D)
            piece = gproj[at, cols]
            grad = grad + mm_nt(piece, w[part])
            slim = slim + mm_nt(piece, u_ref[:, cols])
            gu_ref[:, cols] += 2.0 * mm_tn(narrow, piece)
        slim = slim.astype(BF)
        gd_ref[...] += mm_tn(slim, n[at, :])
        grad = grad + mm_nt(slim, d_ref[...])
        mid[at, :] = gn[at, :] + rms_back(grad, x[at, :].astype(F32), gain0_ref[...])
        stores.append(start(mid.at[at, :], gx_ref.at[at, :], out_sems.at[i]))
    for copy in stores:
        copy.wait()


def layer_back(
    back, gn, mid, g, mixed, w, qkv, aug, n, x, tcol, gain1, gain0, narrow_out, narrow, down_out,
    up_out, down, up, kf, cos, sin,
):
    far = [back, gn, mid, g, mixed, w, qkv, aug, n, x]
    near = [
        tcol, gain1, gain0, narrow_out, narrow, down_out, up_out, down, up, kf, cos, sin,
    ]
    outs = [out((128, D), F32), out((128, D), F32), out((128, 3 * D), F32), out((128, D), F32)]
    anywhere = pl.BlockSpec(memory_space=pl.ANY)
    close = pl.BlockSpec(memory_space=pltpu.VMEM)
    return pl.pallas_call(
        layer_back_body,
        in_specs=[anywhere] * len(far) + [close] * len(near),
        out_specs=[anywhere] + [close] * len(outs),
        out_shape=[out((T, D), F32)] + outs,
        scratch_shapes=[pltpu.VMEM(v.shape, v.dtype) for v in far]
        + [
            pltpu.VMEM((T, D), BF),
            pltpu.VMEM((T, 3 * D), BF),
            pltpu.VMEM((128, T), F32),
            DMA((9,)),
            DMA((NB, 4)),
            DMA((NB,)),
        ],
        compiler_params=pltpu.CompilerParams(vmem_limit_bytes=VMEM_BYTES),
        cost_estimate=pl.CostEstimate(
            flops=int(12 * 10 * T * T * 128 + 2 * T * D * 5 * D), bytes_accessed=int(4e7), transcendentals=0
        ),
        name="layer_back",
    )(*far, *near)


AXES = ("x", "c", "zh", "zl", "y")
EXPERT, SHARD = AXES[:2], AXES[2:]
PIECE = 96


def shared_body(p_ref, o_ref, local, zs, zr, ys, yr, xs, xr, cs, cr):
    x, c, y = (lax.axis_index(name) for name in ("x", "c", "y"))
    z = 2 * lax.axis_index("zh") + lax.axis_index("zl")
    mine, theirs = 2 * x + c, 2 * (1 - x) + c

    def spot(quarter, column, j):
        at = (2 * ((z + 4 - j) % 4) + column) * PIECE
        return o_ref.at[quarter, pl.ds(pl.multiple_of(at, PIECE), PIECE), :]

    others = [{"zh": (z + d) % 4 // 2, "zl": (z + d) % 2} for d in range(1, 4)]
    others += [{"y": 1 - y}, {"x": 1 - x}, {"c": 1 - c}]
    barrier = pltpu.get_barrier_semaphore()
    for who in others:
        pl.semaphore_signal(barrier, inc=1, device_id=who, device_id_type=pl.DeviceIdType.MESH)
    pl.semaphore_wait(barrier, len(others))

    started = []

    def send(source, target, who, send_sem, recv_sem):
        copy = pltpu.make_async_remote_copy(
            src_ref=source,
            dst_ref=target,
            send_sem=send_sem,
            recv_sem=recv_sem,
            device_id=who,
            device_id_type=pl.DeviceIdType.MESH,
        )
        copy.start()
        started.append(copy)
        return copy

    core_copies = []

    def to_core(source, target):
        n = len(core_copies)
        core_copies.append(send(source, target, others[5], cs.at[n], cr.at[n]))

    own = pltpu.make_async_copy(p_ref, spot(mine, y, 0), local.at[0])
    own.start()
    z_copies = [
        send(p_ref, spot(mine, y, 0), others[d], zs.at[d], zr.at[d]) for d in range(3)
    ]
    y_copies = [None] * 6
    x_copies = [None] * 6

    def along_y(n, source, target):
        y_copies[n] = send(source, target, others[3], ys.at[n], yr.at[n])

    def along_x(n, source, target):
        x_copies[n] = send(source, target, others[4], xs.at[n], xr.at[n])

    along_y(0, p_ref, spot(mine, y, 0))
    along_x(0, p_ref, spot(mine, y, 0))
    to_core(p_ref, spot(mine, y, 0))
    for j in range(1, 4):
        z_copies[j - 1].wait_recv()
        piece = spot(mine, y, j)
        along_y(j, piece, piece)
        along_x(j, piece, piece)
        to_core(piece, piece)
    for j in range(4):
        y_copies[j].wait_recv()
        piece = spot(mine, 1 - y, j)
        if j < 2:
            along_x(4 + j, piece, piece)
        to_core(piece, piece)
        x_copies[j].wait_recv()
        piece = spot(theirs, y, j)
        if j >= 2:
            along_y(2 + j, piece, piece)
        to_core(piece, piece)
    for j in range(4):
        (x_copies[4 + j] if j < 2 else y_copies[2 + j]).wait_recv()
        piece = spot(theirs, 1 - y, j)
        to_core(piece, piece)
    for copy in core_copies:
        copy.wait_recv()
    own.wait()
    for copy in started:
        copy.wait_send()


def usual():
    return tuple(lax.axis_size(name) for name in AXES) == (2, 2, 2, 2, 2)


def gather_shared(qkv, output):
    rows_here = qkv.shape[0]
    parts = jnp.concatenate([qkv.reshape(rows_here, 3, D).transpose(1, 0, 2), output[None]])
    if not usual():
        return lax.all_gather(parts, SHARD, axis=1, tiled=True)
    quarter = 2 * lax.axis_index("x") + lax.axis_index("c")
    piece = lax.dynamic_index_in_dim(parts, quarter, axis=0, keepdims=False)
    return comm_call(
        shared_body,
        [piece],
        [jax.ShapeDtypeStruct((4, D, D), BF)],
        [DMA((1,)), DMA((3,)), DMA((3,)), DMA((6,)), DMA((6,)), DMA((6,)), DMA((6,)), DMA((16,)), DMA((16,))],
        "gather_shared",
        0,
        0,
        5e7,
    )[0]


SPAN = 96
UNIT = LAYERS * 2 * 4 * R


def adapters_body(*refs):
    id_ref, parts = refs[0], refs[1 : 1 + 4 * LAYERS]
    o_ref = refs[1 + 4 * LAYERS]
    sbuf, rbuf, tbuf, ubuf, asend, arecv, bsend, brecv = refs[2 + 4 * LAYERS :]
    x, c, y = (lax.axis_index(name) for name in ("x", "c", "y"))
    z = 2 * lax.axis_index("zh") + lax.axis_index("zl")
    mates = []
    for dz in range(4):
        for dy in range(2):
            mates.append(((z + dz) % 4, flip(y, dy)))
    groups = [(flip(x, dx), flip(c, dc)) for dx in range(2) for dc in range(2)]
    barrier = pltpu.get_barrier_semaphore()
    peers = [{"zh": a // 2, "zl": a % 2, "y": b} for a, b in mates[1:]]
    peers += [{"x": a, "c": b} for a, b in groups[1:]]
    for who in peers:
        pl.semaphore_signal(barrier, inc=1, device_id=who, device_id_type=pl.DeviceIdType.MESH)
    row = 0
    for layer in range(LAYERS):
        gd_in, gd_out, gu_in, gu_out = parts[4 * layer : 4 * layer + 4]
        pieces = [gd_in[p * R : (p + 1) * R, :] for p in range(3)] + [gd_out[:R, :]]
        pieces += [gu_in[p * R : (p + 1) * R, p * D : (p + 1) * D] for p in range(3)] + [gu_out[:R, :]]
        for piece in pieces:
            for s in range(8):
                sbuf[s, row : row + R, :] = piece[:, s * SPAN : (s + 1) * SPAN].astype(BF)
            row += R
    sbuf[:, UNIT:, :] = jnp.broadcast_to(id_ref[0].astype(F32).astype(BF), (8, R, SPAN))
    pl.semaphore_wait(barrier, len(peers))
    me = 2 * z + y
    copies = []
    for n, (a, b) in enumerate(mates):
        if n == 0:
            rbuf[0] = sbuf[me]
            continue
        copy = pltpu.make_async_remote_copy(
            src_ref=sbuf.at[2 * a + b],
            dst_ref=rbuf.at[(4 - n // 2) % 4 * 2 + n % 2],
            send_sem=asend.at[n],
            recv_sem=arecv.at[(4 - n // 2) % 4 * 2 + n % 2],
            device_id={"zh": a // 2, "zl": a % 2, "y": b},
            device_id_type=pl.DeviceIdType.MESH,
        )
        copy.start()
        copies.append(copy)
    for copy in copies:
        copy.wait()
    masks = []
    for n in range(8):
        own = rbuf[n, UNIT : UNIT + R, :][0:1, 0:1].astype(F32)
        masks.append([(own == k).astype(F32) for k in range(NA)])

    def add(i, carry):
        at = pl.ds(pl.multiple_of(i * 32, 32), 32)
        sums = [jnp.zeros((32, SPAN), F32) for _ in range(NA)]
        for n in range(8):
            values = rbuf[n, at, :].astype(F32)
            for k in range(NA):
                sums[k] = sums[k] + values * masks[n][k]
        for k in range(NA):
            tbuf[k, at, :] = sums[k].astype(BF)
        return carry

    lax.fori_loop(0, UNIT // 32, add, 0)
    copies = []
    ubuf[0] = tbuf[pl.ds(2 * (2 * x + c), 2)]
    for n, (a, b) in enumerate(groups):
        if n == 0:
            continue
        copy = pltpu.make_async_remote_copy(
            src_ref=tbuf.at[pl.ds(2 * (2 * a + b), 2)],
            dst_ref=ubuf.at[n],
            send_sem=bsend.at[n],
            recv_sem=brecv.at[n],
            device_id={"x": a, "c": b},
            device_id_type=pl.DeviceIdType.MESH,
        )
        copy.start()
        copies.append(copy)
    for copy in copies:
        copy.wait()
    total = ubuf[0].astype(F32)
    for n in range(1, 4):
        total = total + ubuf[n].astype(F32)
    o_ref[...] = total


def adapters(own, parts):
    specs = [pl.BlockSpec(memory_space=pltpu.SMEM)]
    specs += [pl.BlockSpec(memory_space=pltpu.VMEM)] * len(parts)
    return pl.pallas_call(
        adapters_body,
        in_specs=specs,
        out_specs=pl.BlockSpec(memory_space=pltpu.VMEM),
        out_shape=jax.ShapeDtypeStruct((2, UNIT, SPAN), F32),
        scratch_shapes=[
            pltpu.VMEM((8, UNIT + R, SPAN), BF),
            pltpu.VMEM((8, UNIT + R, SPAN), BF),
            pltpu.VMEM((NA, UNIT, SPAN), BF),
            pltpu.VMEM((4, 2, UNIT, SPAN), BF),
            DMA((8,)),
            DMA((8,)),
            DMA((4,)),
            DMA((4,)),
        ],
        compiler_params=pltpu.CompilerParams(
            vmem_limit_bytes=VMEM_BYTES, collective_id=4, has_side_effects=True
        ),
        name="adapters",
    )(own, *parts)


def both_rows(mine, other):
    y = lax.axis_index("y")
    return jnp.where(y == 0, jnp.stack([mine, other]), jnp.stack([other, mine]))


def own_and_other(w):
    y = lax.axis_index("y")
    return [lax.dynamic_index_in_dim(w, e, axis=0, keepdims=False) for e in (y, 1 - y)]


def across_y(v):
    return lax.ppermute(v, "y", [(0, 1), (1, 0)])


def move_expert(w):
    mine, other = own_and_other(w)
    return both_rows(mine, across_y(other))


def gathered(w, axes):
    return lax.all_gather(w, axes, axis=0, tiled=True).reshape(-1, w.shape[-1])


def exchange(v, kind):
    return lax.all_to_all(v, OWNERS[kind], split_axis=0, concat_axis=0, tiled=True)


def pad_to(v, shape):
    return jnp.pad(v, [(0, n - m) for m, n in zip(v.shape, shape)])


def adapters_plain(owners, parts):
    layers = []
    for gd_in, gd_out, gu_in, gu_out in parts:
        downs = [gd_in[p * R : (p + 1) * R] for p in range(3)] + [gd_out[:R]]
        ups = [gu_in[p * R : (p + 1) * R, p * D : (p + 1) * D] for p in range(3)] + [gu_out[:R]]
        layers.append(jnp.concatenate(downs + ups))
    compact = jnp.concatenate(layers).astype(BF)
    ranks = lax.axis_size(SHARD)
    pieces = compact.reshape(UNIT, ranks, D // ranks).transpose(1, 0, 2)
    pieces = lax.all_to_all(pieces, SHARD, split_axis=0, concat_axis=0, tiled=True)
    pick = (owners[None, :] == jnp.arange(NA, dtype=jnp.int32)[:, None]).astype(F32)
    summed = jnp.dot(pick, pieces.reshape(ranks, -1).astype(F32), precision=HIGHEST).astype(BF)
    groups = lax.axis_size(EXPERT)
    summed = lax.all_to_all(
        summed.reshape(groups, NA // groups, -1), EXPERT, split_axis=0, concat_axis=0, tiled=True
    )
    return jnp.sum(summed.astype(F32), axis=0)


def per_device(
    tokens,
    segments,
    parents,
    adapter_of,
    routes,
    norm_gain,
    query_key_value_weight,
    output_weight,
    adapter_down,
    adapter_up,
    router,
    router_residual,
    const_proj,
    const_vec,
    w_gate_up,
    w_down,
    out_grad,
):
    fast = w_gate_up.shape[1] == 2
    kind = PLANE if fast else WIDE_SLICE
    barrier = lax.optimization_barrier
    if fast:
        mine, other = own_and_other(w_gate_up[0])
        parts = [lax.all_gather(mine, ("zh", "zl"), axis=0)]
        shared = [gather_shared(query_key_value_weight[0], output_weight[0])]
        other, down_first, shared[0] = barrier((other, w_down[0], shared[0]))
        parts.append(lax.all_gather(across_y(other), ("zh", "zl"), axis=0))
        gate_up_full = [parts]
        down_full = [gathered(move_expert(down_first), ("zh", "zl"))]
    else:
        shared = [gather_shared(query_key_value_weight[0], output_weight[0])]
        gate_up_full = [[gathered(w_gate_up[layer, 0], SHARD)] for layer in range(LAYERS)]
        down_full = [gathered(w_down[layer, 0], SHARD) for layer in range(LAYERS)]

    which = adapter_of[0]
    down_sel = lax.dynamic_index_in_dim(adapter_down, which, axis=2, keepdims=False)
    up_sel = lax.dynamic_index_in_dim(adapter_up, which, axis=2, keepdims=False)
    down_in = jnp.pad(
        down_sel[:, :3].transpose(0, 2, 1, 3).reshape(LAYERS, D, 3 * R), ((0, 0), (0, 0), (0, 80))
    )
    down_out = jnp.pad(down_sel[:, 3], ((0, 0), (0, 0), (0, 112)))
    up_t = 2.0 * up_sel.transpose(0, 1, 3, 2)
    up_in = jnp.zeros((LAYERS, 128, 3 * D), BF)
    for p in range(3):
        up_in = up_in.at[:, p * R : (p + 1) * R, p * D : (p + 1) * D].set(up_t[:, p])
    up_out = jnp.pad(up_t[:, 3], ((0, 0), (0, 112), (0, 0)))
    rcat = jnp.concatenate([router, const_proj[:, 0], const_proj[:, 1]], axis=2)
    rcat = jnp.pad(rcat, ((0, 0), (0, 0), (0, 112)))
    rcat_t = rcat[:, :, :16].transpose(0, 2, 1)
    residual = pad_to(router_residual, (16, 128))
    residual_t = pad_to(router_residual.T, (16, 128))

    qf, kf, cos, sin, tcol, trow, router_s, router_ts, residual_s, residual_ts = prep(
        parents, segments.reshape(T, 1), routes, rcat, rcat_t, residual, residual_t
    )

    stream = tokens
    earlier = jnp.zeros((T, 128), F32)
    saved = []
    for layer in range(LAYERS):
        gain0 = norm_gain[layer, 0:1]
        gain1 = norm_gain[layer, 1:2]
        normed, narrow, qkv = project(
            stream, gain0, shared[layer], down_in[layer], up_in[layer], cos, sin
        )
        mixed, aug = attend(qkv, qf, kf)
        mid, sent, logits, narrow_out = settle(
            stream, mixed, shared[layer], down_out[layer], up_out[layer], gain1, router_s[layer],
            earlier, residual_s,
        )
        received = exchange(dispatch(trow, sent), kind)
        if layer == 0:
            if fast:
                later = barrier((w_gate_up[1], w_down[1], logits))
                gate_up_full.append([gathered(move_expert(later[0]), ("zh", "zl"))])
                down_full.append(gathered(move_expert(later[1]), ("zh", "zl")))
            later = lax.optimization_barrier(
                (query_key_value_weight[1], output_weight[1], logits)
            )
            shared.append(gather_shared(later[0], later[1]))
            returned, gate, up = expert_forward(received, gate_up_full[0], down_full[0], kind)
        else:
            slot_grads = exchange(dispatch_grad(trow, out_grad, logits, routes), kind)
            back, following, grad_normed, grad_logits = expert_both(
                received, slot_grads, gate_up_full[1][0], down_full[1], mid, out_grad, tcol, logits,
                routes, gain1, const_vec[1], router_ts[1], residual_ts, kind,
            )
            c0 = c1 = None
        if layer == 0:
            following, c0, c1 = combine(
                tcol, returned.reshape(SLOTS, D), mid, logits, routes, gain1, const_vec[0]
            )
        saved.append((stream, normed, narrow, qkv, mixed, aug, mid, logits, narrow_out, c0, c1))
        stream = following
        earlier = logits

    grad = out_grad
    parts = [None] * LAYERS
    for layer in reversed(range(LAYERS)):
        x_in, normed, narrow, qkv, mixed, aug, mid, logits, narrow_out, c0, c1 = saved[layer]
        gain0 = norm_gain[layer, 0:1]
        gain1 = norm_gain[layer, 1:2]
        if layer == 0:
            back, grad_normed = expert_backward(
                gate, up, gate_up_full[0], down_full[0], grad, mid, c0, c1, trow, logits, routes,
                grad_logits, gain1, const_vec[0], router_ts[0], kind,
            )
        grad, gu_out, gd_out, gu_in, gd_in = layer_back(
            back.reshape(SLOTS, D), grad_normed, mid, grad, mixed, shared[layer], qkv, aug, normed,
            x_in, tcol, gain1, gain0, narrow_out, narrow, down_out[layer], up_out[layer],
            down_in[layer], up_in[layer], kf, cos, sin,
        )
        parts[layer] = (gd_in, gd_out, gu_in, gu_out)

    if usual():
        final = adapters(adapter_of, [v for layer in parts for v in layer])
    else:
        final = adapters_plain(lax.all_gather(adapter_of, SHARD, axis=0, tiled=True), parts)
    share = final.shape[0]
    final = final.reshape(share, LAYERS, 2, 4, R, -1).transpose(2, 1, 3, 0, 5, 4)
    return (stream, grad, final[0], final[1])


def solution(mesh):
    owners, shards = mesh.shape["expert"], mesh.shape["shard"]
    each = NFFN // owners
    fine = jax.sharding.Mesh(
        mesh.devices.reshape(owners // 2, 2, shards // each**2, each, each), AXES
    )
    expert, shard, both = EXPERT, SHARD, AXES
    in_specs = (
        P(both, None),
        P(both, None),
        P(both, None),
        P(both),
        P(both, None),
        P(),
        P(None, shard, None),
        P(None, shard, None),
        P(),
        P(),
        P(),
        P(),
        P(),
        P(),
        P(None, expert, shard, None),
        P(None, expert, shard, None),
        P(both, None),
    )
    out_specs = (
        P(both, None),
        P(both, None),
        P(None, None, expert, shard, None),
        P(None, None, expert, shard, None),
    )
    return jax.shard_map(
        per_device, mesh=fine, in_specs=in_specs, out_specs=out_specs, check_vma=False
    )
```

```python
import functools
import math

import jax
import jax.numpy as jnp
from jax import lax
from jax.experimental import pallas as pl
from jax.experimental.pallas import tpu as pltpu
from jax.sharding import PartitionSpec as P

D = 768
HEADS = 12
HD = 64
FF = 2048
NFFN = 8
NEXP = 12
R = 16
NA = 8
NSEG = 13
LAYERS = 2
CAP = 192
T = 1024
SLOTS = NFFN * CAP
RB = 256
NB = T // RB
PAIRS = HEADS // 2
FC = 512
EPSILON = 1e-06
BIG = 2.0**100
LOG_SCALE = math.log2(math.e) / math.sqrt(HD)
F32 = jnp.float32
BF = jnp.bfloat16
HIGHEST = lax.Precision.HIGHEST
VMEM_BYTES = 60 * 1024 * 1024


def mm(a, b):
    return lax.dot_general(a, b, (((1,), (0,)), ((), ())), preferred_element_type=F32)


def mm_nt(a, b):
    return lax.dot_general(a, b, (((1,), (1,)), ((), ())), preferred_element_type=F32)


def mm_tn(a, b):
    return lax.dot_general(a, b, (((0,), (0,)), ((), ())), preferred_element_type=F32)


def mm_exact(a, b):
    return lax.dot_general(
        a, b, (((1,), (0,)), ((), ())), preferred_element_type=F32, precision=HIGHEST
    )


def iota(shape, axis):
    return lax.broadcasted_iota(jnp.int32, shape, axis)


def sigmoid(v):
    return 1.0 / (1.0 + jnp.exp(-v))


def call(body, grid, ins, outs, scratch=(), name=None, flops=0, nbytes=0):
    def spec(entry):
        if entry[1] == "smem":
            return pl.BlockSpec(memory_space=pltpu.SMEM)
        if entry[1] is None:
            shape = entry[0].shape
            return pl.BlockSpec(shape, lambda *_: (0,) * len(shape))
        return pl.BlockSpec(entry[1], entry[2])

    return pl.pallas_call(
        body,
        grid=grid,
        in_specs=[spec(e) for e in ins],
        out_specs=[spec(e) for e in outs],
        out_shape=[jax.ShapeDtypeStruct(e[0].shape, e[0].dtype) for e in outs],
        scratch_shapes=list(scratch),
        compiler_params=pltpu.CompilerParams(
            dimension_semantics=("arbitrary",) * len(grid), vmem_limit_bytes=VMEM_BYTES
        ),
        cost_estimate=pl.CostEstimate(
            flops=int(flops), bytes_accessed=int(nbytes), transcendentals=0
        ),
        name=name,
    )(*[e[0] for e in ins])


def out(shape, dtype):
    return jax.ShapeDtypeStruct(shape, dtype)


def rows(i):
    return (i, 0)


def three(v):
    high = v.astype(BF)
    rest = v - high.astype(F32)
    middle = rest.astype(BF)
    return high, middle, (rest - middle.astype(F32)).astype(BF)


def spread_lanes(v):
    a, b, c = (part.astype(F32) for part in three(v))
    total = a + pltpu.roll(b, 16, 1) + pltpu.roll(c, 32, 1)
    total = total + pltpu.roll(a, 48, 1) + pltpu.roll(b, 64, 1) + pltpu.roll(a, 80, 1)
    return total.astype(BF)


def stack_rows(w):
    a, b, c = three(w)
    return jnp.concatenate([a, a, a, b, b, c, jnp.zeros((32, w.shape[1]), BF)], axis=0)


def prep_body(
    par_ref, seg_ref, rt_ref, rc_ref, rct_ref, res_ref, rest_ref,
    qf_ref, kf_ref, cos_ref, sin_ref, tcol_ref, trow_ref, rs_ref, rts_ref, ress_ref, rests_ref, anc,
):
    for layer in range(LAYERS):
        a, b, c = (part.astype(F32) for part in three(rc_ref[layer]))
        rs_ref[layer] = (a + pltpu.roll(b, 16, 1) + pltpu.roll(c, 32, 1)).astype(BF)
        rts_ref[layer] = stack_rows(rct_ref[layer])
    ress_ref[...] = stack_rows(res_ref[...])
    rests_ref[...] = stack_rows(rest_ref[...])
    first = iota((1, 128), 1) & 63
    anc[...] = jnp.zeros_like(anc)
    anc[0:1, :] = (first == 0).astype(F32)
    for s in range(1, NSEG):
        above = anc[pl.ds(par_ref[0, s], 1), :]
        anc[s : s + 1, :] = jnp.maximum(above, (first == s).astype(F32))
    lane = iota((T, 128), 1)
    lane6 = lane & 63
    low = lane < 64
    member = (seg_ref[...] == lane6).astype(F32)
    ways = mm(jnp.where(low, member, 0.0).astype(BF), anc[...].astype(BF))
    qf_ref[...] = jnp.where(lane6 < NSEG, (ways - 1.0) * BIG, 0.0).astype(BF)
    ones = ((lane6 >= 16) & (lane6 < 19)).astype(F32)
    kf_ref[...] = (member + ones).astype(BF)
    hit0 = (rt_ref[:, 0:1] == lane).astype(F32)
    hit1 = (rt_ref[:, 1:2] == lane).astype(F32)
    hits = hit0 + hit1
    upto = (iota((T, T), 0) >= iota((T, T), 1)).astype(F32).astype(BF)
    seen = mm(upto, jnp.concatenate([member.astype(BF), hits.astype(BF)], axis=1))
    depth = jnp.sum(jnp.where(low, ways * seen[:, :128], 0.0), axis=1, keepdims=True) - 1.0
    before = seen[:, 128:] - hits

    def target(hit, route):
        slot = jnp.sum(hit * before, axis=1, keepdims=True)
        place = route.astype(F32) * CAP + slot
        return jnp.where(route < NFFN, place, 4.0 * SLOTS)

    t0 = target(hit0, rt_ref[:, 0:1])
    t1 = target(hit1, rt_ref[:, 1:2])
    both = jnp.where(lane == 0, t0, jnp.where(lane == 1, t1, 0.0))
    tcol_ref[...] = both.astype(jnp.int32)
    trow_ref[...] = both.T[0:8, :].astype(jnp.int32)
    inverse = jnp.exp((lane & 31).astype(F32) * (-math.log(10000.0) / 32.0))
    angle = depth * inverse
    cos_ref[...] = jnp.cos(angle)
    sine = jnp.sin(angle)
    sin_ref[...] = jnp.where((lane & 32) == 0, -sine, sine)


def prep(parents, seg_col, routes, rcat, rcat_t, residual, residual_t):
    return call(
        prep_body,
        (1,),
        [
            (parents, "smem"),
            (seg_col, None),
            (routes, None),
            (rcat, None),
            (rcat_t, None),
            (residual, None),
            (residual_t, None),
        ],
        [
            (out((T, 128), BF), None),
            (out((T, 128), BF), None),
            (out((T, 128), F32), None),
            (out((T, 128), F32), None),
            (out((T, 128), jnp.int32), None),
            (out((8, T), jnp.int32), None),
            (out((LAYERS, D, 128), BF), None),
            (out((LAYERS, 128, D), BF), None),
            (out((128, 128), BF), None),
            (out((128, 128), BF), None),
        ],
        [pltpu.VMEM((128, 128), F32)],
        name="prep",
        flops=2 * T * T * 256,
        nbytes=3e6,
    )


def turn(v, cos, sin):
    first = (iota(v.shape, 1) & 32) == 0
    other = jnp.where(first, pltpu.roll(v, 96, 1), pltpu.roll(v, 32, 1))
    return v * cos + other * sin


def project_rows(x, gain, w_ref, d_ref, u_ref, cos, sin, n_ref, nar_ref, qkv_ref):
    scale = lax.rsqrt(jnp.mean(x * x, axis=1, keepdims=True) + EPSILON)
    normed = (x * scale * gain).astype(BF)
    n_ref[...] = normed
    narrow = mm(normed, d_ref[...]).astype(BF)
    nar_ref[...] = narrow
    for block in range(3):
        cols = slice(block * D, (block + 1) * D)
        part = mm(normed, w_ref[block]) + mm(narrow, u_ref[:, cols])
        for j in range(PAIRS):
            piece = part[:, j * 128 : (j + 1) * 128]
            if block < 2:
                piece = turn(piece, cos, sin)
            at = block * D + j * 128
            qkv_ref[:, at : at + 128] = piece.astype(BF)


def project_body(x_ref, g_ref, w_ref, d_ref, u_ref, cos_ref, sin_ref, n_ref, nar_ref, qkv_ref):
    project_rows(
        x_ref[...].astype(F32),
        g_ref[...],
        w_ref,
        d_ref,
        u_ref,
        cos_ref[...],
        sin_ref[...],
        n_ref,
        nar_ref,
        qkv_ref,
    )


def project(x, gain, w, down, up, cos, sin):
    return call(
        project_body,
        (NB,),
        [
            (x, (RB, D), rows),
            (gain, None),
            (w, (3, D, D), lambda i: (0, 0, 0)),
            (down, None),
            (up, None),
            (cos, (RB, 128), rows),
            (sin, (RB, 128), rows),
        ],
        [
            (out((T, D), BF), (RB, D), rows),
            (out((T, 128), BF), (RB, 128), rows),
            (out((T, 3 * D), BF), (RB, 3 * D), rows),
        ],
        name="project",
        flops=2 * T * D * 3 * D,
        nbytes=12e6,
    )


def attend_body(q_ref, k_ref, v_ref, qf_ref, kf_ref, mixed_ref, aug_ref):
    low = iota((T, 128), 1) < 64
    k = k_ref[...]
    kf = kf_ref[...]
    v = v_ref[...]
    one = jnp.ones((T, 128), BF)
    keys = (jnp.where(low, k, kf), jnp.where(low, kf, k))
    values = (jnp.where(low, v, one), jnp.where(low, one, v))
    low = low[:RB]
    tri = iota((RB, RB), 0) >= iota((RB, RB), 1)
    lane6 = iota((RB, 128), 1) & 63
    for i in range(NB):
        here = slice(i * RB, (i + 1) * RB)
        q = q_ref[here, :]
        qf = qf_ref[here, :]
        tops = []
        outs = []
        for h in range(2):
            qa = jnp.where(low, q, qf) if h == 0 else jnp.where(low, qf, q)
            diag = jnp.where(tri, mm_nt(qa, keys[h][here]), -BIG)
            top = jnp.max(diag, axis=1, keepdims=True)
            if i:
                off = mm_nt(qa, keys[h][: i * RB])
                top = jnp.maximum(top, jnp.max(off, axis=1, keepdims=True))
            result = mm(jnp.exp2((diag - top) * LOG_SCALE).astype(BF), values[h][here])
            if i:
                weights = jnp.exp2((off - top) * LOG_SCALE).astype(BF)
                result = result + mm(weights, values[h][: i * RB])
            tops.append(top)
            outs.append(result)
        total = jnp.where(low, outs[1], outs[0])
        mixed = jnp.where(low, outs[0], outs[1]) / pltpu.roll(total, 64, 1)
        mixed_ref[here, :] = mixed.astype(BF)
        level = -(jnp.where(low, tops[1], tops[0]) + math.sqrt(HD) * jnp.log(total))
        a, b, c = three(level)
        aug_ref[0, here, :] = jnp.where(
            lane6 == 16, a, jnp.where(lane6 == 17, b, jnp.where(lane6 == 18, c, qf))
        )


def attend(qkv, qf, kf):
    return call(
        attend_body,
        (PAIRS,),
        [
            (qkv, (T, 128), lambda j: (0, j)),
            (qkv, (T, 128), lambda j: (0, PAIRS + j)),
            (qkv, (T, 128), lambda j: (0, 2 * PAIRS + j)),
            (qf, None),
            (kf, None),
        ],
        [
            (out((T, D), BF), (T, 128), lambda j: (0, j)),
            (out((PAIRS, T, 128), BF), (1, T, 128), lambda j: (j, 0, 0)),
        ],
        name="attend",
        flops=12 * 4 * T * T * 128,
        nbytes=8e6,
    )


def settle_body(
    x_ref, mixed_ref, w_ref, d_ref, u_ref, g_ref, rt_ref, earlier_ref, res_ref,
    mid_ref, sent_ref, lg_ref, nar_ref,
):
    mixed = mixed_ref[...]
    narrow = mm(mixed, d_ref[...]).astype(BF)
    nar_ref[...] = narrow
    mid = x_ref[...].astype(F32) + mm(mixed, w_ref[0]) + mm(narrow, u_ref[...])
    mid_ref[...] = mid
    scale = lax.rsqrt(jnp.mean(mid * mid, axis=1, keepdims=True) + EPSILON)
    normed = mid * scale * g_ref[...]
    sent_ref[...] = normed.astype(BF)
    a, b, c = three(normed)
    one, two, last = mm(a, rt_ref[...]), mm(b, rt_ref[...]), mm(c, rt_ref[...])
    total = one + two + last + pltpu.roll(one + two, 112, 1) + pltpu.roll(one, 96, 1)
    lane = iota((RB, 128), 1)
    earlier = jnp.where(lane < NEXP, earlier_ref[...], 0.0)
    extra = mm(spread_lanes(earlier), res_ref[...])
    lg_ref[...] = jnp.where(lane < 16, total + extra, 0.0)


def settle(x, mixed, w, down, up, gain, router, earlier, residual):
    return call(
        settle_body,
        (NB,),
        [
            (x, (RB, D), rows),
            (mixed, (RB, D), rows),
            (w, (1, D, D), lambda i: (3, 0, 0)),
            (down, None),
            (up, None),
            (gain, None),
            (router, None),
            (earlier, (RB, 128), rows),
            (residual, None),
        ],
        [
            (out((T, D), F32), (RB, D), rows),
            (out((T, D), BF), (RB, D), rows),
            (out((T, 128), F32), (RB, 128), rows),
            (out((T, 128), BF), (RB, 128), rows),
        ],
        name="settle",
        flops=2 * T * D * D * 2,
        nbytes=10e6,
    )


def dispatch_body(trow_ref, s_ref, o_ref):
    place = pl.program_id(0) * CAP + iota((CAP, T), 0)
    hit = (trow_ref[0:1, :] == place) | (trow_ref[1:2, :] == place)
    o_ref[0] = mm(hit.astype(F32).astype(BF), s_ref[...]).astype(BF)


def dispatch(trow, sent):
    return call(
        dispatch_body,
        (NFFN,),
        [(trow, None), (sent, None)],
        [(out((NFFN, CAP, D), BF), (1, CAP, D), lambda j: (j, 0, 0))],
        name="dispatch",
        flops=2 * T * SLOTS * D,
        nbytes=4e6,
    )[0]


def dispatch_grad_body(trow_ref, g_ref, lg_ref, rt_ref, o_ref, first, second):
    @pl.when(pl.program_id(0) == 0)
    def _():
        for i in range(NB):
            at = slice(i * RB, (i + 1) * RB)
            gates = mix_terms(lg_ref[at, :], rt_ref[at, :])[0]
            g = g_ref[at, :].astype(F32)
            first[at, :] = (gates[0] * g).astype(BF)
            second[at, :] = (gates[1] * g).astype(BF)

    place = pl.program_id(0) * CAP + iota((CAP, T), 0)
    hit0 = (trow_ref[0:1, :] == place).astype(F32).astype(BF)
    hit1 = (trow_ref[1:2, :] == place).astype(F32).astype(BF)
    o_ref[0] = (mm(hit0, first[...]) + mm(hit1, second[...])).astype(BF)


def dispatch_grad(trow, g, logits, routes):
    return call(
        dispatch_grad_body,
        (NFFN,),
        [(trow, None), (g, None), (logits, None), (routes, None)],
        [(out((NFFN, CAP, D), BF), (1, CAP, D), lambda j: (j, 0, 0))],
        [pltpu.VMEM((T, D), BF), pltpu.VMEM((T, D), BF)],
        name="dispatch_grad",
        flops=4 * T * SLOTS * D,
        nbytes=6e6,
    )[0]


PR = 2 * CAP
NP = NFFN // 2


def split_refs(refs, *counts):
    parts = []
    for count in counts:
        parts.append(refs[:count])
        refs = refs[count:]
    return *parts, refs


def flip(bit, change):
    return bit + change - 2 * bit * change


PLANE, WIDE_SLICE = 0, 1
OWNERS = (("x", "c", "y"), ("x", "c"))


def owner_at(p, h, kind):
    x = lax.axis_index("x")
    far, near, core = ((1, 1, h), (1 - h, h, 0), (1 - h, h, 1), (0, 0, h))[p]
    if kind == WIDE_SLICE:
        x = 2 * flip(x // 2, far) + flip(x % 2, near)
        c = flip(lax.axis_index("c"), core)
        return {"x": x, "c": c}, x * 2 + c
    x, c, y = flip(x, far), flip(lax.axis_index("c"), core), flip(lax.axis_index("y"), near)
    return {"x": x, "c": c, "y": y}, (x * 2 + c) * 2 + y


PLACES = [(p, h) for p in range(NP) for h in range(2)]


def greet(kind):
    barrier = pltpu.get_barrier_semaphore()
    for p, h in PLACES[:-2] + PLACES[-1:]:
        pl.semaphore_signal(
            barrier, inc=1, device_id=owner_at(p, h, kind)[0], device_id_type=pl.DeviceIdType.MESH
        )
    pl.semaphore_wait(barrier, NFFN - 1)


def block_of(ref, p, h):
    return ref.at[p, h * CAP : (h + 1) * CAP, :]


def fetch_weights(split, gate_ups, down_ref, w1, w2, sems):
    copies = []
    if split:
        y = lax.axis_index("y")
        for side, ref in enumerate(gate_ups):
            mine = flip(y, side)
            count, size = ref.shape[0], ref.shape[1]
            for k in range(count):
                at = pl.multiple_of((2 * k + mine) * size, size)
                copies.append(
                    pltpu.make_async_copy(
                        ref.at[k], w1.at[pl.ds(at, size), :], sems.at[side * count + k]
                    )
                )
    else:
        copies.append(pltpu.make_async_copy(gate_ups[0], w1, sems.at[0]))
    copies.append(pltpu.make_async_copy(down_ref, w2, sems.at[8]))
    for copy in copies:
        copy.start()
    return copies


def fetch_blocks(source, rv, sems, kind):
    copies = []
    for n, (p, h) in enumerate(PLACES):
        number = owner_at(p, h, kind)[1]
        copies.append(pltpu.make_async_copy(source.at[number], block_of(rv, p, h), sems.at[n]))
    for copy in copies:
        copy.start()
    return copies


def give_back(pv, p, target, send, recv, kind):
    me = owner_at(NP - 1, 0, kind)[1]
    copies = []
    for h in range(2):
        n = 2 * p + h
        if (p, h) == (NP - 1, 0):
            copy = pltpu.make_async_copy(block_of(pv, p, h), target.at[me], send.at[n])
        else:
            copy = pltpu.make_async_remote_copy(
                src_ref=block_of(pv, p, h),
                dst_ref=target.at[me],
                send_sem=send.at[n],
                recv_sem=recv.at[n],
                device_id=owner_at(p, h, kind)[0],
                device_id_type=pl.DeviceIdType.MESH,
            )
        copy.start()
        copies.append(copy)
    return copies


def chunk_at(f):
    return pl.multiple_of(f * FC, FC)


def forward_chunk(r, w1, w2, f):
    at = chunk_at(f)
    gate = mm(r, w1[:, pl.ds(at, FC)])
    up = mm(r, w1[:, pl.ds(pl.multiple_of(FF + f * FC, FC), FC)])
    active = (gate * sigmoid(gate) * up).astype(BF)
    return gate, up, mm(active, w2[pl.ds(at, FC), :])


def backward_chunk(g, gate, up, w1, w2, f):
    at = chunk_at(f)
    grad = mm_nt(g, w2[pl.ds(at, FC), :])
    s = sigmoid(gate)
    grad_s = grad * s
    grad_gate = (grad_s * up * (1.0 + gate * (1.0 - s))).astype(BF)
    grad_up = (grad_s * gate).astype(BF)
    return mm_nt(grad_gate, w1[:, pl.ds(at, FC)]) + mm_nt(
        grad_up, w1[:, pl.ds(pl.multiple_of(FF + f * FC, FC), FC)]
    )


def expert_body(split, kind, *refs):
    count = 2 if split else 1
    gate_ups = refs[:count]
    down_ref, rec_ref, ret_ref, gate_ref, up_ref = refs[count : count + 5]
    w1, w2, rv, pv, gv, uv, acc, wsem, rsem, gsem, usem, send, recv = refs[count + 5 :]
    weights = fetch_weights(split, gate_ups, down_ref, w1, w2, wsem)
    blocks = fetch_blocks(rec_ref, rv, rsem, kind)
    greet(kind)
    for copy in weights + blocks:
        copy.wait()
    stores = []
    moves = []
    for p in range(NP):
        r = rv[p]
        acc[...] = jnp.zeros_like(acc)

        def step(f, carry):
            gate, up, part = forward_chunk(r, w1, w2, f)
            gv[p, :, pl.ds(chunk_at(f), FC)] = gate.astype(BF)
            uv[p, :, pl.ds(chunk_at(f), FC)] = up.astype(BF)
            acc[...] += part
            return carry

        lax.fori_loop(0, FF // FC, step, 0)
        pv[p] = acc[...].astype(BF)
        moves += give_back(pv, p, ret_ref, send, recv, kind)
        for values, ref, sems in ((gv, gate_ref, gsem), (uv, up_ref, usem)):
            copy = pltpu.make_async_copy(values.at[p], ref.at[p], sems.at[p])
            copy.start()
            stores.append(copy)
    for copy in moves + stores:
        copy.wait()


def own_copies(body, ins, near, outs, near_outs, scratch):
    counts = len(ins), len(near), len(outs), len(near_outs), len(scratch)

    def run(*refs):
        far, near_far, targets, near_targets, inner, close = split_refs(refs, *counts)
        close, near_close, sems = split_refs(close, len(near), len(near_outs))
        loads = [
            pltpu.make_async_copy(source, target, sems[0].at[n])
            for n, (source, target) in enumerate(zip(near_far, close))
        ]
        for copy in loads:
            copy.start()

        def ready():
            for copy in loads:
                copy.wait()

        def done(n):
            copy = pltpu.make_async_copy(near_close[n], near_targets[n], sems[1].at[n])
            copy.start()
            return copy

        body(far, close, targets, near_close, inner, ready, done)

    extra = [pltpu.VMEM(v.shape, v.dtype) for v in (*near, *near_outs)]
    extra += [DMA((max(1, len(near)),)), DMA((max(1, len(near_outs)),))]
    return run, [*ins, *near], [*outs, *near_outs], [*scratch, *extra]


def comm_call(body, ins, outs, scratch, name, number, flops, nbytes, near=(), near_outs=()):
    run, ins, outs, scratch = own_copies(body, ins, near, outs, near_outs, scratch)
    far = {} if number is None else dict(collective_id=number, has_side_effects=True)
    return pl.pallas_call(
        run,
        in_specs=[pl.BlockSpec(memory_space=pl.ANY)] * len(ins),
        out_specs=[pl.BlockSpec(memory_space=pl.ANY)] * len(outs),
        out_shape=outs,
        scratch_shapes=scratch,
        compiler_params=pltpu.CompilerParams(vmem_limit_bytes=VMEM_BYTES, **far),
        cost_estimate=pl.CostEstimate(
            flops=int(flops), bytes_accessed=int(nbytes), transcendentals=0
        ),
        name=name,
    )(*ins)


DMA = pltpu.SemaphoreType.DMA
WEIGHTS = [pltpu.VMEM((D, 2 * FF), BF), pltpu.VMEM((FF, D), BF)]
ROWS = pltpu.VMEM((NP, PR, D), BF)
WIDE = pltpu.VMEM((NP, PR, FF), BF)
SUM = pltpu.VMEM((PR, D), F32)
BLOCKS = jax.ShapeDtypeStruct((NFFN, CAP, D), BF)
KEPT = jax.ShapeDtypeStruct((NP, PR, FF), BF)


def expert_forward(received, gate_ups, down, kind):
    split = len(gate_ups) == 2

    def body(far, near, outs, near_outs, scratch, ready, done):
        expert_body(split, kind, *far, *outs, *scratch)

    return comm_call(
        body,
        [*gate_ups, down, received],
        [BLOCKS, KEPT, KEPT],
        WEIGHTS + [ROWS, ROWS, WIDE, WIDE, SUM]
        + [DMA((9,)), DMA((8,)), DMA((NP,)), DMA((NP,)), DMA((8,)), DMA((8,))],
        "expert_forward",
        1,
        2 * SLOTS * D * FF * 3,
        26e6,
    )


def expert_both_body(kind, far, near, out_near, scratch, ready, done):
    gate_up_ref, down_ref, rec_ref, sg_ref, mid_ref, g_ref, mixed_ref, shared_ref = far
    tcol_ref, lg_ref, rt_ref, gain_ref, cv_ref, wt_ref, res_ref, nar_ref, d_ref, u_ref = near
    out_ref, gm_ref, gle_ref, mix_ref, gu_ref, gd_ref = out_near
    (
        w1, w2, rv, sv, pv, gv, uv, back, gback, mid, g, mixed, w3, acc,
        wsem, rsem, ssem, msem, send, recv, gsend, grecv,
    ) = scratch
    weights = fetch_weights(False, [gate_up_ref], down_ref, w1, w2, wsem)
    blocks = fetch_blocks(rec_ref, rv, rsem, kind)
    greet(kind)
    for copy in weights + blocks:
        copy.wait()
    extra = fetch_blocks(sg_ref, sv, ssem, kind)
    for n, (source, target) in enumerate(
        ((mid_ref, mid), (g_ref, g), (mixed_ref, mixed), (shared_ref.at[3], w3))
    ):
        extra.append(pltpu.make_async_copy(source, target, msem.at[n]))
        extra[-1].start()
    moves = []
    for p in range(NP):
        r = rv[p]
        acc[...] = jnp.zeros_like(acc)

        def step(f, carry):
            gate, up, part = forward_chunk(r, w1, w2, f)
            gv[p, :, pl.ds(chunk_at(f), FC)] = gate.astype(BF)
            uv[p, :, pl.ds(chunk_at(f), FC)] = up.astype(BF)
            acc[...] += part
            return carry

        lax.fori_loop(0, FF // FC, step, 0)
        pv[p] = acc[...].astype(BF)
        moves += give_back(pv, p, back, send, recv, kind)
    for copy in extra:
        copy.wait()
    later = []
    for p in range(NP):
        grads = sv[p]
        acc[...] = jnp.zeros_like(acc)

        def step(f, carry):
            at = pl.ds(chunk_at(f), FC)
            gate = gv[p, :, at].astype(F32)
            up = uv[p, :, at].astype(F32)
            acc[...] += backward_chunk(grads, gate, up, w1, w2, f)
            return carry

        lax.fori_loop(0, FF // FC, step, 0)
        rv[p] = acc[...].astype(BF)
        later += give_back(rv, p, gback, gsend, grecv, kind)
    for copy in moves:
        copy.wait()
    ready()

    def finish(i, carry):
        at = pl.ds(pl.multiple_of(i * RB, RB), RB)
        logits, routes, middle = lg_ref[at, :], rt_ref[at, :], mid[at, :]
        following, chosen = combine_rows(
            tcol_ref[at, :], back, middle, logits, routes, gain_ref[...], cv_ref
        )
        out_ref[at, :] = following
        gm_ref[at, :], gle_ref[at, :] = mix_grad(
            g[at, :].astype(F32), middle, chosen, logits, routes, 0.0, gain_ref[...], cv_ref,
            wt_ref[...], res_ref[...],
        )
        return carry

    lax.fori_loop(0, NB, finish, 0)
    stores = [done(0), done(2)]
    gu_ref[...] = jnp.zeros_like(gu_ref)
    gd_ref[...] = jnp.zeros_like(gd_ref)
    for copy in later:
        copy.wait()

    def settle_one(i, carry):
        at = pl.ds(pl.multiple_of(i * RB, RB), RB)
        refs = (tcol_ref, mid, g, mixed, gain_ref, nar_ref, w3, d_ref, u_ref, gu_ref, gd_ref)
        settle_back(refs, at, gm_ref, mix_ref, gback)
        return carry

    lax.fori_loop(0, NB, settle_one, 0)
    for copy in stores + [done(n) for n in (1, 3, 4, 5)]:
        copy.wait()


def expert_both(
    received, slot_grads, gate_up, down, mid, g, mixed, weights, tcol, logits, routes, gain,
    const_vec, router_t, residual_t, narrow, down_out, up_out, kind,
):
    def body(far, near, outs, near_outs, scratch, ready, done):
        expert_both_body(kind, far, near, near_outs, scratch, ready, done)

    half = pltpu.VMEM((T, D), BF)
    landing = pltpu.VMEM((NFFN, CAP, D), BF)
    return comm_call(
        body,
        [gate_up, down, received, slot_grads, mid, g, mixed, weights],
        [],
        WEIGHTS
        + [ROWS, ROWS, ROWS, WIDE, WIDE, landing, landing]
        + [pltpu.VMEM((T, D), F32), pltpu.VMEM((T, D), g.dtype), half, pltpu.VMEM((D, D), BF), SUM]
        + [DMA((9,)), DMA((8,)), DMA((8,)), DMA((4,))]
        + [DMA((8,)), DMA((8,)), DMA((8,)), DMA((8,))],
        "expert_both",
        2,
        2 * SLOTS * D * FF * 6,
        26e6,
        [tcol, logits, routes, gain, const_vec, router_t, residual_t, narrow, down_out, up_out],
        [out((T, D), F32), out((T, D), F32), out((T, 128), F32), out((T, D), BF)]
        + [out((128, D), F32), out((128, D), F32)],
    )


def expert_back_body(split, kind, far, near, out_near, outs, scratch, ready, done):
    count = 2 if split else 1
    gate_ups, (down_ref, gate_ref, up_ref, g_ref, mid_ref, c0_ref, c1_ref, mixed_ref, shared_ref) = (
        far[:count], far[count:]
    )
    (
        trow_ref, tcol_ref, lg_ref, rt_ref, gl_ref, gain_ref, cv_ref, wt_ref, nar_ref, d_ref, u_ref
    ) = near
    gm_ref, gu_ref, gd_ref = out_near
    mix_out = outs[0]
    (
        w1, w2, sgv, rv, pv, gv, uv, back, first, second, g, mid, c0, c1, mixed, w3, acc,
        wsem, gsem, usem, msem, dsend, drecv, send, recv, osem,
    ) = scratch
    extra = [
        pltpu.make_async_copy(ref, values, msem.at[n])
        for n, (ref, values) in enumerate(
            (
                (g_ref, g), (mid_ref, mid), (c0_ref, c0), (c1_ref, c1), (mixed_ref, mixed),
                (shared_ref.at[3], w3),
            )
        )
    ]
    extra[0].start()
    extra[0].wait()
    ready()

    def gated(i, carry):
        at = pl.ds(pl.multiple_of(i * RB, RB), RB)
        gates = mix_terms(lg_ref[at, :], rt_ref[at, :])[0]
        first[at, :] = (gates[0] * g[at, :]).astype(BF)
        second[at, :] = (gates[1] * g[at, :]).astype(BF)
        return carry

    lax.fori_loop(0, NB, gated, 0)
    weights = fetch_weights(split, gate_ups, down_ref, w1, w2, wsem)
    for p in (3, 0, 1, 2):
        for values, ref, sems in ((gv, gate_ref, gsem), (uv, up_ref, usem)):
            copy = pltpu.make_async_copy(ref.at[p], values.at[p], sems.at[p])
            copy.start()
            weights.append(copy)
    for copy in extra[1:]:
        copy.start()
    greet(kind)
    arrivals = {}
    for p, h in PLACES[:-2] + [(3, 1), (3, 0)]:
        where, number = owner_at(p, h, kind)
        place = number * CAP + iota((CAP, T), 0)
        hit0 = (trow_ref[0:1, :] == place).astype(F32).astype(BF)
        hit1 = (trow_ref[1:2, :] == place).astype(F32).astype(BF)
        values = (mm(hit0, first[...]) + mm(hit1, second[...])).astype(BF)
        n = 2 * p + h
        if (p, h) == (NP - 1, 0):
            rv[p, h * CAP : (h + 1) * CAP, :] = values
            continue
        sgv[p, h * CAP : (h + 1) * CAP, :] = values
        copy = pltpu.make_async_remote_copy(
            src_ref=block_of(sgv, p, h),
            dst_ref=block_of(rv, p, h),
            send_sem=dsend.at[n],
            recv_sem=drecv.at[n],
            device_id=where,
            device_id_type=pl.DeviceIdType.MESH,
        )
        copy.start()
        arrivals[p, h] = copy
    for copy in weights + extra[1:]:
        copy.wait()
    moves = []

    for p in (3, 0, 1, 2):
        for h in range(2):
            if (p, h) in arrivals:
                arrivals[p, h].wait()
        grads = rv[p]
        acc[...] = jnp.zeros_like(acc)

        def step(f, carry):
            at = pl.ds(chunk_at(f), FC)
            gate = gv[p, :, at].astype(F32)
            up = uv[p, :, at].astype(F32)
            acc[...] += backward_chunk(grads, gate, up, w1, w2, f)
            return carry

        lax.fori_loop(0, FF // FC, step, 0)
        pv[p] = acc[...].astype(BF)
        moves += give_back(pv, p, back, send, recv, kind)

    def tidy(i, carry):
        at = pl.ds(pl.multiple_of(i * RB, RB), RB)
        gm_ref[at, :] = mix_grad(
            g[at, :], mid[at, :], (c0[at, :], c1[at, :]), lg_ref[at, :], rt_ref[at, :],
            gl_ref[at, :], gain_ref[...], cv_ref, wt_ref[...], None,
        )[0]
        return carry

    lax.fori_loop(0, NB, tidy, 0)
    gu_ref[...] = jnp.zeros_like(gu_ref)
    gd_ref[...] = jnp.zeros_like(gd_ref)
    for copy in moves:
        copy.wait()

    def settle_one(i, carry):
        at = pl.ds(pl.multiple_of(i * RB, RB), RB)
        refs = (tcol_ref, mid, g, mixed, gain_ref, nar_ref, w3, d_ref, u_ref, gu_ref, gd_ref)
        settle_back(refs, at, gm_ref, first, back)
        return carry

    lax.fori_loop(0, NB, settle_one, 0)
    last = pltpu.make_async_copy(first, mix_out, osem.at[0])
    last.start()
    for copy in [last] + [done(n) for n in range(3)]:
        copy.wait()


def expert_backward(
    gate, up, gate_ups, down, g, mid, c0, c1, mixed, weights, trow, tcol, logits, routes, gl, gain,
    const_vec, router_t, narrow, down_out, up_out, kind,
):
    split = len(gate_ups) == 2

    def body(far, near, outs, near_outs, scratch, ready, done):
        expert_back_body(split, kind, far, near, near_outs, outs, scratch, ready, done)

    half, full = pltpu.VMEM((T, D), BF), pltpu.VMEM((T, D), F32)
    mix, gm, gu, gd = comm_call(
        body,
        [*gate_ups, down, gate, up, g, mid, c0, c1, mixed, weights],
        [out((T, D), BF)],
        WEIGHTS
        + [ROWS, ROWS, ROWS, WIDE, WIDE, pltpu.VMEM((NFFN, CAP, D), BF)]
        + [half, half, full, full, half, half, half, pltpu.VMEM((D, D), BF), SUM]
        + [DMA((9,)), DMA((NP,)), DMA((NP,)), DMA((6,))]
        + [DMA((8,)), DMA((8,)), DMA((8,)), DMA((8,)), DMA((1,))],
        "expert_backward",
        3,
        2 * SLOTS * D * FF * 3,
        26e6,
        [
            trow, tcol, logits, routes, gl, gain, const_vec, router_t, narrow, down_out, up_out,
        ],
        [out((T, D), F32), out((128, D), F32), out((128, D), F32)],
    )
    return gm, mix, gu, gd


def mix_terms(logits, routes):
    lane = iota(logits.shape, 1)

    def at(place):
        return jnp.sum(jnp.where(lane == place, logits, 0.0), axis=1, keepdims=True)

    r0, r1 = routes[:, 0:1], routes[:, 1:2]
    gap = at(r0) - at(r1)
    gates = (sigmoid(gap), sigmoid(-gap))

    def weight(e):
        return jnp.where(r0 == e, gates[0], 0.0) + jnp.where(r1 == e, gates[1], 0.0)

    shares = []
    for c in range(2):
        apart = logits[:, 12 + 2 * c : 13 + 2 * c] - logits[:, 13 + 2 * c : 14 + 2 * c]
        shares.append((sigmoid(apart), sigmoid(-apart)))
    weights = [weight(NFFN + 1), weight(NFFN + 2), weight(NFFN + 3)]
    return gates, weights, shares


def rms_scale(v):
    return lax.rsqrt(jnp.mean(v * v, axis=1, keepdims=True) + EPSILON)


def combine_rows(tcol, back_ref, mid, logits, routes, gain, cv_ref):
    place = iota((RB, SLOTS), 1)
    back = back_ref[...].reshape(SLOTS, D)
    chosen = []
    for k in range(2):
        hit = (tcol[:, k : k + 1] == place).astype(F32).astype(BF)
        chosen.append(mm(hit, back))
    normed = mid * rms_scale(mid) * gain
    gates, weights, shares = mix_terms(logits, routes)
    same = weights[0] + weights[1] * shares[0][0] + weights[2] * shares[1][0]
    moe = gates[0] * chosen[0] + gates[1] * chosen[1] + same * normed
    moe = moe + (weights[1] * shares[0][1]) * cv_ref[0:1, :]
    moe = moe + (weights[2] * shares[1][1]) * cv_ref[1:2, :]
    return mid + moe, chosen


def combine_body(tcol_ref, ret_ref, mid_ref, lg_ref, rt_ref, g_ref, cv_ref, x_ref, c0_ref, c1_ref):
    x_ref[...], chosen = combine_rows(
        tcol_ref[...], ret_ref, mid_ref[...], lg_ref[...], rt_ref[...], g_ref[...], cv_ref
    )
    c0_ref[...] = chosen[0].astype(BF)
    c1_ref[...] = chosen[1].astype(BF)


def combine(tcol, returned, mid, logits, routes, gain, const_vec):
    return call(
        combine_body,
        (NB,),
        [
            (tcol, (RB, 128), rows),
            (returned, None),
            (mid, (RB, D), rows),
            (logits, (RB, 128), rows),
            (routes, (RB, 2), rows),
            (gain, None),
            (const_vec, None),
        ],
        [
            (out((T, D), F32), (RB, D), rows),
            (out((T, D), BF), (RB, D), rows),
            (out((T, D), BF), (RB, D), rows),
        ],
        name="combine",
        flops=4 * T * SLOTS * D,
        nbytes=12e6,
    )


def mix_grad(g, mid, chosen, logits, routes, grad, gain, cv_ref, wt, res):
    normed = mid * rms_scale(mid) * gain
    gates, weights, shares = mix_terms(logits, routes)

    def along(v):
        return jnp.sum(g * v, axis=1, keepdims=True)

    same = along(normed)
    const = [along(cv_ref[c : c + 1, :]) for c in range(2)]
    gate_grads = []
    for k in range(2):
        r = routes[:, k : k + 1]
        value = along(chosen[k].astype(F32)) + jnp.where(r == NFFN + 1, same, 0.0)
        for c in range(2):
            mixed = shares[c][0] * same + shares[c][1] * const[c]
            value = value + jnp.where(r == NFFN + 2 + c, mixed, 0.0)
        gate_grads.append(value)
    slope = gates[0] * gates[1] * (gate_grads[0] - gate_grads[1])
    lane = iota((RB, 128), 1)
    grad = grad + jnp.where(lane == routes[:, 0:1], slope, 0.0)
    grad = grad - jnp.where(lane == routes[:, 1:2], slope, 0.0)
    only = grad
    for c in range(2):
        tilt = weights[1 + c] * shares[c][0] * shares[c][1] * (same - const[c])
        grad = grad + jnp.where(lane == 12 + 2 * c, tilt, 0.0)
        grad = grad - jnp.where(lane == 13 + 2 * c, tilt, 0.0)
    keep = weights[0] + weights[1] * shares[0][0] + weights[2] * shares[1][0]
    residual = None if res is None else mm(spread_lanes(only), res)
    return mm(spread_lanes(grad), wt) + keep * g, residual


def settle_back(refs, at, gm_ref, mix_ref, back_ref):
    tcol_ref, mid_ref, g_ref, mixed_ref, gain_ref, nar_ref, w_ref, d_ref, u_ref, gu_ref, gd_ref = refs
    place = iota((RB, SLOTS), 1)
    tcol = tcol_ref[at, :]
    hit = (tcol[:, 0:1] == place) | (tcol[:, 1:2] == place)
    grad = gm_ref[at, :] + mm(hit.astype(F32).astype(BF), back_ref[...].reshape(SLOTS, D))
    grad = g_ref[at, :].astype(F32) + rms_back(grad, mid_ref[at, :], gain_ref[...])
    gm_ref[at, :] = grad
    grad = grad.astype(BF)
    slim = mm_nt(grad, u_ref[...]).astype(BF)
    gu_ref[...] += 2.0 * mm_tn(nar_ref[at, :], grad)
    gd_ref[...] += mm_tn(slim, mixed_ref[at, :])
    mix_ref[at, :] = (mm_nt(grad, w_ref[...]) + mm_nt(slim, d_ref[...])).astype(BF)


def rms_back(grad, v, gain):
    scale = rms_scale(v)
    inner = grad * gain
    return scale * inner - v * (scale**3 * jnp.mean(v * inner, axis=1, keepdims=True))


def attend_back(q, k, v, aug, kf, g, mixed, dqt):
    lane = iota((T, 128), 1)
    low = lane < 64
    lane6 = lane & 63
    product = g.astype(F32) * mixed.astype(F32)
    d0 = jnp.sum(jnp.where(low, product, 0.0), axis=1, keepdims=True)
    d1 = jnp.sum(jnp.where(low, 0.0, product), axis=1, keepdims=True)
    a, b, c = three(-jnp.where(low, d1, d0))
    zero = jnp.zeros((T, 128), BF)
    ga = jnp.where(lane6 == 0, a, jnp.where(lane6 == 1, b, jnp.where(lane6 == 2, c, zero)))
    va = (lane6 < 3).astype(F32).astype(BF)
    qs = (jnp.where(low, q, aug), jnp.where(low, aug, q))
    ks = (jnp.where(low, k, kf), jnp.where(low, kf, k))
    vs = (jnp.where(low, v, va), jnp.where(low, va, v))
    gs = (jnp.where(low, g, ga), jnp.where(low, ga, g))
    kt = k.T
    tri = iota((RB, RB), 0) <= iota((RB, RB), 1)
    low = low[:RB]
    dks = []
    dvs = []
    for i in range(NB):
        here = slice(i * RB, (i + 1) * RB)
        dk = [None, None]
        dv = [None, None]
        for h in range(2):
            half = slice(h * 64, (h + 1) * 64)
            for start, stop in ((i * RB, (i + 1) * RB), ((i + 1) * RB, T)):
                if start == stop:
                    continue
                there = slice(start, stop)
                p = jnp.exp2(mm_nt(ks[h][here], qs[h][there]) * LOG_SCALE)
                if stop == (i + 1) * RB:
                    p = jnp.where(tri, p, 0.0)
                ds = (p * mm_nt(vs[h][here], gs[h][there])).astype(BF)
                p = p.astype(BF)
                dv_part = mm(p, g[there])
                dk_part = mm(ds, q[there])
                dk[h] = dk_part if dk[h] is None else dk[h] + dk_part
                dv[h] = dv_part if dv[h] is None else dv[h] + dv_part
                part = mm(kt[half, here], ds)
                if i == 0:
                    dqt[half, there] = part
                else:
                    dqt[half, there] += part
        dvs.append(jnp.where(low, dv[0], dv[1]))
        dks.append(jnp.where(low, dk[0], dk[1]))
    return dqt[...].T, jnp.concatenate(dks), jnp.concatenate(dvs)


def layer_back_body(far, near, out_near, gx_ref, scratch, ready, done):
    gm_ref, mix_ref, mixed_ref, w_ref, qkv_ref, aug_ref, n_ref, x_ref = far
    gain_ref, nar_ref, d_ref, u_ref, kf_ref, cos_ref, sin_ref = near
    gu_ref, gd_ref = out_near
    gm, mix, mixed, w, qkv, aug, n, x, gproj, dqt, sems, pair_sems, out_sems = scratch

    def start(source, target, sem):
        copy = pltpu.make_async_copy(source, target, sem)
        copy.start()
        return copy

    def cols(part, j):
        return pl.ds(pl.multiple_of(part * D + j * 128, 128), 128)

    def of_pair(j):
        copies = [
            pltpu.make_async_copy(
                qkv_ref.at[:, cols(part, j)], qkv.at[:, cols(part, j)], pair_sems.at[j, part]
            )
            for part in range(3)
        ]
        for k, (source, target) in enumerate(((mix_ref, mix), (mixed_ref, mixed))):
            copies.append(
                pltpu.make_async_copy(
                    source.at[:, cols(0, j)], target.at[:, cols(0, j)], pair_sems.at[j, 3 + k]
                )
            )
        copies.append(pltpu.make_async_copy(aug_ref.at[j], aug.at[j], pair_sems.at[j, 5]))
        return copies

    for j in range(PAIRS):
        for copy in of_pair(j):
            copy.start()
    third = [start(w_ref.at[k], w.at[k], sems.at[k]) for k in range(3)]
    third += [
        start(source, target, sems.at[3 + k])
        for k, (source, target) in enumerate(((n_ref, n), (x_ref, x), (gm_ref, gm)))
    ]
    ready()

    def pair(j, carry):
        for copy in of_pair(j):
            copy.wait()
        dq, dk, dv = attend_back(
            qkv[:, cols(0, j)], qkv[:, cols(1, j)], qkv[:, cols(2, j)], aug[j], kf_ref[...],
            mix[:, cols(0, j)], mixed[:, cols(0, j)], dqt,
        )
        for part, value in enumerate((dq, dk)):
            value = (value * (1.0 / math.sqrt(HD))).astype(BF).astype(F32)
            gproj[:, cols(part, j)] = turn(value, cos_ref[...], -sin_ref[...]).astype(BF)
        gproj[:, cols(2, j)] = dv.astype(BF)
        return carry

    lax.fori_loop(0, PAIRS, pair, 0)
    for copy in third:
        copy.wait()
    gu_ref[...] = jnp.zeros_like(gu_ref)
    gd_ref[...] = jnp.zeros_like(gd_ref)
    stores = []
    for i in range(NB):
        at = slice(i * RB, (i + 1) * RB)
        grad = jnp.zeros((RB, D), F32)
        slim = jnp.zeros((RB, 128), F32)
        narrow = nar_ref[at, :]
        for part in range(3):
            columns = slice(part * D, (part + 1) * D)
            piece = gproj[at, columns]
            grad = grad + mm_nt(piece, w[part])
            slim = slim + mm_nt(piece, u_ref[:, columns])
            gu_ref[:, columns] += 2.0 * mm_tn(narrow, piece)
        slim = slim.astype(BF)
        gd_ref[...] += mm_tn(slim, n[at, :])
        grad = grad + mm_nt(slim, d_ref[...])
        gm[at, :] = gm[at, :] + rms_back(grad, x[at, :].astype(F32), gain_ref[...])
        stores.append(start(gm.at[at, :], gx_ref.at[at, :], out_sems.at[i]))
    for copy in stores + [done(0), done(1)]:
        copy.wait()


def layer_back(gm, mix, mixed, w, qkv, aug, n, x, gain0, narrow, down, up, kf, cos, sin):
    far = [gm, mix, mixed, w, qkv, aug, n, x]

    def body(far, near, outs, near_outs, scratch, ready, done):
        layer_back_body(far, near, near_outs, outs[0], scratch, ready, done)

    shapes = [out((3, D, D), BF) if v is w else v for v in far]
    return comm_call(
        body,
        far,
        [out((T, D), F32)],
        [pltpu.VMEM(v.shape, v.dtype) for v in shapes]
        + [pltpu.VMEM((T, 3 * D), BF), pltpu.VMEM((128, T), F32)]
        + [DMA((6,)), DMA((PAIRS, 6)), DMA((NB,))],
        "layer_back",
        None,
        12 * 10 * T * T * 128 + 2 * T * D * 3 * D,
        4e7,
        [gain0, narrow, down, up, kf, cos, sin],
        [out((128, 3 * D), F32), out((128, D), F32)],
    )


AXES = ("x", "c", "zh", "zl", "y")
EXPERT, SHARD = AXES[:2], AXES[2:]
PIECE = 96


def shared_body(count, *refs):
    (p_ref,), away, (o_ref,), came, sems = split_refs(refs, 1, count, 1, count)
    local, zs, zr, ys, yr, xs, xr, cs, cr, ws, wr = sems
    x, c, y = (lax.axis_index(name) for name in ("x", "c", "y"))
    z = 2 * lax.axis_index("zh") + lax.axis_index("zl")
    mine, theirs = 2 * x + c, 2 * (1 - x) + c

    def spot(quarter, column, j):
        at = (2 * ((z + 4 - j) % 4) + column) * PIECE
        return o_ref.at[quarter, pl.ds(pl.multiple_of(at, PIECE), PIECE), :]

    others = [{"zh": (z + d) % 4 // 2, "zl": (z + d) % 2} for d in range(1, 4)]
    others += [{"y": 1 - y}, {"x": 1 - x}, {"c": 1 - c}]
    barrier = pltpu.get_barrier_semaphore()
    for who in others:
        pl.semaphore_signal(barrier, inc=1, device_id=who, device_id_type=pl.DeviceIdType.MESH)
    pl.semaphore_wait(barrier, len(others))

    started = []

    def send(source, target, who, send_sem, recv_sem):
        copy = pltpu.make_async_remote_copy(
            src_ref=source,
            dst_ref=target,
            send_sem=send_sem,
            recv_sem=recv_sem,
            device_id=who,
            device_id_type=pl.DeviceIdType.MESH,
        )
        copy.start()
        started.append(copy)
        return copy

    core_copies = []

    def to_core(source, target):
        n = len(core_copies)
        core_copies.append(send(source, target, others[5], cs.at[n], cr.at[n]))

    own = pltpu.make_async_copy(p_ref, spot(mine, y, 0), local.at[0])
    own.start()
    z_copies = [
        send(p_ref, spot(mine, y, 0), others[d], zs.at[d], zr.at[d]) for d in range(3)
    ]
    y_copies = [None] * 6
    x_copies = [None] * 6

    def along_y(n, source, target):
        y_copies[n] = send(source, target, others[3], ys.at[n], yr.at[n])

    def along_x(n, source, target):
        x_copies[n] = send(source, target, others[4], xs.at[n], xr.at[n])

    along_y(0, p_ref, spot(mine, y, 0))
    along_x(0, p_ref, spot(mine, y, 0))
    to_core(p_ref, spot(mine, y, 0))
    swaps = [
        send(source, target, others[3], ws.at[n], wr.at[n])
        for n, (source, target) in enumerate(zip(away, came))
    ]
    for j in range(1, 4):
        z_copies[j - 1].wait_recv()
        piece = spot(mine, y, j)
        along_y(j, piece, piece)
        along_x(j, piece, piece)
        to_core(piece, piece)
    for j in range(4):
        y_copies[j].wait_recv()
        piece = spot(mine, 1 - y, j)
        if j < 2:
            along_x(4 + j, piece, piece)
        to_core(piece, piece)
        x_copies[j].wait_recv()
        piece = spot(theirs, y, j)
        if j >= 2:
            along_y(2 + j, piece, piece)
        to_core(piece, piece)
    for j in range(4):
        (x_copies[4 + j] if j < 2 else y_copies[2 + j]).wait_recv()
        piece = spot(theirs, 1 - y, j)
        to_core(piece, piece)
    for copy in core_copies + swaps:
        copy.wait_recv()
    own.wait()
    for copy in started:
        copy.wait_send()


def usual():
    return tuple(lax.axis_size(name) for name in AXES) == (2, 2, 2, 2, 2)


def gather_shared(qkv, output, away=()):
    rows_here = qkv.shape[0]
    parts = jnp.concatenate([qkv.reshape(rows_here, 3, D).transpose(1, 0, 2), output[None]])
    if not usual():
        return [lax.all_gather(parts, SHARD, axis=1, tiled=True)]
    quarter = 2 * lax.axis_index("x") + lax.axis_index("c")
    piece = lax.dynamic_index_in_dim(parts, quarter, axis=0, keepdims=False)
    return comm_call(
        lambda far, near, outs, near_outs, scratch, ready, done: shared_body(
            len(away), *far, *outs, *scratch
        ),
        [piece, *away],
        [jax.ShapeDtypeStruct(v.shape, v.dtype) for v in (out((4, D, D), BF), *away)],
        [DMA((n,)) for n in (1, 3, 3, 6, 6, 6, 6, 16, 16, 2, 2)],
        "gather_shared",
        5 if away else 0,
        0,
        5e7,
    )


SPAN = 96
UNIT = LAYERS * 2 * 4 * R


def adapters_body(*refs):
    id_ref, parts = refs[0], refs[1 : 1 + 4 * LAYERS]
    o_ref = refs[1 + 4 * LAYERS]
    sbuf, rbuf, tbuf, ubuf, asend, arecv, bsend, brecv = refs[2 + 4 * LAYERS :]
    x, c, y = (lax.axis_index(name) for name in ("x", "c", "y"))
    z = 2 * lax.axis_index("zh") + lax.axis_index("zl")
    mates = []
    for dz in range(4):
        for dy in range(2):
            mates.append(((z + dz) % 4, flip(y, dy)))
    groups = [(flip(x, dx), flip(c, dc)) for dx in range(2) for dc in range(2)]
    barrier = pltpu.get_barrier_semaphore()
    peers = [{"zh": a // 2, "zl": a % 2, "y": b} for a, b in mates[1:]]
    peers += [{"x": a, "c": b} for a, b in groups[1:]]
    for who in peers:
        pl.semaphore_signal(barrier, inc=1, device_id=who, device_id_type=pl.DeviceIdType.MESH)
    for layer in range(LAYERS):
        gd_in, gd_out, gu_in, gu_out = parts[4 * layer : 4 * layer + 4]
        pieces = [gd_in[p * R : (p + 1) * R, :] for p in range(3)] + [gd_out[:R, :]]
        pieces += [gu_in[p * R : (p + 1) * R, p * D : (p + 1) * D] for p in range(3)] + [gu_out[:R, :]]
        sbuf[:, layer * 128 : (layer + 1) * 128] = jnp.concatenate(pieces).T.astype(BF)
    sbuf[:, UNIT:] = jnp.broadcast_to(id_ref[0].astype(F32).astype(BF), (D, 128))

    def share(k):
        return sbuf.at[pl.ds(pl.multiple_of(k * SPAN, SPAN), SPAN), :]

    pl.semaphore_wait(barrier, len(peers))
    me = 2 * z + y
    copies = []
    for n, (a, b) in enumerate(mates):
        if n == 0:
            rbuf[0] = share(me)[...]
            continue
        copy = pltpu.make_async_remote_copy(
            src_ref=share(2 * a + b),
            dst_ref=rbuf.at[(4 - n // 2) % 4 * 2 + n % 2],
            send_sem=asend.at[n],
            recv_sem=arecv.at[(4 - n // 2) % 4 * 2 + n % 2],
            device_id={"zh": a // 2, "zl": a % 2, "y": b},
            device_id_type=pl.DeviceIdType.MESH,
        )
        copy.start()
        copies.append(copy)
    for copy in copies:
        copy.wait()
    masks = []
    for n in range(8):
        own = rbuf[n, 0:16, UNIT:][0:1, 0:1].astype(F32)
        masks.append([(own == k).astype(F32) for k in range(NA)])

    def add(i, carry):
        at = pl.ds(pl.multiple_of(i * 16, 16), 16)
        sums = [jnp.zeros((16, UNIT), F32) for _ in range(NA)]
        for n in range(8):
            values = rbuf[n, at, :UNIT].astype(F32)
            for k in range(NA):
                sums[k] = sums[k] + values * masks[n][k]
        for k in range(NA):
            tbuf[k, at, :] = sums[k].astype(BF)
        return carry

    lax.fori_loop(0, SPAN // 16, add, 0)
    copies = []
    ubuf[0] = tbuf[pl.ds(2 * (2 * x + c), 2)]
    for n, (a, b) in enumerate(groups):
        if n == 0:
            continue
        copy = pltpu.make_async_remote_copy(
            src_ref=tbuf.at[pl.ds(2 * (2 * a + b), 2)],
            dst_ref=ubuf.at[n],
            send_sem=bsend.at[n],
            recv_sem=brecv.at[n],
            device_id={"x": a, "c": b},
            device_id_type=pl.DeviceIdType.MESH,
        )
        copy.start()
        copies.append(copy)
    for copy in copies:
        copy.wait()
    total = ubuf[0].astype(F32)
    for n in range(1, 4):
        total = total + ubuf[n].astype(F32)
    o_ref[...] = total


def adapters(own, parts):
    specs = [pl.BlockSpec(memory_space=pltpu.SMEM)]
    specs += [pl.BlockSpec(memory_space=pltpu.VMEM)] * len(parts)
    return pl.pallas_call(
        adapters_body,
        in_specs=specs,
        out_specs=pl.BlockSpec(memory_space=pltpu.VMEM),
        out_shape=jax.ShapeDtypeStruct((2, SPAN, UNIT), F32),
        scratch_shapes=[
            pltpu.VMEM((D, UNIT + 128), BF),
            pltpu.VMEM((8, SPAN, UNIT + 128), BF),
            pltpu.VMEM((NA, SPAN, UNIT), BF),
            pltpu.VMEM((4, 2, SPAN, UNIT), BF),
            DMA((8,)),
            DMA((8,)),
            DMA((4,)),
            DMA((4,)),
        ],
        compiler_params=pltpu.CompilerParams(
            vmem_limit_bytes=VMEM_BYTES, collective_id=4, has_side_effects=True
        ),
        name="adapters",
    )(own, *parts)


def both_rows(mine, other):
    y = lax.axis_index("y")
    return jnp.where(y == 0, jnp.stack([mine, other]), jnp.stack([other, mine]))


def own_and_other(w):
    y = lax.axis_index("y")
    return [lax.dynamic_index_in_dim(w, e, axis=0, keepdims=False) for e in (y, 1 - y)]


def across_y(v):
    return lax.ppermute(v, "y", [(0, 1), (1, 0)])


def swapped(w):
    mine, other = own_and_other(w)
    return both_rows(mine, across_y(other))


def gathered(w, axes):
    return lax.all_gather(w, axes, axis=0, tiled=True).reshape(-1, w.shape[-1])


def exchange(v, kind):
    return lax.all_to_all(v, OWNERS[kind], split_axis=0, concat_axis=0, tiled=True)


def pad_to(v, shape):
    return jnp.pad(v, [(0, n - m) for m, n in zip(v.shape, shape)])


def adapters_plain(owners, parts):
    layers = []
    for gd_in, gd_out, gu_in, gu_out in parts:
        downs = [gd_in[p * R : (p + 1) * R] for p in range(3)] + [gd_out[:R]]
        ups = [gu_in[p * R : (p + 1) * R, p * D : (p + 1) * D] for p in range(3)] + [gu_out[:R]]
        layers.append(jnp.concatenate(downs + ups))
    compact = jnp.concatenate(layers).astype(BF)
    ranks = lax.axis_size(SHARD)
    pieces = compact.reshape(UNIT, ranks, D // ranks).transpose(1, 0, 2)
    pieces = lax.all_to_all(pieces, SHARD, split_axis=0, concat_axis=0, tiled=True)
    pick = (owners[None, :] == jnp.arange(NA, dtype=jnp.int32)[:, None]).astype(F32)
    summed = jnp.dot(pick, pieces.reshape(ranks, -1).astype(F32), precision=HIGHEST).astype(BF)
    groups = lax.axis_size(EXPERT)
    summed = lax.all_to_all(
        summed.reshape(groups, NA // groups, -1), EXPERT, split_axis=0, concat_axis=0, tiled=True
    )
    summed = jnp.sum(summed.astype(F32), axis=0)
    return summed.reshape(summed.shape[0], UNIT, -1).transpose(0, 2, 1)


def per_device(
    tokens,
    segments,
    parents,
    adapter_of,
    routes,
    norm_gain,
    query_key_value_weight,
    output_weight,
    adapter_down,
    adapter_up,
    router,
    router_residual,
    const_proj,
    const_vec,
    w_gate_up,
    w_down,
    out_grad,
):
    fast = w_gate_up.shape[1] == 2
    kind = PLANE if fast else WIDE_SLICE
    barrier = lax.optimization_barrier
    if fast:
        mine, other = own_and_other(w_gate_up[0])
        parts = [lax.all_gather(mine, ("zh", "zl"), axis=0)]
        down_mine, down_other = own_and_other(w_down[0])
        first, other, down_other = gather_shared(
            query_key_value_weight[0], output_weight[0], (other, down_other)
        )
        shared = [first]
        parts.append(lax.all_gather(other, ("zh", "zl"), axis=0))
        gate_up_full = [parts]
        down_full = [gathered(both_rows(down_mine, down_other), ("zh", "zl"))]
    else:
        shared = gather_shared(query_key_value_weight[0], output_weight[0])
        gate_up_full = [[gathered(w_gate_up[layer, 0], SHARD)] for layer in range(LAYERS)]
        down_full = [gathered(w_down[layer, 0], SHARD) for layer in range(LAYERS)]

    which = adapter_of[0]
    down_sel = lax.dynamic_index_in_dim(adapter_down, which, axis=2, keepdims=False)
    up_sel = lax.dynamic_index_in_dim(adapter_up, which, axis=2, keepdims=False)
    down_in = jnp.pad(
        down_sel[:, :3].transpose(0, 2, 1, 3).reshape(LAYERS, D, 3 * R), ((0, 0), (0, 0), (0, 80))
    )
    down_out = jnp.pad(down_sel[:, 3], ((0, 0), (0, 0), (0, 112)))
    up_t = 2.0 * up_sel.transpose(0, 1, 3, 2)
    up_in = jnp.zeros((LAYERS, 128, 3 * D), BF)
    for p in range(3):
        up_in = up_in.at[:, p * R : (p + 1) * R, p * D : (p + 1) * D].set(up_t[:, p])
    up_out = jnp.pad(up_t[:, 3], ((0, 0), (0, 112), (0, 0)))
    rcat = jnp.concatenate([router, const_proj[:, 0], const_proj[:, 1]], axis=2)
    rcat = jnp.pad(rcat, ((0, 0), (0, 0), (0, 112)))
    rcat_t = rcat[:, :, :16].transpose(0, 2, 1)
    residual = pad_to(router_residual, (16, 128))
    residual_t = pad_to(router_residual.T, (16, 128))

    qf, kf, cos, sin, tcol, trow, router_s, router_ts, residual_s, residual_ts = prep(
        parents, segments.reshape(T, 1), routes, rcat, rcat_t, residual, residual_t
    )

    stream = tokens
    earlier = jnp.zeros((T, 128), F32)
    saved = []
    for layer in range(LAYERS):
        gain0 = norm_gain[layer, 0:1]
        gain1 = norm_gain[layer, 1:2]
        normed, narrow, qkv = project(
            stream, gain0, shared[layer], down_in[layer], up_in[layer], cos, sin
        )
        mixed, aug = attend(qkv, qf, kf)
        mid, sent, logits, narrow_out = settle(
            stream, mixed, shared[layer], down_out[layer], up_out[layer], gain1, router_s[layer],
            earlier, residual_s,
        )
        buffer = dispatch(trow, sent)
        received = exchange(buffer, kind)
        if layer == 0:
            if fast:
                later = barrier((w_gate_up[1], w_down[1], logits))
                gate_up_full.append([gathered(swapped(later[0]), ("zh", "zl"))])
                down_full.append(gathered(swapped(later[1]), ("zh", "zl")))
            later = lax.optimization_barrier(
                (query_key_value_weight[1], output_weight[1], logits)
            )
            shared += gather_shared(later[0], later[1])
            returned, gate, up = expert_forward(received, gate_up_full[0], down_full[0], kind)
        else:
            slot_grads = exchange(dispatch_grad(trow, out_grad, logits, routes), kind)
            following, grad_mid, grad_logits, grad_mixed, gu_out, gd_out = expert_both(
                received, slot_grads, gate_up_full[1][0], down_full[1], mid, out_grad, mixed,
                shared[1], tcol, logits, routes, gain1, const_vec[1], router_ts[1], residual_ts,
                narrow_out, down_out[1], up_out[1], kind,
            )
            c0 = c1 = None
        if layer == 0:
            following, c0, c1 = combine(
                tcol, returned.reshape(SLOTS, D), mid, logits, routes, gain1, const_vec[0]
            )
        saved.append((stream, normed, narrow, qkv, mixed, aug, mid, logits, narrow_out, c0, c1))
        stream = following
        earlier = logits

    grad = out_grad
    parts = [None] * LAYERS
    for layer in reversed(range(LAYERS)):
        x_in, normed, narrow, qkv, mixed, aug, mid, logits, narrow_out, c0, c1 = saved[layer]
        gain0 = norm_gain[layer, 0:1]
        gain1 = norm_gain[layer, 1:2]
        if layer == 0:
            grad_mid, grad_mixed, gu_out, gd_out = expert_backward(
                gate, up, gate_up_full[0], down_full[0], grad, mid, c0, c1, mixed, shared[0], trow,
                tcol, logits, routes, grad_logits, gain1, const_vec[0], router_ts[0], narrow_out,
                down_out[0], up_out[0], kind,
            )
        grad, gu_in, gd_in = layer_back(
            grad_mid, grad_mixed, mixed, shared[layer], qkv, aug, normed, x_in, gain0, narrow,
            down_in[layer], up_in[layer], kf, cos, sin,
        )
        parts[layer] = (gd_in, gd_out, gu_in, gu_out)

    if usual():
        final = adapters(adapter_of, [v for layer in parts for v in layer])
    else:
        final = adapters_plain(lax.all_gather(adapter_of, SHARD, axis=0, tiled=True), parts)
    final = final.reshape(*final.shape[:2], LAYERS, 2, 4, R).transpose(3, 2, 4, 0, 1, 5)
    return (stream, grad, final[0], final[1])


def solution(mesh):
    owners, shards = mesh.shape["expert"], mesh.shape["shard"]
    each = NFFN // owners
    fine = jax.sharding.Mesh(
        mesh.devices.reshape(owners // 2, 2, shards // each**2, each, each), AXES
    )
    expert, shard, both = EXPERT, SHARD, AXES
    in_specs = (
        P(both, None),
        P(both, None),
        P(both, None),
        P(both),
        P(both, None),
        P(),
        P(None, shard, None),
        P(None, shard, None),
        P(),
        P(),
        P(),
        P(),
        P(),
        P(),
        P(None, expert, shard, None),
        P(None, expert, shard, None),
        P(both, None),
    )
    out_specs = (
        P(both, None),
        P(both, None),
        P(None, None, expert, shard, None),
        P(None, None, expert, shard, None),
    )
    return jax.shard_map(
        per_device, mesh=fine, in_specs=in_specs, out_specs=out_specs, check_vma=False
    )
```

```python
import functools
import math

import jax
import jax.numpy as jnp
from jax import lax
from jax.experimental import pallas as pl
from jax.experimental.pallas import tpu as pltpu
from jax.sharding import PartitionSpec as P

D = 768
HEADS = 12
HD = 64
FF = 2048
NFFN = 8
NEXP = 12
R = 16
NA = 8
NSEG = 13
LAYERS = 2
CAP = 192
T = 1024
SLOTS = NFFN * CAP
RB = 256
NB = T // RB
PAIRS = HEADS // 2
FC = 512
EPSILON = 1e-06
BIG = 2.0**100
LOG_SCALE = math.log2(math.e) / math.sqrt(HD)
F32 = jnp.float32
BF = jnp.bfloat16
HIGHEST = lax.Precision.HIGHEST
VMEM_BYTES = 60 * 1024 * 1024


def mm(a, b):
    return lax.dot_general(a, b, (((1,), (0,)), ((), ())), preferred_element_type=F32)


def mm_nt(a, b):
    return lax.dot_general(a, b, (((1,), (1,)), ((), ())), preferred_element_type=F32)


def mm_tn(a, b):
    return lax.dot_general(a, b, (((0,), (0,)), ((), ())), preferred_element_type=F32)


def mm_exact(a, b):
    return lax.dot_general(
        a, b, (((1,), (0,)), ((), ())), preferred_element_type=F32, precision=HIGHEST
    )


def iota(shape, axis):
    return lax.broadcasted_iota(jnp.int32, shape, axis)


def sigmoid(v):
    return 1.0 / (1.0 + jnp.exp(-v))


def call(body, grid, ins, outs, scratch=(), name=None, flops=0, nbytes=0):
    def spec(entry):
        if entry[1] == "smem":
            return pl.BlockSpec(memory_space=pltpu.SMEM)
        if entry[1] is None:
            shape = entry[0].shape
            return pl.BlockSpec(shape, lambda *_: (0,) * len(shape))
        return pl.BlockSpec(entry[1], entry[2])

    return pl.pallas_call(
        body,
        grid=grid,
        in_specs=[spec(e) for e in ins],
        out_specs=[spec(e) for e in outs],
        out_shape=[jax.ShapeDtypeStruct(e[0].shape, e[0].dtype) for e in outs],
        scratch_shapes=list(scratch),
        compiler_params=pltpu.CompilerParams(
            dimension_semantics=("arbitrary",) * len(grid), vmem_limit_bytes=VMEM_BYTES
        ),
        cost_estimate=pl.CostEstimate(
            flops=int(flops), bytes_accessed=int(nbytes), transcendentals=0
        ),
        name=name,
    )(*[e[0] for e in ins])


def out(shape, dtype):
    return jax.ShapeDtypeStruct(shape, dtype)


def rows(i):
    return (i, 0)


def three(v):
    high = v.astype(BF)
    rest = v - high.astype(F32)
    middle = rest.astype(BF)
    return high, middle, (rest - middle.astype(F32)).astype(BF)


def spread_lanes(v):
    a, b, c = (part.astype(F32) for part in three(v))
    total = a + pltpu.roll(b, 16, 1) + pltpu.roll(c, 32, 1)
    total = total + pltpu.roll(a, 48, 1) + pltpu.roll(b, 64, 1) + pltpu.roll(a, 80, 1)
    return total.astype(BF)


def stack_rows(w):
    a, b, c = three(w)
    return jnp.concatenate([a, a, a, b, b, c, jnp.zeros((32, w.shape[1]), BF)], axis=0)


def prep_body(
    par_ref, seg_ref, rt_ref, rc_ref, rct_ref, res_ref, rest_ref,
    qf_ref, kf_ref, cos_ref, sin_ref, tcol_ref, trow_ref, rs_ref, rts_ref, ress_ref, rests_ref, anc,
):
    for layer in range(LAYERS):
        a, b, c = (part.astype(F32) for part in three(rc_ref[layer]))
        rs_ref[layer] = (a + pltpu.roll(b, 16, 1) + pltpu.roll(c, 32, 1)).astype(BF)
        rts_ref[layer] = stack_rows(rct_ref[layer])
    ress_ref[...] = stack_rows(res_ref[...])
    rests_ref[...] = stack_rows(rest_ref[...])
    first = iota((1, 128), 1) & 63
    anc[...] = jnp.zeros_like(anc)
    anc[0:1, :] = (first == 0).astype(F32)
    for s in range(1, NSEG):
        above = anc[pl.ds(par_ref[0, s], 1), :]
        anc[s : s + 1, :] = jnp.maximum(above, (first == s).astype(F32))
    lane = iota((T, 128), 1)
    lane6 = lane & 63
    low = lane < 64
    member = (seg_ref[...] == lane6).astype(F32)
    ways = mm(jnp.where(low, member, 0.0).astype(BF), anc[...].astype(BF))
    qf_ref[...] = jnp.where(lane6 < NSEG, (ways - 1.0) * BIG, 0.0).astype(BF)
    ones = ((lane6 >= 16) & (lane6 < 19)).astype(F32)
    kf_ref[...] = (member + ones).astype(BF)
    hit0 = (rt_ref[:, 0:1] == lane).astype(F32)
    hit1 = (rt_ref[:, 1:2] == lane).astype(F32)
    hits = hit0 + hit1
    upto = (iota((T, T), 0) >= iota((T, T), 1)).astype(F32).astype(BF)
    seen = mm(upto, jnp.concatenate([member.astype(BF), hits.astype(BF)], axis=1))
    depth = jnp.sum(jnp.where(low, ways * seen[:, :128], 0.0), axis=1, keepdims=True) - 1.0
    before = seen[:, 128:] - hits

    def target(hit, route):
        slot = jnp.sum(hit * before, axis=1, keepdims=True)
        place = route.astype(F32) * CAP + slot
        return jnp.where(route < NFFN, place, 4.0 * SLOTS)

    t0 = target(hit0, rt_ref[:, 0:1])
    t1 = target(hit1, rt_ref[:, 1:2])
    both = jnp.where(lane == 0, t0, jnp.where(lane == 1, t1, 0.0))
    tcol_ref[...] = both.astype(jnp.int32)
    trow_ref[...] = both.T[0:8, :].astype(jnp.int32)
    inverse = jnp.exp((lane & 31).astype(F32) * (-math.log(10000.0) / 32.0))
    angle = depth * inverse
    cos_ref[...] = jnp.cos(angle)
    sine = jnp.sin(angle)
    sin_ref[...] = jnp.where((lane & 32) == 0, -sine, sine)


def prep(parents, seg_col, routes, rcat, rcat_t, residual, residual_t):
    return call(
        prep_body,
        (1,),
        [
            (parents, "smem"),
            (seg_col, None),
            (routes, None),
            (rcat, None),
            (rcat_t, None),
            (residual, None),
            (residual_t, None),
        ],
        [
            (out((T, 128), BF), None),
            (out((T, 128), BF), None),
            (out((T, 128), F32), None),
            (out((T, 128), F32), None),
            (out((T, 128), jnp.int32), None),
            (out((8, T), jnp.int32), None),
            (out((LAYERS, D, 128), BF), None),
            (out((LAYERS, 128, D), BF), None),
            (out((128, 128), BF), None),
            (out((128, 128), BF), None),
        ],
        [pltpu.VMEM((128, 128), F32)],
        name="prep",
        flops=2 * T * T * 256,
        nbytes=3e6,
    )


def turn(v, cos, sin):
    first = (iota(v.shape, 1) & 32) == 0
    other = jnp.where(first, pltpu.roll(v, 96, 1), pltpu.roll(v, 32, 1))
    return v * cos + other * sin


def project_rows(x, gain, w_ref, d_ref, u_ref, cos, sin, n_ref, nar_ref, qkv_ref):
    scale = lax.rsqrt(jnp.mean(x * x, axis=1, keepdims=True) + EPSILON)
    normed = (x * scale * gain).astype(BF)
    n_ref[...] = normed
    narrow = mm(normed, d_ref[...]).astype(BF)
    nar_ref[...] = narrow
    for block in range(3):
        cols = slice(block * D, (block + 1) * D)
        part = mm(normed, w_ref[block]) + mm(narrow, u_ref[:, cols])
        for j in range(PAIRS):
            piece = part[:, j * 128 : (j + 1) * 128]
            if block < 2:
                piece = turn(piece, cos, sin)
            at = block * D + j * 128
            qkv_ref[:, at : at + 128] = piece.astype(BF)


def project_body(x_ref, g_ref, w_ref, d_ref, u_ref, cos_ref, sin_ref, n_ref, nar_ref, qkv_ref):
    project_rows(
        x_ref[...].astype(F32),
        g_ref[...],
        w_ref,
        d_ref,
        u_ref,
        cos_ref[...],
        sin_ref[...],
        n_ref,
        nar_ref,
        qkv_ref,
    )


def project(x, gain, w, down, up, cos, sin):
    return call(
        project_body,
        (NB,),
        [
            (x, (RB, D), rows),
            (gain, None),
            (w, (3, D, D), lambda i: (0, 0, 0)),
            (down, None),
            (up, None),
            (cos, (RB, 128), rows),
            (sin, (RB, 128), rows),
        ],
        [
            (out((T, D), BF), (RB, D), rows),
            (out((T, 128), BF), (RB, 128), rows),
            (out((T, 3 * D), BF), (RB, 3 * D), rows),
        ],
        name="project",
        flops=2 * T * D * 3 * D,
        nbytes=12e6,
    )


def attend_body(q_ref, k_ref, v_ref, qf_ref, kf_ref, mixed_ref, aug_ref):
    low = iota((T, 128), 1) < 64
    k = k_ref[...]
    kf = kf_ref[...]
    v = v_ref[...]
    one = jnp.ones((T, 128), BF)
    keys = (jnp.where(low, k, kf), jnp.where(low, kf, k))
    values = (jnp.where(low, v, one), jnp.where(low, one, v))
    low = low[:RB]
    tri = iota((RB, RB), 0) >= iota((RB, RB), 1)
    lane6 = iota((RB, 128), 1) & 63
    for i in range(NB):
        here = slice(i * RB, (i + 1) * RB)
        q = q_ref[here, :]
        qf = qf_ref[here, :]
        tops = []
        outs = []
        for h in range(2):
            qa = jnp.where(low, q, qf) if h == 0 else jnp.where(low, qf, q)
            diag = jnp.where(tri, mm_nt(qa, keys[h][here]), -BIG)
            top = jnp.max(diag, axis=1, keepdims=True)
            if i:
                off = mm_nt(qa, keys[h][: i * RB])
                top = jnp.maximum(top, jnp.max(off, axis=1, keepdims=True))
            result = mm(jnp.exp2((diag - top) * LOG_SCALE).astype(BF), values[h][here])
            if i:
                weights = jnp.exp2((off - top) * LOG_SCALE).astype(BF)
                result = result + mm(weights, values[h][: i * RB])
            tops.append(top)
            outs.append(result)
        total = jnp.where(low, outs[1], outs[0])
        mixed = jnp.where(low, outs[0], outs[1]) / pltpu.roll(total, 64, 1)
        mixed_ref[here, :] = mixed.astype(BF)
        level = -(jnp.where(low, tops[1], tops[0]) + math.sqrt(HD) * jnp.log(total))
        a, b, c = three(level)
        aug_ref[0, here, :] = jnp.where(
            lane6 == 16, a, jnp.where(lane6 == 17, b, jnp.where(lane6 == 18, c, qf))
        )


def attend(qkv, qf, kf):
    return call(
        attend_body,
        (PAIRS,),
        [
            (qkv, (T, 128), lambda j: (0, j)),
            (qkv, (T, 128), lambda j: (0, PAIRS + j)),
            (qkv, (T, 128), lambda j: (0, 2 * PAIRS + j)),
            (qf, None),
            (kf, None),
        ],
        [
            (out((T, D), BF), (T, 128), lambda j: (0, j)),
            (out((PAIRS, T, 128), BF), (1, T, 128), lambda j: (j, 0, 0)),
        ],
        name="attend",
        flops=12 * 4 * T * T * 128,
        nbytes=8e6,
    )


def settle_body(
    x_ref, mixed_ref, w_ref, d_ref, u_ref, g_ref, rt_ref, earlier_ref, res_ref,
    mid_ref, sent_ref, lg_ref, nar_ref,
):
    mixed = mixed_ref[...]
    narrow = mm(mixed, d_ref[...]).astype(BF)
    nar_ref[...] = narrow
    mid = x_ref[...].astype(F32) + mm(mixed, w_ref[0]) + mm(narrow, u_ref[...])
    mid_ref[...] = mid
    scale = lax.rsqrt(jnp.mean(mid * mid, axis=1, keepdims=True) + EPSILON)
    normed = mid * scale * g_ref[...]
    sent_ref[...] = normed.astype(BF)
    a, b, c = three(normed)
    one, two, last = mm(a, rt_ref[...]), mm(b, rt_ref[...]), mm(c, rt_ref[...])
    total = one + two + last + pltpu.roll(one + two, 112, 1) + pltpu.roll(one, 96, 1)
    lane = iota((RB, 128), 1)
    earlier = jnp.where(lane < NEXP, earlier_ref[...], 0.0)
    extra = mm(spread_lanes(earlier), res_ref[...])
    lg_ref[...] = jnp.where(lane < 16, total + extra, 0.0)


def settle(x, mixed, w, down, up, gain, router, earlier, residual):
    return call(
        settle_body,
        (NB,),
        [
            (x, (RB, D), rows),
            (mixed, (RB, D), rows),
            (w, (1, D, D), lambda i: (3, 0, 0)),
            (down, None),
            (up, None),
            (gain, None),
            (router, None),
            (earlier, (RB, 128), rows),
            (residual, None),
        ],
        [
            (out((T, D), F32), (RB, D), rows),
            (out((T, D), BF), (RB, D), rows),
            (out((T, 128), F32), (RB, 128), rows),
            (out((T, 128), BF), (RB, 128), rows),
        ],
        name="settle",
        flops=2 * T * D * D * 2,
        nbytes=10e6,
    )


def dispatch_body(trow_ref, s_ref, o_ref):
    place = pl.program_id(0) * CAP + iota((CAP, T), 0)
    hit = (trow_ref[0:1, :] == place) | (trow_ref[1:2, :] == place)
    o_ref[0] = mm(hit.astype(F32).astype(BF), s_ref[...]).astype(BF)


def dispatch(trow, sent):
    return call(
        dispatch_body,
        (NFFN,),
        [(trow, None), (sent, None)],
        [(out((NFFN, CAP, D), BF), (1, CAP, D), lambda j: (j, 0, 0))],
        name="dispatch",
        flops=2 * T * SLOTS * D,
        nbytes=4e6,
    )[0]


def dispatch_grad_body(trow_ref, g_ref, lg_ref, rt_ref, o_ref, first, second):
    @pl.when(pl.program_id(0) == 0)
    def _():
        for i in range(NB):
            at = slice(i * RB, (i + 1) * RB)
            gates = mix_terms(lg_ref[at, :], rt_ref[at, :])[0]
            g = g_ref[at, :].astype(F32)
            first[at, :] = (gates[0] * g).astype(BF)
            second[at, :] = (gates[1] * g).astype(BF)

    place = pl.program_id(0) * CAP + iota((CAP, T), 0)
    hit0 = (trow_ref[0:1, :] == place).astype(F32).astype(BF)
    hit1 = (trow_ref[1:2, :] == place).astype(F32).astype(BF)
    o_ref[0] = (mm(hit0, first[...]) + mm(hit1, second[...])).astype(BF)


def dispatch_grad(trow, g, logits, routes):
    return call(
        dispatch_grad_body,
        (NFFN,),
        [(trow, None), (g, None), (logits, None), (routes, None)],
        [(out((NFFN, CAP, D), BF), (1, CAP, D), lambda j: (j, 0, 0))],
        [pltpu.VMEM((T, D), BF), pltpu.VMEM((T, D), BF)],
        name="dispatch_grad",
        flops=4 * T * SLOTS * D,
        nbytes=6e6,
    )[0]


PR = 2 * CAP
NP = NFFN // 2


def split_refs(refs, *counts):
    parts = []
    for count in counts:
        parts.append(refs[:count])
        refs = refs[count:]
    return *parts, refs


def flip(bit, change):
    return bit + change - 2 * bit * change


PLANE, WIDE_SLICE = 0, 1
OWNERS = (("x", "c", "y"), ("x", "c"))


def owner_at(p, h, kind):
    x = lax.axis_index("x")
    far, near, core = ((1, 1, h), (1 - h, h, 0), (1 - h, h, 1), (0, 0, h))[p]
    if kind == WIDE_SLICE:
        x = 2 * flip(x // 2, far) + flip(x % 2, near)
        c = flip(lax.axis_index("c"), core)
        return {"x": x, "c": c}, x * 2 + c
    x, c, y = flip(x, far), flip(lax.axis_index("c"), core), flip(lax.axis_index("y"), near)
    return {"x": x, "c": c, "y": y}, (x * 2 + c) * 2 + y


PLACES = [(p, h) for p in range(NP) for h in range(2)]


def greet(kind):
    barrier = pltpu.get_barrier_semaphore()
    for p, h in PLACES[:-2] + PLACES[-1:]:
        pl.semaphore_signal(
            barrier, inc=1, device_id=owner_at(p, h, kind)[0], device_id_type=pl.DeviceIdType.MESH
        )
    pl.semaphore_wait(barrier, NFFN - 1)


def block_of(ref, p, h):
    return ref.at[p, h * CAP : (h + 1) * CAP, :]


def fetch_weights(split, gate_ups, down_ref, w1, w2, sems):
    copies = []
    if split:
        y = lax.axis_index("y")
        for side, ref in enumerate(gate_ups):
            mine = flip(y, side)
            count, size = ref.shape[0], ref.shape[1]
            for k in range(count):
                at = pl.multiple_of((2 * k + mine) * size, size)
                copies.append(
                    pltpu.make_async_copy(
                        ref.at[k], w1.at[pl.ds(at, size), :], sems.at[side * count + k]
                    )
                )
    else:
        copies.append(pltpu.make_async_copy(gate_ups[0], w1, sems.at[0]))
    copies.append(pltpu.make_async_copy(down_ref, w2, sems.at[8]))
    for copy in copies:
        copy.start()
    return copies


def fetch_blocks(source, rv, sems, kind):
    copies = []
    for n, (p, h) in enumerate(PLACES):
        number = owner_at(p, h, kind)[1]
        copies.append(pltpu.make_async_copy(source.at[number], block_of(rv, p, h), sems.at[n]))
    for copy in copies:
        copy.start()
    return copies


def give_back(pv, p, target, send, recv, kind):
    me = owner_at(NP - 1, 0, kind)[1]
    copies = []
    for h in range(2):
        n = 2 * p + h
        if (p, h) == (NP - 1, 0):
            copy = pltpu.make_async_copy(block_of(pv, p, h), target.at[me], send.at[n])
        else:
            copy = pltpu.make_async_remote_copy(
                src_ref=block_of(pv, p, h),
                dst_ref=target.at[me],
                send_sem=send.at[n],
                recv_sem=recv.at[n],
                device_id=owner_at(p, h, kind)[0],
                device_id_type=pl.DeviceIdType.MESH,
            )
        copy.start()
        copies.append(copy)
    return copies


def chunk_at(f):
    return pl.multiple_of(f * FC, FC)


def forward_chunk(r, w1, w2, f):
    at = chunk_at(f)
    gate = mm(r, w1[:, pl.ds(at, FC)])
    up = mm(r, w1[:, pl.ds(pl.multiple_of(FF + f * FC, FC), FC)])
    active = (gate * sigmoid(gate) * up).astype(BF)
    return gate, up, mm(active, w2[pl.ds(at, FC), :])


def backward_chunk(g, gate, up, w1, w2, f):
    at = chunk_at(f)
    grad = mm_nt(g, w2[pl.ds(at, FC), :])
    s = sigmoid(gate)
    grad_s = grad * s
    grad_gate = (grad_s * up * (1.0 + gate * (1.0 - s))).astype(BF)
    grad_up = (grad_s * gate).astype(BF)
    return mm_nt(grad_gate, w1[:, pl.ds(at, FC)]) + mm_nt(
        grad_up, w1[:, pl.ds(pl.multiple_of(FF + f * FC, FC), FC)]
    )


def expert_body(split, kind, *refs):
    count = 2 if split else 1
    gate_ups = refs[:count]
    down_ref, rec_ref, ret_ref, gate_ref, up_ref = refs[count : count + 5]
    w1, w2, rv, pv, gv, uv, acc, wsem, rsem, gsem, usem, send, recv = refs[count + 5 :]
    weights = fetch_weights(split, gate_ups, down_ref, w1, w2, wsem)
    blocks = fetch_blocks(rec_ref, rv, rsem, kind)
    greet(kind)
    for copy in weights + blocks:
        copy.wait()
    stores = []
    moves = []
    for p in range(NP):
        r = rv[p]
        acc[...] = jnp.zeros_like(acc)

        def step(f, carry):
            gate, up, part = forward_chunk(r, w1, w2, f)
            gv[p, :, pl.ds(chunk_at(f), FC)] = gate.astype(BF)
            uv[p, :, pl.ds(chunk_at(f), FC)] = up.astype(BF)
            acc[...] += part
            return carry

        lax.fori_loop(0, FF // FC, step, 0)
        pv[p] = acc[...].astype(BF)
        moves += give_back(pv, p, ret_ref, send, recv, kind)
        for values, ref, sems in ((gv, gate_ref, gsem), (uv, up_ref, usem)):
            copy = pltpu.make_async_copy(values.at[p], ref.at[p], sems.at[p])
            copy.start()
            stores.append(copy)
    for copy in moves + stores:
        copy.wait()


def own_copies(body, ins, near, outs, near_outs, scratch):
    counts = len(ins), len(near), len(outs), len(near_outs), len(scratch)

    def run(*refs):
        far, near_far, targets, near_targets, inner, close = split_refs(refs, *counts)
        close, near_close, sems = split_refs(close, len(near), len(near_outs))
        loads = [
            pltpu.make_async_copy(source, target, sems[0].at[n])
            for n, (source, target) in enumerate(zip(near_far, close))
        ]
        for copy in loads:
            copy.start()

        def ready():
            for copy in loads:
                copy.wait()

        def done(n):
            copy = pltpu.make_async_copy(near_close[n], near_targets[n], sems[1].at[n])
            copy.start()
            return copy

        body(far, close, targets, near_close, inner, ready, done)

    extra = [pltpu.VMEM(v.shape, v.dtype) for v in (*near, *near_outs)]
    extra += [DMA((max(1, len(near)),)), DMA((max(1, len(near_outs)),))]
    return run, [*ins, *near], [*outs, *near_outs], [*scratch, *extra]


def comm_call(body, ins, outs, scratch, name, number, flops, nbytes, near=(), near_outs=()):
    run, ins, outs, scratch = own_copies(body, ins, near, outs, near_outs, scratch)
    far = {} if number is None else dict(collective_id=number, has_side_effects=True)
    return pl.pallas_call(
        run,
        in_specs=[pl.BlockSpec(memory_space=pl.ANY)] * len(ins),
        out_specs=[pl.BlockSpec(memory_space=pl.ANY)] * len(outs),
        out_shape=outs,
        scratch_shapes=scratch,
        compiler_params=pltpu.CompilerParams(vmem_limit_bytes=VMEM_BYTES, **far),
        cost_estimate=pl.CostEstimate(
            flops=int(flops), bytes_accessed=int(nbytes), transcendentals=0
        ),
        name=name,
    )(*ins)


DMA = pltpu.SemaphoreType.DMA
WEIGHTS = [pltpu.VMEM((D, 2 * FF), BF), pltpu.VMEM((FF, D), BF)]
ROWS = pltpu.VMEM((NP, PR, D), BF)
WIDE = pltpu.VMEM((NP, PR, FF), BF)
SUM = pltpu.VMEM((PR, D), F32)
BLOCKS = jax.ShapeDtypeStruct((NFFN, CAP, D), BF)
KEPT = jax.ShapeDtypeStruct((NP, PR, FF), BF)


def expert_forward(received, gate_ups, down, kind):
    split = len(gate_ups) == 2

    def body(far, near, outs, near_outs, scratch, ready, done):
        expert_body(split, kind, *far, *outs, *scratch)

    return comm_call(
        body,
        [*gate_ups, down, received],
        [BLOCKS, KEPT, KEPT],
        WEIGHTS + [ROWS, ROWS, WIDE, WIDE, SUM]
        + [DMA((9,)), DMA((8,)), DMA((NP,)), DMA((NP,)), DMA((8,)), DMA((8,))],
        "expert_forward",
        1,
        2 * SLOTS * D * FF * 3,
        26e6,
    )


def expert_parts_body(kind, far, outs, scratch):
    gate_up_ref, rec_ref = far
    w1, rv, wsem, rsem, osem, *kept = scratch
    load = pltpu.make_async_copy(gate_up_ref, w1, wsem.at[0])
    load.start()
    for copy in fetch_blocks(rec_ref, rv, rsem, kind) + [load]:
        copy.wait()
    stores = []
    for p in range(NP):
        r = rv[p]

        def step(f, carry):
            at = pl.ds(chunk_at(f), FC)
            gate = mm(r, w1[:, at])
            up = mm(r, w1[:, pl.ds(pl.multiple_of(FF + f * FC, FC), FC)])
            s = sigmoid(gate)
            silu = gate * s
            kept[0][p, :, at] = (silu * up).astype(BF)
            kept[1][p, :, at] = (up * s * (1.0 + gate * (1.0 - s))).astype(BF)
            kept[2][p, :, at] = silu.astype(BF)
            return carry

        lax.fori_loop(0, FF // FC, step, 0)
        for n in range(3):
            stores.append(pltpu.make_async_copy(kept[n].at[p], outs[n].at[p], osem.at[p, n]))
            stores[-1].start()
    for copy in stores:
        copy.wait()


def expert_parts(received, gate_up, kind):
    def body(far, near, outs, near_outs, scratch, ready, done):
        expert_parts_body(kind, far, outs, scratch)

    return comm_call(
        body,
        [gate_up, received],
        [KEPT, KEPT, KEPT],
        [WEIGHTS[0], ROWS, DMA((1,)), DMA((8,)), DMA((NP, 3)), WIDE, WIDE, WIDE],
        "expert_parts",
        None,
        2 * SLOTS * D * FF * 2,
        28e6,
    )


def expert_both_body(kind, far, near, mix_out, out_near, scratch, ready, done):
    (
        gate_up_ref, down_ref, active_ref, to_gate_ref, to_up_ref, sg_ref, mid_ref, g_ref,
        mixed_ref, shared_ref,
    ) = far
    tcol_ref, lg_ref, rt_ref, gain_ref, cv_ref, wt_ref, res_ref, nar_ref, d_ref, u_ref = near
    out_ref, gm_ref, gle_ref, gu_ref, gd_ref = out_near
    (
        w1, w2, qv, sv, pv, to_gate, to_up, av, back, gback, mid, g, mixed, w3, acc,
        wsem, asem, ssem, msem, send, recv, gsend, grecv,
    ) = scratch

    def start(source, target, sem):
        copy = pltpu.make_async_copy(source, target, sem)
        copy.start()
        return copy

    load = start(down_ref, w2, wsem.at[0])
    actives = [start(active_ref.at[p], av.at[p], asem.at[p]) for p in range(2)]
    greet(kind)
    load.wait()
    moves = []
    extra = []
    for p in range(NP):
        actives[p].wait()
        pv[p] = mm(av[p % 2], w2[...]).astype(BF)
        moves += give_back(pv, p, back, send, recv, kind)
        if p + 2 < NP:
            actives.append(start(active_ref.at[p + 2], av.at[p % 2], asem.at[p + 2]))
        if p == 0:
            extra = fetch_blocks(sg_ref, sv, ssem, kind)
            extra.append(start(gate_up_ref, w1, wsem.at[1]))
            for n, (source, target) in enumerate(
                (
                    (to_gate_ref, to_gate), (to_up_ref, to_up), (mid_ref, mid), (g_ref, g),
                    (mixed_ref, mixed), (shared_ref.at[3], w3),
                )
            ):
                extra.append(start(source, target, msem.at[n]))
    for copy in extra:
        copy.wait()
    later = []
    for p in range(NP):
        grads = sv[p]
        acc[...] = jnp.zeros_like(acc)

        def step(f, carry):
            at = pl.ds(chunk_at(f), FC)
            grad = mm_nt(grads, w2[at, :])
            first = (grad * to_gate[p, :, at].astype(F32)).astype(BF)
            second = (grad * to_up[p, :, at].astype(F32)).astype(BF)
            acc[...] += mm_nt(first, w1[:, at]) + mm_nt(
                second, w1[:, pl.ds(pl.multiple_of(FF + f * FC, FC), FC)]
            )
            return carry

        lax.fori_loop(0, FF // FC, step, 0)
        qv[p] = acc[...].astype(BF)
        later += give_back(qv, p, gback, gsend, grecv, kind)
    for copy in moves:
        copy.wait()
    ready()

    def finish(i, carry):
        at = pl.ds(pl.multiple_of(i * RB, RB), RB)
        logits, routes, middle = lg_ref[at, :], rt_ref[at, :], mid[at, :]
        following, chosen = combine_rows(
            tcol_ref[at, :], back, middle, logits, routes, gain_ref[...], cv_ref
        )
        out_ref[at, :] = following
        gm_ref[at, :], gle_ref[at, :] = mix_grad(
            g[at, :].astype(F32), middle, chosen, logits, routes, 0.0, gain_ref[...], cv_ref,
            wt_ref[...], res_ref[...],
        )
        return carry

    lax.fori_loop(0, NB, finish, 0)
    stores = [done(0), done(2)]
    gu_ref[...] = jnp.zeros_like(gu_ref)
    gd_ref[...] = jnp.zeros_like(gd_ref)
    for copy in later:
        copy.wait()

    def settle_one(i, carry):
        at = pl.ds(pl.multiple_of(i * RB, RB), RB)
        refs = (tcol_ref, mid, g, mixed, gain_ref, nar_ref, w3, d_ref, u_ref, gu_ref, gd_ref)
        settle_back(refs, at, gm_ref, mixed, gback)
        return carry

    lax.fori_loop(0, NB, settle_one, 0)
    stores.append(start(mixed, mix_out, msem.at[6]))
    for copy in stores + [done(n) for n in (1, 3, 4)]:
        copy.wait()


def expert_both(
    active, to_gate, to_up, slot_grads, gate_up, down, mid, g, mixed, weights, tcol, logits, routes, gain,
    const_vec, router_t, residual_t, narrow, down_out, up_out, kind,
):
    def body(far, near, outs, near_outs, scratch, ready, done):
        expert_both_body(kind, far, near, outs[0], near_outs, scratch, ready, done)

    half = pltpu.VMEM((T, D), BF)
    landing = pltpu.VMEM((NFFN, CAP, D), BF)
    return comm_call(
        body,
        [gate_up, down, active, to_gate, to_up, slot_grads, mid, g, mixed, weights],
        [out((T, D), BF)],
        WEIGHTS
        + [ROWS, ROWS, ROWS, WIDE, WIDE, pltpu.VMEM((2, PR, FF), BF), landing, landing]
        + [pltpu.VMEM((T, D), F32), pltpu.VMEM((T, D), g.dtype), half, pltpu.VMEM((D, D), BF), SUM]
        + [DMA((2,)), DMA((NP,)), DMA((8,)), DMA((7,))]
        + [DMA((8,)), DMA((8,)), DMA((8,)), DMA((8,))],
        "expert_both",
        2,
        2 * SLOTS * D * FF * 4,
        40e6,
        [tcol, logits, routes, gain, const_vec, router_t, residual_t, narrow, down_out, up_out],
        [out((T, D), F32), out((T, D), F32), out((T, 128), F32)]
        + [out((128, D), F32), out((128, D), F32)],
    )


def expert_back_body(split, kind, far, near, out_near, outs, scratch, ready, done):
    count = 2 if split else 1
    gate_ups, (down_ref, gate_ref, up_ref, g_ref, mid_ref, c0_ref, c1_ref, mixed_ref, shared_ref) = (
        far[:count], far[count:]
    )
    (
        trow_ref, tcol_ref, lg_ref, rt_ref, gl_ref, gain_ref, cv_ref, wt_ref, nar_ref, d_ref, u_ref
    ) = near
    gm_ref, gu_ref, gd_ref = out_near
    mix_out = outs[0]
    (
        w1, w2, sgv, rv, pv, gv, uv, back, first, second, g, mid, c0, c1, mixed, w3, acc,
        wsem, gsem, usem, msem, dsend, drecv, send, recv, osem,
    ) = scratch
    extra = [
        pltpu.make_async_copy(ref, values, msem.at[n])
        for n, (ref, values) in enumerate(
            (
                (g_ref, g), (mid_ref, mid), (c0_ref, c0), (c1_ref, c1), (mixed_ref, mixed),
                (shared_ref.at[3], w3),
            )
        )
    ]
    extra[0].start()
    extra[0].wait()
    ready()

    def gated(i, carry):
        at = pl.ds(pl.multiple_of(i * RB, RB), RB)
        gates = mix_terms(lg_ref[at, :], rt_ref[at, :])[0]
        first[at, :] = (gates[0] * g[at, :]).astype(BF)
        second[at, :] = (gates[1] * g[at, :]).astype(BF)
        return carry

    lax.fori_loop(0, NB, gated, 0)
    weights = fetch_weights(split, gate_ups, down_ref, w1, w2, wsem)
    for p in (3, 0, 1, 2):
        for values, ref, sems in ((gv, gate_ref, gsem), (uv, up_ref, usem)):
            copy = pltpu.make_async_copy(ref.at[p], values.at[p], sems.at[p])
            copy.start()
            weights.append(copy)
    for copy in extra[1:]:
        copy.start()
    greet(kind)
    arrivals = {}
    for p, h in PLACES[:-2] + [(3, 1), (3, 0)]:
        where, number = owner_at(p, h, kind)
        place = number * CAP + iota((CAP, T), 0)
        hit0 = (trow_ref[0:1, :] == place).astype(F32).astype(BF)
        hit1 = (trow_ref[1:2, :] == place).astype(F32).astype(BF)
        values = (mm(hit0, first[...]) + mm(hit1, second[...])).astype(BF)
        n = 2 * p + h
        if (p, h) == (NP - 1, 0):
            rv[p, h * CAP : (h + 1) * CAP, :] = values
            continue
        sgv[p, h * CAP : (h + 1) * CAP, :] = values
        copy = pltpu.make_async_remote_copy(
            src_ref=block_of(sgv, p, h),
            dst_ref=block_of(rv, p, h),
            send_sem=dsend.at[n],
            recv_sem=drecv.at[n],
            device_id=where,
            device_id_type=pl.DeviceIdType.MESH,
        )
        copy.start()
        arrivals[p, h] = copy
    for copy in weights + extra[1:]:
        copy.wait()
    moves = []

    for p in (3, 0, 1, 2):
        for h in range(2):
            if (p, h) in arrivals:
                arrivals[p, h].wait()
        grads = rv[p]
        acc[...] = jnp.zeros_like(acc)

        def step(f, carry):
            at = pl.ds(chunk_at(f), FC)
            gate = gv[p, :, at].astype(F32)
            up = uv[p, :, at].astype(F32)
            acc[...] += backward_chunk(grads, gate, up, w1, w2, f)
            return carry

        lax.fori_loop(0, FF // FC, step, 0)
        pv[p] = acc[...].astype(BF)
        moves += give_back(pv, p, back, send, recv, kind)

    def tidy(i, carry):
        at = pl.ds(pl.multiple_of(i * RB, RB), RB)
        gm_ref[at, :] = mix_grad(
            g[at, :], mid[at, :], (c0[at, :], c1[at, :]), lg_ref[at, :], rt_ref[at, :],
            gl_ref[at, :], gain_ref[...], cv_ref, wt_ref[...], None,
        )[0]
        return carry

    lax.fori_loop(0, NB, tidy, 0)
    gu_ref[...] = jnp.zeros_like(gu_ref)
    gd_ref[...] = jnp.zeros_like(gd_ref)
    for copy in moves:
        copy.wait()

    def settle_one(i, carry):
        at = pl.ds(pl.multiple_of(i * RB, RB), RB)
        refs = (tcol_ref, mid, g, mixed, gain_ref, nar_ref, w3, d_ref, u_ref, gu_ref, gd_ref)
        settle_back(refs, at, gm_ref, first, back)
        return carry

    lax.fori_loop(0, NB, settle_one, 0)
    last = pltpu.make_async_copy(first, mix_out, osem.at[0])
    last.start()
    for copy in [last] + [done(n) for n in range(3)]:
        copy.wait()


def expert_backward(
    gate, up, gate_ups, down, g, mid, c0, c1, mixed, weights, trow, tcol, logits, routes, gl, gain,
    const_vec, router_t, narrow, down_out, up_out, kind,
):
    split = len(gate_ups) == 2

    def body(far, near, outs, near_outs, scratch, ready, done):
        expert_back_body(split, kind, far, near, near_outs, outs, scratch, ready, done)

    half, full = pltpu.VMEM((T, D), BF), pltpu.VMEM((T, D), F32)
    mix, gm, gu, gd = comm_call(
        body,
        [*gate_ups, down, gate, up, g, mid, c0, c1, mixed, weights],
        [out((T, D), BF)],
        WEIGHTS
        + [ROWS, ROWS, ROWS, WIDE, WIDE, pltpu.VMEM((NFFN, CAP, D), BF)]
        + [half, half, full, full, half, half, half, pltpu.VMEM((D, D), BF), SUM]
        + [DMA((9,)), DMA((NP,)), DMA((NP,)), DMA((6,))]
        + [DMA((8,)), DMA((8,)), DMA((8,)), DMA((8,)), DMA((1,))],
        "expert_backward",
        3,
        2 * SLOTS * D * FF * 3,
        26e6,
        [
            trow, tcol, logits, routes, gl, gain, const_vec, router_t, narrow, down_out, up_out,
        ],
        [out((T, D), F32), out((128, D), F32), out((128, D), F32)],
    )
    return gm, mix, gu, gd


def mix_terms(logits, routes):
    lane = iota(logits.shape, 1)

    def at(place):
        return jnp.sum(jnp.where(lane == place, logits, 0.0), axis=1, keepdims=True)

    r0, r1 = routes[:, 0:1], routes[:, 1:2]
    gap = at(r0) - at(r1)
    gates = (sigmoid(gap), sigmoid(-gap))

    def weight(e):
        return jnp.where(r0 == e, gates[0], 0.0) + jnp.where(r1 == e, gates[1], 0.0)

    shares = []
    for c in range(2):
        apart = logits[:, 12 + 2 * c : 13 + 2 * c] - logits[:, 13 + 2 * c : 14 + 2 * c]
        shares.append((sigmoid(apart), sigmoid(-apart)))
    weights = [weight(NFFN + 1), weight(NFFN + 2), weight(NFFN + 3)]
    return gates, weights, shares


def rms_scale(v):
    return lax.rsqrt(jnp.mean(v * v, axis=1, keepdims=True) + EPSILON)


def combine_rows(tcol, back_ref, mid, logits, routes, gain, cv_ref):
    place = iota((RB, SLOTS), 1)
    back = back_ref[...].reshape(SLOTS, D)
    chosen = []
    for k in range(2):
        hit = (tcol[:, k : k + 1] == place).astype(F32).astype(BF)
        chosen.append(mm(hit, back))
    normed = mid * rms_scale(mid) * gain
    gates, weights, shares = mix_terms(logits, routes)
    same = weights[0] + weights[1] * shares[0][0] + weights[2] * shares[1][0]
    moe = gates[0] * chosen[0] + gates[1] * chosen[1] + same * normed
    moe = moe + (weights[1] * shares[0][1]) * cv_ref[0:1, :]
    moe = moe + (weights[2] * shares[1][1]) * cv_ref[1:2, :]
    return mid + moe, chosen


def combine_body(tcol_ref, ret_ref, mid_ref, lg_ref, rt_ref, g_ref, cv_ref, x_ref, c0_ref, c1_ref):
    x_ref[...], chosen = combine_rows(
        tcol_ref[...], ret_ref, mid_ref[...], lg_ref[...], rt_ref[...], g_ref[...], cv_ref
    )
    c0_ref[...] = chosen[0].astype(BF)
    c1_ref[...] = chosen[1].astype(BF)


def combine(tcol, returned, mid, logits, routes, gain, const_vec):
    return call(
        combine_body,
        (NB,),
        [
            (tcol, (RB, 128), rows),
            (returned, None),
            (mid, (RB, D), rows),
            (logits, (RB, 128), rows),
            (routes, (RB, 2), rows),
            (gain, None),
            (const_vec, None),
        ],
        [
            (out((T, D), F32), (RB, D), rows),
            (out((T, D), BF), (RB, D), rows),
            (out((T, D), BF), (RB, D), rows),
        ],
        name="combine",
        flops=4 * T * SLOTS * D,
        nbytes=12e6,
    )


def mix_grad(g, mid, chosen, logits, routes, grad, gain, cv_ref, wt, res):
    normed = mid * rms_scale(mid) * gain
    gates, weights, shares = mix_terms(logits, routes)

    def along(v):
        return jnp.sum(g * v, axis=1, keepdims=True)

    same = along(normed)
    const = [along(cv_ref[c : c + 1, :]) for c in range(2)]
    gate_grads = []
    for k in range(2):
        r = routes[:, k : k + 1]
        value = along(chosen[k].astype(F32)) + jnp.where(r == NFFN + 1, same, 0.0)
        for c in range(2):
            mixed = shares[c][0] * same + shares[c][1] * const[c]
            value = value + jnp.where(r == NFFN + 2 + c, mixed, 0.0)
        gate_grads.append(value)
    slope = gates[0] * gates[1] * (gate_grads[0] - gate_grads[1])
    lane = iota((RB, 128), 1)
    grad = grad + jnp.where(lane == routes[:, 0:1], slope, 0.0)
    grad = grad - jnp.where(lane == routes[:, 1:2], slope, 0.0)
    only = grad
    for c in range(2):
        tilt = weights[1 + c] * shares[c][0] * shares[c][1] * (same - const[c])
        grad = grad + jnp.where(lane == 12 + 2 * c, tilt, 0.0)
        grad = grad - jnp.where(lane == 13 + 2 * c, tilt, 0.0)
    keep = weights[0] + weights[1] * shares[0][0] + weights[2] * shares[1][0]
    residual = None if res is None else mm(spread_lanes(only), res)
    return mm(spread_lanes(grad), wt) + keep * g, residual


def settle_back(refs, at, gm_ref, mix_ref, back_ref):
    tcol_ref, mid_ref, g_ref, mixed_ref, gain_ref, nar_ref, w_ref, d_ref, u_ref, gu_ref, gd_ref = refs
    place = iota((RB, SLOTS), 1)
    tcol = tcol_ref[at, :]
    hit = (tcol[:, 0:1] == place) | (tcol[:, 1:2] == place)
    grad = gm_ref[at, :] + mm(hit.astype(F32).astype(BF), back_ref[...].reshape(SLOTS, D))
    grad = g_ref[at, :].astype(F32) + rms_back(grad, mid_ref[at, :], gain_ref[...])
    gm_ref[at, :] = grad
    grad = grad.astype(BF)
    slim = mm_nt(grad, u_ref[...]).astype(BF)
    gu_ref[...] += 2.0 * mm_tn(nar_ref[at, :], grad)
    gd_ref[...] += mm_tn(slim, mixed_ref[at, :])
    mix_ref[at, :] = (mm_nt(grad, w_ref[...]) + mm_nt(slim, d_ref[...])).astype(BF)


def rms_back(grad, v, gain):
    scale = rms_scale(v)
    inner = grad * gain
    return scale * inner - v * (scale**3 * jnp.mean(v * inner, axis=1, keepdims=True))


def attend_back(q, k, v, aug, kf, g, mixed, dqt):
    lane = iota((T, 128), 1)
    low = lane < 64
    lane6 = lane & 63
    product = g.astype(F32) * mixed.astype(F32)
    d0 = jnp.sum(jnp.where(low, product, 0.0), axis=1, keepdims=True)
    d1 = jnp.sum(jnp.where(low, 0.0, product), axis=1, keepdims=True)
    a, b, c = three(-jnp.where(low, d1, d0))
    zero = jnp.zeros((T, 128), BF)
    ga = jnp.where(lane6 == 0, a, jnp.where(lane6 == 1, b, jnp.where(lane6 == 2, c, zero)))
    va = (lane6 < 3).astype(F32).astype(BF)
    qs = (jnp.where(low, q, aug), jnp.where(low, aug, q))
    ks = (jnp.where(low, k, kf), jnp.where(low, kf, k))
    vs = (jnp.where(low, v, va), jnp.where(low, va, v))
    gs = (jnp.where(low, g, ga), jnp.where(low, ga, g))
    kt = k.T
    tri = iota((RB, RB), 0) <= iota((RB, RB), 1)
    low = low[:RB]
    dks = []
    dvs = []
    for i in range(NB):
        here = slice(i * RB, (i + 1) * RB)
        dk = [None, None]
        dv = [None, None]
        for h in range(2):
            half = slice(h * 64, (h + 1) * 64)
            for start, stop in ((i * RB, (i + 1) * RB), ((i + 1) * RB, T)):
                if start == stop:
                    continue
                there = slice(start, stop)
                p = jnp.exp2(mm_nt(ks[h][here], qs[h][there]) * LOG_SCALE)
                if stop == (i + 1) * RB:
                    p = jnp.where(tri, p, 0.0)
                ds = (p * mm_nt(vs[h][here], gs[h][there])).astype(BF)
                p = p.astype(BF)
                dv_part = mm(p, g[there])
                dk_part = mm(ds, q[there])
                dk[h] = dk_part if dk[h] is None else dk[h] + dk_part
                dv[h] = dv_part if dv[h] is None else dv[h] + dv_part
                part = mm(kt[half, here], ds)
                if i == 0:
                    dqt[half, there] = part
                else:
                    dqt[half, there] += part
        dvs.append(jnp.where(low, dv[0], dv[1]))
        dks.append(jnp.where(low, dk[0], dk[1]))
    return dqt[...].T, jnp.concatenate(dks), jnp.concatenate(dvs)


def layer_back_body(far, near, out_near, gx_ref, scratch, ready, done):
    gm_ref, mix_ref, mixed_ref, w_ref, qkv_ref, aug_ref, n_ref, x_ref = far
    gain_ref, nar_ref, d_ref, u_ref, kf_ref, cos_ref, sin_ref = near
    gu_ref, gd_ref = out_near
    gm, mix, mixed, w, qkv, aug, n, x, gproj, dqt, sems, pair_sems, out_sems = scratch

    def start(source, target, sem):
        copy = pltpu.make_async_copy(source, target, sem)
        copy.start()
        return copy

    def cols(part, j):
        return pl.ds(pl.multiple_of(part * D + j * 128, 128), 128)

    def of_pair(j):
        copies = [
            pltpu.make_async_copy(
                qkv_ref.at[:, cols(part, j)], qkv.at[:, cols(part, j)], pair_sems.at[j, part]
            )
            for part in range(3)
        ]
        for k, (source, target) in enumerate(((mix_ref, mix), (mixed_ref, mixed))):
            copies.append(
                pltpu.make_async_copy(
                    source.at[:, cols(0, j)], target.at[:, cols(0, j)], pair_sems.at[j, 3 + k]
                )
            )
        copies.append(pltpu.make_async_copy(aug_ref.at[j], aug.at[j], pair_sems.at[j, 5]))
        return copies

    for j in range(PAIRS):
        for copy in of_pair(j):
            copy.start()
    third = [start(w_ref.at[k], w.at[k], sems.at[k]) for k in range(3)]
    third += [
        start(source, target, sems.at[3 + k])
        for k, (source, target) in enumerate(((n_ref, n), (x_ref, x), (gm_ref, gm)))
    ]
    ready()

    def pair(j, carry):
        for copy in of_pair(j):
            copy.wait()
        dq, dk, dv = attend_back(
            qkv[:, cols(0, j)], qkv[:, cols(1, j)], qkv[:, cols(2, j)], aug[j], kf_ref[...],
            mix[:, cols(0, j)], mixed[:, cols(0, j)], dqt,
        )
        for part, value in enumerate((dq, dk)):
            value = (value * (1.0 / math.sqrt(HD))).astype(BF).astype(F32)
            gproj[:, cols(part, j)] = turn(value, cos_ref[...], -sin_ref[...]).astype(BF)
        gproj[:, cols(2, j)] = dv.astype(BF)
        return carry

    lax.fori_loop(0, PAIRS, pair, 0)
    for copy in third:
        copy.wait()
    gu_ref[...] = jnp.zeros_like(gu_ref)
    gd_ref[...] = jnp.zeros_like(gd_ref)
    stores = []
    for i in range(NB):
        at = slice(i * RB, (i + 1) * RB)
        grad = jnp.zeros((RB, D), F32)
        slim = jnp.zeros((RB, 128), F32)
        narrow = nar_ref[at, :]
        for part in range(3):
            columns = slice(part * D, (part + 1) * D)
            piece = gproj[at, columns]
            grad = grad + mm_nt(piece, w[part])
            slim = slim + mm_nt(piece, u_ref[:, columns])
            gu_ref[:, columns] += 2.0 * mm_tn(narrow, piece)
        slim = slim.astype(BF)
        gd_ref[...] += mm_tn(slim, n[at, :])
        grad = grad + mm_nt(slim, d_ref[...])
        gm[at, :] = gm[at, :] + rms_back(grad, x[at, :].astype(F32), gain_ref[...])
        stores.append(start(gm.at[at, :], gx_ref.at[at, :], out_sems.at[i]))
    for copy in stores + [done(0), done(1)]:
        copy.wait()


def layer_back(gm, mix, mixed, w, qkv, aug, n, x, gain0, narrow, down, up, kf, cos, sin):
    far = [gm, mix, mixed, w, qkv, aug, n, x]

    def body(far, near, outs, near_outs, scratch, ready, done):
        layer_back_body(far, near, near_outs, outs[0], scratch, ready, done)

    shapes = [out((3, D, D), BF) if v is w else v for v in far]
    return comm_call(
        body,
        far,
        [out((T, D), F32)],
        [pltpu.VMEM(v.shape, v.dtype) for v in shapes]
        + [pltpu.VMEM((T, 3 * D), BF), pltpu.VMEM((128, T), F32)]
        + [DMA((6,)), DMA((PAIRS, 6)), DMA((NB,))],
        "layer_back",
        None,
        12 * 10 * T * T * 128 + 2 * T * D * 3 * D,
        4e7,
        [gain0, narrow, down, up, kf, cos, sin],
        [out((128, 3 * D), F32), out((128, D), F32)],
    )


AXES = ("x", "c", "zh", "zl", "y")
EXPERT, SHARD = AXES[:2], AXES[2:]
PIECE = 96


def shared_body(count, *refs):
    (p_ref,), away, (o_ref,), came, sems = split_refs(refs, 1, count, 1, count)
    local, zs, zr, ys, yr, xs, xr, cs, cr, ws, wr = sems
    x, c, y = (lax.axis_index(name) for name in ("x", "c", "y"))
    z = 2 * lax.axis_index("zh") + lax.axis_index("zl")
    mine, theirs = 2 * x + c, 2 * (1 - x) + c

    def spot(quarter, column, j):
        at = (2 * ((z + 4 - j) % 4) + column) * PIECE
        return o_ref.at[quarter, pl.ds(pl.multiple_of(at, PIECE), PIECE), :]

    others = [{"zh": (z + d) % 4 // 2, "zl": (z + d) % 2} for d in range(1, 4)]
    others += [{"y": 1 - y}, {"x": 1 - x}, {"c": 1 - c}]
    barrier = pltpu.get_barrier_semaphore()
    for who in others:
        pl.semaphore_signal(barrier, inc=1, device_id=who, device_id_type=pl.DeviceIdType.MESH)
    pl.semaphore_wait(barrier, len(others))

    started = []

    def send(source, target, who, send_sem, recv_sem):
        copy = pltpu.make_async_remote_copy(
            src_ref=source,
            dst_ref=target,
            send_sem=send_sem,
            recv_sem=recv_sem,
            device_id=who,
            device_id_type=pl.DeviceIdType.MESH,
        )
        copy.start()
        started.append(copy)
        return copy

    core_copies = []

    def to_core(source, target):
        n = len(core_copies)
        core_copies.append(send(source, target, others[5], cs.at[n], cr.at[n]))

    own = pltpu.make_async_copy(p_ref, spot(mine, y, 0), local.at[0])
    own.start()
    z_copies = [
        send(p_ref, spot(mine, y, 0), others[d], zs.at[d], zr.at[d]) for d in range(3)
    ]
    y_copies = [None] * 6
    x_copies = [None] * 6

    def along_y(n, source, target):
        y_copies[n] = send(source, target, others[3], ys.at[n], yr.at[n])

    def along_x(n, source, target):
        x_copies[n] = send(source, target, others[4], xs.at[n], xr.at[n])

    along_y(0, p_ref, spot(mine, y, 0))
    along_x(0, p_ref, spot(mine, y, 0))
    to_core(p_ref, spot(mine, y, 0))
    swaps = [
        send(source, target, others[3], ws.at[n], wr.at[n])
        for n, (source, target) in enumerate(zip(away, came))
    ]
    for j in range(1, 4):
        z_copies[j - 1].wait_recv()
        piece = spot(mine, y, j)
        along_y(j, piece, piece)
        along_x(j, piece, piece)
        to_core(piece, piece)
    for j in range(4):
        y_copies[j].wait_recv()
        piece = spot(mine, 1 - y, j)
        if j < 2:
            along_x(4 + j, piece, piece)
        to_core(piece, piece)
        x_copies[j].wait_recv()
        piece = spot(theirs, y, j)
        if j >= 2:
            along_y(2 + j, piece, piece)
        to_core(piece, piece)
    for j in range(4):
        (x_copies[4 + j] if j < 2 else y_copies[2 + j]).wait_recv()
        piece = spot(theirs, 1 - y, j)
        to_core(piece, piece)
    for copy in core_copies + swaps:
        copy.wait_recv()
    own.wait()
    for copy in started:
        copy.wait_send()


def usual():
    return tuple(lax.axis_size(name) for name in AXES) == (2, 2, 2, 2, 2)


def gather_shared(qkv, output, away=()):
    rows_here = qkv.shape[0]
    parts = jnp.concatenate([qkv.reshape(rows_here, 3, D).transpose(1, 0, 2), output[None]])
    if not usual():
        return [lax.all_gather(parts, SHARD, axis=1, tiled=True)]
    quarter = 2 * lax.axis_index("x") + lax.axis_index("c")
    piece = lax.dynamic_index_in_dim(parts, quarter, axis=0, keepdims=False)
    return comm_call(
        lambda far, near, outs, near_outs, scratch, ready, done: shared_body(
            len(away), *far, *outs, *scratch
        ),
        [piece, *away],
        [jax.ShapeDtypeStruct(v.shape, v.dtype) for v in (out((4, D, D), BF), *away)],
        [DMA((n,)) for n in (1, 3, 3, 6, 6, 6, 6, 16, 16, 2, 2)],
        "gather_shared",
        5 if away else 0,
        0,
        5e7,
    )


SPAN = 96
UNIT = LAYERS * 2 * 4 * R


def adapters_body(*refs):
    id_ref, parts = refs[0], refs[1 : 1 + 4 * LAYERS]
    o_ref = refs[1 + 4 * LAYERS]
    sbuf, rbuf, tbuf, ubuf, asend, arecv, bsend, brecv = refs[2 + 4 * LAYERS :]
    x, c, y = (lax.axis_index(name) for name in ("x", "c", "y"))
    z = 2 * lax.axis_index("zh") + lax.axis_index("zl")
    mates = []
    for dz in range(4):
        for dy in range(2):
            mates.append(((z + dz) % 4, flip(y, dy)))
    groups = [(flip(x, dx), flip(c, dc)) for dx in range(2) for dc in range(2)]
    barrier = pltpu.get_barrier_semaphore()
    peers = [{"zh": a // 2, "zl": a % 2, "y": b} for a, b in mates[1:]]
    peers += [{"x": a, "c": b} for a, b in groups[1:]]
    for who in peers:
        pl.semaphore_signal(barrier, inc=1, device_id=who, device_id_type=pl.DeviceIdType.MESH)
    for layer in range(LAYERS):
        gd_in, gd_out, gu_in, gu_out = parts[4 * layer : 4 * layer + 4]
        pieces = [gd_in[p * R : (p + 1) * R, :] for p in range(3)] + [gd_out[:R, :]]
        pieces += [gu_in[p * R : (p + 1) * R, p * D : (p + 1) * D] for p in range(3)] + [gu_out[:R, :]]
        sbuf[:, layer * 128 : (layer + 1) * 128] = jnp.concatenate(pieces).T.astype(BF)
    sbuf[:, UNIT:] = jnp.broadcast_to(id_ref[0].astype(F32).astype(BF), (D, 128))

    def share(k):
        return sbuf.at[pl.ds(pl.multiple_of(k * SPAN, SPAN), SPAN), :]

    pl.semaphore_wait(barrier, len(peers))
    me = 2 * z + y
    copies = []
    for n, (a, b) in enumerate(mates):
        if n == 0:
            rbuf[0] = share(me)[...]
            continue
        copy = pltpu.make_async_remote_copy(
            src_ref=share(2 * a + b),
            dst_ref=rbuf.at[(4 - n // 2) % 4 * 2 + n % 2],
            send_sem=asend.at[n],
            recv_sem=arecv.at[(4 - n // 2) % 4 * 2 + n % 2],
            device_id={"zh": a // 2, "zl": a % 2, "y": b},
            device_id_type=pl.DeviceIdType.MESH,
        )
        copy.start()
        copies.append(copy)
    for copy in copies:
        copy.wait()
    masks = []
    for n in range(8):
        own = rbuf[n, 0:16, UNIT:][0:1, 0:1].astype(F32)
        masks.append([(own == k).astype(F32) for k in range(NA)])

    def add(i, carry):
        at = pl.ds(pl.multiple_of(i * 16, 16), 16)
        sums = [jnp.zeros((16, UNIT), F32) for _ in range(NA)]
        for n in range(8):
            values = rbuf[n, at, :UNIT].astype(F32)
            for k in range(NA):
                sums[k] = sums[k] + values * masks[n][k]
        for k in range(NA):
            tbuf[k, at, :] = sums[k].astype(BF)
        return carry

    lax.fori_loop(0, SPAN // 16, add, 0)
    copies = []
    ubuf[0] = tbuf[pl.ds(2 * (2 * x + c), 2)]
    for n, (a, b) in enumerate(groups):
        if n == 0:
            continue
        copy = pltpu.make_async_remote_copy(
            src_ref=tbuf.at[pl.ds(2 * (2 * a + b), 2)],
            dst_ref=ubuf.at[n],
            send_sem=bsend.at[n],
            recv_sem=brecv.at[n],
            device_id={"x": a, "c": b},
            device_id_type=pl.DeviceIdType.MESH,
        )
        copy.start()
        copies.append(copy)
    for copy in copies:
        copy.wait()
    total = ubuf[0].astype(F32)
    for n in range(1, 4):
        total = total + ubuf[n].astype(F32)
    o_ref[...] = total


def adapters(own, parts):
    specs = [pl.BlockSpec(memory_space=pltpu.SMEM)]
    specs += [pl.BlockSpec(memory_space=pltpu.VMEM)] * len(parts)
    return pl.pallas_call(
        adapters_body,
        in_specs=specs,
        out_specs=pl.BlockSpec(memory_space=pltpu.VMEM),
        out_shape=jax.ShapeDtypeStruct((2, SPAN, UNIT), F32),
        scratch_shapes=[
            pltpu.VMEM((D, UNIT + 128), BF),
            pltpu.VMEM((8, SPAN, UNIT + 128), BF),
            pltpu.VMEM((NA, SPAN, UNIT), BF),
            pltpu.VMEM((4, 2, SPAN, UNIT), BF),
            DMA((8,)),
            DMA((8,)),
            DMA((4,)),
            DMA((4,)),
        ],
        compiler_params=pltpu.CompilerParams(
            vmem_limit_bytes=VMEM_BYTES, collective_id=4, has_side_effects=True
        ),
        name="adapters",
    )(own, *parts)


def both_rows(mine, other):
    y = lax.axis_index("y")
    return jnp.where(y == 0, jnp.stack([mine, other]), jnp.stack([other, mine]))


def own_and_other(w):
    y = lax.axis_index("y")
    return [lax.dynamic_index_in_dim(w, e, axis=0, keepdims=False) for e in (y, 1 - y)]


def across_y(v):
    return lax.ppermute(v, "y", [(0, 1), (1, 0)])


def swapped(w):
    mine, other = own_and_other(w)
    return both_rows(mine, across_y(other))


def gathered(w, axes):
    return lax.all_gather(w, axes, axis=0, tiled=True).reshape(-1, w.shape[-1])


def exchange(v, kind):
    return lax.all_to_all(v, OWNERS[kind], split_axis=0, concat_axis=0, tiled=True)


def pad_to(v, shape):
    return jnp.pad(v, [(0, n - m) for m, n in zip(v.shape, shape)])


def adapters_plain(owners, parts):
    layers = []
    for gd_in, gd_out, gu_in, gu_out in parts:
        downs = [gd_in[p * R : (p + 1) * R] for p in range(3)] + [gd_out[:R]]
        ups = [gu_in[p * R : (p + 1) * R, p * D : (p + 1) * D] for p in range(3)] + [gu_out[:R]]
        layers.append(jnp.concatenate(downs + ups))
    compact = jnp.concatenate(layers).astype(BF)
    ranks = lax.axis_size(SHARD)
    pieces = compact.reshape(UNIT, ranks, D // ranks).transpose(1, 0, 2)
    pieces = lax.all_to_all(pieces, SHARD, split_axis=0, concat_axis=0, tiled=True)
    pick = (owners[None, :] == jnp.arange(NA, dtype=jnp.int32)[:, None]).astype(F32)
    summed = jnp.dot(pick, pieces.reshape(ranks, -1).astype(F32), precision=HIGHEST).astype(BF)
    groups = lax.axis_size(EXPERT)
    summed = lax.all_to_all(
        summed.reshape(groups, NA // groups, -1), EXPERT, split_axis=0, concat_axis=0, tiled=True
    )
    summed = jnp.sum(summed.astype(F32), axis=0)
    return summed.reshape(summed.shape[0], UNIT, -1).transpose(0, 2, 1)


def per_device(
    tokens,
    segments,
    parents,
    adapter_of,
    routes,
    norm_gain,
    query_key_value_weight,
    output_weight,
    adapter_down,
    adapter_up,
    router,
    router_residual,
    const_proj,
    const_vec,
    w_gate_up,
    w_down,
    out_grad,
):
    fast = w_gate_up.shape[1] == 2
    kind = PLANE if fast else WIDE_SLICE
    barrier = lax.optimization_barrier
    if fast:
        mine, other = own_and_other(w_gate_up[0])
        parts = [lax.all_gather(mine, ("zh", "zl"), axis=0)]
        down_mine, down_other = own_and_other(w_down[0])
        first, other, down_other = gather_shared(
            query_key_value_weight[0], output_weight[0], (other, down_other)
        )
        shared = [first]
        parts.append(lax.all_gather(other, ("zh", "zl"), axis=0))
        gate_up_full = [parts]
        down_full = [gathered(both_rows(down_mine, down_other), ("zh", "zl"))]
    else:
        shared = gather_shared(query_key_value_weight[0], output_weight[0])
        gate_up_full = [[gathered(w_gate_up[layer, 0], SHARD)] for layer in range(LAYERS)]
        down_full = [gathered(w_down[layer, 0], SHARD) for layer in range(LAYERS)]

    which = adapter_of[0]
    down_sel = lax.dynamic_index_in_dim(adapter_down, which, axis=2, keepdims=False)
    up_sel = lax.dynamic_index_in_dim(adapter_up, which, axis=2, keepdims=False)
    down_in = jnp.pad(
        down_sel[:, :3].transpose(0, 2, 1, 3).reshape(LAYERS, D, 3 * R), ((0, 0), (0, 0), (0, 80))
    )
    down_out = jnp.pad(down_sel[:, 3], ((0, 0), (0, 0), (0, 112)))
    up_t = 2.0 * up_sel.transpose(0, 1, 3, 2)
    up_in = jnp.zeros((LAYERS, 128, 3 * D), BF)
    for p in range(3):
        up_in = up_in.at[:, p * R : (p + 1) * R, p * D : (p + 1) * D].set(up_t[:, p])
    up_out = jnp.pad(up_t[:, 3], ((0, 0), (0, 112), (0, 0)))
    rcat = jnp.concatenate([router, const_proj[:, 0], const_proj[:, 1]], axis=2)
    rcat = jnp.pad(rcat, ((0, 0), (0, 0), (0, 112)))
    rcat_t = rcat[:, :, :16].transpose(0, 2, 1)
    residual = pad_to(router_residual, (16, 128))
    residual_t = pad_to(router_residual.T, (16, 128))

    qf, kf, cos, sin, tcol, trow, router_s, router_ts, residual_s, residual_ts = prep(
        parents, segments.reshape(T, 1), routes, rcat, rcat_t, residual, residual_t
    )

    stream = tokens
    earlier = jnp.zeros((T, 128), F32)
    saved = []
    for layer in range(LAYERS):
        gain0 = norm_gain[layer, 0:1]
        gain1 = norm_gain[layer, 1:2]
        normed, narrow, qkv = project(
            stream, gain0, shared[layer], down_in[layer], up_in[layer], cos, sin
        )
        mixed, aug = attend(qkv, qf, kf)
        mid, sent, logits, narrow_out = settle(
            stream, mixed, shared[layer], down_out[layer], up_out[layer], gain1, router_s[layer],
            earlier, residual_s,
        )
        buffer = dispatch(trow, sent)
        received = exchange(buffer, kind)
        if layer == 0:
            if fast:
                later = barrier((w_gate_up[1], w_down[1], logits))
                gate_up_next, down_next = barrier((swapped(later[0]), later[1]))
                gate_up_full.append([gathered(gate_up_next, ("zh", "zl"))])
                down_full.append(gathered(swapped(down_next), ("zh", "zl")))
            later = lax.optimization_barrier(
                (query_key_value_weight[1], output_weight[1], logits)
            )
            shared += gather_shared(later[0], later[1])
            returned, gate, up = expert_forward(received, gate_up_full[0], down_full[0], kind)
        else:
            slot_grads = exchange(dispatch_grad(trow, out_grad, logits, routes), kind)
            grad_mixed, following, grad_mid, grad_logits, gu_out, gd_out = expert_both(
                *expert_parts(received, gate_up_full[1][0], kind), slot_grads, gate_up_full[1][0], down_full[1], mid, out_grad, mixed,
                shared[1], tcol, logits, routes, gain1, const_vec[1], router_ts[1], residual_ts,
                narrow_out, down_out[1], up_out[1], kind,
            )
            c0 = c1 = None
        if layer == 0:
            following, c0, c1 = combine(
                tcol, returned.reshape(SLOTS, D), mid, logits, routes, gain1, const_vec[0]
            )
        saved.append((stream, normed, narrow, qkv, mixed, aug, mid, logits, narrow_out, c0, c1))
        stream = following
        earlier = logits

    grad = out_grad
    parts = [None] * LAYERS
    for layer in reversed(range(LAYERS)):
        x_in, normed, narrow, qkv, mixed, aug, mid, logits, narrow_out, c0, c1 = saved[layer]
        gain0 = norm_gain[layer, 0:1]
        gain1 = norm_gain[layer, 1:2]
        if layer == 0:
            grad_mid, grad_mixed, gu_out, gd_out = expert_backward(
                gate, up, gate_up_full[0], down_full[0], grad, mid, c0, c1, mixed, shared[0], trow,
                tcol, logits, routes, grad_logits, gain1, const_vec[0], router_ts[0], narrow_out,
                down_out[0], up_out[0], kind,
            )
        grad, gu_in, gd_in = layer_back(
            grad_mid, grad_mixed, mixed, shared[layer], qkv, aug, normed, x_in, gain0, narrow,
            down_in[layer], up_in[layer], kf, cos, sin,
        )
        parts[layer] = (gd_in, gd_out, gu_in, gu_out)

    if usual():
        final = adapters(adapter_of, [v for layer in parts for v in layer])
    else:
        final = adapters_plain(lax.all_gather(adapter_of, SHARD, axis=0, tiled=True), parts)
    final = final.reshape(*final.shape[:2], LAYERS, 2, 4, R).transpose(3, 2, 4, 0, 1, 5)
    return (stream, grad, final[0], final[1])


def solution(mesh):
    owners, shards = mesh.shape["expert"], mesh.shape["shard"]
    each = NFFN // owners
    fine = jax.sharding.Mesh(
        mesh.devices.reshape(owners // 2, 2, shards // each**2, each, each), AXES
    )
    expert, shard, both = EXPERT, SHARD, AXES
    in_specs = (
        P(both, None),
        P(both, None),
        P(both, None),
        P(both),
        P(both, None),
        P(),
        P(None, shard, None),
        P(None, shard, None),
        P(),
        P(),
        P(),
        P(),
        P(),
        P(),
        P(None, expert, shard, None),
        P(None, expert, shard, None),
        P(both, None),
    )
    out_specs = (
        P(both, None),
        P(both, None),
        P(None, None, expert, shard, None),
        P(None, None, expert, shard, None),
    )
    return jax.shard_map(
        per_device, mesh=fine, in_specs=in_specs, out_specs=out_specs, check_vma=False
    )
```

```python
import functools
import math

import jax
import jax.numpy as jnp
from jax import lax
from jax.experimental import pallas as pl
from jax.experimental.pallas import tpu as pltpu
from jax.sharding import PartitionSpec as P

D = 768
HEADS = 12
HD = 64
FF = 2048
NFFN = 8
NEXP = 12
R = 16
NA = 8
NSEG = 13
LAYERS = 2
CAP = 192
T = 1024
SLOTS = NFFN * CAP
RB = 256
NB = T // RB
PAIRS = HEADS // 2
FC = 512
EPSILON = 1e-06
BIG = 2.0**100
LOG_SCALE = math.log2(math.e) / math.sqrt(HD)
F32 = jnp.float32
BF = jnp.bfloat16
HIGHEST = lax.Precision.HIGHEST
VMEM_BYTES = 60 * 1024 * 1024


def mm(a, b):
    return lax.dot_general(a, b, (((1,), (0,)), ((), ())), preferred_element_type=F32)


def mm_nt(a, b):
    return lax.dot_general(a, b, (((1,), (1,)), ((), ())), preferred_element_type=F32)


def mm_tn(a, b):
    return lax.dot_general(a, b, (((0,), (0,)), ((), ())), preferred_element_type=F32)


def mm_exact(a, b):
    return lax.dot_general(
        a, b, (((1,), (0,)), ((), ())), preferred_element_type=F32, precision=HIGHEST
    )


def iota(shape, axis):
    return lax.broadcasted_iota(jnp.int32, shape, axis)


def sigmoid(v):
    return 1.0 / (1.0 + jnp.exp(-v))


def call(body, grid, ins, outs, scratch=(), name=None, flops=0, nbytes=0):
    def spec(entry):
        if entry[1] == "smem":
            return pl.BlockSpec(memory_space=pltpu.SMEM)
        if entry[1] is None:
            shape = entry[0].shape
            return pl.BlockSpec(shape, lambda *_: (0,) * len(shape))
        return pl.BlockSpec(entry[1], entry[2])

    return pl.pallas_call(
        body,
        grid=grid,
        in_specs=[spec(e) for e in ins],
        out_specs=[spec(e) for e in outs],
        out_shape=[jax.ShapeDtypeStruct(e[0].shape, e[0].dtype) for e in outs],
        scratch_shapes=list(scratch),
        compiler_params=pltpu.CompilerParams(
            dimension_semantics=("arbitrary",) * len(grid), vmem_limit_bytes=VMEM_BYTES
        ),
        cost_estimate=pl.CostEstimate(
            flops=int(flops), bytes_accessed=int(nbytes), transcendentals=0
        ),
        name=name,
    )(*[e[0] for e in ins])


def out(shape, dtype):
    return jax.ShapeDtypeStruct(shape, dtype)


def rows(i):
    return (i, 0)


def three(v):
    high = v.astype(BF)
    rest = v - high.astype(F32)
    middle = rest.astype(BF)
    return high, middle, (rest - middle.astype(F32)).astype(BF)


def spread_lanes(v):
    a, b, c = (part.astype(F32) for part in three(v))
    total = a + pltpu.roll(b, 16, 1) + pltpu.roll(c, 32, 1)
    total = total + pltpu.roll(a, 48, 1) + pltpu.roll(b, 64, 1) + pltpu.roll(a, 80, 1)
    return total.astype(BF)


def stack_rows(w):
    a, b, c = three(w)
    return jnp.concatenate([a, a, a, b, b, c, jnp.zeros((32, w.shape[1]), BF)], axis=0)


def prep_body(
    par_ref, seg_ref, rt_ref, rc_ref, rct_ref, res_ref, rest_ref,
    qf_ref, kf_ref, cos_ref, sin_ref, tcol_ref, trow_ref, rs_ref, rts_ref, ress_ref, rests_ref, anc,
):
    for layer in range(LAYERS):
        a, b, c = (part.astype(F32) for part in three(rc_ref[layer]))
        rs_ref[layer] = (a + pltpu.roll(b, 16, 1) + pltpu.roll(c, 32, 1)).astype(BF)
        rts_ref[layer] = stack_rows(rct_ref[layer])
    ress_ref[...] = stack_rows(res_ref[...])
    rests_ref[...] = stack_rows(rest_ref[...])
    first = iota((1, 128), 1) & 63
    anc[...] = jnp.zeros_like(anc)
    anc[0:1, :] = (first == 0).astype(F32)
    for s in range(1, NSEG):
        above = anc[pl.ds(par_ref[0, s], 1), :]
        anc[s : s + 1, :] = jnp.maximum(above, (first == s).astype(F32))
    lane = iota((T, 128), 1)
    lane6 = lane & 63
    low = lane < 64
    member = (seg_ref[...] == lane6).astype(F32)
    ways = mm(jnp.where(low, member, 0.0).astype(BF), anc[...].astype(BF))
    qf_ref[...] = jnp.where(lane6 < NSEG, (ways - 1.0) * BIG, 0.0).astype(BF)
    ones = ((lane6 >= 16) & (lane6 < 19)).astype(F32)
    kf_ref[...] = (member + ones).astype(BF)
    hit0 = (rt_ref[:, 0:1] == lane).astype(F32)
    hit1 = (rt_ref[:, 1:2] == lane).astype(F32)
    hits = hit0 + hit1
    upto = (iota((T, T), 0) >= iota((T, T), 1)).astype(F32).astype(BF)
    seen = mm(upto, jnp.concatenate([member.astype(BF), hits.astype(BF)], axis=1))
    depth = jnp.sum(jnp.where(low, ways * seen[:, :128], 0.0), axis=1, keepdims=True) - 1.0
    before = seen[:, 128:] - hits

    def target(hit, route):
        slot = jnp.sum(hit * before, axis=1, keepdims=True)
        place = route.astype(F32) * CAP + slot
        return jnp.where(route < NFFN, place, 4.0 * SLOTS)

    t0 = target(hit0, rt_ref[:, 0:1])
    t1 = target(hit1, rt_ref[:, 1:2])
    both = jnp.where(lane == 0, t0, jnp.where(lane == 1, t1, 0.0))
    tcol_ref[...] = both.astype(jnp.int32)
    trow_ref[...] = both.T[0:8, :].astype(jnp.int32)
    inverse = jnp.exp((lane & 31).astype(F32) * (-math.log(10000.0) / 32.0))
    angle = depth * inverse
    cos_ref[...] = jnp.cos(angle)
    sine = jnp.sin(angle)
    sin_ref[...] = jnp.where((lane & 32) == 0, -sine, sine)


def prep(parents, seg_col, routes, rcat, rcat_t, residual, residual_t):
    return call(
        prep_body,
        (1,),
        [
            (parents, "smem"),
            (seg_col, None),
            (routes, None),
            (rcat, None),
            (rcat_t, None),
            (residual, None),
            (residual_t, None),
        ],
        [
            (out((T, 128), BF), None),
            (out((T, 128), BF), None),
            (out((T, 128), F32), None),
            (out((T, 128), F32), None),
            (out((T, 128), jnp.int32), None),
            (out((8, T), jnp.int32), None),
            (out((LAYERS, D, 128), BF), None),
            (out((LAYERS, 128, D), BF), None),
            (out((128, 128), BF), None),
            (out((128, 128), BF), None),
        ],
        [pltpu.VMEM((128, 128), F32)],
        name="prep",
        flops=2 * T * T * 256,
        nbytes=3e6,
    )


def turn(v, cos, sin):
    first = (iota(v.shape, 1) & 32) == 0
    other = jnp.where(first, pltpu.roll(v, 96, 1), pltpu.roll(v, 32, 1))
    return v * cos + other * sin


def project_rows(x, gain, w_ref, d_ref, u_ref, cos, sin, n_ref, nar_ref, qkv_ref):
    scale = lax.rsqrt(jnp.mean(x * x, axis=1, keepdims=True) + EPSILON)
    normed = (x * scale * gain).astype(BF)
    n_ref[...] = normed
    narrow = mm(normed, d_ref[...]).astype(BF)
    nar_ref[...] = narrow
    for block in range(3):
        cols = slice(block * D, (block + 1) * D)
        part = mm(normed, w_ref[block]) + mm(narrow, u_ref[:, cols])
        for j in range(PAIRS):
            piece = part[:, j * 128 : (j + 1) * 128]
            if block < 2:
                piece = turn(piece, cos, sin)
            at = block * D + j * 128
            qkv_ref[:, at : at + 128] = piece.astype(BF)


def project_body(x_ref, g_ref, w_ref, d_ref, u_ref, cos_ref, sin_ref, n_ref, nar_ref, qkv_ref):
    project_rows(
        x_ref[...].astype(F32),
        g_ref[...],
        w_ref,
        d_ref,
        u_ref,
        cos_ref[...],
        sin_ref[...],
        n_ref,
        nar_ref,
        qkv_ref,
    )


def project(x, gain, w, down, up, cos, sin):
    return call(
        project_body,
        (NB,),
        [
            (x, (RB, D), rows),
            (gain, None),
            (w, (3, D, D), lambda i: (0, 0, 0)),
            (down, None),
            (up, None),
            (cos, (RB, 128), rows),
            (sin, (RB, 128), rows),
        ],
        [
            (out((T, D), BF), (RB, D), rows),
            (out((T, 128), BF), (RB, 128), rows),
            (out((T, 3 * D), BF), (RB, 3 * D), rows),
        ],
        name="project",
        flops=2 * T * D * 3 * D,
        nbytes=12e6,
    )


def attend_body(q_ref, k_ref, v_ref, qf_ref, kf_ref, mixed_ref, aug_ref):
    low = iota((T, 128), 1) < 64
    k = k_ref[...]
    kf = kf_ref[...]
    v = v_ref[...]
    one = jnp.ones((T, 128), BF)
    keys = (jnp.where(low, k, kf), jnp.where(low, kf, k))
    values = (jnp.where(low, v, one), jnp.where(low, one, v))
    low = low[:RB]
    tri = iota((RB, RB), 0) >= iota((RB, RB), 1)
    lane6 = iota((RB, 128), 1) & 63
    for i in range(NB):
        here = slice(i * RB, (i + 1) * RB)
        q = q_ref[here, :]
        qf = qf_ref[here, :]
        tops = []
        outs = []
        for h in range(2):
            qa = jnp.where(low, q, qf) if h == 0 else jnp.where(low, qf, q)
            diag = jnp.where(tri, mm_nt(qa, keys[h][here]), -BIG)
            top = jnp.max(diag, axis=1, keepdims=True)
            if i:
                off = mm_nt(qa, keys[h][: i * RB])
                top = jnp.maximum(top, jnp.max(off, axis=1, keepdims=True))
            result = mm(jnp.exp2((diag - top) * LOG_SCALE).astype(BF), values[h][here])
            if i:
                weights = jnp.exp2((off - top) * LOG_SCALE).astype(BF)
                result = result + mm(weights, values[h][: i * RB])
            tops.append(top)
            outs.append(result)
        total = jnp.where(low, outs[1], outs[0])
        mixed = jnp.where(low, outs[0], outs[1]) / pltpu.roll(total, 64, 1)
        mixed_ref[here, :] = mixed.astype(BF)
        level = -(jnp.where(low, tops[1], tops[0]) + math.sqrt(HD) * jnp.log(total))
        a, b, c = three(level)
        aug_ref[0, here, :] = jnp.where(
            lane6 == 16, a, jnp.where(lane6 == 17, b, jnp.where(lane6 == 18, c, qf))
        )


def attend(qkv, qf, kf):
    return call(
        attend_body,
        (PAIRS,),
        [
            (qkv, (T, 128), lambda j: (0, j)),
            (qkv, (T, 128), lambda j: (0, PAIRS + j)),
            (qkv, (T, 128), lambda j: (0, 2 * PAIRS + j)),
            (qf, None),
            (kf, None),
        ],
        [
            (out((T, D), BF), (T, 128), lambda j: (0, j)),
            (out((PAIRS, T, 128), BF), (1, T, 128), lambda j: (j, 0, 0)),
        ],
        name="attend",
        flops=12 * 4 * T * T * 128,
        nbytes=8e6,
    )


def settle_body(
    x_ref, mixed_ref, w_ref, d_ref, u_ref, g_ref, rt_ref, earlier_ref, res_ref,
    mid_ref, sent_ref, lg_ref, nar_ref,
):
    mixed = mixed_ref[...]
    narrow = mm(mixed, d_ref[...]).astype(BF)
    nar_ref[...] = narrow
    mid = x_ref[...].astype(F32) + mm(mixed, w_ref[0]) + mm(narrow, u_ref[...])
    mid_ref[...] = mid
    scale = lax.rsqrt(jnp.mean(mid * mid, axis=1, keepdims=True) + EPSILON)
    normed = mid * scale * g_ref[...]
    sent_ref[...] = normed.astype(BF)
    a, b, c = three(normed)
    one, two, last = mm(a, rt_ref[...]), mm(b, rt_ref[...]), mm(c, rt_ref[...])
    total = one + two + last + pltpu.roll(one + two, 112, 1) + pltpu.roll(one, 96, 1)
    lane = iota((RB, 128), 1)
    earlier = jnp.where(lane < NEXP, earlier_ref[...], 0.0)
    extra = mm(spread_lanes(earlier), res_ref[...])
    lg_ref[...] = jnp.where(lane < 16, total + extra, 0.0)


def settle(x, mixed, w, down, up, gain, router, earlier, residual):
    return call(
        settle_body,
        (NB,),
        [
            (x, (RB, D), rows),
            (mixed, (RB, D), rows),
            (w, (1, D, D), lambda i: (3, 0, 0)),
            (down, None),
            (up, None),
            (gain, None),
            (router, None),
            (earlier, (RB, 128), rows),
            (residual, None),
        ],
        [
            (out((T, D), F32), (RB, D), rows),
            (out((T, D), BF), (RB, D), rows),
            (out((T, 128), F32), (RB, 128), rows),
            (out((T, 128), BF), (RB, 128), rows),
        ],
        name="settle",
        flops=2 * T * D * D * 2,
        nbytes=10e6,
    )


def dispatch_body(trow_ref, s_ref, o_ref):
    place = pl.program_id(0) * CAP + iota((CAP, T), 0)
    hit = (trow_ref[0:1, :] == place) | (trow_ref[1:2, :] == place)
    o_ref[0] = mm(hit.astype(F32).astype(BF), s_ref[...]).astype(BF)


def dispatch(trow, sent):
    return call(
        dispatch_body,
        (NFFN,),
        [(trow, None), (sent, None)],
        [(out((NFFN, CAP, D), BF), (1, CAP, D), lambda j: (j, 0, 0))],
        name="dispatch",
        flops=2 * T * SLOTS * D,
        nbytes=4e6,
    )[0]


def dispatch_grad_body(trow_ref, g_ref, lg_ref, rt_ref, o_ref, first, second):
    @pl.when(pl.program_id(0) == 0)
    def _():
        for i in range(NB):
            at = slice(i * RB, (i + 1) * RB)
            gates = mix_terms(lg_ref[at, :], rt_ref[at, :])[0]
            g = g_ref[at, :].astype(F32)
            first[at, :] = (gates[0] * g).astype(BF)
            second[at, :] = (gates[1] * g).astype(BF)

    place = pl.program_id(0) * CAP + iota((CAP, T), 0)
    hit0 = (trow_ref[0:1, :] == place).astype(F32).astype(BF)
    hit1 = (trow_ref[1:2, :] == place).astype(F32).astype(BF)
    o_ref[0] = (mm(hit0, first[...]) + mm(hit1, second[...])).astype(BF)


def dispatch_grad(trow, g, logits, routes):
    return call(
        dispatch_grad_body,
        (NFFN,),
        [(trow, None), (g, None), (logits, None), (routes, None)],
        [(out((NFFN, CAP, D), BF), (1, CAP, D), lambda j: (j, 0, 0))],
        [pltpu.VMEM((T, D), BF), pltpu.VMEM((T, D), BF)],
        name="dispatch_grad",
        flops=4 * T * SLOTS * D,
        nbytes=6e6,
    )[0]


PR = 2 * CAP
NP = NFFN // 2


def split_refs(refs, *counts):
    parts = []
    for count in counts:
        parts.append(refs[:count])
        refs = refs[count:]
    return *parts, refs


def flip(bit, change):
    return bit + change - 2 * bit * change


PLANE, WIDE_SLICE = 0, 1
OWNERS = (("x", "c", "y"), ("x", "c"))


def owner_at(p, h, kind):
    x = lax.axis_index("x")
    far, near, core = ((1, 1, h), (1 - h, h, 0), (1 - h, h, 1), (0, 0, h))[p]
    if kind == WIDE_SLICE:
        x = 2 * flip(x // 2, far) + flip(x % 2, near)
        c = flip(lax.axis_index("c"), core)
        return {"x": x, "c": c}, x * 2 + c
    x, c, y = flip(x, far), flip(lax.axis_index("c"), core), flip(lax.axis_index("y"), near)
    return {"x": x, "c": c, "y": y}, (x * 2 + c) * 2 + y


PLACES = [(p, h) for p in range(NP) for h in range(2)]


def greet(kind):
    barrier = pltpu.get_barrier_semaphore()
    for p, h in PLACES[:-2] + PLACES[-1:]:
        pl.semaphore_signal(
            barrier, inc=1, device_id=owner_at(p, h, kind)[0], device_id_type=pl.DeviceIdType.MESH
        )
    pl.semaphore_wait(barrier, NFFN - 1)


def block_of(ref, p, h):
    return ref.at[p, h * CAP : (h + 1) * CAP, :]


def fetch_weights(split, gate_ups, down_ref, w1, w2, sems):
    copies = []
    if split:
        y = lax.axis_index("y")
        for side, ref in enumerate(gate_ups):
            mine = flip(y, side)
            count, size = ref.shape[0], ref.shape[1]
            for k in range(count):
                at = pl.multiple_of((2 * k + mine) * size, size)
                copies.append(
                    pltpu.make_async_copy(
                        ref.at[k], w1.at[pl.ds(at, size), :], sems.at[side * count + k]
                    )
                )
    else:
        copies.append(pltpu.make_async_copy(gate_ups[0], w1, sems.at[0]))
    copies.append(pltpu.make_async_copy(down_ref, w2, sems.at[8]))
    for copy in copies:
        copy.start()
    return copies


def fetch_blocks(source, rv, sems, kind):
    copies = []
    for n, (p, h) in enumerate(PLACES):
        number = owner_at(p, h, kind)[1]
        copies.append(pltpu.make_async_copy(source.at[number], block_of(rv, p, h), sems.at[n]))
    for copy in copies:
        copy.start()
    return copies


def give_back(pv, p, target, send, recv, kind):
    me = owner_at(NP - 1, 0, kind)[1]
    copies = []
    for h in range(2):
        n = 2 * p + h
        if (p, h) == (NP - 1, 0):
            copy = pltpu.make_async_copy(block_of(pv, p, h), target.at[me], send.at[n])
        else:
            copy = pltpu.make_async_remote_copy(
                src_ref=block_of(pv, p, h),
                dst_ref=target.at[me],
                send_sem=send.at[n],
                recv_sem=recv.at[n],
                device_id=owner_at(p, h, kind)[0],
                device_id_type=pl.DeviceIdType.MESH,
            )
        copy.start()
        copies.append(copy)
    return copies


def chunk_at(f):
    return pl.multiple_of(f * FC, FC)


def forward_chunk(r, w1, w2, f):
    at = chunk_at(f)
    gate = mm(r, w1[:, pl.ds(at, FC)])
    up = mm(r, w1[:, pl.ds(pl.multiple_of(FF + f * FC, FC), FC)])
    active = (gate * sigmoid(gate) * up).astype(BF)
    return gate, up, mm(active, w2[pl.ds(at, FC), :])


def backward_chunk(g, gate, up, w1, w2, f):
    at = chunk_at(f)
    grad = mm_nt(g, w2[pl.ds(at, FC), :])
    s = sigmoid(gate)
    grad_s = grad * s
    grad_gate = (grad_s * up * (1.0 + gate * (1.0 - s))).astype(BF)
    grad_up = (grad_s * gate).astype(BF)
    return mm_nt(grad_gate, w1[:, pl.ds(at, FC)]) + mm_nt(
        grad_up, w1[:, pl.ds(pl.multiple_of(FF + f * FC, FC), FC)]
    )


def expert_body(split, kind, *refs):
    count = 2 if split else 1
    gate_ups = refs[:count]
    down_ref, rec_ref, ret_ref, gate_ref, up_ref = refs[count : count + 5]
    w1, w2, rv, pv, gv, uv, acc, wsem, rsem, gsem, usem, send, recv = refs[count + 5 :]
    weights = fetch_weights(split, gate_ups, down_ref, w1, w2, wsem)
    blocks = fetch_blocks(rec_ref, rv, rsem, kind)
    greet(kind)
    for copy in weights + blocks:
        copy.wait()
    stores = []
    moves = []
    for p in range(NP):
        r = rv[p]
        acc[...] = jnp.zeros_like(acc)

        def step(f, carry):
            gate, up, part = forward_chunk(r, w1, w2, f)
            gv[p, :, pl.ds(chunk_at(f), FC)] = gate.astype(BF)
            uv[p, :, pl.ds(chunk_at(f), FC)] = up.astype(BF)
            acc[...] += part
            return carry

        lax.fori_loop(0, FF // FC, step, 0)
        pv[p] = acc[...].astype(BF)
        moves += give_back(pv, p, ret_ref, send, recv, kind)
        for values, ref, sems in ((gv, gate_ref, gsem), (uv, up_ref, usem)):
            copy = pltpu.make_async_copy(values.at[p], ref.at[p], sems.at[p])
            copy.start()
            stores.append(copy)
    for copy in moves + stores:
        copy.wait()


def own_copies(body, ins, near, outs, near_outs, scratch):
    counts = len(ins), len(near), len(outs), len(near_outs), len(scratch)

    def run(*refs):
        far, near_far, targets, near_targets, inner, close = split_refs(refs, *counts)
        close, near_close, sems = split_refs(close, len(near), len(near_outs))
        loads = [
            pltpu.make_async_copy(source, target, sems[0].at[n])
            for n, (source, target) in enumerate(zip(near_far, close))
        ]
        for copy in loads:
            copy.start()

        def ready():
            for copy in loads:
                copy.wait()

        def done(n):
            copy = pltpu.make_async_copy(near_close[n], near_targets[n], sems[1].at[n])
            copy.start()
            return copy

        body(far, close, targets, near_close, inner, ready, done)

    extra = [pltpu.VMEM(v.shape, v.dtype) for v in (*near, *near_outs)]
    extra += [DMA((max(1, len(near)),)), DMA((max(1, len(near_outs)),))]
    return run, [*ins, *near], [*outs, *near_outs], [*scratch, *extra]


def comm_call(body, ins, outs, scratch, name, number, flops, nbytes, near=(), near_outs=()):
    run, ins, outs, scratch = own_copies(body, ins, near, outs, near_outs, scratch)
    far = {} if number is None else dict(collective_id=number, has_side_effects=True)
    return pl.pallas_call(
        run,
        in_specs=[pl.BlockSpec(memory_space=pl.ANY)] * len(ins),
        out_specs=[pl.BlockSpec(memory_space=pl.ANY)] * len(outs),
        out_shape=outs,
        scratch_shapes=scratch,
        compiler_params=pltpu.CompilerParams(vmem_limit_bytes=VMEM_BYTES, **far),
        cost_estimate=pl.CostEstimate(
            flops=int(flops), bytes_accessed=int(nbytes), transcendentals=0
        ),
        name=name,
    )(*ins)


DMA = pltpu.SemaphoreType.DMA
WEIGHTS = [pltpu.VMEM((D, 2 * FF), BF), pltpu.VMEM((FF, D), BF)]
ROWS = pltpu.VMEM((NP, PR, D), BF)
WIDE = pltpu.VMEM((NP, PR, FF), BF)
SUM = pltpu.VMEM((PR, D), F32)
BLOCKS = jax.ShapeDtypeStruct((NFFN, CAP, D), BF)
KEPT = jax.ShapeDtypeStruct((NP, PR, FF), BF)


def expert_forward(received, gate_ups, down, kind):
    split = len(gate_ups) == 2

    def body(far, near, outs, near_outs, scratch, ready, done):
        expert_body(split, kind, *far, *outs, *scratch)

    return comm_call(
        body,
        [*gate_ups, down, received],
        [BLOCKS, KEPT, KEPT],
        WEIGHTS + [ROWS, ROWS, WIDE, WIDE, SUM]
        + [DMA((9,)), DMA((8,)), DMA((NP,)), DMA((NP,)), DMA((8,)), DMA((8,))],
        "expert_forward",
        1,
        2 * SLOTS * D * FF * 3,
        26e6,
    )


def expert_parts_body(kind, far, outs, scratch):
    gate_up_ref, rec_ref = far
    w1, rv, wsem, rsem, osem, *kept = scratch
    load = pltpu.make_async_copy(gate_up_ref, w1, wsem.at[0])
    load.start()
    for copy in fetch_blocks(rec_ref, rv, rsem, kind) + [load]:
        copy.wait()
    stores = []
    for p in range(NP):
        r = rv[p]

        def step(f, carry):
            at = pl.ds(chunk_at(f), FC)
            gate = mm(r, w1[:, at])
            up = mm(r, w1[:, pl.ds(pl.multiple_of(FF + f * FC, FC), FC)])
            s = sigmoid(gate)
            silu = gate * s
            kept[0][p, :, at] = (silu * up).astype(BF)
            kept[1][p, :, at] = (up * s * (1.0 + gate * (1.0 - s))).astype(BF)
            kept[2][p, :, at] = silu.astype(BF)
            return carry

        lax.fori_loop(0, FF // FC, step, 0)
        for n in range(3):
            stores.append(pltpu.make_async_copy(kept[n].at[p], outs[n].at[p], osem.at[p, n]))
            stores[-1].start()
    for copy in stores:
        copy.wait()


def expert_parts(received, gate_up, kind):
    def body(far, near, outs, near_outs, scratch, ready, done):
        expert_parts_body(kind, far, outs, scratch)

    return comm_call(
        body,
        [gate_up, received],
        [KEPT, KEPT, KEPT],
        [WEIGHTS[0], ROWS, DMA((1,)), DMA((8,)), DMA((NP, 3)), WIDE, WIDE, WIDE],
        "expert_parts",
        None,
        2 * SLOTS * D * FF * 2,
        28e6,
    )


def expert_both_body(kind, far, near, mix_out, out_near, scratch, ready, done):
    (
        gate_up_ref, down_ref, active_ref, to_gate_ref, to_up_ref, sg_ref, mid_ref, g_ref,
        mixed_ref, shared_ref,
    ) = far
    tcol_ref, lg_ref, rt_ref, gain_ref, cv_ref, wt_ref, res_ref, nar_ref, d_ref, u_ref = near
    out_ref, gm_ref, gle_ref, gu_ref, gd_ref = out_near
    (
        w1, w2, qv, sv, pv, to_gate, to_up, av, back, gback, mid, g, mixed, w3, acc,
        wsem, asem, ssem, msem, send, recv, gsend, grecv,
    ) = scratch

    def start(source, target, sem):
        copy = pltpu.make_async_copy(source, target, sem)
        copy.start()
        return copy

    load = start(down_ref, w2, wsem.at[0])
    actives = [start(active_ref.at[p], av.at[p], asem.at[p]) for p in range(2)]
    greet(kind)
    load.wait()
    moves = []
    extra = []
    for p in range(NP):
        actives[p].wait()
        pv[p] = mm(av[p % 2], w2[...]).astype(BF)
        moves += give_back(pv, p, back, send, recv, kind)
        if p + 2 < NP:
            actives.append(start(active_ref.at[p + 2], av.at[p % 2], asem.at[p + 2]))
        if p == 0:
            extra = fetch_blocks(sg_ref, sv, ssem, kind)
            extra.append(start(gate_up_ref, w1, wsem.at[1]))
            for n, (source, target) in enumerate(
                (
                    (to_gate_ref, to_gate), (to_up_ref, to_up), (mid_ref, mid), (g_ref, g),
                    (mixed_ref, mixed), (shared_ref.at[3], w3),
                )
            ):
                extra.append(start(source, target, msem.at[n]))
    for copy in extra:
        copy.wait()
    later = []
    for p in range(NP):
        grads = sv[p]
        acc[...] = jnp.zeros_like(acc)

        def step(f, carry):
            at = pl.ds(chunk_at(f), FC)
            grad = mm_nt(grads, w2[at, :])
            first = (grad * to_gate[p, :, at].astype(F32)).astype(BF)
            second = (grad * to_up[p, :, at].astype(F32)).astype(BF)
            acc[...] += mm_nt(first, w1[:, at]) + mm_nt(
                second, w1[:, pl.ds(pl.multiple_of(FF + f * FC, FC), FC)]
            )
            return carry

        lax.fori_loop(0, FF // FC, step, 0)
        qv[p] = acc[...].astype(BF)
        later += give_back(qv, p, gback, gsend, grecv, kind)
    for copy in moves:
        copy.wait()
    ready()

    def finish(i, carry):
        at = pl.ds(pl.multiple_of(i * RB, RB), RB)
        logits, routes, middle = lg_ref[at, :], rt_ref[at, :], mid[at, :]
        following, chosen = combine_rows(
            tcol_ref[at, :], back, middle, logits, routes, gain_ref[...], cv_ref
        )
        out_ref[at, :] = following
        gm_ref[at, :], gle_ref[at, :] = mix_grad(
            g[at, :].astype(F32), middle, chosen, logits, routes, 0.0, gain_ref[...], cv_ref,
            wt_ref[...], res_ref[...],
        )
        return carry

    lax.fori_loop(0, NB, finish, 0)
    stores = [done(0), done(2)]
    gu_ref[...] = jnp.zeros_like(gu_ref)
    gd_ref[...] = jnp.zeros_like(gd_ref)
    for copy in later:
        copy.wait()

    def settle_one(i, carry):
        at = pl.ds(pl.multiple_of(i * RB, RB), RB)
        refs = (tcol_ref, mid, g, mixed, gain_ref, nar_ref, w3, d_ref, u_ref, gu_ref, gd_ref)
        settle_back(refs, at, gm_ref, mixed, gback)
        return carry

    lax.fori_loop(0, NB, settle_one, 0)
    stores.append(start(mixed, mix_out, msem.at[6]))
    for copy in stores + [done(n) for n in (1, 3, 4)]:
        copy.wait()


def expert_both(
    active, to_gate, to_up, slot_grads, gate_up, down, mid, g, mixed, weights, tcol, logits, routes, gain,
    const_vec, router_t, residual_t, narrow, down_out, up_out, kind,
):
    def body(far, near, outs, near_outs, scratch, ready, done):
        expert_both_body(kind, far, near, outs[0], near_outs, scratch, ready, done)

    half = pltpu.VMEM((T, D), BF)
    landing = pltpu.VMEM((NFFN, CAP, D), BF)
    return comm_call(
        body,
        [gate_up, down, active, to_gate, to_up, slot_grads, mid, g, mixed, weights],
        [out((T, D), BF)],
        WEIGHTS
        + [ROWS, ROWS, ROWS, WIDE, WIDE, pltpu.VMEM((2, PR, FF), BF), landing, landing]
        + [pltpu.VMEM((T, D), F32), pltpu.VMEM((T, D), g.dtype), half, pltpu.VMEM((D, D), BF), SUM]
        + [DMA((2,)), DMA((NP,)), DMA((8,)), DMA((7,))]
        + [DMA((8,)), DMA((8,)), DMA((8,)), DMA((8,))],
        "expert_both",
        2,
        2 * SLOTS * D * FF * 4,
        40e6,
        [tcol, logits, routes, gain, const_vec, router_t, residual_t, narrow, down_out, up_out],
        [out((T, D), F32), out((T, D), F32), out((T, 128), F32)]
        + [out((128, D), F32), out((128, D), F32)],
    )


def expert_back_body(split, kind, far, near, out_near, outs, scratch, ready, done):
    count = 2 if split else 1
    gate_ups, (down_ref, gate_ref, up_ref, g_ref, mid_ref, c0_ref, c1_ref, mixed_ref, shared_ref) = (
        far[:count], far[count:]
    )
    (
        trow_ref, tcol_ref, lg_ref, rt_ref, gl_ref, gain_ref, cv_ref, wt_ref, nar_ref, d_ref, u_ref
    ) = near
    gm_ref, gu_ref, gd_ref = out_near
    mix_out = outs[0]
    (
        w1, w2, sgv, rv, pv, gv, uv, back, first, second, g, mid, c0, c1, mixed, w3, acc,
        wsem, gsem, usem, msem, dsend, drecv, send, recv, osem,
    ) = scratch
    extra = [
        pltpu.make_async_copy(ref, values, msem.at[n])
        for n, (ref, values) in enumerate(
            (
                (g_ref, g), (mid_ref, mid), (c0_ref, c0), (c1_ref, c1), (mixed_ref, mixed),
                (shared_ref.at[3], w3),
            )
        )
    ]
    extra[0].start()
    extra[0].wait()
    ready()

    def gated(i, carry):
        at = pl.ds(pl.multiple_of(i * RB, RB), RB)
        gates = mix_terms(lg_ref[at, :], rt_ref[at, :])[0]
        first[at, :] = (gates[0] * g[at, :]).astype(BF)
        second[at, :] = (gates[1] * g[at, :]).astype(BF)
        return carry

    lax.fori_loop(0, NB, gated, 0)
    weights = fetch_weights(split, gate_ups, down_ref, w1, w2, wsem)
    for p in (3, 0, 1, 2):
        for values, ref, sems in ((gv, gate_ref, gsem), (uv, up_ref, usem)):
            copy = pltpu.make_async_copy(ref.at[p], values.at[p], sems.at[p])
            copy.start()
            weights.append(copy)
    for copy in extra[1:]:
        copy.start()
    greet(kind)
    arrivals = {}
    for p, h in PLACES[:-2] + [(3, 1), (3, 0)]:
        where, number = owner_at(p, h, kind)
        place = number * CAP + iota((CAP, T), 0)
        hit0 = (trow_ref[0:1, :] == place).astype(F32).astype(BF)
        hit1 = (trow_ref[1:2, :] == place).astype(F32).astype(BF)
        values = (mm(hit0, first[...]) + mm(hit1, second[...])).astype(BF)
        n = 2 * p + h
        if (p, h) == (NP - 1, 0):
            rv[p, h * CAP : (h + 1) * CAP, :] = values
            continue
        sgv[p, h * CAP : (h + 1) * CAP, :] = values
        copy = pltpu.make_async_remote_copy(
            src_ref=block_of(sgv, p, h),
            dst_ref=block_of(rv, p, h),
            send_sem=dsend.at[n],
            recv_sem=drecv.at[n],
            device_id=where,
            device_id_type=pl.DeviceIdType.MESH,
        )
        copy.start()
        arrivals[p, h] = copy
    for copy in weights + extra[1:]:
        copy.wait()
    moves = []

    for p in (3, 0, 1, 2):
        for h in range(2):
            if (p, h) in arrivals:
                arrivals[p, h].wait()
        grads = rv[p]
        acc[...] = jnp.zeros_like(acc)

        def step(f, carry):
            at = pl.ds(chunk_at(f), FC)
            gate = gv[p, :, at].astype(F32)
            up = uv[p, :, at].astype(F32)
            acc[...] += backward_chunk(grads, gate, up, w1, w2, f)
            return carry

        lax.fori_loop(0, FF // FC, step, 0)
        pv[p] = acc[...].astype(BF)
        moves += give_back(pv, p, back, send, recv, kind)

    def tidy(i, carry):
        at = pl.ds(pl.multiple_of(i * RB, RB), RB)
        gm_ref[at, :] = mix_grad(
            g[at, :], mid[at, :], (c0[at, :], c1[at, :]), lg_ref[at, :], rt_ref[at, :],
            gl_ref[at, :], gain_ref[...], cv_ref, wt_ref[...], None,
        )[0]
        return carry

    lax.fori_loop(0, NB, tidy, 0)
    gu_ref[...] = jnp.zeros_like(gu_ref)
    gd_ref[...] = jnp.zeros_like(gd_ref)
    for copy in moves:
        copy.wait()

    def settle_one(i, carry):
        at = pl.ds(pl.multiple_of(i * RB, RB), RB)
        refs = (tcol_ref, mid, g, mixed, gain_ref, nar_ref, w3, d_ref, u_ref, gu_ref, gd_ref)
        settle_back(refs, at, gm_ref, first, back)
        return carry

    lax.fori_loop(0, NB, settle_one, 0)
    last = pltpu.make_async_copy(first, mix_out, osem.at[0])
    last.start()
    for copy in [last] + [done(n) for n in range(3)]:
        copy.wait()


def expert_backward(
    gate, up, gate_ups, down, g, mid, c0, c1, mixed, weights, trow, tcol, logits, routes, gl, gain,
    const_vec, router_t, narrow, down_out, up_out, kind,
):
    split = len(gate_ups) == 2

    def body(far, near, outs, near_outs, scratch, ready, done):
        expert_back_body(split, kind, far, near, near_outs, outs, scratch, ready, done)

    half, full = pltpu.VMEM((T, D), BF), pltpu.VMEM((T, D), F32)
    mix, gm, gu, gd = comm_call(
        body,
        [*gate_ups, down, gate, up, g, mid, c0, c1, mixed, weights],
        [out((T, D), BF)],
        WEIGHTS
        + [ROWS, ROWS, ROWS, WIDE, WIDE, pltpu.VMEM((NFFN, CAP, D), BF)]
        + [half, half, full, full, half, half, half, pltpu.VMEM((D, D), BF), SUM]
        + [DMA((9,)), DMA((NP,)), DMA((NP,)), DMA((6,))]
        + [DMA((8,)), DMA((8,)), DMA((8,)), DMA((8,)), DMA((1,))],
        "expert_backward",
        3,
        2 * SLOTS * D * FF * 3,
        26e6,
        [
            trow, tcol, logits, routes, gl, gain, const_vec, router_t, narrow, down_out, up_out,
        ],
        [out((T, D), F32), out((128, D), F32), out((128, D), F32)],
    )
    return gm, mix, gu, gd


def mix_terms(logits, routes):
    lane = iota(logits.shape, 1)

    def at(place):
        return jnp.sum(jnp.where(lane == place, logits, 0.0), axis=1, keepdims=True)

    r0, r1 = routes[:, 0:1], routes[:, 1:2]
    gap = at(r0) - at(r1)
    gates = (sigmoid(gap), sigmoid(-gap))

    def weight(e):
        return jnp.where(r0 == e, gates[0], 0.0) + jnp.where(r1 == e, gates[1], 0.0)

    shares = []
    for c in range(2):
        apart = logits[:, 12 + 2 * c : 13 + 2 * c] - logits[:, 13 + 2 * c : 14 + 2 * c]
        shares.append((sigmoid(apart), sigmoid(-apart)))
    weights = [weight(NFFN + 1), weight(NFFN + 2), weight(NFFN + 3)]
    return gates, weights, shares


def rms_scale(v):
    return lax.rsqrt(jnp.mean(v * v, axis=1, keepdims=True) + EPSILON)


def combine_rows(tcol, back_ref, mid, logits, routes, gain, cv_ref):
    place = iota((RB, SLOTS), 1)
    back = back_ref[...].reshape(SLOTS, D)
    chosen = []
    for k in range(2):
        hit = (tcol[:, k : k + 1] == place).astype(F32).astype(BF)
        chosen.append(mm(hit, back))
    normed = mid * rms_scale(mid) * gain
    gates, weights, shares = mix_terms(logits, routes)
    same = weights[0] + weights[1] * shares[0][0] + weights[2] * shares[1][0]
    moe = gates[0] * chosen[0] + gates[1] * chosen[1] + same * normed
    moe = moe + (weights[1] * shares[0][1]) * cv_ref[0:1, :]
    moe = moe + (weights[2] * shares[1][1]) * cv_ref[1:2, :]
    return mid + moe, chosen


def combine_body(tcol_ref, ret_ref, mid_ref, lg_ref, rt_ref, g_ref, cv_ref, x_ref, c0_ref, c1_ref):
    x_ref[...], chosen = combine_rows(
        tcol_ref[...], ret_ref, mid_ref[...], lg_ref[...], rt_ref[...], g_ref[...], cv_ref
    )
    c0_ref[...] = chosen[0].astype(BF)
    c1_ref[...] = chosen[1].astype(BF)


def combine(tcol, returned, mid, logits, routes, gain, const_vec):
    return call(
        combine_body,
        (NB,),
        [
            (tcol, (RB, 128), rows),
            (returned, None),
            (mid, (RB, D), rows),
            (logits, (RB, 128), rows),
            (routes, (RB, 2), rows),
            (gain, None),
            (const_vec, None),
        ],
        [
            (out((T, D), F32), (RB, D), rows),
            (out((T, D), BF), (RB, D), rows),
            (out((T, D), BF), (RB, D), rows),
        ],
        name="combine",
        flops=4 * T * SLOTS * D,
        nbytes=12e6,
    )


def mix_grad(g, mid, chosen, logits, routes, grad, gain, cv_ref, wt, res):
    normed = mid * rms_scale(mid) * gain
    gates, weights, shares = mix_terms(logits, routes)

    def along(v):
        return jnp.sum(g * v, axis=1, keepdims=True)

    same = along(normed)
    const = [along(cv_ref[c : c + 1, :]) for c in range(2)]
    gate_grads = []
    for k in range(2):
        r = routes[:, k : k + 1]
        value = along(chosen[k].astype(F32)) + jnp.where(r == NFFN + 1, same, 0.0)
        for c in range(2):
            mixed = shares[c][0] * same + shares[c][1] * const[c]
            value = value + jnp.where(r == NFFN + 2 + c, mixed, 0.0)
        gate_grads.append(value)
    slope = gates[0] * gates[1] * (gate_grads[0] - gate_grads[1])
    lane = iota((RB, 128), 1)
    grad = grad + jnp.where(lane == routes[:, 0:1], slope, 0.0)
    grad = grad - jnp.where(lane == routes[:, 1:2], slope, 0.0)
    only = grad
    for c in range(2):
        tilt = weights[1 + c] * shares[c][0] * shares[c][1] * (same - const[c])
        grad = grad + jnp.where(lane == 12 + 2 * c, tilt, 0.0)
        grad = grad - jnp.where(lane == 13 + 2 * c, tilt, 0.0)
    keep = weights[0] + weights[1] * shares[0][0] + weights[2] * shares[1][0]
    residual = None if res is None else mm(spread_lanes(only), res)
    return mm(spread_lanes(grad), wt) + keep * g, residual


def settle_back(refs, at, gm_ref, mix_ref, back_ref):
    tcol_ref, mid_ref, g_ref, mixed_ref, gain_ref, nar_ref, w_ref, d_ref, u_ref, gu_ref, gd_ref = refs
    place = iota((RB, SLOTS), 1)
    tcol = tcol_ref[at, :]
    hit = (tcol[:, 0:1] == place) | (tcol[:, 1:2] == place)
    grad = gm_ref[at, :] + mm(hit.astype(F32).astype(BF), back_ref[...].reshape(SLOTS, D))
    grad = g_ref[at, :].astype(F32) + rms_back(grad, mid_ref[at, :], gain_ref[...])
    gm_ref[at, :] = grad
    grad = grad.astype(BF)
    slim = mm_nt(grad, u_ref[...]).astype(BF)
    gu_ref[...] += 2.0 * mm_tn(nar_ref[at, :], grad)
    gd_ref[...] += mm_tn(slim, mixed_ref[at, :])
    mix_ref[at, :] = (mm_nt(grad, w_ref[...]) + mm_nt(slim, d_ref[...])).astype(BF)


def rms_back(grad, v, gain):
    scale = rms_scale(v)
    inner = grad * gain
    return scale * inner - v * (scale**3 * jnp.mean(v * inner, axis=1, keepdims=True))


def attend_back(q, k, v, aug, kf, g, mixed, dqt):
    lane = iota((T, 128), 1)
    low = lane < 64
    lane6 = lane & 63
    product = g.astype(F32) * mixed.astype(F32)
    d0 = jnp.sum(jnp.where(low, product, 0.0), axis=1, keepdims=True)
    d1 = jnp.sum(jnp.where(low, 0.0, product), axis=1, keepdims=True)
    a, b, c = three(-jnp.where(low, d1, d0))
    zero = jnp.zeros((T, 128), BF)
    ga = jnp.where(lane6 == 0, a, jnp.where(lane6 == 1, b, jnp.where(lane6 == 2, c, zero)))
    va = (lane6 < 3).astype(F32).astype(BF)
    qs = (jnp.where(low, q, aug), jnp.where(low, aug, q))
    ks = (jnp.where(low, k, kf), jnp.where(low, kf, k))
    vs = (jnp.where(low, v, va), jnp.where(low, va, v))
    gs = (jnp.where(low, g, ga), jnp.where(low, ga, g))
    kt = k.T
    tri = iota((RB, RB), 0) <= iota((RB, RB), 1)
    low = low[:RB]
    dks = []
    dvs = []
    for i in range(NB):
        here = slice(i * RB, (i + 1) * RB)
        dk = [None, None]
        dv = [None, None]
        for h in range(2):
            half = slice(h * 64, (h + 1) * 64)
            for start, stop in ((i * RB, (i + 1) * RB), ((i + 1) * RB, T)):
                if start == stop:
                    continue
                there = slice(start, stop)
                p = jnp.exp2(mm_nt(ks[h][here], qs[h][there]) * LOG_SCALE)
                if stop == (i + 1) * RB:
                    p = jnp.where(tri, p, 0.0)
                ds = (p * mm_nt(vs[h][here], gs[h][there])).astype(BF)
                p = p.astype(BF)
                dv_part = mm(p, g[there])
                dk_part = mm(ds, q[there])
                dk[h] = dk_part if dk[h] is None else dk[h] + dk_part
                dv[h] = dv_part if dv[h] is None else dv[h] + dv_part
                part = mm(kt[half, here], ds)
                if i == 0:
                    dqt[half, there] = part
                else:
                    dqt[half, there] += part
        dvs.append(jnp.where(low, dv[0], dv[1]))
        dks.append(jnp.where(low, dk[0], dk[1]))
    return dqt[...].T, jnp.concatenate(dks), jnp.concatenate(dvs)


def layer_back_body(far, near, out_near, gx_ref, scratch, ready, done):
    gm_ref, mix_ref, mixed_ref, w_ref, qkv_ref, aug_ref, n_ref, x_ref = far
    gain_ref, nar_ref, d_ref, u_ref, kf_ref, cos_ref, sin_ref = near
    gu_ref, gd_ref = out_near
    gm, mix, mixed, w, qkv, aug, n, x, gproj, dqt, sems, pair_sems, out_sems = scratch

    def start(source, target, sem):
        copy = pltpu.make_async_copy(source, target, sem)
        copy.start()
        return copy

    def cols(part, j):
        return pl.ds(pl.multiple_of(part * D + j * 128, 128), 128)

    def of_pair(j):
        copies = [
            pltpu.make_async_copy(
                qkv_ref.at[:, cols(part, j)], qkv.at[:, cols(part, j)], pair_sems.at[j, part]
            )
            for part in range(3)
        ]
        for k, (source, target) in enumerate(((mix_ref, mix), (mixed_ref, mixed))):
            copies.append(
                pltpu.make_async_copy(
                    source.at[:, cols(0, j)], target.at[:, cols(0, j)], pair_sems.at[j, 3 + k]
                )
            )
        copies.append(pltpu.make_async_copy(aug_ref.at[j], aug.at[j], pair_sems.at[j, 5]))
        return copies

    for j in range(PAIRS):
        for copy in of_pair(j):
            copy.start()
    third = [start(w_ref.at[k], w.at[k], sems.at[k]) for k in range(3)]
    third += [
        start(source, target, sems.at[3 + k])
        for k, (source, target) in enumerate(((n_ref, n), (x_ref, x), (gm_ref, gm)))
    ]
    ready()

    def pair(j, carry):
        for copy in of_pair(j):
            copy.wait()
        dq, dk, dv = attend_back(
            qkv[:, cols(0, j)], qkv[:, cols(1, j)], qkv[:, cols(2, j)], aug[j], kf_ref[...],
            mix[:, cols(0, j)], mixed[:, cols(0, j)], dqt,
        )
        for part, value in enumerate((dq, dk)):
            value = (value * (1.0 / math.sqrt(HD))).astype(BF).astype(F32)
            gproj[:, cols(part, j)] = turn(value, cos_ref[...], -sin_ref[...]).astype(BF)
        gproj[:, cols(2, j)] = dv.astype(BF)
        return carry

    lax.fori_loop(0, PAIRS, pair, 0)
    for copy in third:
        copy.wait()
    gu_ref[...] = jnp.zeros_like(gu_ref)
    gd_ref[...] = jnp.zeros_like(gd_ref)
    stores = []
    for i in range(NB):
        at = slice(i * RB, (i + 1) * RB)
        grad = jnp.zeros((RB, D), F32)
        slim = jnp.zeros((RB, 128), F32)
        narrow = nar_ref[at, :]
        for part in range(3):
            columns = slice(part * D, (part + 1) * D)
            piece = gproj[at, columns]
            grad = grad + mm_nt(piece, w[part])
            slim = slim + mm_nt(piece, u_ref[:, columns])
            gu_ref[:, columns] += 2.0 * mm_tn(narrow, piece)
        slim = slim.astype(BF)
        gd_ref[...] += mm_tn(slim, n[at, :])
        grad = grad + mm_nt(slim, d_ref[...])
        gm[at, :] = gm[at, :] + rms_back(grad, x[at, :].astype(F32), gain_ref[...])
        stores.append(start(gm.at[at, :], gx_ref.at[at, :], out_sems.at[i]))
    for copy in stores + [done(0), done(1)]:
        copy.wait()


def layer_back(gm, mix, mixed, w, qkv, aug, n, x, gain0, narrow, down, up, kf, cos, sin):
    far = [gm, mix, mixed, w, qkv, aug, n, x]

    def body(far, near, outs, near_outs, scratch, ready, done):
        layer_back_body(far, near, near_outs, outs[0], scratch, ready, done)

    shapes = [out((3, D, D), BF) if v is w else v for v in far]
    return comm_call(
        body,
        far,
        [out((T, D), F32)],
        [pltpu.VMEM(v.shape, v.dtype) for v in shapes]
        + [pltpu.VMEM((T, 3 * D), BF), pltpu.VMEM((128, T), F32)]
        + [DMA((6,)), DMA((PAIRS, 6)), DMA((NB,))],
        "layer_back",
        None,
        12 * 10 * T * T * 128 + 2 * T * D * 3 * D,
        4e7,
        [gain0, narrow, down, up, kf, cos, sin],
        [out((128, 3 * D), F32), out((128, D), F32)],
    )


AXES = ("x", "c", "zh", "zl", "y")
EXPERT, SHARD = AXES[:2], AXES[2:]
PIECE = 96


def shared_body(count, *refs):
    (p_ref,), away, (o_ref,), came, sems = split_refs(refs, 1, count, 1, count)
    local, zs, zr, ys, yr, xs, xr, cs, cr, ws, wr = sems
    x, c, y = (lax.axis_index(name) for name in ("x", "c", "y"))
    z = 2 * lax.axis_index("zh") + lax.axis_index("zl")
    mine, theirs = 2 * x + c, 2 * (1 - x) + c

    def spot(quarter, column, j):
        at = (2 * ((z + 4 - j) % 4) + column) * PIECE
        return o_ref.at[quarter, pl.ds(pl.multiple_of(at, PIECE), PIECE), :]

    others = [{"zh": (z + d) % 4 // 2, "zl": (z + d) % 2} for d in range(1, 4)]
    others += [{"y": 1 - y}, {"x": 1 - x}, {"c": 1 - c}]
    barrier = pltpu.get_barrier_semaphore()
    for who in others:
        pl.semaphore_signal(barrier, inc=1, device_id=who, device_id_type=pl.DeviceIdType.MESH)
    pl.semaphore_wait(barrier, len(others))

    started = []

    def send(source, target, who, send_sem, recv_sem):
        copy = pltpu.make_async_remote_copy(
            src_ref=source,
            dst_ref=target,
            send_sem=send_sem,
            recv_sem=recv_sem,
            device_id=who,
            device_id_type=pl.DeviceIdType.MESH,
        )
        copy.start()
        started.append(copy)
        return copy

    core_copies = []

    def to_core(source, target):
        n = len(core_copies)
        core_copies.append(send(source, target, others[5], cs.at[n], cr.at[n]))

    own = pltpu.make_async_copy(p_ref, spot(mine, y, 0), local.at[0])
    own.start()
    z_copies = [
        send(p_ref, spot(mine, y, 0), others[d], zs.at[d], zr.at[d]) for d in range(3)
    ]
    y_copies = [None] * 6
    x_copies = [None] * 6

    def along_y(n, source, target):
        y_copies[n] = send(source, target, others[3], ys.at[n], yr.at[n])

    def along_x(n, source, target):
        x_copies[n] = send(source, target, others[4], xs.at[n], xr.at[n])

    along_y(0, p_ref, spot(mine, y, 0))
    along_x(0, p_ref, spot(mine, y, 0))
    to_core(p_ref, spot(mine, y, 0))
    swaps = [
        send(source, target, others[3], ws.at[n], wr.at[n])
        for n, (source, target) in enumerate(zip(away, came))
    ]
    for j in range(1, 4):
        z_copies[j - 1].wait_recv()
        piece = spot(mine, y, j)
        along_y(j, piece, piece)
        along_x(j, piece, piece)
        to_core(piece, piece)
    for j in range(4):
        y_copies[j].wait_recv()
        piece = spot(mine, 1 - y, j)
        if j < 2:
            along_x(4 + j, piece, piece)
        to_core(piece, piece)
        x_copies[j].wait_recv()
        piece = spot(theirs, y, j)
        if j >= 2:
            along_y(2 + j, piece, piece)
        to_core(piece, piece)
    for j in range(4):
        (x_copies[4 + j] if j < 2 else y_copies[2 + j]).wait_recv()
        piece = spot(theirs, 1 - y, j)
        to_core(piece, piece)
    for copy in core_copies + swaps:
        copy.wait_recv()
    own.wait()
    for copy in started:
        copy.wait_send()


def usual():
    return tuple(lax.axis_size(name) for name in AXES) == (2, 2, 2, 2, 2)


def gather_shared(qkv, output, away=()):
    rows_here = qkv.shape[0]
    parts = jnp.concatenate([qkv.reshape(rows_here, 3, D).transpose(1, 0, 2), output[None]])
    if not usual():
        return [lax.all_gather(parts, SHARD, axis=1, tiled=True)]
    quarter = 2 * lax.axis_index("x") + lax.axis_index("c")
    piece = lax.dynamic_index_in_dim(parts, quarter, axis=0, keepdims=False)
    return comm_call(
        lambda far, near, outs, near_outs, scratch, ready, done: shared_body(
            len(away), *far, *outs, *scratch
        ),
        [piece, *away],
        [jax.ShapeDtypeStruct(v.shape, v.dtype) for v in (out((4, D, D), BF), *away)],
        [DMA((n,)) for n in (1, 3, 3, 6, 6, 6, 6, 16, 16, 2, 2)],
        "gather_shared",
        5 if away else 0,
        0,
        5e7,
    )


SPAN = 96
UNIT = LAYERS * 2 * 4 * R


def adapters_body(*refs):
    id_ref, parts = refs[0], refs[1 : 1 + 4 * LAYERS]
    o_ref = refs[1 + 4 * LAYERS]
    sbuf, rbuf, tbuf, ubuf, ibuf, jbuf, asend, arecv, bsend, brecv, isend, irecv = refs[2 + 4 * LAYERS :]
    x, c, y = (lax.axis_index(name) for name in ("x", "c", "y"))
    z = 2 * lax.axis_index("zh") + lax.axis_index("zl")
    mates = []
    for dz in range(4):
        for dy in range(2):
            mates.append(((z + dz) % 4, flip(y, dy)))
    groups = [(flip(x, dx), flip(c, dc)) for dx in range(2) for dc in range(2)]
    barrier = pltpu.get_barrier_semaphore()
    peers = [{"zh": a // 2, "zl": a % 2, "y": b} for a, b in mates[1:]]
    peers += [{"x": a, "c": b} for a, b in groups[1:]]
    for who in peers:
        pl.semaphore_signal(barrier, inc=1, device_id=who, device_id_type=pl.DeviceIdType.MESH)
    for layer in range(LAYERS):
        gd_in, gd_out, gu_in, gu_out = parts[4 * layer : 4 * layer + 4]
        pieces = [gd_in[p * R : (p + 1) * R, :] for p in range(3)] + [gd_out[:R, :]]
        pieces += [gu_in[p * R : (p + 1) * R, p * D : (p + 1) * D] for p in range(3)] + [gu_out[:R, :]]
        sbuf[:, layer * 128 : (layer + 1) * 128] = jnp.concatenate(pieces).T.astype(BF)
    ibuf[...] = jnp.broadcast_to(id_ref[0].astype(F32).astype(BF), (16, 128))

    def share(k):
        return sbuf.at[pl.ds(pl.multiple_of(k * SPAN, SPAN), SPAN), :]

    pl.semaphore_wait(barrier, len(peers))
    me = 2 * z + y
    copies = []
    for n, (a, b) in enumerate(mates):
        if n == 0:
            rbuf[0] = share(me)[...]
            jbuf[0] = ibuf[...]
            continue
        at = (4 - n // 2) % 4 * 2 + n % 2
        copy = pltpu.make_async_remote_copy(
            src_ref=ibuf,
            dst_ref=jbuf.at[at],
            send_sem=isend.at[n],
            recv_sem=irecv.at[at],
            device_id={"zh": a // 2, "zl": a % 2, "y": b},
            device_id_type=pl.DeviceIdType.MESH,
        )
        copy.start()
        copies.append(copy)
        copy = pltpu.make_async_remote_copy(
            src_ref=share(2 * a + b),
            dst_ref=rbuf.at[at],
            send_sem=asend.at[n],
            recv_sem=arecv.at[at],
            device_id={"zh": a // 2, "zl": a % 2, "y": b},
            device_id_type=pl.DeviceIdType.MESH,
        )
        copy.start()
        copies.append(copy)
    for copy in copies:
        copy.wait()
    masks = []
    for n in range(8):
        own = jbuf[n][0:1, 0:1].astype(F32)
        masks.append([(own == k).astype(F32) for k in range(NA)])

    def add(i, carry):
        at = pl.ds(pl.multiple_of(i * 16, 16), 16)
        sums = [jnp.zeros((16, UNIT), F32) for _ in range(NA)]
        for n in range(8):
            values = rbuf[n, at, :].astype(F32)
            for k in range(NA):
                sums[k] = sums[k] + values * masks[n][k]
        for k in range(NA):
            tbuf[k, at, :] = sums[k].astype(BF)
        return carry

    lax.fori_loop(0, SPAN // 16, add, 0)
    copies = []
    ubuf[0] = tbuf[pl.ds(2 * (2 * x + c), 2)]
    for n, (a, b) in enumerate(groups):
        if n == 0:
            continue
        copy = pltpu.make_async_remote_copy(
            src_ref=tbuf.at[pl.ds(2 * (2 * a + b), 2)],
            dst_ref=ubuf.at[n],
            send_sem=bsend.at[n],
            recv_sem=brecv.at[n],
            device_id={"x": a, "c": b},
            device_id_type=pl.DeviceIdType.MESH,
        )
        copy.start()
        copies.append(copy)
    for copy in copies:
        copy.wait()
    total = ubuf[0].astype(F32)
    for n in range(1, 4):
        total = total + ubuf[n].astype(F32)
    o_ref[...] = total


def adapters(own, parts):
    specs = [pl.BlockSpec(memory_space=pltpu.SMEM)]
    specs += [pl.BlockSpec(memory_space=pltpu.VMEM)] * len(parts)
    return pl.pallas_call(
        adapters_body,
        in_specs=specs,
        out_specs=pl.BlockSpec(memory_space=pltpu.VMEM),
        out_shape=jax.ShapeDtypeStruct((2, SPAN, UNIT), F32),
        scratch_shapes=[
            pltpu.VMEM((D, UNIT), BF),
            pltpu.VMEM((8, SPAN, UNIT), BF),
            pltpu.VMEM((NA, SPAN, UNIT), BF),
            pltpu.VMEM((4, 2, SPAN, UNIT), BF),
            pltpu.VMEM((16, 128), BF),
            pltpu.VMEM((8, 16, 128), BF),
            DMA((8,)),
            DMA((8,)),
            DMA((4,)),
            DMA((4,)),
            DMA((8,)),
            DMA((8,)),
        ],
        compiler_params=pltpu.CompilerParams(
            vmem_limit_bytes=VMEM_BYTES, collective_id=4, has_side_effects=True
        ),
        name="adapters",
    )(own, *parts)


def both_rows(mine, other):
    y = lax.axis_index("y")
    return jnp.where(y == 0, jnp.stack([mine, other]), jnp.stack([other, mine]))


def own_and_other(w):
    y = lax.axis_index("y")
    return [lax.dynamic_index_in_dim(w, e, axis=0, keepdims=False) for e in (y, 1 - y)]


def across_y(v):
    return lax.ppermute(v, "y", [(0, 1), (1, 0)])


def swapped(w):
    mine, other = own_and_other(w)
    return both_rows(mine, across_y(other))


def gathered(w, axes):
    return lax.all_gather(w, axes, axis=0, tiled=True).reshape(-1, w.shape[-1])


def exchange(v, kind):
    return lax.all_to_all(v, OWNERS[kind], split_axis=0, concat_axis=0, tiled=True)


def pad_to(v, shape):
    return jnp.pad(v, [(0, n - m) for m, n in zip(v.shape, shape)])


def adapters_plain(owners, parts):
    layers = []
    for gd_in, gd_out, gu_in, gu_out in parts:
        downs = [gd_in[p * R : (p + 1) * R] for p in range(3)] + [gd_out[:R]]
        ups = [gu_in[p * R : (p + 1) * R, p * D : (p + 1) * D] for p in range(3)] + [gu_out[:R]]
        layers.append(jnp.concatenate(downs + ups))
    compact = jnp.concatenate(layers).astype(BF)
    ranks = lax.axis_size(SHARD)
    pieces = compact.reshape(UNIT, ranks, D // ranks).transpose(1, 0, 2)
    pieces = lax.all_to_all(pieces, SHARD, split_axis=0, concat_axis=0, tiled=True)
    pick = (owners[None, :] == jnp.arange(NA, dtype=jnp.int32)[:, None]).astype(F32)
    summed = jnp.dot(pick, pieces.reshape(ranks, -1).astype(F32), precision=HIGHEST).astype(BF)
    groups = lax.axis_size(EXPERT)
    summed = lax.all_to_all(
        summed.reshape(groups, NA // groups, -1), EXPERT, split_axis=0, concat_axis=0, tiled=True
    )
    summed = jnp.sum(summed.astype(F32), axis=0)
    return summed.reshape(summed.shape[0], UNIT, -1).transpose(0, 2, 1)


def per_device(
    tokens,
    segments,
    parents,
    adapter_of,
    routes,
    norm_gain,
    query_key_value_weight,
    output_weight,
    adapter_down,
    adapter_up,
    router,
    router_residual,
    const_proj,
    const_vec,
    w_gate_up,
    w_down,
    out_grad,
):
    fast = w_gate_up.shape[1] == 2
    kind = PLANE if fast else WIDE_SLICE
    barrier = lax.optimization_barrier
    if fast:
        mine, other = own_and_other(w_gate_up[0])
        parts = [lax.all_gather(mine, ("zh", "zl"), axis=0)]
        down_mine, down_other = own_and_other(w_down[0])
        first, other, down_other = gather_shared(
            query_key_value_weight[0], output_weight[0], (other, down_other)
        )
        shared = [first]
        parts.append(lax.all_gather(other, ("zh", "zl"), axis=0))
        gate_up_full = [parts]
        down_full = [gathered(both_rows(down_mine, down_other), ("zh", "zl"))]
    else:
        shared = gather_shared(query_key_value_weight[0], output_weight[0])
        gate_up_full = [[gathered(w_gate_up[layer, 0], SHARD)] for layer in range(LAYERS)]
        down_full = [gathered(w_down[layer, 0], SHARD) for layer in range(LAYERS)]

    which = adapter_of[0]
    down_sel = lax.dynamic_index_in_dim(adapter_down, which, axis=2, keepdims=False)
    up_sel = lax.dynamic_index_in_dim(adapter_up, which, axis=2, keepdims=False)
    down_in = jnp.pad(
        down_sel[:, :3].transpose(0, 2, 1, 3).reshape(LAYERS, D, 3 * R), ((0, 0), (0, 0), (0, 80))
    )
    down_out = jnp.pad(down_sel[:, 3], ((0, 0), (0, 0), (0, 112)))
    up_t = 2.0 * up_sel.transpose(0, 1, 3, 2)
    up_in = jnp.zeros((LAYERS, 128, 3 * D), BF)
    for p in range(3):
        up_in = up_in.at[:, p * R : (p + 1) * R, p * D : (p + 1) * D].set(up_t[:, p])
    up_out = jnp.pad(up_t[:, 3], ((0, 0), (0, 112), (0, 0)))
    rcat = jnp.concatenate([router, const_proj[:, 0], const_proj[:, 1]], axis=2)
    rcat = jnp.pad(rcat, ((0, 0), (0, 0), (0, 112)))
    rcat_t = rcat[:, :, :16].transpose(0, 2, 1)
    residual = pad_to(router_residual, (16, 128))
    residual_t = pad_to(router_residual.T, (16, 128))

    qf, kf, cos, sin, tcol, trow, router_s, router_ts, residual_s, residual_ts = prep(
        parents, segments.reshape(T, 1), routes, rcat, rcat_t, residual, residual_t
    )

    stream = tokens
    earlier = jnp.zeros((T, 128), F32)
    saved = []
    for layer in range(LAYERS):
        gain0 = norm_gain[layer, 0:1]
        gain1 = norm_gain[layer, 1:2]
        normed, narrow, qkv = project(
            stream, gain0, shared[layer], down_in[layer], up_in[layer], cos, sin
        )
        mixed, aug = attend(qkv, qf, kf)
        mid, sent, logits, narrow_out = settle(
            stream, mixed, shared[layer], down_out[layer], up_out[layer], gain1, router_s[layer],
            earlier, residual_s,
        )
        buffer = dispatch(trow, sent)
        received = exchange(buffer, kind)
        if layer == 0:
            if fast:
                later = barrier((w_gate_up[1], w_down[1], logits))
                gate_up_next, down_next = barrier((swapped(later[0]), later[1]))
                gate_up_full.append([gathered(gate_up_next, ("zh", "zl"))])
                down_full.append(gathered(swapped(down_next), ("zh", "zl")))
            later = lax.optimization_barrier(
                (query_key_value_weight[1], output_weight[1], logits)
            )
            shared += gather_shared(later[0], later[1])
            returned, gate, up = expert_forward(received, gate_up_full[0], down_full[0], kind)
        else:
            slot_grads = exchange(dispatch_grad(trow, out_grad, logits, routes), kind)
            grad_mixed, following, grad_mid, grad_logits, gu_out, gd_out = expert_both(
                *expert_parts(received, gate_up_full[1][0], kind), slot_grads, gate_up_full[1][0], down_full[1], mid, out_grad, mixed,
                shared[1], tcol, logits, routes, gain1, const_vec[1], router_ts[1], residual_ts,
                narrow_out, down_out[1], up_out[1], kind,
            )
            c0 = c1 = None
        if layer == 0:
            following, c0, c1 = combine(
                tcol, returned.reshape(SLOTS, D), mid, logits, routes, gain1, const_vec[0]
            )
        saved.append((stream, normed, narrow, qkv, mixed, aug, mid, logits, narrow_out, c0, c1))
        stream = following
        earlier = logits

    grad = out_grad
    parts = [None] * LAYERS
    for layer in reversed(range(LAYERS)):
        x_in, normed, narrow, qkv, mixed, aug, mid, logits, narrow_out, c0, c1 = saved[layer]
        gain0 = norm_gain[layer, 0:1]
        gain1 = norm_gain[layer, 1:2]
        if layer == 0:
            grad_mid, grad_mixed, gu_out, gd_out = expert_backward(
                gate, up, gate_up_full[0], down_full[0], grad, mid, c0, c1, mixed, shared[0], trow,
                tcol, logits, routes, grad_logits, gain1, const_vec[0], router_ts[0], narrow_out,
                down_out[0], up_out[0], kind,
            )
        grad, gu_in, gd_in = layer_back(
            grad_mid, grad_mixed, mixed, shared[layer], qkv, aug, normed, x_in, gain0, narrow,
            down_in[layer], up_in[layer], kf, cos, sin,
        )
        parts[layer] = (gd_in, gd_out, gu_in, gu_out)

    if usual():
        final = adapters(adapter_of, [v for layer in parts for v in layer])
    else:
        final = adapters_plain(lax.all_gather(adapter_of, SHARD, axis=0, tiled=True), parts)
    final = final.reshape(*final.shape[:2], LAYERS, 2, 4, R).transpose(3, 2, 4, 0, 1, 5)
    return (stream, grad, final[0], final[1])


def solution(mesh):
    owners, shards = mesh.shape["expert"], mesh.shape["shard"]
    each = NFFN // owners
    fine = jax.sharding.Mesh(
        mesh.devices.reshape(owners // 2, 2, shards // each**2, each, each), AXES
    )
    expert, shard, both = EXPERT, SHARD, AXES
    in_specs = (
        P(both, None),
        P(both, None),
        P(both, None),
        P(both),
        P(both, None),
        P(),
        P(None, shard, None),
        P(None, shard, None),
        P(),
        P(),
        P(),
        P(),
        P(),
        P(),
        P(None, expert, shard, None),
        P(None, expert, shard, None),
        P(both, None),
    )
    out_specs = (
        P(both, None),
        P(both, None),
        P(None, None, expert, shard, None),
        P(None, None, expert, shard, None),
    )
    return jax.shard_map(
        per_device, mesh=fine, in_specs=in_specs, out_specs=out_specs, check_vma=False
    )
```

```python
import functools
import math

import jax
import jax.numpy as jnp
from jax import lax
from jax.experimental import pallas as pl
from jax.experimental.pallas import tpu as pltpu
from jax.sharding import PartitionSpec as P

D = 768
HEADS = 12
HD = 64
FF = 2048
NFFN = 8
NEXP = 12
R = 16
NA = 8
NSEG = 13
LAYERS = 2
CAP = 192
T = 1024
SLOTS = NFFN * CAP
RB = 256
NB = T // RB
PAIRS = HEADS // 2
FC = 512
EPSILON = 1e-06
BIG = 2.0**100
LOG_SCALE = math.log2(math.e) / math.sqrt(HD)
F32 = jnp.float32
BF = jnp.bfloat16
HIGHEST = lax.Precision.HIGHEST
VMEM_BYTES = 60 * 1024 * 1024


def mm(a, b):
    return lax.dot_general(a, b, (((1,), (0,)), ((), ())), preferred_element_type=F32)


def mm_nt(a, b):
    return lax.dot_general(a, b, (((1,), (1,)), ((), ())), preferred_element_type=F32)


def mm_tn(a, b):
    return lax.dot_general(a, b, (((0,), (0,)), ((), ())), preferred_element_type=F32)


def mm_exact(a, b):
    return lax.dot_general(
        a, b, (((1,), (0,)), ((), ())), preferred_element_type=F32, precision=HIGHEST
    )


def iota(shape, axis):
    return lax.broadcasted_iota(jnp.int32, shape, axis)


def sigmoid(v):
    return 1.0 / (1.0 + jnp.exp(-v))


def call(body, grid, ins, outs, scratch=(), name=None, flops=0, nbytes=0):
    def spec(entry):
        if entry[1] == "smem":
            return pl.BlockSpec(memory_space=pltpu.SMEM)
        if entry[1] is None:
            shape = entry[0].shape
            return pl.BlockSpec(shape, lambda *_: (0,) * len(shape))
        return pl.BlockSpec(entry[1], entry[2])

    return pl.pallas_call(
        body,
        grid=grid,
        in_specs=[spec(e) for e in ins],
        out_specs=[spec(e) for e in outs],
        out_shape=[jax.ShapeDtypeStruct(e[0].shape, e[0].dtype) for e in outs],
        scratch_shapes=list(scratch),
        compiler_params=pltpu.CompilerParams(
            dimension_semantics=("arbitrary",) * len(grid), vmem_limit_bytes=VMEM_BYTES
        ),
        cost_estimate=pl.CostEstimate(
            flops=int(flops), bytes_accessed=int(nbytes), transcendentals=0
        ),
        name=name,
    )(*[e[0] for e in ins])


def out(shape, dtype):
    return jax.ShapeDtypeStruct(shape, dtype)


def rows(i):
    return (i, 0)


def three(v):
    high = v.astype(BF)
    rest = v - high.astype(F32)
    middle = rest.astype(BF)
    return high, middle, (rest - middle.astype(F32)).astype(BF)


def spread_lanes(v):
    a, b, c = (part.astype(F32) for part in three(v))
    total = a + pltpu.roll(b, 16, 1) + pltpu.roll(c, 32, 1)
    total = total + pltpu.roll(a, 48, 1) + pltpu.roll(b, 64, 1) + pltpu.roll(a, 80, 1)
    return total.astype(BF)


def stack_rows(w):
    a, b, c = three(w)
    return jnp.concatenate([a, a, a, b, b, c, jnp.zeros((32, w.shape[1]), BF)], axis=0)


def prep_body(
    par_ref, seg_ref, rt_ref, rc_ref, rct_ref, res_ref, rest_ref,
    qf_ref, kf_ref, cos_ref, sin_ref, tcol_ref, trow_ref, rs_ref, rts_ref, ress_ref, rests_ref, anc,
):
    for layer in range(LAYERS):
        a, b, c = (part.astype(F32) for part in three(rc_ref[layer]))
        rs_ref[layer] = (a + pltpu.roll(b, 16, 1) + pltpu.roll(c, 32, 1)).astype(BF)
        rts_ref[layer] = stack_rows(rct_ref[layer])
    ress_ref[...] = stack_rows(res_ref[...])
    rests_ref[...] = stack_rows(rest_ref[...])
    first = iota((1, 128), 1) & 63
    anc[...] = jnp.zeros_like(anc)
    anc[0:1, :] = (first == 0).astype(F32)
    for s in range(1, NSEG):
        above = anc[pl.ds(par_ref[0, s], 1), :]
        anc[s : s + 1, :] = jnp.maximum(above, (first == s).astype(F32))
    lane = iota((T, 128), 1)
    lane6 = lane & 63
    low = lane < 64
    member = (seg_ref[...] == lane6).astype(F32)
    ways = mm(jnp.where(low, member, 0.0).astype(BF), anc[...].astype(BF))
    qf_ref[...] = jnp.where(lane6 < NSEG, (ways - 1.0) * BIG, 0.0).astype(BF)
    ones = ((lane6 >= 16) & (lane6 < 19)).astype(F32)
    kf_ref[...] = (member + ones).astype(BF)
    hit0 = (rt_ref[:, 0:1] == lane).astype(F32)
    hit1 = (rt_ref[:, 1:2] == lane).astype(F32)
    hits = hit0 + hit1
    upto = (iota((T, T), 0) >= iota((T, T), 1)).astype(F32).astype(BF)
    seen = mm(upto, jnp.concatenate([member.astype(BF), hits.astype(BF)], axis=1))
    depth = jnp.sum(jnp.where(low, ways * seen[:, :128], 0.0), axis=1, keepdims=True) - 1.0
    before = seen[:, 128:] - hits

    def target(hit, route):
        slot = jnp.sum(hit * before, axis=1, keepdims=True)
        place = route.astype(F32) * CAP + slot
        return jnp.where(route < NFFN, place, 4.0 * SLOTS)

    t0 = target(hit0, rt_ref[:, 0:1])
    t1 = target(hit1, rt_ref[:, 1:2])
    both = jnp.where(lane == 0, t0, jnp.where(lane == 1, t1, 0.0))
    tcol_ref[...] = both.astype(jnp.int32)
    trow_ref[...] = both.T[0:8, :].astype(jnp.int32)
    inverse = jnp.exp((lane & 31).astype(F32) * (-math.log(10000.0) / 32.0))
    angle = depth * inverse
    cos_ref[...] = jnp.cos(angle)
    sine = jnp.sin(angle)
    sin_ref[...] = jnp.where((lane & 32) == 0, -sine, sine)


def prep(parents, seg_col, routes, rcat, rcat_t, residual, residual_t):
    return call(
        prep_body,
        (1,),
        [
            (parents, "smem"),
            (seg_col, None),
            (routes, None),
            (rcat, None),
            (rcat_t, None),
            (residual, None),
            (residual_t, None),
        ],
        [
            (out((T, 128), BF), None),
            (out((T, 128), BF), None),
            (out((T, 128), F32), None),
            (out((T, 128), F32), None),
            (out((T, 128), jnp.int32), None),
            (out((8, T), jnp.int32), None),
            (out((LAYERS, D, 128), BF), None),
            (out((LAYERS, 128, D), BF), None),
            (out((128, 128), BF), None),
            (out((128, 128), BF), None),
        ],
        [pltpu.VMEM((128, 128), F32)],
        name="prep",
        flops=2 * T * T * 256,
        nbytes=3e6,
    )


def turn(v, cos, sin):
    first = (iota(v.shape, 1) & 32) == 0
    other = jnp.where(first, pltpu.roll(v, 96, 1), pltpu.roll(v, 32, 1))
    return v * cos + other * sin


def project_rows(x, gain, w_ref, d_ref, u_ref, cos, sin, n_ref, nar_ref, qkv_ref):
    scale = lax.rsqrt(jnp.mean(x * x, axis=1, keepdims=True) + EPSILON)
    normed = (x * scale * gain).astype(BF)
    n_ref[...] = normed
    narrow = mm(normed, d_ref[...]).astype(BF)
    nar_ref[...] = narrow
    for block in range(3):
        cols = slice(block * D, (block + 1) * D)
        part = mm(normed, w_ref[block]) + mm(narrow, u_ref[:, cols])
        for j in range(PAIRS):
            piece = part[:, j * 128 : (j + 1) * 128]
            if block < 2:
                piece = turn(piece, cos, sin)
            at = block * D + j * 128
            qkv_ref[:, at : at + 128] = piece.astype(BF)


def project_body(x_ref, g_ref, w_ref, d_ref, u_ref, cos_ref, sin_ref, n_ref, nar_ref, qkv_ref):
    project_rows(
        x_ref[...].astype(F32),
        g_ref[...],
        w_ref,
        d_ref,
        u_ref,
        cos_ref[...],
        sin_ref[...],
        n_ref,
        nar_ref,
        qkv_ref,
    )


def project(x, gain, w, down, up, cos, sin):
    return call(
        project_body,
        (NB,),
        [
            (x, (RB, D), rows),
            (gain, None),
            (w, (3, D, D), lambda i: (0, 0, 0)),
            (down, None),
            (up, None),
            (cos, (RB, 128), rows),
            (sin, (RB, 128), rows),
        ],
        [
            (out((T, D), BF), (RB, D), rows),
            (out((T, 128), BF), (RB, 128), rows),
            (out((T, 3 * D), BF), (RB, 3 * D), rows),
        ],
        name="project",
        flops=2 * T * D * 3 * D,
        nbytes=12e6,
    )


def attend_body(q_ref, k_ref, v_ref, qf_ref, kf_ref, mixed_ref, aug_ref):
    low = iota((T, 128), 1) < 64
    k = k_ref[...]
    kf = kf_ref[...]
    v = v_ref[...]
    one = jnp.ones((T, 128), BF)
    keys = (jnp.where(low, k, kf), jnp.where(low, kf, k))
    values = (jnp.where(low, v, one), jnp.where(low, one, v))
    low = low[:RB]
    tri = iota((RB, RB), 0) >= iota((RB, RB), 1)
    lane6 = iota((RB, 128), 1) & 63
    for i in range(NB):
        here = slice(i * RB, (i + 1) * RB)
        q = q_ref[here, :]
        qf = qf_ref[here, :]
        tops = []
        outs = []
        for h in range(2):
            qa = jnp.where(low, q, qf) if h == 0 else jnp.where(low, qf, q)
            diag = jnp.where(tri, mm_nt(qa, keys[h][here]), -BIG)
            top = jnp.max(diag, axis=1, keepdims=True)
            if i:
                off = mm_nt(qa, keys[h][: i * RB])
                top = jnp.maximum(top, jnp.max(off, axis=1, keepdims=True))
            result = mm(jnp.exp2((diag - top) * LOG_SCALE).astype(BF), values[h][here])
            if i:
                weights = jnp.exp2((off - top) * LOG_SCALE).astype(BF)
                result = result + mm(weights, values[h][: i * RB])
            tops.append(top)
            outs.append(result)
        total = jnp.where(low, outs[1], outs[0])
        mixed = jnp.where(low, outs[0], outs[1]) / pltpu.roll(total, 64, 1)
        mixed_ref[here, :] = mixed.astype(BF)
        level = -(jnp.where(low, tops[1], tops[0]) + math.sqrt(HD) * jnp.log(total))
        a, b, c = three(level)
        aug_ref[0, here, :] = jnp.where(
            lane6 == 16, a, jnp.where(lane6 == 17, b, jnp.where(lane6 == 18, c, qf))
        )


def attend(qkv, qf, kf):
    return call(
        attend_body,
        (PAIRS,),
        [
            (qkv, (T, 128), lambda j: (0, j)),
            (qkv, (T, 128), lambda j: (0, PAIRS + j)),
            (qkv, (T, 128), lambda j: (0, 2 * PAIRS + j)),
            (qf, None),
            (kf, None),
        ],
        [
            (out((T, D), BF), (T, 128), lambda j: (0, j)),
            (out((PAIRS, T, 128), BF), (1, T, 128), lambda j: (j, 0, 0)),
        ],
        name="attend",
        flops=12 * 4 * T * T * 128,
        nbytes=8e6,
    )


def settle_body(
    x_ref, mixed_ref, w_ref, d_ref, u_ref, g_ref, rt_ref, earlier_ref, res_ref,
    mid_ref, sent_ref, lg_ref, nar_ref,
):
    mixed = mixed_ref[...]
    narrow = mm(mixed, d_ref[...]).astype(BF)
    nar_ref[...] = narrow
    mid = x_ref[...].astype(F32) + mm(mixed, w_ref[0]) + mm(narrow, u_ref[...])
    mid_ref[...] = mid
    scale = lax.rsqrt(jnp.mean(mid * mid, axis=1, keepdims=True) + EPSILON)
    normed = mid * scale * g_ref[...]
    sent_ref[...] = normed.astype(BF)
    a, b, c = three(normed)
    one, two, last = mm(a, rt_ref[...]), mm(b, rt_ref[...]), mm(c, rt_ref[...])
    total = one + two + last + pltpu.roll(one + two, 112, 1) + pltpu.roll(one, 96, 1)
    lane = iota((RB, 128), 1)
    earlier = jnp.where(lane < NEXP, earlier_ref[...], 0.0)
    extra = mm(spread_lanes(earlier), res_ref[...])
    lg_ref[...] = jnp.where(lane < 16, total + extra, 0.0)


def settle(x, mixed, w, down, up, gain, router, earlier, residual):
    return call(
        settle_body,
        (NB,),
        [
            (x, (RB, D), rows),
            (mixed, (RB, D), rows),
            (w, (1, D, D), lambda i: (3, 0, 0)),
            (down, None),
            (up, None),
            (gain, None),
            (router, None),
            (earlier, (RB, 128), rows),
            (residual, None),
        ],
        [
            (out((T, D), F32), (RB, D), rows),
            (out((T, D), BF), (RB, D), rows),
            (out((T, 128), F32), (RB, 128), rows),
            (out((T, 128), BF), (RB, 128), rows),
        ],
        name="settle",
        flops=2 * T * D * D * 2,
        nbytes=10e6,
    )


def dispatch_body(trow_ref, s_ref, o_ref):
    place = pl.program_id(0) * CAP + iota((CAP, T), 0)
    hit = (trow_ref[0:1, :] == place) | (trow_ref[1:2, :] == place)
    o_ref[0] = mm(hit.astype(F32).astype(BF), s_ref[...]).astype(BF)


def dispatch(trow, sent):
    return call(
        dispatch_body,
        (NFFN,),
        [(trow, None), (sent, None)],
        [(out((NFFN, CAP, D), BF), (1, CAP, D), lambda j: (j, 0, 0))],
        name="dispatch",
        flops=2 * T * SLOTS * D,
        nbytes=4e6,
    )[0]


def dispatch_grad_body(trow_ref, g_ref, lg_ref, rt_ref, o_ref, first, second):
    @pl.when(pl.program_id(0) == 0)
    def _():
        for i in range(NB):
            at = slice(i * RB, (i + 1) * RB)
            gates = mix_terms(lg_ref[at, :], rt_ref[at, :])[0]
            g = g_ref[at, :].astype(F32)
            first[at, :] = (gates[0] * g).astype(BF)
            second[at, :] = (gates[1] * g).astype(BF)

    place = pl.program_id(0) * CAP + iota((CAP, T), 0)
    hit0 = (trow_ref[0:1, :] == place).astype(F32).astype(BF)
    hit1 = (trow_ref[1:2, :] == place).astype(F32).astype(BF)
    o_ref[0] = (mm(hit0, first[...]) + mm(hit1, second[...])).astype(BF)


def dispatch_grad(trow, g, logits, routes):
    return call(
        dispatch_grad_body,
        (NFFN,),
        [(trow, None), (g, None), (logits, None), (routes, None)],
        [(out((NFFN, CAP, D), BF), (1, CAP, D), lambda j: (j, 0, 0))],
        [pltpu.VMEM((T, D), BF), pltpu.VMEM((T, D), BF)],
        name="dispatch_grad",
        flops=4 * T * SLOTS * D,
        nbytes=6e6,
    )[0]


PR = 2 * CAP
NP = NFFN // 2


def split_refs(refs, *counts):
    parts = []
    for count in counts:
        parts.append(refs[:count])
        refs = refs[count:]
    return *parts, refs


def flip(bit, change):
    return bit + change - 2 * bit * change


PLANE, WIDE_SLICE = 0, 1
OWNERS = (("x", "c", "y"), ("x", "c"))


def owner_at(p, h, kind):
    x = lax.axis_index("x")
    far, near, core = ((1, 1, h), (1 - h, h, 0), (1 - h, h, 1), (0, 0, h))[p]
    if kind == WIDE_SLICE:
        x = 2 * flip(x // 2, far) + flip(x % 2, near)
        c = flip(lax.axis_index("c"), core)
        return {"x": x, "c": c}, x * 2 + c
    x, c, y = flip(x, far), flip(lax.axis_index("c"), core), flip(lax.axis_index("y"), near)
    return {"x": x, "c": c, "y": y}, (x * 2 + c) * 2 + y


PLACES = [(p, h) for p in range(NP) for h in range(2)]


def greet(kind):
    barrier = pltpu.get_barrier_semaphore()
    for p, h in PLACES[:-2] + PLACES[-1:]:
        pl.semaphore_signal(
            barrier, inc=1, device_id=owner_at(p, h, kind)[0], device_id_type=pl.DeviceIdType.MESH
        )
    pl.semaphore_wait(barrier, NFFN - 1)


def block_of(ref, p, h):
    return ref.at[p, h * CAP : (h + 1) * CAP, :]


def fetch_weights(split, gate_ups, down_ref, w1, w2, sems):
    copies = []
    if split:
        y = lax.axis_index("y")
        for side, ref in enumerate(gate_ups):
            mine = flip(y, side)
            count, size = ref.shape[0], ref.shape[1]
            for k in range(count):
                at = pl.multiple_of((2 * k + mine) * size, size)
                copies.append(
                    pltpu.make_async_copy(
                        ref.at[k], w1.at[pl.ds(at, size), :], sems.at[side * count + k]
                    )
                )
    else:
        copies.append(pltpu.make_async_copy(gate_ups[0], w1, sems.at[0]))
    copies.append(pltpu.make_async_copy(down_ref, w2, sems.at[8]))
    for copy in copies:
        copy.start()
    return copies


def fetch_blocks(source, rv, sems, kind):
    copies = []
    for n, (p, h) in enumerate(PLACES):
        number = owner_at(p, h, kind)[1]
        copies.append(pltpu.make_async_copy(source.at[number], block_of(rv, p, h), sems.at[n]))
    for copy in copies:
        copy.start()
    return copies


def give_back(pv, p, target, send, recv, kind):
    me = owner_at(NP - 1, 0, kind)[1]
    copies = []
    for h in range(2):
        n = 2 * p + h
        if (p, h) == (NP - 1, 0):
            copy = pltpu.make_async_copy(block_of(pv, p, h), target.at[me], send.at[n])
        else:
            copy = pltpu.make_async_remote_copy(
                src_ref=block_of(pv, p, h),
                dst_ref=target.at[me],
                send_sem=send.at[n],
                recv_sem=recv.at[n],
                device_id=owner_at(p, h, kind)[0],
                device_id_type=pl.DeviceIdType.MESH,
            )
        copy.start()
        copies.append(copy)
    return copies


def chunk_at(f):
    return pl.multiple_of(f * FC, FC)


def forward_chunk(r, w1, w2, f):
    at = chunk_at(f)
    gate = mm(r, w1[:, pl.ds(at, FC)])
    up = mm(r, w1[:, pl.ds(pl.multiple_of(FF + f * FC, FC), FC)])
    active = (gate * sigmoid(gate) * up).astype(BF)
    return gate, up, mm(active, w2[pl.ds(at, FC), :])


def backward_chunk(g, gate, up, w1, w2, f):
    at = chunk_at(f)
    grad = mm_nt(g, w2[pl.ds(at, FC), :])
    s = sigmoid(gate)
    grad_s = grad * s
    grad_gate = (grad_s * up * (1.0 + gate * (1.0 - s))).astype(BF)
    grad_up = (grad_s * gate).astype(BF)
    return mm_nt(grad_gate, w1[:, pl.ds(at, FC)]) + mm_nt(
        grad_up, w1[:, pl.ds(pl.multiple_of(FF + f * FC, FC), FC)]
    )


def expert_body(split, kind, *refs):
    count = 2 if split else 1
    gate_ups = refs[:count]
    down_ref, rec_ref, ret_ref, gate_ref, up_ref = refs[count : count + 5]
    w1, w2, rv, pv, gv, uv, acc, wsem, rsem, gsem, usem, send, recv = refs[count + 5 :]
    weights = fetch_weights(split, gate_ups, down_ref, w1, w2, wsem)
    blocks = fetch_blocks(rec_ref, rv, rsem, kind)
    greet(kind)
    for copy in weights + blocks:
        copy.wait()
    stores = []
    moves = []
    for p in range(NP):
        r = rv[p]
        acc[...] = jnp.zeros_like(acc)

        def step(f, carry):
            gate, up, part = forward_chunk(r, w1, w2, f)
            gv[p, :, pl.ds(chunk_at(f), FC)] = gate.astype(BF)
            uv[p, :, pl.ds(chunk_at(f), FC)] = up.astype(BF)
            acc[...] += part
            return carry

        lax.fori_loop(0, FF // FC, step, 0)
        pv[p] = acc[...].astype(BF)
        moves += give_back(pv, p, ret_ref, send, recv, kind)
        for values, ref, sems in ((gv, gate_ref, gsem), (uv, up_ref, usem)):
            copy = pltpu.make_async_copy(values.at[p], ref.at[p], sems.at[p])
            copy.start()
            stores.append(copy)
    for copy in moves + stores:
        copy.wait()


def own_copies(body, ins, near, outs, near_outs, scratch):
    counts = len(ins), len(near), len(outs), len(near_outs), len(scratch)

    def run(*refs):
        far, near_far, targets, near_targets, inner, close = split_refs(refs, *counts)
        close, near_close, sems = split_refs(close, len(near), len(near_outs))
        loads = [
            pltpu.make_async_copy(source, target, sems[0].at[n])
            for n, (source, target) in enumerate(zip(near_far, close))
        ]
        for copy in loads:
            copy.start()

        def ready():
            for copy in loads:
                copy.wait()

        def done(n):
            copy = pltpu.make_async_copy(near_close[n], near_targets[n], sems[1].at[n])
            copy.start()
            return copy

        body(far, close, targets, near_close, inner, ready, done)

    extra = [pltpu.VMEM(v.shape, v.dtype) for v in (*near, *near_outs)]
    extra += [DMA((max(1, len(near)),)), DMA((max(1, len(near_outs)),))]
    return run, [*ins, *near], [*outs, *near_outs], [*scratch, *extra]


def comm_call(body, ins, outs, scratch, name, number, flops, nbytes, near=(), near_outs=()):
    run, ins, outs, scratch = own_copies(body, ins, near, outs, near_outs, scratch)
    far = {} if number is None else dict(collective_id=number, has_side_effects=True)
    return pl.pallas_call(
        run,
        in_specs=[pl.BlockSpec(memory_space=pl.ANY)] * len(ins),
        out_specs=[pl.BlockSpec(memory_space=pl.ANY)] * len(outs),
        out_shape=outs,
        scratch_shapes=scratch,
        compiler_params=pltpu.CompilerParams(vmem_limit_bytes=VMEM_BYTES, **far),
        cost_estimate=pl.CostEstimate(
            flops=int(flops), bytes_accessed=int(nbytes), transcendentals=0
        ),
        name=name,
    )(*ins)


DMA = pltpu.SemaphoreType.DMA
WEIGHTS = [pltpu.VMEM((D, 2 * FF), BF), pltpu.VMEM((FF, D), BF)]
ROWS = pltpu.VMEM((NP, PR, D), BF)
WIDE = pltpu.VMEM((NP, PR, FF), BF)
SUM = pltpu.VMEM((PR, D), F32)
BLOCKS = jax.ShapeDtypeStruct((NFFN, CAP, D), BF)
KEPT = jax.ShapeDtypeStruct((NP, PR, FF), BF)


def expert_forward(received, gate_ups, down, kind):
    split = len(gate_ups) == 2

    def body(far, near, outs, near_outs, scratch, ready, done):
        expert_body(split, kind, *far, *outs, *scratch)

    return comm_call(
        body,
        [*gate_ups, down, received],
        [BLOCKS, KEPT, KEPT],
        WEIGHTS + [ROWS, ROWS, WIDE, WIDE, SUM]
        + [DMA((9,)), DMA((8,)), DMA((NP,)), DMA((NP,)), DMA((8,)), DMA((8,))],
        "expert_forward",
        1,
        2 * SLOTS * D * FF * 3,
        26e6,
    )


def expert_parts_body(kind, far, outs, scratch):
    gate_up_ref, rec_ref = far
    w1, rv, wsem, rsem, osem, *kept = scratch
    load = pltpu.make_async_copy(gate_up_ref, w1, wsem.at[0])
    load.start()
    for copy in fetch_blocks(rec_ref, rv, rsem, kind) + [load]:
        copy.wait()
    stores = []
    for p in range(NP):
        r = rv[p]

        def step(f, carry):
            at = pl.ds(chunk_at(f), FC)
            gate = mm(r, w1[:, at])
            up = mm(r, w1[:, pl.ds(pl.multiple_of(FF + f * FC, FC), FC)])
            s = sigmoid(gate)
            silu = gate * s
            kept[0][p, :, at] = (silu * up).astype(BF)
            kept[1][p, :, at] = (up * s * (1.0 + gate * (1.0 - s))).astype(BF)
            kept[2][p, :, at] = silu.astype(BF)
            return carry

        lax.fori_loop(0, FF // FC, step, 0)
        for n in range(3):
            stores.append(pltpu.make_async_copy(kept[n].at[p], outs[n].at[p], osem.at[p, n]))
            stores[-1].start()
    for copy in stores:
        copy.wait()


def expert_parts(received, gate_up, kind):
    def body(far, near, outs, near_outs, scratch, ready, done):
        expert_parts_body(kind, far, outs, scratch)

    return comm_call(
        body,
        [gate_up, received],
        [KEPT, KEPT, KEPT],
        [WEIGHTS[0], ROWS, DMA((1,)), DMA((8,)), DMA((NP, 3)), WIDE, WIDE, WIDE],
        "expert_parts",
        None,
        2 * SLOTS * D * FF * 2,
        28e6,
    )


def expert_both_body(kind, far, near, mix_out, out_near, scratch, ready, done):
    (
        gate_up_ref, down_ref, active_ref, to_gate_ref, to_up_ref, sg_ref, mid_ref, g_ref,
        mixed_ref, shared_ref,
    ) = far
    tcol_ref, lg_ref, rt_ref, gain_ref, cv_ref, wt_ref, res_ref, nar_ref, d_ref, u_ref = near
    out_ref, gm_ref, gle_ref, gu_ref, gd_ref = out_near
    (
        w1, w2, qv, sv, pv, to_gate, to_up, av, back, gback, mid, g, mixed, w3, acc,
        wsem, asem, ssem, msem, send, recv, gsend, grecv,
    ) = scratch

    def start(source, target, sem):
        copy = pltpu.make_async_copy(source, target, sem)
        copy.start()
        return copy

    load = start(down_ref, w2, wsem.at[0])
    actives = [start(active_ref.at[p], av.at[p], asem.at[p]) for p in range(2)]
    greet(kind)
    load.wait()
    moves = []
    extra = []
    for p in range(NP):
        actives[p].wait()
        pv[p] = mm(av[p % 2], w2[...]).astype(BF)
        moves += give_back(pv, p, back, send, recv, kind)
        if p + 2 < NP:
            actives.append(start(active_ref.at[p + 2], av.at[p % 2], asem.at[p + 2]))
        if p == 0:
            extra = fetch_blocks(sg_ref, sv, ssem, kind)
            extra.append(start(gate_up_ref, w1, wsem.at[1]))
            for n, (source, target) in enumerate(
                (
                    (to_gate_ref, to_gate), (to_up_ref, to_up), (mid_ref, mid), (g_ref, g),
                    (mixed_ref, mixed), (shared_ref.at[3], w3),
                )
            ):
                extra.append(start(source, target, msem.at[n]))
    for copy in extra:
        copy.wait()
    later = []
    for p in range(NP):
        grads = sv[p]
        acc[...] = jnp.zeros_like(acc)

        def step(f, carry):
            at = pl.ds(chunk_at(f), FC)
            grad = mm_nt(grads, w2[at, :])
            first = (grad * to_gate[p, :, at].astype(F32)).astype(BF)
            second = (grad * to_up[p, :, at].astype(F32)).astype(BF)
            acc[...] += mm_nt(first, w1[:, at]) + mm_nt(
                second, w1[:, pl.ds(pl.multiple_of(FF + f * FC, FC), FC)]
            )
            return carry

        lax.fori_loop(0, FF // FC, step, 0)
        qv[p] = acc[...].astype(BF)
        later += give_back(qv, p, gback, gsend, grecv, kind)
    for copy in moves:
        copy.wait()
    ready()

    def finish(i, carry):
        at = pl.ds(pl.multiple_of(i * RB, RB), RB)
        logits, routes, middle = lg_ref[at, :], rt_ref[at, :], mid[at, :]
        following, chosen = combine_rows(
            tcol_ref[at, :], back, middle, logits, routes, gain_ref[...], cv_ref
        )
        out_ref[at, :] = following
        gm_ref[at, :], gle_ref[at, :] = mix_grad(
            g[at, :].astype(F32), middle, chosen, logits, routes, 0.0, gain_ref[...], cv_ref,
            wt_ref[...], res_ref[...],
        )
        return carry

    lax.fori_loop(0, NB, finish, 0)
    stores = [done(0), done(2)]
    gu_ref[...] = jnp.zeros_like(gu_ref)
    gd_ref[...] = jnp.zeros_like(gd_ref)
    for p in range(NP):
        for copy in later[2 * p : 2 * p + 2]:
            copy.wait()
        collect(p, kind, tcol_ref, gm_ref, gback)

    def settle_one(i, carry):
        at = pl.ds(pl.multiple_of(i * RB, RB), RB)
        refs = (mid, g, mixed, gain_ref, nar_ref, w3, d_ref, u_ref, gu_ref, gd_ref)
        settle_back(refs, at, gm_ref, mixed)
        return carry

    lax.fori_loop(0, NB, settle_one, 0)
    stores.append(start(mixed, mix_out, msem.at[6]))
    for copy in stores + [done(n) for n in (1, 3, 4)]:
        copy.wait()


def expert_both(
    active, to_gate, to_up, slot_grads, gate_up, down, mid, g, mixed, weights, tcol, logits, routes, gain,
    const_vec, router_t, residual_t, narrow, down_out, up_out, kind,
):
    def body(far, near, outs, near_outs, scratch, ready, done):
        expert_both_body(kind, far, near, outs[0], near_outs, scratch, ready, done)

    half = pltpu.VMEM((T, D), BF)
    landing = pltpu.VMEM((NFFN, CAP, D), BF)
    return comm_call(
        body,
        [gate_up, down, active, to_gate, to_up, slot_grads, mid, g, mixed, weights],
        [out((T, D), BF)],
        WEIGHTS
        + [ROWS, ROWS, ROWS, WIDE, WIDE, pltpu.VMEM((2, PR, FF), BF), landing, landing]
        + [pltpu.VMEM((T, D), F32), pltpu.VMEM((T, D), g.dtype), half, pltpu.VMEM((D, D), BF), SUM]
        + [DMA((2,)), DMA((NP,)), DMA((8,)), DMA((7,))]
        + [DMA((8,)), DMA((8,)), DMA((8,)), DMA((8,))],
        "expert_both",
        2,
        2 * SLOTS * D * FF * 4,
        40e6,
        [tcol, logits, routes, gain, const_vec, router_t, residual_t, narrow, down_out, up_out],
        [out((T, D), F32), out((T, D), F32), out((T, 128), F32)]
        + [out((128, D), F32), out((128, D), F32)],
    )


def expert_back_body(split, kind, far, near, out_near, outs, scratch, ready, done):
    count = 2 if split else 1
    gate_ups, (down_ref, gate_ref, up_ref, g_ref, mid_ref, c0_ref, c1_ref, mixed_ref, shared_ref) = (
        far[:count], far[count:]
    )
    (
        trow_ref, tcol_ref, lg_ref, rt_ref, gl_ref, gain_ref, cv_ref, wt_ref, nar_ref, d_ref, u_ref
    ) = near
    gm_ref, gu_ref, gd_ref = out_near
    mix_out = outs[0]
    (
        w1, w2, sgv, rv, pv, gv, uv, back, first, second, g, mid, c0, c1, mixed, w3, acc,
        wsem, gsem, usem, msem, dsend, drecv, send, recv, osem,
    ) = scratch
    extra = [
        pltpu.make_async_copy(ref, values, msem.at[n])
        for n, (ref, values) in enumerate(
            (
                (g_ref, g), (mid_ref, mid), (c0_ref, c0), (c1_ref, c1), (mixed_ref, mixed),
                (shared_ref.at[3], w3),
            )
        )
    ]
    extra[0].start()
    extra[0].wait()
    ready()

    def gated(i, carry):
        at = pl.ds(pl.multiple_of(i * RB, RB), RB)
        gates = mix_terms(lg_ref[at, :], rt_ref[at, :])[0]
        first[at, :] = (gates[0] * g[at, :]).astype(BF)
        second[at, :] = (gates[1] * g[at, :]).astype(BF)
        return carry

    lax.fori_loop(0, NB, gated, 0)
    weights = fetch_weights(split, gate_ups, down_ref, w1, w2, wsem)
    for p in (3, 0, 1, 2):
        for values, ref, sems in ((gv, gate_ref, gsem), (uv, up_ref, usem)):
            copy = pltpu.make_async_copy(ref.at[p], values.at[p], sems.at[p])
            copy.start()
            weights.append(copy)
    for copy in extra[1:]:
        copy.start()
    greet(kind)
    arrivals = {}
    for p, h in PLACES[:-2] + [(3, 1), (3, 0)]:
        where, number = owner_at(p, h, kind)
        place = number * CAP + iota((CAP, T), 0)
        hit0 = (trow_ref[0:1, :] == place).astype(F32).astype(BF)
        hit1 = (trow_ref[1:2, :] == place).astype(F32).astype(BF)
        values = (mm(hit0, first[...]) + mm(hit1, second[...])).astype(BF)
        n = 2 * p + h
        if (p, h) == (NP - 1, 0):
            rv[p, h * CAP : (h + 1) * CAP, :] = values
            continue
        sgv[p, h * CAP : (h + 1) * CAP, :] = values
        copy = pltpu.make_async_remote_copy(
            src_ref=block_of(sgv, p, h),
            dst_ref=block_of(rv, p, h),
            send_sem=dsend.at[n],
            recv_sem=drecv.at[n],
            device_id=where,
            device_id_type=pl.DeviceIdType.MESH,
        )
        copy.start()
        arrivals[p, h] = copy
    for copy in weights + extra[1:]:
        copy.wait()
    moves = []

    for p in (3, 0, 1, 2):
        for h in range(2):
            if (p, h) in arrivals:
                arrivals[p, h].wait()
        grads = rv[p]
        acc[...] = jnp.zeros_like(acc)

        def step(f, carry):
            at = pl.ds(chunk_at(f), FC)
            gate = gv[p, :, at].astype(F32)
            up = uv[p, :, at].astype(F32)
            acc[...] += backward_chunk(grads, gate, up, w1, w2, f)
            return carry

        lax.fori_loop(0, FF // FC, step, 0)
        pv[p] = acc[...].astype(BF)
        moves += give_back(pv, p, back, send, recv, kind)

    def tidy(i, carry):
        at = pl.ds(pl.multiple_of(i * RB, RB), RB)
        gm_ref[at, :] = mix_grad(
            g[at, :], mid[at, :], (c0[at, :], c1[at, :]), lg_ref[at, :], rt_ref[at, :],
            gl_ref[at, :], gain_ref[...], cv_ref, wt_ref[...], None,
        )[0]
        return carry

    lax.fori_loop(0, NB, tidy, 0)
    gu_ref[...] = jnp.zeros_like(gu_ref)
    gd_ref[...] = jnp.zeros_like(gd_ref)
    for n, p in enumerate((3, 0, 1, 2)):
        for copy in moves[2 * n : 2 * n + 2]:
            copy.wait()
        collect(p, kind, tcol_ref, gm_ref, back)

    def settle_one(i, carry):
        at = pl.ds(pl.multiple_of(i * RB, RB), RB)
        refs = (mid, g, mixed, gain_ref, nar_ref, w3, d_ref, u_ref, gu_ref, gd_ref)
        settle_back(refs, at, gm_ref, first)
        return carry

    lax.fori_loop(0, NB, settle_one, 0)
    last = pltpu.make_async_copy(first, mix_out, osem.at[0])
    last.start()
    for copy in [last] + [done(n) for n in range(3)]:
        copy.wait()


def expert_backward(
    gate, up, gate_ups, down, g, mid, c0, c1, mixed, weights, trow, tcol, logits, routes, gl, gain,
    const_vec, router_t, narrow, down_out, up_out, kind,
):
    split = len(gate_ups) == 2

    def body(far, near, outs, near_outs, scratch, ready, done):
        expert_back_body(split, kind, far, near, near_outs, outs, scratch, ready, done)

    half, full = pltpu.VMEM((T, D), BF), pltpu.VMEM((T, D), F32)
    mix, gm, gu, gd = comm_call(
        body,
        [*gate_ups, down, gate, up, g, mid, c0, c1, mixed, weights],
        [out((T, D), BF)],
        WEIGHTS
        + [ROWS, ROWS, ROWS, WIDE, WIDE, pltpu.VMEM((NFFN, CAP, D), BF)]
        + [half, half, full, full, half, half, half, pltpu.VMEM((D, D), BF), SUM]
        + [DMA((9,)), DMA((NP,)), DMA((NP,)), DMA((6,))]
        + [DMA((8,)), DMA((8,)), DMA((8,)), DMA((8,)), DMA((1,))],
        "expert_backward",
        3,
        2 * SLOTS * D * FF * 3,
        26e6,
        [
            trow, tcol, logits, routes, gl, gain, const_vec, router_t, narrow, down_out, up_out,
        ],
        [out((T, D), F32), out((128, D), F32), out((128, D), F32)],
    )
    return gm, mix, gu, gd


def mix_terms(logits, routes):
    lane = iota(logits.shape, 1)

    def at(place):
        return jnp.sum(jnp.where(lane == place, logits, 0.0), axis=1, keepdims=True)

    r0, r1 = routes[:, 0:1], routes[:, 1:2]
    gap = at(r0) - at(r1)
    gates = (sigmoid(gap), sigmoid(-gap))

    def weight(e):
        return jnp.where(r0 == e, gates[0], 0.0) + jnp.where(r1 == e, gates[1], 0.0)

    shares = []
    for c in range(2):
        apart = logits[:, 12 + 2 * c : 13 + 2 * c] - logits[:, 13 + 2 * c : 14 + 2 * c]
        shares.append((sigmoid(apart), sigmoid(-apart)))
    weights = [weight(NFFN + 1), weight(NFFN + 2), weight(NFFN + 3)]
    return gates, weights, shares


def rms_scale(v):
    return lax.rsqrt(jnp.mean(v * v, axis=1, keepdims=True) + EPSILON)


def combine_rows(tcol, back_ref, mid, logits, routes, gain, cv_ref):
    place = iota((RB, SLOTS), 1)
    back = back_ref[...].reshape(SLOTS, D)
    chosen = []
    for k in range(2):
        hit = (tcol[:, k : k + 1] == place).astype(F32).astype(BF)
        chosen.append(mm(hit, back))
    normed = mid * rms_scale(mid) * gain
    gates, weights, shares = mix_terms(logits, routes)
    same = weights[0] + weights[1] * shares[0][0] + weights[2] * shares[1][0]
    moe = gates[0] * chosen[0] + gates[1] * chosen[1] + same * normed
    moe = moe + (weights[1] * shares[0][1]) * cv_ref[0:1, :]
    moe = moe + (weights[2] * shares[1][1]) * cv_ref[1:2, :]
    return mid + moe, chosen


def combine_body(tcol_ref, ret_ref, mid_ref, lg_ref, rt_ref, g_ref, cv_ref, x_ref, c0_ref, c1_ref):
    x_ref[...], chosen = combine_rows(
        tcol_ref[...], ret_ref, mid_ref[...], lg_ref[...], rt_ref[...], g_ref[...], cv_ref
    )
    c0_ref[...] = chosen[0].astype(BF)
    c1_ref[...] = chosen[1].astype(BF)


def combine(tcol, returned, mid, logits, routes, gain, const_vec):
    return call(
        combine_body,
        (NB,),
        [
            (tcol, (RB, 128), rows),
            (returned, None),
            (mid, (RB, D), rows),
            (logits, (RB, 128), rows),
            (routes, (RB, 2), rows),
            (gain, None),
            (const_vec, None),
        ],
        [
            (out((T, D), F32), (RB, D), rows),
            (out((T, D), BF), (RB, D), rows),
            (out((T, D), BF), (RB, D), rows),
        ],
        name="combine",
        flops=4 * T * SLOTS * D,
        nbytes=12e6,
    )


def mix_grad(g, mid, chosen, logits, routes, grad, gain, cv_ref, wt, res):
    normed = mid * rms_scale(mid) * gain
    gates, weights, shares = mix_terms(logits, routes)

    def along(v):
        return jnp.sum(g * v, axis=1, keepdims=True)

    same = along(normed)
    const = [along(cv_ref[c : c + 1, :]) for c in range(2)]
    gate_grads = []
    for k in range(2):
        r = routes[:, k : k + 1]
        value = along(chosen[k].astype(F32)) + jnp.where(r == NFFN + 1, same, 0.0)
        for c in range(2):
            mixed = shares[c][0] * same + shares[c][1] * const[c]
            value = value + jnp.where(r == NFFN + 2 + c, mixed, 0.0)
        gate_grads.append(value)
    slope = gates[0] * gates[1] * (gate_grads[0] - gate_grads[1])
    lane = iota((RB, 128), 1)
    grad = grad + jnp.where(lane == routes[:, 0:1], slope, 0.0)
    grad = grad - jnp.where(lane == routes[:, 1:2], slope, 0.0)
    only = grad
    for c in range(2):
        tilt = weights[1 + c] * shares[c][0] * shares[c][1] * (same - const[c])
        grad = grad + jnp.where(lane == 12 + 2 * c, tilt, 0.0)
        grad = grad - jnp.where(lane == 13 + 2 * c, tilt, 0.0)
    keep = weights[0] + weights[1] * shares[0][0] + weights[2] * shares[1][0]
    residual = None if res is None else mm(spread_lanes(only), res)
    return mm(spread_lanes(grad), wt) + keep * g, residual


def collect(p, kind, tcol_ref, gm_ref, back_ref):
    numbers = [owner_at(p, h, kind)[1] for h in range(2)]

    def one(i, carry):
        at = pl.ds(pl.multiple_of(i * RB, RB), RB)
        tcol = tcol_ref[at, :]
        total = gm_ref[at, :]
        for number in numbers:
            place = number * CAP + iota((RB, CAP), 1)
            hit = (tcol[:, 0:1] == place) | (tcol[:, 1:2] == place)
            total = total + mm(hit.astype(F32).astype(BF), back_ref[number])
        gm_ref[at, :] = total
        return carry

    lax.fori_loop(0, NB, one, 0)


def settle_back(refs, at, gm_ref, mix_ref):
    mid_ref, g_ref, mixed_ref, gain_ref, nar_ref, w_ref, d_ref, u_ref, gu_ref, gd_ref = refs
    grad = g_ref[at, :].astype(F32) + rms_back(gm_ref[at, :], mid_ref[at, :], gain_ref[...])
    gm_ref[at, :] = grad
    grad = grad.astype(BF)
    slim = mm_nt(grad, u_ref[...]).astype(BF)
    gu_ref[...] += 2.0 * mm_tn(nar_ref[at, :], grad)
    gd_ref[...] += mm_tn(slim, mixed_ref[at, :])
    mix_ref[at, :] = (mm_nt(grad, w_ref[...]) + mm_nt(slim, d_ref[...])).astype(BF)


def rms_back(grad, v, gain):
    scale = rms_scale(v)
    inner = grad * gain
    return scale * inner - v * (scale**3 * jnp.mean(v * inner, axis=1, keepdims=True))


def attend_back(q, k, v, aug, kf, g, mixed, dqt):
    lane = iota((T, 128), 1)
    low = lane < 64
    lane6 = lane & 63
    product = g.astype(F32) * mixed.astype(F32)
    d0 = jnp.sum(jnp.where(low, product, 0.0), axis=1, keepdims=True)
    d1 = jnp.sum(jnp.where(low, 0.0, product), axis=1, keepdims=True)
    a, b, c = three(-jnp.where(low, d1, d0))
    zero = jnp.zeros((T, 128), BF)
    ga = jnp.where(lane6 == 0, a, jnp.where(lane6 == 1, b, jnp.where(lane6 == 2, c, zero)))
    va = (lane6 < 3).astype(F32).astype(BF)
    qs = (jnp.where(low, q, aug), jnp.where(low, aug, q))
    ks = (jnp.where(low, k, kf), jnp.where(low, kf, k))
    vs = (jnp.where(low, v, va), jnp.where(low, va, v))
    gs = (jnp.where(low, g, ga), jnp.where(low, ga, g))
    kt = k.T
    tri = iota((RB, RB), 0) <= iota((RB, RB), 1)
    low = low[:RB]
    dks = []
    dvs = []
    for i in range(NB):
        here = slice(i * RB, (i + 1) * RB)
        dk = [None, None]
        dv = [None, None]
        for h in range(2):
            half = slice(h * 64, (h + 1) * 64)
            for start, stop in ((i * RB, (i + 1) * RB), ((i + 1) * RB, T)):
                if start == stop:
                    continue
                there = slice(start, stop)
                p = jnp.exp2(mm_nt(ks[h][here], qs[h][there]) * LOG_SCALE)
                if stop == (i + 1) * RB:
                    p = jnp.where(tri, p, 0.0)
                ds = (p * mm_nt(vs[h][here], gs[h][there])).astype(BF)
                p = p.astype(BF)
                dv_part = mm(p, g[there])
                dk_part = mm(ds, q[there])
                dk[h] = dk_part if dk[h] is None else dk[h] + dk_part
                dv[h] = dv_part if dv[h] is None else dv[h] + dv_part
                part = mm(kt[half, here], ds)
                if i == 0:
                    dqt[half, there] = part
                else:
                    dqt[half, there] += part
        dvs.append(jnp.where(low, dv[0], dv[1]))
        dks.append(jnp.where(low, dk[0], dk[1]))
    return dqt[...].T, jnp.concatenate(dks), jnp.concatenate(dvs)


def layer_back_body(far, near, out_near, gx_ref, scratch, ready, done):
    gm_ref, mix_ref, mixed_ref, w_ref, qkv_ref, aug_ref, n_ref, x_ref = far
    gain_ref, nar_ref, d_ref, u_ref, kf_ref, cos_ref, sin_ref = near
    gu_ref, gd_ref = out_near
    gm, mix, mixed, w, qkv, aug, n, x, gproj, dqt, sems, pair_sems, out_sems = scratch

    def start(source, target, sem):
        copy = pltpu.make_async_copy(source, target, sem)
        copy.start()
        return copy

    def cols(part, j):
        return pl.ds(pl.multiple_of(part * D + j * 128, 128), 128)

    def of_pair(j):
        copies = [
            pltpu.make_async_copy(
                qkv_ref.at[:, cols(part, j)], qkv.at[:, cols(part, j)], pair_sems.at[j, part]
            )
            for part in range(3)
        ]
        for k, (source, target) in enumerate(((mix_ref, mix), (mixed_ref, mixed))):
            copies.append(
                pltpu.make_async_copy(
                    source.at[:, cols(0, j)], target.at[:, cols(0, j)], pair_sems.at[j, 3 + k]
                )
            )
        copies.append(pltpu.make_async_copy(aug_ref.at[j], aug.at[j], pair_sems.at[j, 5]))
        return copies

    for j in range(PAIRS):
        for copy in of_pair(j):
            copy.start()
    third = [start(w_ref.at[k], w.at[k], sems.at[k]) for k in range(3)]
    third += [
        start(source, target, sems.at[3 + k])
        for k, (source, target) in enumerate(((n_ref, n), (x_ref, x), (gm_ref, gm)))
    ]
    ready()

    def pair(j, carry):
        for copy in of_pair(j):
            copy.wait()
        dq, dk, dv = attend_back(
            qkv[:, cols(0, j)], qkv[:, cols(1, j)], qkv[:, cols(2, j)], aug[j], kf_ref[...],
            mix[:, cols(0, j)], mixed[:, cols(0, j)], dqt,
        )
        for part, value in enumerate((dq, dk)):
            value = (value * (1.0 / math.sqrt(HD))).astype(BF).astype(F32)
            gproj[:, cols(part, j)] = turn(value, cos_ref[...], -sin_ref[...]).astype(BF)
        gproj[:, cols(2, j)] = dv.astype(BF)
        return carry

    lax.fori_loop(0, PAIRS, pair, 0)
    for copy in third:
        copy.wait()
    gu_ref[...] = jnp.zeros_like(gu_ref)
    gd_ref[...] = jnp.zeros_like(gd_ref)
    stores = []
    for i in range(NB):
        at = slice(i * RB, (i + 1) * RB)
        grad = jnp.zeros((RB, D), F32)
        slim = jnp.zeros((RB, 128), F32)
        narrow = nar_ref[at, :]
        for part in range(3):
            columns = slice(part * D, (part + 1) * D)
            piece = gproj[at, columns]
            grad = grad + mm_nt(piece, w[part])
            slim = slim + mm_nt(piece, u_ref[:, columns])
            gu_ref[:, columns] += 2.0 * mm_tn(narrow, piece)
        slim = slim.astype(BF)
        gd_ref[...] += mm_tn(slim, n[at, :])
        grad = grad + mm_nt(slim, d_ref[...])
        gm[at, :] = gm[at, :] + rms_back(grad, x[at, :].astype(F32), gain_ref[...])
        stores.append(start(gm.at[at, :], gx_ref.at[at, :], out_sems.at[i]))
    for copy in stores + [done(0), done(1)]:
        copy.wait()


def layer_back(gm, mix, mixed, w, qkv, aug, n, x, gain0, narrow, down, up, kf, cos, sin):
    far = [gm, mix, mixed, w, qkv, aug, n, x]

    def body(far, near, outs, near_outs, scratch, ready, done):
        layer_back_body(far, near, near_outs, outs[0], scratch, ready, done)

    shapes = [out((3, D, D), BF) if v is w else v for v in far]
    return comm_call(
        body,
        far,
        [out((T, D), F32)],
        [pltpu.VMEM(v.shape, v.dtype) for v in shapes]
        + [pltpu.VMEM((T, 3 * D), BF), pltpu.VMEM((128, T), F32)]
        + [DMA((6,)), DMA((PAIRS, 6)), DMA((NB,))],
        "layer_back",
        None,
        12 * 10 * T * T * 128 + 2 * T * D * 3 * D,
        4e7,
        [gain0, narrow, down, up, kf, cos, sin],
        [out((128, 3 * D), F32), out((128, D), F32)],
    )


AXES = ("x", "c", "zh", "zl", "y")
EXPERT, SHARD = AXES[:2], AXES[2:]
PIECE = 96


def shared_body(count, *refs):
    (p_ref,), away, (o_ref,), came, sems = split_refs(refs, 1, count, 1, count)
    local, zs, zr, ys, yr, xs, xr, cs, cr, ws, wr = sems
    x, c, y = (lax.axis_index(name) for name in ("x", "c", "y"))
    z = 2 * lax.axis_index("zh") + lax.axis_index("zl")
    mine, theirs = 2 * x + c, 2 * (1 - x) + c

    def spot(quarter, column, j):
        at = (2 * ((z + 4 - j) % 4) + column) * PIECE
        return o_ref.at[quarter, pl.ds(pl.multiple_of(at, PIECE), PIECE), :]

    others = [{"zh": (z + d) % 4 // 2, "zl": (z + d) % 2} for d in range(1, 4)]
    others += [{"y": 1 - y}, {"x": 1 - x}, {"c": 1 - c}]
    barrier = pltpu.get_barrier_semaphore()
    for who in others:
        pl.semaphore_signal(barrier, inc=1, device_id=who, device_id_type=pl.DeviceIdType.MESH)
    pl.semaphore_wait(barrier, len(others))

    started = []

    def send(source, target, who, send_sem, recv_sem):
        copy = pltpu.make_async_remote_copy(
            src_ref=source,
            dst_ref=target,
            send_sem=send_sem,
            recv_sem=recv_sem,
            device_id=who,
            device_id_type=pl.DeviceIdType.MESH,
        )
        copy.start()
        started.append(copy)
        return copy

    core_copies = []

    def to_core(source, target):
        n = len(core_copies)
        core_copies.append(send(source, target, others[5], cs.at[n], cr.at[n]))

    own = pltpu.make_async_copy(p_ref, spot(mine, y, 0), local.at[0])
    own.start()
    z_copies = [
        send(p_ref, spot(mine, y, 0), others[d], zs.at[d], zr.at[d]) for d in range(3)
    ]
    y_copies = [None] * 6
    x_copies = [None] * 6

    def along_y(n, source, target):
        y_copies[n] = send(source, target, others[3], ys.at[n], yr.at[n])

    def along_x(n, source, target):
        x_copies[n] = send(source, target, others[4], xs.at[n], xr.at[n])

    along_y(0, p_ref, spot(mine, y, 0))
    along_x(0, p_ref, spot(mine, y, 0))
    to_core(p_ref, spot(mine, y, 0))
    swaps = [
        send(source, target, others[3], ws.at[n], wr.at[n])
        for n, (source, target) in enumerate(zip(away, came))
    ]
    for j in range(1, 4):
        z_copies[j - 1].wait_recv()
        piece = spot(mine, y, j)
        along_y(j, piece, piece)
        along_x(j, piece, piece)
        to_core(piece, piece)
    for j in range(4):
        y_copies[j].wait_recv()
        piece = spot(mine, 1 - y, j)
        if j < 2:
            along_x(4 + j, piece, piece)
        to_core(piece, piece)
        x_copies[j].wait_recv()
        piece = spot(theirs, y, j)
        if j >= 2:
            along_y(2 + j, piece, piece)
        to_core(piece, piece)
    for j in range(4):
        (x_copies[4 + j] if j < 2 else y_copies[2 + j]).wait_recv()
        piece = spot(theirs, 1 - y, j)
        to_core(piece, piece)
    for copy in core_copies + swaps:
        copy.wait_recv()
    own.wait()
    for copy in started:
        copy.wait_send()


def usual():
    return tuple(lax.axis_size(name) for name in AXES) == (2, 2, 2, 2, 2)


def gather_shared(qkv, output, away=()):
    rows_here = qkv.shape[0]
    parts = jnp.concatenate([qkv.reshape(rows_here, 3, D).transpose(1, 0, 2), output[None]])
    if not usual():
        return [lax.all_gather(parts, SHARD, axis=1, tiled=True)]
    quarter = 2 * lax.axis_index("x") + lax.axis_index("c")
    piece = lax.dynamic_index_in_dim(parts, quarter, axis=0, keepdims=False)
    return comm_call(
        lambda far, near, outs, near_outs, scratch, ready, done: shared_body(
            len(away), *far, *outs, *scratch
        ),
        [piece, *away],
        [jax.ShapeDtypeStruct(v.shape, v.dtype) for v in (out((4, D, D), BF), *away)],
        [DMA((n,)) for n in (1, 3, 3, 6, 6, 6, 6, 16, 16, 2, 2)],
        "gather_shared",
        5 if away else 0,
        0,
        5e7,
    )


SPAN = 96
UNIT = LAYERS * 2 * 4 * R


def adapters_body(*refs):
    id_ref, parts = refs[0], refs[1 : 1 + 4 * LAYERS]
    o_ref = refs[1 + 4 * LAYERS]
    sbuf, rbuf, tbuf, ubuf, ibuf, jbuf, asend, arecv, bsend, brecv, isend, irecv = refs[2 + 4 * LAYERS :]
    x, c, y = (lax.axis_index(name) for name in ("x", "c", "y"))
    z = 2 * lax.axis_index("zh") + lax.axis_index("zl")
    mates = []
    for dz in range(4):
        for dy in range(2):
            mates.append(((z + dz) % 4, flip(y, dy)))
    groups = [(flip(x, dx), flip(c, dc)) for dx in range(2) for dc in range(2)]
    barrier = pltpu.get_barrier_semaphore()
    peers = [{"zh": a // 2, "zl": a % 2, "y": b} for a, b in mates[1:]]
    peers += [{"x": a, "c": b} for a, b in groups[1:]]
    for who in peers:
        pl.semaphore_signal(barrier, inc=1, device_id=who, device_id_type=pl.DeviceIdType.MESH)
    for layer in range(LAYERS):
        gd_in, gd_out, gu_in, gu_out = parts[4 * layer : 4 * layer + 4]
        pieces = [gd_in[p * R : (p + 1) * R, :] for p in range(3)] + [gd_out[:R, :]]
        pieces += [gu_in[p * R : (p + 1) * R, p * D : (p + 1) * D] for p in range(3)] + [gu_out[:R, :]]
        sbuf[:, layer * 128 : (layer + 1) * 128] = jnp.concatenate(pieces).T.astype(BF)
    ibuf[...] = jnp.broadcast_to(id_ref[0].astype(F32).astype(BF), (16, 128))

    def share(k):
        return sbuf.at[pl.ds(pl.multiple_of(k * SPAN, SPAN), SPAN), :]

    pl.semaphore_wait(barrier, len(peers))
    me = 2 * z + y
    copies = []
    for n, (a, b) in enumerate(mates):
        if n == 0:
            rbuf[0] = share(me)[...]
            jbuf[0] = ibuf[...]
            continue
        at = (4 - n // 2) % 4 * 2 + n % 2
        copy = pltpu.make_async_remote_copy(
            src_ref=ibuf,
            dst_ref=jbuf.at[at],
            send_sem=isend.at[n],
            recv_sem=irecv.at[at],
            device_id={"zh": a // 2, "zl": a % 2, "y": b},
            device_id_type=pl.DeviceIdType.MESH,
        )
        copy.start()
        copies.append(copy)
        copy = pltpu.make_async_remote_copy(
            src_ref=share(2 * a + b),
            dst_ref=rbuf.at[at],
            send_sem=asend.at[n],
            recv_sem=arecv.at[at],
            device_id={"zh": a // 2, "zl": a % 2, "y": b},
            device_id_type=pl.DeviceIdType.MESH,
        )
        copy.start()
        copies.append(copy)
    for copy in copies:
        copy.wait()
    masks = []
    for n in range(8):
        own = jbuf[n][0:1, 0:1].astype(F32)
        masks.append([(own == k).astype(F32) for k in range(NA)])

    def add(i, carry):
        at = pl.ds(pl.multiple_of(i * 16, 16), 16)
        sums = [jnp.zeros((16, UNIT), F32) for _ in range(NA)]
        for n in range(8):
            values = rbuf[n, at, :].astype(F32)
            for k in range(NA):
                sums[k] = sums[k] + values * masks[n][k]
        for k in range(NA):
            tbuf[k, at, :] = sums[k].astype(BF)
        return carry

    lax.fori_loop(0, SPAN // 16, add, 0)
    copies = []
    ubuf[0] = tbuf[pl.ds(2 * (2 * x + c), 2)]
    for n, (a, b) in enumerate(groups):
        if n == 0:
            continue
        copy = pltpu.make_async_remote_copy(
            src_ref=tbuf.at[pl.ds(2 * (2 * a + b), 2)],
            dst_ref=ubuf.at[n],
            send_sem=bsend.at[n],
            recv_sem=brecv.at[n],
            device_id={"x": a, "c": b},
            device_id_type=pl.DeviceIdType.MESH,
        )
        copy.start()
        copies.append(copy)
    for copy in copies:
        copy.wait()
    total = ubuf[0].astype(F32)
    for n in range(1, 4):
        total = total + ubuf[n].astype(F32)
    o_ref[...] = total


def adapters(own, parts):
    specs = [pl.BlockSpec(memory_space=pltpu.SMEM)]
    specs += [pl.BlockSpec(memory_space=pltpu.VMEM)] * len(parts)
    return pl.pallas_call(
        adapters_body,
        in_specs=specs,
        out_specs=pl.BlockSpec(memory_space=pltpu.VMEM),
        out_shape=jax.ShapeDtypeStruct((2, SPAN, UNIT), F32),
        scratch_shapes=[
            pltpu.VMEM((D, UNIT), BF),
            pltpu.VMEM((8, SPAN, UNIT), BF),
            pltpu.VMEM((NA, SPAN, UNIT), BF),
            pltpu.VMEM((4, 2, SPAN, UNIT), BF),
            pltpu.VMEM((16, 128), BF),
            pltpu.VMEM((8, 16, 128), BF),
            DMA((8,)),
            DMA((8,)),
            DMA((4,)),
            DMA((4,)),
            DMA((8,)),
            DMA((8,)),
        ],
        compiler_params=pltpu.CompilerParams(
            vmem_limit_bytes=VMEM_BYTES, collective_id=4, has_side_effects=True
        ),
        name="adapters",
    )(own, *parts)


def both_rows(mine, other):
    y = lax.axis_index("y")
    return jnp.where(y == 0, jnp.stack([mine, other]), jnp.stack([other, mine]))


def own_and_other(w):
    y = lax.axis_index("y")
    return [lax.dynamic_index_in_dim(w, e, axis=0, keepdims=False) for e in (y, 1 - y)]


def across_y(v):
    return lax.ppermute(v, "y", [(0, 1), (1, 0)])


def swapped(w):
    mine, other = own_and_other(w)
    return both_rows(mine, across_y(other))


def gathered(w, axes):
    return lax.all_gather(w, axes, axis=0, tiled=True).reshape(-1, w.shape[-1])


def exchange(v, kind):
    return lax.all_to_all(v, OWNERS[kind], split_axis=0, concat_axis=0, tiled=True)


def pad_to(v, shape):
    return jnp.pad(v, [(0, n - m) for m, n in zip(v.shape, shape)])


def adapters_plain(owners, parts):
    layers = []
    for gd_in, gd_out, gu_in, gu_out in parts:
        downs = [gd_in[p * R : (p + 1) * R] for p in range(3)] + [gd_out[:R]]
        ups = [gu_in[p * R : (p + 1) * R, p * D : (p + 1) * D] for p in range(3)] + [gu_out[:R]]
        layers.append(jnp.concatenate(downs + ups))
    compact = jnp.concatenate(layers).astype(BF)
    ranks = lax.axis_size(SHARD)
    pieces = compact.reshape(UNIT, ranks, D // ranks).transpose(1, 0, 2)
    pieces = lax.all_to_all(pieces, SHARD, split_axis=0, concat_axis=0, tiled=True)
    pick = (owners[None, :] == jnp.arange(NA, dtype=jnp.int32)[:, None]).astype(F32)
    summed = jnp.dot(pick, pieces.reshape(ranks, -1).astype(F32), precision=HIGHEST).astype(BF)
    groups = lax.axis_size(EXPERT)
    summed = lax.all_to_all(
        summed.reshape(groups, NA // groups, -1), EXPERT, split_axis=0, concat_axis=0, tiled=True
    )
    summed = jnp.sum(summed.astype(F32), axis=0)
    return summed.reshape(summed.shape[0], UNIT, -1).transpose(0, 2, 1)


def per_device(
    tokens,
    segments,
    parents,
    adapter_of,
    routes,
    norm_gain,
    query_key_value_weight,
    output_weight,
    adapter_down,
    adapter_up,
    router,
    router_residual,
    const_proj,
    const_vec,
    w_gate_up,
    w_down,
    out_grad,
):
    fast = w_gate_up.shape[1] == 2
    kind = PLANE if fast else WIDE_SLICE
    barrier = lax.optimization_barrier
    if fast:
        mine, other = own_and_other(w_gate_up[0])
        parts = [lax.all_gather(mine, ("zh", "zl"), axis=0)]
        down_mine, down_other = own_and_other(w_down[0])
        first, other, down_other = gather_shared(
            query_key_value_weight[0], output_weight[0], (other, down_other)
        )
        shared = [first]
        parts.append(lax.all_gather(other, ("zh", "zl"), axis=0))
        gate_up_full = [parts]
        down_full = [gathered(both_rows(down_mine, down_other), ("zh", "zl"))]
    else:
        shared = gather_shared(query_key_value_weight[0], output_weight[0])
        gate_up_full = [[gathered(w_gate_up[layer, 0], SHARD)] for layer in range(LAYERS)]
        down_full = [gathered(w_down[layer, 0], SHARD) for layer in range(LAYERS)]

    which = adapter_of[0]
    down_sel = lax.dynamic_index_in_dim(adapter_down, which, axis=2, keepdims=False)
    up_sel = lax.dynamic_index_in_dim(adapter_up, which, axis=2, keepdims=False)
    down_in = jnp.pad(
        down_sel[:, :3].transpose(0, 2, 1, 3).reshape(LAYERS, D, 3 * R), ((0, 0), (0, 0), (0, 80))
    )
    down_out = jnp.pad(down_sel[:, 3], ((0, 0), (0, 0), (0, 112)))
    up_t = 2.0 * up_sel.transpose(0, 1, 3, 2)
    up_in = jnp.zeros((LAYERS, 128, 3 * D), BF)
    for p in range(3):
        up_in = up_in.at[:, p * R : (p + 1) * R, p * D : (p + 1) * D].set(up_t[:, p])
    up_out = jnp.pad(up_t[:, 3], ((0, 0), (0, 112), (0, 0)))
    rcat = jnp.concatenate([router, const_proj[:, 0], const_proj[:, 1]], axis=2)
    rcat = jnp.pad(rcat, ((0, 0), (0, 0), (0, 112)))
    rcat_t = rcat[:, :, :16].transpose(0, 2, 1)
    residual = pad_to(router_residual, (16, 128))
    residual_t = pad_to(router_residual.T, (16, 128))

    qf, kf, cos, sin, tcol, trow, router_s, router_ts, residual_s, residual_ts = prep(
        parents, segments.reshape(T, 1), routes, rcat, rcat_t, residual, residual_t
    )

    stream = tokens
    earlier = jnp.zeros((T, 128), F32)
    saved = []
    for layer in range(LAYERS):
        gain0 = norm_gain[layer, 0:1]
        gain1 = norm_gain[layer, 1:2]
        normed, narrow, qkv = project(
            stream, gain0, shared[layer], down_in[layer], up_in[layer], cos, sin
        )
        mixed, aug = attend(qkv, qf, kf)
        mid, sent, logits, narrow_out = settle(
            stream, mixed, shared[layer], down_out[layer], up_out[layer], gain1, router_s[layer],
            earlier, residual_s,
        )
        buffer = dispatch(trow, sent)
        received = exchange(buffer, kind)
        if layer == 0:
            if fast:
                later = barrier((w_gate_up[1], w_down[1], logits))
                gate_up_next, down_next = barrier((swapped(later[0]), later[1]))
                gate_up_full.append([gathered(gate_up_next, ("zh", "zl"))])
                down_full.append(gathered(swapped(down_next), ("zh", "zl")))
            later = lax.optimization_barrier(
                (query_key_value_weight[1], output_weight[1], logits)
            )
            shared += gather_shared(later[0], later[1])
            returned, gate, up = expert_forward(received, gate_up_full[0], down_full[0], kind)
        else:
            slot_grads = exchange(dispatch_grad(trow, out_grad, logits, routes), kind)
            grad_mixed, following, grad_mid, grad_logits, gu_out, gd_out = expert_both(
                *expert_parts(received, gate_up_full[1][0], kind), slot_grads, gate_up_full[1][0], down_full[1], mid, out_grad, mixed,
                shared[1], tcol, logits, routes, gain1, const_vec[1], router_ts[1], residual_ts,
                narrow_out, down_out[1], up_out[1], kind,
            )
            c0 = c1 = None
        if layer == 0:
            following, c0, c1 = combine(
                tcol, returned.reshape(SLOTS, D), mid, logits, routes, gain1, const_vec[0]
            )
        saved.append((stream, normed, narrow, qkv, mixed, aug, mid, logits, narrow_out, c0, c1))
        stream = following
        earlier = logits

    grad = out_grad
    parts = [None] * LAYERS
    for layer in reversed(range(LAYERS)):
        x_in, normed, narrow, qkv, mixed, aug, mid, logits, narrow_out, c0, c1 = saved[layer]
        gain0 = norm_gain[layer, 0:1]
        gain1 = norm_gain[layer, 1:2]
        if layer == 0:
            grad_mid, grad_mixed, gu_out, gd_out = expert_backward(
                gate, up, gate_up_full[0], down_full[0], grad, mid, c0, c1, mixed, shared[0], trow,
                tcol, logits, routes, grad_logits, gain1, const_vec[0], router_ts[0], narrow_out,
                down_out[0], up_out[0], kind,
            )
        grad, gu_in, gd_in = layer_back(
            grad_mid, grad_mixed, mixed, shared[layer], qkv, aug, normed, x_in, gain0, narrow,
            down_in[layer], up_in[layer], kf, cos, sin,
        )
        parts[layer] = (gd_in, gd_out, gu_in, gu_out)

    if usual():
        final = adapters(adapter_of, [v for layer in parts for v in layer])
    else:
        final = adapters_plain(lax.all_gather(adapter_of, SHARD, axis=0, tiled=True), parts)
    final = final.reshape(*final.shape[:2], LAYERS, 2, 4, R).transpose(3, 2, 4, 0, 1, 5)
    return (stream, grad, final[0], final[1])


def solution(mesh):
    owners, shards = mesh.shape["expert"], mesh.shape["shard"]
    each = NFFN // owners
    fine = jax.sharding.Mesh(
        mesh.devices.reshape(owners // 2, 2, shards // each**2, each, each), AXES
    )
    expert, shard, both = EXPERT, SHARD, AXES
    in_specs = (
        P(both, None),
        P(both, None),
        P(both, None),
        P(both),
        P(both, None),
        P(),
        P(None, shard, None),
        P(None, shard, None),
        P(),
        P(),
        P(),
        P(),
        P(),
        P(),
        P(None, expert, shard, None),
        P(None, expert, shard, None),
        P(both, None),
    )
    out_specs = (
        P(both, None),
        P(both, None),
        P(None, None, expert, shard, None),
        P(None, None, expert, shard, None),
    )
    return jax.shard_map(
        per_device, mesh=fine, in_specs=in_specs, out_specs=out_specs, check_vma=False
    )
```

```python
import functools
import math

import jax
import jax.numpy as jnp
from jax import lax
from jax.experimental import pallas as pl
from jax.experimental.pallas import tpu as pltpu
from jax.sharding import PartitionSpec as P

D = 768
HEADS = 12
HD = 64
FF = 2048
NFFN = 8
NEXP = 12
R = 16
NA = 8
NSEG = 13
LAYERS = 2
CAP = 192
T = 1024
SLOTS = NFFN * CAP
RB = 256
NB = T // RB
PAIRS = HEADS // 2
FC = 512
EPSILON = 1e-06
BIG = 2.0**100
LOG_SCALE = math.log2(math.e) / math.sqrt(HD)
F32 = jnp.float32
BF = jnp.bfloat16
HIGHEST = lax.Precision.HIGHEST
VMEM_BYTES = 60 * 1024 * 1024


def mm(a, b):
    return lax.dot_general(a, b, (((1,), (0,)), ((), ())), preferred_element_type=F32)


def mm_nt(a, b):
    return lax.dot_general(a, b, (((1,), (1,)), ((), ())), preferred_element_type=F32)


def mm_tn(a, b):
    return lax.dot_general(a, b, (((0,), (0,)), ((), ())), preferred_element_type=F32)


def mm_exact(a, b):
    return lax.dot_general(
        a, b, (((1,), (0,)), ((), ())), preferred_element_type=F32, precision=HIGHEST
    )


def iota(shape, axis):
    return lax.broadcasted_iota(jnp.int32, shape, axis)


def sigmoid(v):
    return 1.0 / (1.0 + jnp.exp(-v))


def call(body, grid, ins, outs, scratch=(), name=None, flops=0, nbytes=0):
    def spec(entry):
        if entry[1] == "smem":
            return pl.BlockSpec(memory_space=pltpu.SMEM)
        if entry[1] is None:
            shape = entry[0].shape
            return pl.BlockSpec(shape, lambda *_: (0,) * len(shape))
        return pl.BlockSpec(entry[1], entry[2])

    return pl.pallas_call(
        body,
        grid=grid,
        in_specs=[spec(e) for e in ins],
        out_specs=[spec(e) for e in outs],
        out_shape=[jax.ShapeDtypeStruct(e[0].shape, e[0].dtype) for e in outs],
        scratch_shapes=list(scratch),
        compiler_params=pltpu.CompilerParams(
            dimension_semantics=("arbitrary",) * len(grid), vmem_limit_bytes=VMEM_BYTES
        ),
        cost_estimate=pl.CostEstimate(
            flops=int(flops), bytes_accessed=int(nbytes), transcendentals=0
        ),
        name=name,
    )(*[e[0] for e in ins])


def out(shape, dtype):
    return jax.ShapeDtypeStruct(shape, dtype)


def rows(i):
    return (i, 0)


def three(v):
    high = v.astype(BF)
    rest = v - high.astype(F32)
    middle = rest.astype(BF)
    return high, middle, (rest - middle.astype(F32)).astype(BF)


def spread_lanes(v):
    a, b, c = (part.astype(F32) for part in three(v))
    total = a + pltpu.roll(b, 16, 1) + pltpu.roll(c, 32, 1)
    total = total + pltpu.roll(a, 48, 1) + pltpu.roll(b, 64, 1) + pltpu.roll(a, 80, 1)
    return total.astype(BF)


def stack_rows(w):
    a, b, c = three(w)
    return jnp.concatenate([a, a, a, b, b, c, jnp.zeros((32, w.shape[1]), BF)], axis=0)


def prep_body(
    par_ref, seg_ref, rt_ref, rc_ref, rct_ref, res_ref, rest_ref,
    qf_ref, kf_ref, cos_ref, sin_ref, tcol_ref, trow_ref, rs_ref, rts_ref, ress_ref, rests_ref, anc,
):
    for layer in range(LAYERS):
        a, b, c = (part.astype(F32) for part in three(rc_ref[layer]))
        rs_ref[layer] = (a + pltpu.roll(b, 16, 1) + pltpu.roll(c, 32, 1)).astype(BF)
        rts_ref[layer] = stack_rows(rct_ref[layer])
    ress_ref[...] = stack_rows(res_ref[...])
    rests_ref[...] = stack_rows(rest_ref[...])
    first = iota((1, 128), 1) & 63
    anc[...] = jnp.zeros_like(anc)
    anc[0:1, :] = (first == 0).astype(F32)
    for s in range(1, NSEG):
        above = anc[pl.ds(par_ref[0, s], 1), :]
        anc[s : s + 1, :] = jnp.maximum(above, (first == s).astype(F32))
    lane = iota((T, 128), 1)
    lane6 = lane & 63
    low = lane < 64
    member = (seg_ref[...] == lane6).astype(F32)
    ways = mm(jnp.where(low, member, 0.0).astype(BF), anc[...].astype(BF))
    qf_ref[...] = jnp.where(lane6 < NSEG, (ways - 1.0) * BIG, 0.0).astype(BF)
    ones = ((lane6 >= 16) & (lane6 < 19)).astype(F32)
    kf_ref[...] = (member + ones).astype(BF)
    hit0 = (rt_ref[:, 0:1] == lane).astype(F32)
    hit1 = (rt_ref[:, 1:2] == lane).astype(F32)
    hits = hit0 + hit1
    upto = (iota((T, T), 0) >= iota((T, T), 1)).astype(F32).astype(BF)
    seen = mm(upto, jnp.concatenate([member.astype(BF), hits.astype(BF)], axis=1))
    depth = jnp.sum(jnp.where(low, ways * seen[:, :128], 0.0), axis=1, keepdims=True) - 1.0
    before = seen[:, 128:] - hits

    def target(hit, route):
        slot = jnp.sum(hit * before, axis=1, keepdims=True)
        place = route.astype(F32) * CAP + slot
        return jnp.where(route < NFFN, place, 4.0 * SLOTS)

    t0 = target(hit0, rt_ref[:, 0:1])
    t1 = target(hit1, rt_ref[:, 1:2])
    both = jnp.where(lane == 0, t0, jnp.where(lane == 1, t1, 0.0))
    tcol_ref[...] = both.astype(jnp.int32)
    trow_ref[...] = both.T[0:8, :].astype(jnp.int32)
    inverse = jnp.exp((lane & 31).astype(F32) * (-math.log(10000.0) / 32.0))
    angle = depth * inverse
    cos_ref[...] = jnp.cos(angle)
    sine = jnp.sin(angle)
    sin_ref[...] = jnp.where((lane & 32) == 0, -sine, sine)


def prep(parents, seg_col, routes, rcat, rcat_t, residual, residual_t):
    return call(
        prep_body,
        (1,),
        [
            (parents, "smem"),
            (seg_col, None),
            (routes, None),
            (rcat, None),
            (rcat_t, None),
            (residual, None),
            (residual_t, None),
        ],
        [
            (out((T, 128), BF), None),
            (out((T, 128), BF), None),
            (out((T, 128), F32), None),
            (out((T, 128), F32), None),
            (out((T, 128), jnp.int32), None),
            (out((8, T), jnp.int32), None),
            (out((LAYERS, D, 128), BF), None),
            (out((LAYERS, 128, D), BF), None),
            (out((128, 128), BF), None),
            (out((128, 128), BF), None),
        ],
        [pltpu.VMEM((128, 128), F32)],
        name="prep",
        flops=2 * T * T * 256,
        nbytes=3e6,
    )


def turn(v, cos, sin):
    first = (iota(v.shape, 1) & 32) == 0
    other = jnp.where(first, pltpu.roll(v, 96, 1), pltpu.roll(v, 32, 1))
    return v * cos + other * sin


def project_rows(x, gain, w_ref, d_ref, u_ref, cos, sin, n_ref, nar_ref, qkv_ref):
    scale = lax.rsqrt(jnp.mean(x * x, axis=1, keepdims=True) + EPSILON)
    normed = (x * scale * gain).astype(BF)
    n_ref[...] = normed
    narrow = mm(normed, d_ref[...]).astype(BF)
    nar_ref[...] = narrow
    for block in range(3):
        cols = slice(block * D, (block + 1) * D)
        part = mm(normed, w_ref[block]) + mm(narrow, u_ref[:, cols])
        for j in range(PAIRS):
            piece = part[:, j * 128 : (j + 1) * 128]
            if block < 2:
                piece = turn(piece, cos, sin)
            at = block * D + j * 128
            qkv_ref[:, at : at + 128] = piece.astype(BF)


def project_body(x_ref, g_ref, w_ref, d_ref, u_ref, cos_ref, sin_ref, n_ref, nar_ref, qkv_ref):
    project_rows(
        x_ref[...].astype(F32),
        g_ref[...],
        w_ref,
        d_ref,
        u_ref,
        cos_ref[...],
        sin_ref[...],
        n_ref,
        nar_ref,
        qkv_ref,
    )


def project(x, gain, w, down, up, cos, sin):
    return call(
        project_body,
        (NB,),
        [
            (x, (RB, D), rows),
            (gain, None),
            (w, (3, D, D), lambda i: (0, 0, 0)),
            (down, None),
            (up, None),
            (cos, (RB, 128), rows),
            (sin, (RB, 128), rows),
        ],
        [
            (out((T, D), BF), (RB, D), rows),
            (out((T, 128), BF), (RB, 128), rows),
            (out((T, 3 * D), BF), (RB, 3 * D), rows),
        ],
        name="project",
        flops=2 * T * D * 3 * D,
        nbytes=12e6,
    )


def attend_body(q_ref, k_ref, v_ref, qf_ref, kf_ref, mixed_ref, aug_ref):
    low = iota((T, 128), 1) < 64
    k = k_ref[...]
    kf = kf_ref[...]
    v = v_ref[...]
    one = jnp.ones((T, 128), BF)
    keys = (jnp.where(low, k, kf), jnp.where(low, kf, k))
    values = (jnp.where(low, v, one), jnp.where(low, one, v))
    low = low[:RB]
    tri = iota((RB, RB), 0) >= iota((RB, RB), 1)
    lane6 = iota((RB, 128), 1) & 63
    for i in range(NB):
        here = slice(i * RB, (i + 1) * RB)
        q = q_ref[here, :]
        qf = qf_ref[here, :]
        tops = []
        outs = []
        for h in range(2):
            qa = jnp.where(low, q, qf) if h == 0 else jnp.where(low, qf, q)
            diag = jnp.where(tri, mm_nt(qa, keys[h][here]), -BIG)
            top = jnp.max(diag, axis=1, keepdims=True)
            if i:
                off = mm_nt(qa, keys[h][: i * RB])
                top = jnp.maximum(top, jnp.max(off, axis=1, keepdims=True))
            result = mm(jnp.exp2((diag - top) * LOG_SCALE).astype(BF), values[h][here])
            if i:
                weights = jnp.exp2((off - top) * LOG_SCALE).astype(BF)
                result = result + mm(weights, values[h][: i * RB])
            tops.append(top)
            outs.append(result)
        total = jnp.where(low, outs[1], outs[0])
        mixed = jnp.where(low, outs[0], outs[1]) / pltpu.roll(total, 64, 1)
        mixed_ref[here, :] = mixed.astype(BF)
        level = -(jnp.where(low, tops[1], tops[0]) + math.sqrt(HD) * jnp.log(total))
        a, b, c = three(level)
        aug_ref[0, here, :] = jnp.where(
            lane6 == 16, a, jnp.where(lane6 == 17, b, jnp.where(lane6 == 18, c, qf))
        )


def attend(qkv, qf, kf):
    return call(
        attend_body,
        (PAIRS,),
        [
            (qkv, (T, 128), lambda j: (0, j)),
            (qkv, (T, 128), lambda j: (0, PAIRS + j)),
            (qkv, (T, 128), lambda j: (0, 2 * PAIRS + j)),
            (qf, None),
            (kf, None),
        ],
        [
            (out((T, D), BF), (T, 128), lambda j: (0, j)),
            (out((PAIRS, T, 128), BF), (1, T, 128), lambda j: (j, 0, 0)),
        ],
        name="attend",
        flops=12 * 4 * T * T * 128,
        nbytes=8e6,
    )


def settle_body(
    x_ref, mixed_ref, w_ref, d_ref, u_ref, g_ref, rt_ref, earlier_ref, res_ref,
    mid_ref, sent_ref, lg_ref, nar_ref,
):
    mixed = mixed_ref[...]
    narrow = mm(mixed, d_ref[...]).astype(BF)
    nar_ref[...] = narrow
    mid = x_ref[...].astype(F32) + mm(mixed, w_ref[0]) + mm(narrow, u_ref[...])
    mid_ref[...] = mid
    scale = lax.rsqrt(jnp.mean(mid * mid, axis=1, keepdims=True) + EPSILON)
    normed = mid * scale * g_ref[...]
    sent_ref[...] = normed.astype(BF)
    a, b, c = three(normed)
    one, two, last = mm(a, rt_ref[...]), mm(b, rt_ref[...]), mm(c, rt_ref[...])
    total = one + two + last + pltpu.roll(one + two, 112, 1) + pltpu.roll(one, 96, 1)
    lane = iota((RB, 128), 1)
    earlier = jnp.where(lane < NEXP, earlier_ref[...], 0.0)
    extra = mm(spread_lanes(earlier), res_ref[...])
    lg_ref[...] = jnp.where(lane < 16, total + extra, 0.0)


def settle(x, mixed, w, down, up, gain, router, earlier, residual):
    return call(
        settle_body,
        (NB,),
        [
            (x, (RB, D), rows),
            (mixed, (RB, D), rows),
            (w, (1, D, D), lambda i: (3, 0, 0)),
            (down, None),
            (up, None),
            (gain, None),
            (router, None),
            (earlier, (RB, 128), rows),
            (residual, None),
        ],
        [
            (out((T, D), F32), (RB, D), rows),
            (out((T, D), BF), (RB, D), rows),
            (out((T, 128), F32), (RB, 128), rows),
            (out((T, 128), BF), (RB, 128), rows),
        ],
        name="settle",
        flops=2 * T * D * D * 2,
        nbytes=10e6,
    )


def dispatch_body(trow_ref, s_ref, o_ref):
    place = pl.program_id(0) * CAP + iota((CAP, T), 0)
    hit = (trow_ref[0:1, :] == place) | (trow_ref[1:2, :] == place)
    o_ref[0] = mm(hit.astype(F32).astype(BF), s_ref[...]).astype(BF)


def dispatch(trow, sent):
    return call(
        dispatch_body,
        (NFFN,),
        [(trow, None), (sent, None)],
        [(out((NFFN, CAP, D), BF), (1, CAP, D), lambda j: (j, 0, 0))],
        name="dispatch",
        flops=2 * T * SLOTS * D,
        nbytes=4e6,
    )[0]


def dispatch_grad_body(trow_ref, g_ref, lg_ref, rt_ref, o_ref, first, second):
    @pl.when(pl.program_id(0) == 0)
    def _():
        for i in range(NB):
            at = slice(i * RB, (i + 1) * RB)
            gates = mix_terms(lg_ref[at, :], rt_ref[at, :])[0]
            g = g_ref[at, :].astype(F32)
            first[at, :] = (gates[0] * g).astype(BF)
            second[at, :] = (gates[1] * g).astype(BF)

    place = pl.program_id(0) * CAP + iota((CAP, T), 0)
    hit0 = (trow_ref[0:1, :] == place).astype(F32).astype(BF)
    hit1 = (trow_ref[1:2, :] == place).astype(F32).astype(BF)
    o_ref[0] = (mm(hit0, first[...]) + mm(hit1, second[...])).astype(BF)


def dispatch_grad(trow, g, logits, routes):
    return call(
        dispatch_grad_body,
        (NFFN,),
        [(trow, None), (g, None), (logits, None), (routes, None)],
        [(out((NFFN, CAP, D), BF), (1, CAP, D), lambda j: (j, 0, 0))],
        [pltpu.VMEM((T, D), BF), pltpu.VMEM((T, D), BF)],
        name="dispatch_grad",
        flops=4 * T * SLOTS * D,
        nbytes=6e6,
    )[0]


PR = 2 * CAP
NP = NFFN // 2


def split_refs(refs, *counts):
    parts = []
    for count in counts:
        parts.append(refs[:count])
        refs = refs[count:]
    return *parts, refs


def flip(bit, change):
    return bit + change - 2 * bit * change


PLANE, WIDE_SLICE = 0, 1
OWNERS = (("x", "c", "y"), ("x", "c"))


def owner_at(p, h, kind):
    x = lax.axis_index("x")
    far, near, core = ((1, 1, h), (1 - h, h, 0), (1 - h, h, 1), (0, 0, h))[p]
    if kind == WIDE_SLICE:
        x = 2 * flip(x // 2, far) + flip(x % 2, near)
        c = flip(lax.axis_index("c"), core)
        return {"x": x, "c": c}, x * 2 + c
    x, c, y = flip(x, far), flip(lax.axis_index("c"), core), flip(lax.axis_index("y"), near)
    return {"x": x, "c": c, "y": y}, (x * 2 + c) * 2 + y


PLACES = [(p, h) for p in range(NP) for h in range(2)]


def greet(kind):
    barrier = pltpu.get_barrier_semaphore()
    for p, h in PLACES[:-2] + PLACES[-1:]:
        pl.semaphore_signal(
            barrier, inc=1, device_id=owner_at(p, h, kind)[0], device_id_type=pl.DeviceIdType.MESH
        )
    pl.semaphore_wait(barrier, NFFN - 1)


def block_of(ref, p, h):
    return ref.at[p, h * CAP : (h + 1) * CAP, :]


def fetch_weights(split, gate_ups, down_ref, w1, w2, sems):
    copies = []
    if split:
        y = lax.axis_index("y")
        for side, ref in enumerate(gate_ups):
            mine = flip(y, side)
            count, size = ref.shape[0], ref.shape[1]
            for k in range(count):
                at = pl.multiple_of((2 * k + mine) * size, size)
                copies.append(
                    pltpu.make_async_copy(
                        ref.at[k], w1.at[pl.ds(at, size), :], sems.at[side * count + k]
                    )
                )
    else:
        copies.append(pltpu.make_async_copy(gate_ups[0], w1, sems.at[0]))
    copies.append(pltpu.make_async_copy(down_ref, w2, sems.at[8]))
    for copy in copies:
        copy.start()
    return copies


def fetch_blocks(source, rv, sems, kind):
    copies = []
    for n, (p, h) in enumerate(PLACES):
        number = owner_at(p, h, kind)[1]
        copies.append(pltpu.make_async_copy(source.at[number], block_of(rv, p, h), sems.at[n]))
    for copy in copies:
        copy.start()
    return copies


def give_back(pv, p, target, send, recv, kind):
    me = owner_at(NP - 1, 0, kind)[1]
    copies = []
    for h in range(2):
        n = 2 * p + h
        if (p, h) == (NP - 1, 0):
            copy = pltpu.make_async_copy(block_of(pv, p, h), target.at[me], send.at[n])
        else:
            copy = pltpu.make_async_remote_copy(
                src_ref=block_of(pv, p, h),
                dst_ref=target.at[me],
                send_sem=send.at[n],
                recv_sem=recv.at[n],
                device_id=owner_at(p, h, kind)[0],
                device_id_type=pl.DeviceIdType.MESH,
            )
        copy.start()
        copies.append(copy)
    return copies


def chunk_at(f):
    return pl.multiple_of(f * FC, FC)


def forward_chunk(r, w1, w2, f):
    at = chunk_at(f)
    gate = mm(r, w1[:, pl.ds(at, FC)])
    up = mm(r, w1[:, pl.ds(pl.multiple_of(FF + f * FC, FC), FC)])
    active = (gate * sigmoid(gate) * up).astype(BF)
    return gate, up, mm(active, w2[pl.ds(at, FC), :])


def backward_chunk(g, gate, up, w1, w2, f):
    at = chunk_at(f)
    grad = mm_nt(g, w2[pl.ds(at, FC), :])
    s = sigmoid(gate)
    grad_s = grad * s
    grad_gate = (grad_s * up * (1.0 + gate * (1.0 - s))).astype(BF)
    grad_up = (grad_s * gate).astype(BF)
    return mm_nt(grad_gate, w1[:, pl.ds(at, FC)]) + mm_nt(
        grad_up, w1[:, pl.ds(pl.multiple_of(FF + f * FC, FC), FC)]
    )


def expert_body(split, kind, *refs):
    count = 2 if split else 1
    gate_ups = refs[:count]
    down_ref, rec_ref, ret_ref, gate_ref, up_ref = refs[count : count + 5]
    w1, w2, rv, pv, gv, uv, acc, wsem, rsem, gsem, usem, send, recv = refs[count + 5 :]
    weights = fetch_weights(split, gate_ups, down_ref, w1, w2, wsem)
    blocks = fetch_blocks(rec_ref, rv, rsem, kind)
    greet(kind)
    for copy in weights + blocks:
        copy.wait()
    stores = []
    moves = []
    for p in range(NP):
        r = rv[p]
        acc[...] = jnp.zeros_like(acc)

        def step(f, carry):
            gate, up, part = forward_chunk(r, w1, w2, f)
            gv[p, :, pl.ds(chunk_at(f), FC)] = gate.astype(BF)
            uv[p, :, pl.ds(chunk_at(f), FC)] = up.astype(BF)
            acc[...] += part
            return carry

        lax.fori_loop(0, FF // FC, step, 0, unroll=2)
        pv[p] = acc[...].astype(BF)
        moves += give_back(pv, p, ret_ref, send, recv, kind)
        for values, ref, sems in ((gv, gate_ref, gsem), (uv, up_ref, usem)):
            copy = pltpu.make_async_copy(values.at[p], ref.at[p], sems.at[p])
            copy.start()
            stores.append(copy)
    for copy in moves + stores:
        copy.wait()


def own_copies(body, ins, near, outs, near_outs, scratch):
    counts = len(ins), len(near), len(outs), len(near_outs), len(scratch)

    def run(*refs):
        far, near_far, targets, near_targets, inner, close = split_refs(refs, *counts)
        close, near_close, sems = split_refs(close, len(near), len(near_outs))
        loads = [
            pltpu.make_async_copy(source, target, sems[0].at[n])
            for n, (source, target) in enumerate(zip(near_far, close))
        ]
        for copy in loads:
            copy.start()

        def ready():
            for copy in loads:
                copy.wait()

        def done(n):
            copy = pltpu.make_async_copy(near_close[n], near_targets[n], sems[1].at[n])
            copy.start()
            return copy

        body(far, close, targets, near_close, inner, ready, done)

    extra = [pltpu.VMEM(v.shape, v.dtype) for v in (*near, *near_outs)]
    extra += [DMA((max(1, len(near)),)), DMA((max(1, len(near_outs)),))]
    return run, [*ins, *near], [*outs, *near_outs], [*scratch, *extra]


def comm_call(body, ins, outs, scratch, name, number, flops, nbytes, near=(), near_outs=()):
    run, ins, outs, scratch = own_copies(body, ins, near, outs, near_outs, scratch)
    far = {} if number is None else dict(collective_id=number, has_side_effects=True)
    return pl.pallas_call(
        run,
        in_specs=[pl.BlockSpec(memory_space=pl.ANY)] * len(ins),
        out_specs=[pl.BlockSpec(memory_space=pl.ANY)] * len(outs),
        out_shape=outs,
        scratch_shapes=scratch,
        compiler_params=pltpu.CompilerParams(vmem_limit_bytes=VMEM_BYTES, **far),
        cost_estimate=pl.CostEstimate(
            flops=int(flops), bytes_accessed=int(nbytes), transcendentals=0
        ),
        name=name,
    )(*ins)


DMA = pltpu.SemaphoreType.DMA
WEIGHTS = [pltpu.VMEM((D, 2 * FF), BF), pltpu.VMEM((FF, D), BF)]
ROWS = pltpu.VMEM((NP, PR, D), BF)
WIDE = pltpu.VMEM((NP, PR, FF), BF)
SUM = pltpu.VMEM((PR, D), F32)
BLOCKS = jax.ShapeDtypeStruct((NFFN, CAP, D), BF)
KEPT = jax.ShapeDtypeStruct((NP, PR, FF), BF)


def expert_forward(received, gate_ups, down, kind):
    split = len(gate_ups) == 2

    def body(far, near, outs, near_outs, scratch, ready, done):
        expert_body(split, kind, *far, *outs, *scratch)

    return comm_call(
        body,
        [*gate_ups, down, received],
        [BLOCKS, KEPT, KEPT],
        WEIGHTS + [ROWS, ROWS, WIDE, WIDE, SUM]
        + [DMA((9,)), DMA((8,)), DMA((NP,)), DMA((NP,)), DMA((8,)), DMA((8,))],
        "expert_forward",
        1,
        2 * SLOTS * D * FF * 3,
        26e6,
    )


def expert_parts_body(kind, far, outs, scratch):
    gate_up_ref, rec_ref = far
    w1, rv, wsem, rsem, osem, *kept = scratch
    load = pltpu.make_async_copy(gate_up_ref, w1, wsem.at[0])
    load.start()
    for copy in fetch_blocks(rec_ref, rv, rsem, kind) + [load]:
        copy.wait()
    stores = []
    for p in range(NP):
        r = rv[p]

        def step(f, carry):
            at = pl.ds(chunk_at(f), FC)
            gate = mm(r, w1[:, at])
            up = mm(r, w1[:, pl.ds(pl.multiple_of(FF + f * FC, FC), FC)])
            s = sigmoid(gate)
            silu = gate * s
            kept[0][p, :, at] = (silu * up).astype(BF)
            kept[1][p, :, at] = (up * s * (1.0 + gate * (1.0 - s))).astype(BF)
            kept[2][p, :, at] = silu.astype(BF)
            return carry

        lax.fori_loop(0, FF // FC, step, 0, unroll=2)
        for n in range(3):
            stores.append(pltpu.make_async_copy(kept[n].at[p], outs[n].at[p], osem.at[p, n]))
            stores[-1].start()
    for copy in stores:
        copy.wait()


def expert_parts(received, gate_up, kind):
    def body(far, near, outs, near_outs, scratch, ready, done):
        expert_parts_body(kind, far, outs, scratch)

    return comm_call(
        body,
        [gate_up, received],
        [KEPT, KEPT, KEPT],
        [WEIGHTS[0], ROWS, DMA((1,)), DMA((8,)), DMA((NP, 3)), WIDE, WIDE, WIDE],
        "expert_parts",
        None,
        2 * SLOTS * D * FF * 2,
        28e6,
    )


def expert_both_body(kind, far, near, mix_out, out_near, scratch, ready, done):
    (
        gate_up_ref, down_ref, active_ref, to_gate_ref, to_up_ref, sg_ref, mid_ref, g_ref,
        mixed_ref, shared_ref,
    ) = far
    tcol_ref, lg_ref, rt_ref, gain_ref, cv_ref, wt_ref, res_ref, nar_ref, d_ref, u_ref = near
    out_ref, gm_ref, gle_ref, gu_ref, gd_ref = out_near
    (
        w1, w2, qv, sv, pv, to_gate, to_up, av, back, gback, mid, g, mixed, w3, acc,
        wsem, asem, ssem, msem, send, recv, gsend, grecv,
    ) = scratch

    def start(source, target, sem):
        copy = pltpu.make_async_copy(source, target, sem)
        copy.start()
        return copy

    load = start(down_ref, w2, wsem.at[0])
    actives = [start(active_ref.at[p], av.at[p], asem.at[p]) for p in range(2)]
    greet(kind)
    load.wait()
    moves = []
    extra = []
    for p in range(NP):
        actives[p].wait()
        pv[p] = mm(av[p % 2], w2[...]).astype(BF)
        moves += give_back(pv, p, back, send, recv, kind)
        if p + 2 < NP:
            actives.append(start(active_ref.at[p + 2], av.at[p % 2], asem.at[p + 2]))
        if p == 0:
            extra = fetch_blocks(sg_ref, sv, ssem, kind)
            extra.append(start(gate_up_ref, w1, wsem.at[1]))
            for n, (source, target) in enumerate(
                (
                    (to_gate_ref, to_gate), (to_up_ref, to_up), (mid_ref, mid), (g_ref, g),
                    (mixed_ref, mixed), (shared_ref.at[3], w3),
                )
            ):
                extra.append(start(source, target, msem.at[n]))
    for copy in extra:
        copy.wait()
    later = []
    for p in range(NP):
        grads = sv[p]
        acc[...] = jnp.zeros_like(acc)

        def step(f, carry):
            at = pl.ds(chunk_at(f), FC)
            grad = mm_nt(grads, w2[at, :])
            first = (grad * to_gate[p, :, at].astype(F32)).astype(BF)
            second = (grad * to_up[p, :, at].astype(F32)).astype(BF)
            acc[...] += mm_nt(first, w1[:, at]) + mm_nt(
                second, w1[:, pl.ds(pl.multiple_of(FF + f * FC, FC), FC)]
            )
            return carry

        lax.fori_loop(0, FF // FC, step, 0, unroll=2)
        qv[p] = acc[...].astype(BF)
        later += give_back(qv, p, gback, gsend, grecv, kind)
    for copy in moves:
        copy.wait()
    ready()

    def finish(i, carry):
        at = pl.ds(pl.multiple_of(i * RB, RB), RB)
        logits, routes, middle = lg_ref[at, :], rt_ref[at, :], mid[at, :]
        following, chosen = combine_rows(
            tcol_ref[at, :], back, middle, logits, routes, gain_ref[...], cv_ref
        )
        out_ref[at, :] = following
        gm_ref[at, :], gle_ref[at, :] = mix_grad(
            g[at, :].astype(F32), middle, chosen, logits, routes, 0.0, gain_ref[...], cv_ref,
            wt_ref[...], res_ref[...],
        )
        return carry

    lax.fori_loop(0, NB, finish, 0)
    stores = [done(0), done(2)]
    gu_ref[...] = jnp.zeros_like(gu_ref)
    gd_ref[...] = jnp.zeros_like(gd_ref)
    for p in range(NP):
        for copy in later[2 * p : 2 * p + 2]:
            copy.wait()
        collect(p, kind, tcol_ref, gm_ref, gback)

    def settle_one(i, carry):
        at = pl.ds(pl.multiple_of(i * RB, RB), RB)
        refs = (mid, g, mixed, gain_ref, nar_ref, w3, d_ref, u_ref, gu_ref, gd_ref)
        settle_back(refs, at, gm_ref, mixed)
        return carry

    lax.fori_loop(0, NB, settle_one, 0)
    stores.append(start(mixed, mix_out, msem.at[6]))
    for copy in stores + [done(n) for n in (1, 3, 4)]:
        copy.wait()


def expert_both(
    active, to_gate, to_up, slot_grads, gate_up, down, mid, g, mixed, weights, tcol, logits, routes, gain,
    const_vec, router_t, residual_t, narrow, down_out, up_out, kind,
):
    def body(far, near, outs, near_outs, scratch, ready, done):
        expert_both_body(kind, far, near, outs[0], near_outs, scratch, ready, done)

    half = pltpu.VMEM((T, D), BF)
    landing = pltpu.VMEM((NFFN, CAP, D), BF)
    return comm_call(
        body,
        [gate_up, down, active, to_gate, to_up, slot_grads, mid, g, mixed, weights],
        [out((T, D), BF)],
        WEIGHTS
        + [ROWS, ROWS, ROWS, WIDE, WIDE, pltpu.VMEM((2, PR, FF), BF), landing, landing]
        + [pltpu.VMEM((T, D), F32), pltpu.VMEM((T, D), g.dtype), half, pltpu.VMEM((D, D), BF), SUM]
        + [DMA((2,)), DMA((NP,)), DMA((8,)), DMA((7,))]
        + [DMA((8,)), DMA((8,)), DMA((8,)), DMA((8,))],
        "expert_both",
        2,
        2 * SLOTS * D * FF * 4,
        40e6,
        [tcol, logits, routes, gain, const_vec, router_t, residual_t, narrow, down_out, up_out],
        [out((T, D), F32), out((T, D), F32), out((T, 128), F32)]
        + [out((128, D), F32), out((128, D), F32)],
    )


def expert_back_body(split, kind, far, near, out_near, outs, scratch, ready, done):
    count = 2 if split else 1
    gate_ups, (down_ref, gate_ref, up_ref, g_ref, mid_ref, c0_ref, c1_ref, mixed_ref, shared_ref) = (
        far[:count], far[count:]
    )
    (
        trow_ref, tcol_ref, lg_ref, rt_ref, gl_ref, gain_ref, cv_ref, wt_ref, nar_ref, d_ref, u_ref
    ) = near
    gm_ref, gu_ref, gd_ref = out_near
    mix_out = outs[0]
    (
        w1, w2, sgv, rv, pv, gv, uv, back, first, second, g, mid, c0, c1, mixed, w3, acc,
        wsem, gsem, usem, msem, dsend, drecv, send, recv, osem,
    ) = scratch
    extra = [
        pltpu.make_async_copy(ref, values, msem.at[n])
        for n, (ref, values) in enumerate(
            (
                (g_ref, g), (mid_ref, mid), (c0_ref, c0), (c1_ref, c1), (mixed_ref, mixed),
                (shared_ref.at[3], w3),
            )
        )
    ]
    extra[0].start()
    extra[0].wait()
    ready()

    def gated(i, carry):
        at = pl.ds(pl.multiple_of(i * RB, RB), RB)
        gates = mix_terms(lg_ref[at, :], rt_ref[at, :])[0]
        first[at, :] = (gates[0] * g[at, :]).astype(BF)
        second[at, :] = (gates[1] * g[at, :]).astype(BF)
        return carry

    lax.fori_loop(0, NB, gated, 0)
    weights = fetch_weights(split, gate_ups, down_ref, w1, w2, wsem)
    for p in (3, 0, 1, 2):
        for values, ref, sems in ((gv, gate_ref, gsem), (uv, up_ref, usem)):
            copy = pltpu.make_async_copy(ref.at[p], values.at[p], sems.at[p])
            copy.start()
            weights.append(copy)
    for copy in extra[1:]:
        copy.start()
    greet(kind)
    arrivals = {}
    for p, h in PLACES[:-2] + [(3, 1), (3, 0)]:
        where, number = owner_at(p, h, kind)
        place = number * CAP + iota((CAP, T), 0)
        hit0 = (trow_ref[0:1, :] == place).astype(F32).astype(BF)
        hit1 = (trow_ref[1:2, :] == place).astype(F32).astype(BF)
        values = (mm(hit0, first[...]) + mm(hit1, second[...])).astype(BF)
        n = 2 * p + h
        if (p, h) == (NP - 1, 0):
            rv[p, h * CAP : (h + 1) * CAP, :] = values
            continue
        sgv[p, h * CAP : (h + 1) * CAP, :] = values
        copy = pltpu.make_async_remote_copy(
            src_ref=block_of(sgv, p, h),
            dst_ref=block_of(rv, p, h),
            send_sem=dsend.at[n],
            recv_sem=drecv.at[n],
            device_id=where,
            device_id_type=pl.DeviceIdType.MESH,
        )
        copy.start()
        arrivals[p, h] = copy
    for copy in weights + extra[1:]:
        copy.wait()
    moves = []

    for p in (3, 0, 1, 2):
        for h in range(2):
            if (p, h) in arrivals:
                arrivals[p, h].wait()
        grads = rv[p]
        acc[...] = jnp.zeros_like(acc)

        def step(f, carry):
            at = pl.ds(chunk_at(f), FC)
            gate = gv[p, :, at].astype(F32)
            up = uv[p, :, at].astype(F32)
            acc[...] += backward_chunk(grads, gate, up, w1, w2, f)
            return carry

        lax.fori_loop(0, FF // FC, step, 0, unroll=2)
        pv[p] = acc[...].astype(BF)
        moves += give_back(pv, p, back, send, recv, kind)

    def tidy(i, carry):
        at = pl.ds(pl.multiple_of(i * RB, RB), RB)
        gm_ref[at, :] = mix_grad(
            g[at, :], mid[at, :], (c0[at, :], c1[at, :]), lg_ref[at, :], rt_ref[at, :],
            gl_ref[at, :], gain_ref[...], cv_ref, wt_ref[...], None,
        )[0]
        return carry

    lax.fori_loop(0, NB, tidy, 0)
    gu_ref[...] = jnp.zeros_like(gu_ref)
    gd_ref[...] = jnp.zeros_like(gd_ref)
    for n, p in enumerate((3, 0, 1, 2)):
        for copy in moves[2 * n : 2 * n + 2]:
            copy.wait()
        collect(p, kind, tcol_ref, gm_ref, back)

    def settle_one(i, carry):
        at = pl.ds(pl.multiple_of(i * RB, RB), RB)
        refs = (mid, g, mixed, gain_ref, nar_ref, w3, d_ref, u_ref, gu_ref, gd_ref)
        settle_back(refs, at, gm_ref, first)
        return carry

    lax.fori_loop(0, NB, settle_one, 0)
    last = pltpu.make_async_copy(first, mix_out, osem.at[0])
    last.start()
    for copy in [last] + [done(n) for n in range(3)]:
        copy.wait()


def expert_backward(
    gate, up, gate_ups, down, g, mid, c0, c1, mixed, weights, trow, tcol, logits, routes, gl, gain,
    const_vec, router_t, narrow, down_out, up_out, kind,
):
    split = len(gate_ups) == 2

    def body(far, near, outs, near_outs, scratch, ready, done):
        expert_back_body(split, kind, far, near, near_outs, outs, scratch, ready, done)

    half, full = pltpu.VMEM((T, D), BF), pltpu.VMEM((T, D), F32)
    mix, gm, gu, gd = comm_call(
        body,
        [*gate_ups, down, gate, up, g, mid, c0, c1, mixed, weights],
        [out((T, D), BF)],
        WEIGHTS
        + [ROWS, ROWS, ROWS, WIDE, WIDE, pltpu.VMEM((NFFN, CAP, D), BF)]
        + [half, half, full, full, half, half, half, pltpu.VMEM((D, D), BF), SUM]
        + [DMA((9,)), DMA((NP,)), DMA((NP,)), DMA((6,))]
        + [DMA((8,)), DMA((8,)), DMA((8,)), DMA((8,)), DMA((1,))],
        "expert_backward",
        3,
        2 * SLOTS * D * FF * 3,
        26e6,
        [
            trow, tcol, logits, routes, gl, gain, const_vec, router_t, narrow, down_out, up_out,
        ],
        [out((T, D), F32), out((128, D), F32), out((128, D), F32)],
    )
    return gm, mix, gu, gd


def mix_terms(logits, routes):
    lane = iota(logits.shape, 1)

    def at(place):
        return jnp.sum(jnp.where(lane == place, logits, 0.0), axis=1, keepdims=True)

    r0, r1 = routes[:, 0:1], routes[:, 1:2]
    gap = at(r0) - at(r1)
    gates = (sigmoid(gap), sigmoid(-gap))

    def weight(e):
        return jnp.where(r0 == e, gates[0], 0.0) + jnp.where(r1 == e, gates[1], 0.0)

    shares = []
    for c in range(2):
        apart = logits[:, 12 + 2 * c : 13 + 2 * c] - logits[:, 13 + 2 * c : 14 + 2 * c]
        shares.append((sigmoid(apart), sigmoid(-apart)))
    weights = [weight(NFFN + 1), weight(NFFN + 2), weight(NFFN + 3)]
    return gates, weights, shares


def rms_scale(v):
    return lax.rsqrt(jnp.mean(v * v, axis=1, keepdims=True) + EPSILON)


def combine_rows(tcol, back_ref, mid, logits, routes, gain, cv_ref):
    place = iota((RB, SLOTS), 1)
    back = back_ref[...].reshape(SLOTS, D)
    chosen = []
    for k in range(2):
        hit = (tcol[:, k : k + 1] == place).astype(F32).astype(BF)
        chosen.append(mm(hit, back))
    normed = mid * rms_scale(mid) * gain
    gates, weights, shares = mix_terms(logits, routes)
    same = weights[0] + weights[1] * shares[0][0] + weights[2] * shares[1][0]
    moe = gates[0] * chosen[0] + gates[1] * chosen[1] + same * normed
    moe = moe + (weights[1] * shares[0][1]) * cv_ref[0:1, :]
    moe = moe + (weights[2] * shares[1][1]) * cv_ref[1:2, :]
    return mid + moe, chosen


def combine_body(tcol_ref, ret_ref, mid_ref, lg_ref, rt_ref, g_ref, cv_ref, x_ref, c0_ref, c1_ref):
    x_ref[...], chosen = combine_rows(
        tcol_ref[...], ret_ref, mid_ref[...], lg_ref[...], rt_ref[...], g_ref[...], cv_ref
    )
    c0_ref[...] = chosen[0].astype(BF)
    c1_ref[...] = chosen[1].astype(BF)


def combine(tcol, returned, mid, logits, routes, gain, const_vec):
    return call(
        combine_body,
        (NB,),
        [
            (tcol, (RB, 128), rows),
            (returned, None),
            (mid, (RB, D), rows),
            (logits, (RB, 128), rows),
            (routes, (RB, 2), rows),
            (gain, None),
            (const_vec, None),
        ],
        [
            (out((T, D), F32), (RB, D), rows),
            (out((T, D), BF), (RB, D), rows),
            (out((T, D), BF), (RB, D), rows),
        ],
        name="combine",
        flops=4 * T * SLOTS * D,
        nbytes=12e6,
    )


def mix_grad(g, mid, chosen, logits, routes, grad, gain, cv_ref, wt, res):
    normed = mid * rms_scale(mid) * gain
    gates, weights, shares = mix_terms(logits, routes)

    def along(v):
        return jnp.sum(g * v, axis=1, keepdims=True)

    same = along(normed)
    const = [along(cv_ref[c : c + 1, :]) for c in range(2)]
    gate_grads = []
    for k in range(2):
        r = routes[:, k : k + 1]
        value = along(chosen[k].astype(F32)) + jnp.where(r == NFFN + 1, same, 0.0)
        for c in range(2):
            mixed = shares[c][0] * same + shares[c][1] * const[c]
            value = value + jnp.where(r == NFFN + 2 + c, mixed, 0.0)
        gate_grads.append(value)
    slope = gates[0] * gates[1] * (gate_grads[0] - gate_grads[1])
    lane = iota((RB, 128), 1)
    grad = grad + jnp.where(lane == routes[:, 0:1], slope, 0.0)
    grad = grad - jnp.where(lane == routes[:, 1:2], slope, 0.0)
    only = grad
    for c in range(2):
        tilt = weights[1 + c] * shares[c][0] * shares[c][1] * (same - const[c])
        grad = grad + jnp.where(lane == 12 + 2 * c, tilt, 0.0)
        grad = grad - jnp.where(lane == 13 + 2 * c, tilt, 0.0)
    keep = weights[0] + weights[1] * shares[0][0] + weights[2] * shares[1][0]
    residual = None if res is None else mm(spread_lanes(only), res)
    return mm(spread_lanes(grad), wt) + keep * g, residual


def collect(p, kind, tcol_ref, gm_ref, back_ref):
    numbers = [owner_at(p, h, kind)[1] for h in range(2)]

    def one(i, carry):
        at = pl.ds(pl.multiple_of(i * RB, RB), RB)
        tcol = tcol_ref[at, :]
        total = gm_ref[at, :]
        for number in numbers:
            place = number * CAP + iota((RB, CAP), 1)
            hit = (tcol[:, 0:1] == place) | (tcol[:, 1:2] == place)
            total = total + mm(hit.astype(F32).astype(BF), back_ref[number])
        gm_ref[at, :] = total
        return carry

    lax.fori_loop(0, NB, one, 0)


def settle_back(refs, at, gm_ref, mix_ref):
    mid_ref, g_ref, mixed_ref, gain_ref, nar_ref, w_ref, d_ref, u_ref, gu_ref, gd_ref = refs
    grad = g_ref[at, :].astype(F32) + rms_back(gm_ref[at, :], mid_ref[at, :], gain_ref[...])
    gm_ref[at, :] = grad
    grad = grad.astype(BF)
    slim = mm_nt(grad, u_ref[...]).astype(BF)
    gu_ref[...] += 2.0 * mm_tn(nar_ref[at, :], grad)
    gd_ref[...] += mm_tn(slim, mixed_ref[at, :])
    mix_ref[at, :] = (mm_nt(grad, w_ref[...]) + mm_nt(slim, d_ref[...])).astype(BF)


def rms_back(grad, v, gain):
    scale = rms_scale(v)
    inner = grad * gain
    return scale * inner - v * (scale**3 * jnp.mean(v * inner, axis=1, keepdims=True))


def attend_back(q, k, v, aug, kf, g, mixed, dqt):
    lane = iota((T, 128), 1)
    low = lane < 64
    lane6 = lane & 63
    product = g.astype(F32) * mixed.astype(F32)
    d0 = jnp.sum(jnp.where(low, product, 0.0), axis=1, keepdims=True)
    d1 = jnp.sum(jnp.where(low, 0.0, product), axis=1, keepdims=True)
    a, b, c = three(-jnp.where(low, d1, d0))
    zero = jnp.zeros((T, 128), BF)
    ga = jnp.where(lane6 == 0, a, jnp.where(lane6 == 1, b, jnp.where(lane6 == 2, c, zero)))
    va = (lane6 < 3).astype(F32).astype(BF)
    qs = (jnp.where(low, q, aug), jnp.where(low, aug, q))
    ks = (jnp.where(low, k, kf), jnp.where(low, kf, k))
    vs = (jnp.where(low, v, va), jnp.where(low, va, v))
    gs = (jnp.where(low, g, ga), jnp.where(low, ga, g))
    kt = k.T
    tri = iota((RB, RB), 0) <= iota((RB, RB), 1)
    low = low[:RB]
    dks = []
    dvs = []
    for i in range(NB):
        here = slice(i * RB, (i + 1) * RB)
        dk = [None, None]
        dv = [None, None]
        for h in range(2):
            half = slice(h * 64, (h + 1) * 64)
            for start, stop in ((i * RB, (i + 1) * RB), ((i + 1) * RB, T)):
                if start == stop:
                    continue
                there = slice(start, stop)
                p = jnp.exp2(mm_nt(ks[h][here], qs[h][there]) * LOG_SCALE)
                if stop == (i + 1) * RB:
                    p = jnp.where(tri, p, 0.0)
                ds = (p * mm_nt(vs[h][here], gs[h][there])).astype(BF)
                p = p.astype(BF)
                dv_part = mm(p, g[there])
                dk_part = mm(ds, q[there])
                dk[h] = dk_part if dk[h] is None else dk[h] + dk_part
                dv[h] = dv_part if dv[h] is None else dv[h] + dv_part
                part = mm(kt[half, here], ds)
                if i == 0:
                    dqt[half, there] = part
                else:
                    dqt[half, there] += part
        dvs.append(jnp.where(low, dv[0], dv[1]))
        dks.append(jnp.where(low, dk[0], dk[1]))
    return dqt[...].T, jnp.concatenate(dks), jnp.concatenate(dvs)


def layer_back_body(far, near, out_near, gx_ref, scratch, ready, done):
    gm_ref, mix_ref, mixed_ref, w_ref, qkv_ref, aug_ref, n_ref, x_ref = far
    gain_ref, nar_ref, d_ref, u_ref, kf_ref, cos_ref, sin_ref = near
    gu_ref, gd_ref = out_near
    gm, mix, mixed, w, qkv, aug, n, x, gproj, dqt, sems, pair_sems, out_sems = scratch

    def start(source, target, sem):
        copy = pltpu.make_async_copy(source, target, sem)
        copy.start()
        return copy

    def cols(part, j):
        return pl.ds(pl.multiple_of(part * D + j * 128, 128), 128)

    def of_pair(j):
        copies = [
            pltpu.make_async_copy(
                qkv_ref.at[:, cols(part, j)], qkv.at[:, cols(part, j)], pair_sems.at[j, part]
            )
            for part in range(3)
        ]
        for k, (source, target) in enumerate(((mix_ref, mix), (mixed_ref, mixed))):
            copies.append(
                pltpu.make_async_copy(
                    source.at[:, cols(0, j)], target.at[:, cols(0, j)], pair_sems.at[j, 3 + k]
                )
            )
        copies.append(pltpu.make_async_copy(aug_ref.at[j], aug.at[j], pair_sems.at[j, 5]))
        return copies

    for j in range(PAIRS):
        for copy in of_pair(j):
            copy.start()
    third = [start(w_ref.at[k], w.at[k], sems.at[k]) for k in range(3)]
    third += [
        start(source, target, sems.at[3 + k])
        for k, (source, target) in enumerate(((n_ref, n), (x_ref, x), (gm_ref, gm)))
    ]
    ready()

    def pair(j, carry):
        for copy in of_pair(j):
            copy.wait()
        dq, dk, dv = attend_back(
            qkv[:, cols(0, j)], qkv[:, cols(1, j)], qkv[:, cols(2, j)], aug[j], kf_ref[...],
            mix[:, cols(0, j)], mixed[:, cols(0, j)], dqt,
        )
        for part, value in enumerate((dq, dk)):
            value = (value * (1.0 / math.sqrt(HD))).astype(BF).astype(F32)
            gproj[:, cols(part, j)] = turn(value, cos_ref[...], -sin_ref[...]).astype(BF)
        gproj[:, cols(2, j)] = dv.astype(BF)
        return carry

    lax.fori_loop(0, PAIRS, pair, 0)
    for copy in third:
        copy.wait()
    gu_ref[...] = jnp.zeros_like(gu_ref)
    gd_ref[...] = jnp.zeros_like(gd_ref)
    stores = []
    for i in range(NB):
        at = slice(i * RB, (i + 1) * RB)
        grad = jnp.zeros((RB, D), F32)
        slim = jnp.zeros((RB, 128), F32)
        narrow = nar_ref[at, :]
        for part in range(3):
            columns = slice(part * D, (part + 1) * D)
            piece = gproj[at, columns]
            grad = grad + mm_nt(piece, w[part])
            slim = slim + mm_nt(piece, u_ref[:, columns])
            gu_ref[:, columns] += 2.0 * mm_tn(narrow, piece)
        slim = slim.astype(BF)
        gd_ref[...] += mm_tn(slim, n[at, :])
        grad = grad + mm_nt(slim, d_ref[...])
        gm[at, :] = gm[at, :] + rms_back(grad, x[at, :].astype(F32), gain_ref[...])
        stores.append(start(gm.at[at, :], gx_ref.at[at, :], out_sems.at[i]))
    for copy in stores + [done(0), done(1)]:
        copy.wait()


def layer_back(gm, mix, mixed, w, qkv, aug, n, x, gain0, narrow, down, up, kf, cos, sin):
    far = [gm, mix, mixed, w, qkv, aug, n, x]

    def body(far, near, outs, near_outs, scratch, ready, done):
        layer_back_body(far, near, near_outs, outs[0], scratch, ready, done)

    shapes = [out((3, D, D), BF) if v is w else v for v in far]
    return comm_call(
        body,
        far,
        [out((T, D), F32)],
        [pltpu.VMEM(v.shape, v.dtype) for v in shapes]
        + [pltpu.VMEM((T, 3 * D), BF), pltpu.VMEM((128, T), F32)]
        + [DMA((6,)), DMA((PAIRS, 6)), DMA((NB,))],
        "layer_back",
        None,
        12 * 10 * T * T * 128 + 2 * T * D * 3 * D,
        4e7,
        [gain0, narrow, down, up, kf, cos, sin],
        [out((128, 3 * D), F32), out((128, D), F32)],
    )


AXES = ("x", "c", "zh", "zl", "y")
EXPERT, SHARD = AXES[:2], AXES[2:]
PIECE = 96


def shared_body(count, *refs):
    (p_ref,), away, (o_ref,), came, sems = split_refs(refs, 1, count, 1, count)
    local, zs, zr, ys, yr, xs, xr, cs, cr, ws, wr = sems
    x, c, y = (lax.axis_index(name) for name in ("x", "c", "y"))
    z = 2 * lax.axis_index("zh") + lax.axis_index("zl")
    mine, theirs = 2 * x + c, 2 * (1 - x) + c

    def spot(quarter, column, j):
        at = (2 * ((z + 4 - j) % 4) + column) * PIECE
        return o_ref.at[quarter, pl.ds(pl.multiple_of(at, PIECE), PIECE), :]

    others = [{"zh": (z + d) % 4 // 2, "zl": (z + d) % 2} for d in range(1, 4)]
    others += [{"y": 1 - y}, {"x": 1 - x}, {"c": 1 - c}]
    barrier = pltpu.get_barrier_semaphore()
    for who in others:
        pl.semaphore_signal(barrier, inc=1, device_id=who, device_id_type=pl.DeviceIdType.MESH)
    pl.semaphore_wait(barrier, len(others))

    started = []

    def send(source, target, who, send_sem, recv_sem):
        copy = pltpu.make_async_remote_copy(
            src_ref=source,
            dst_ref=target,
            send_sem=send_sem,
            recv_sem=recv_sem,
            device_id=who,
            device_id_type=pl.DeviceIdType.MESH,
        )
        copy.start()
        started.append(copy)
        return copy

    core_copies = []

    def to_core(source, target):
        n = len(core_copies)
        core_copies.append(send(source, target, others[5], cs.at[n], cr.at[n]))

    own = pltpu.make_async_copy(p_ref, spot(mine, y, 0), local.at[0])
    own.start()
    z_copies = [
        send(p_ref, spot(mine, y, 0), others[d], zs.at[d], zr.at[d]) for d in range(3)
    ]
    y_copies = [None] * 6
    x_copies = [None] * 6

    def along_y(n, source, target):
        y_copies[n] = send(source, target, others[3], ys.at[n], yr.at[n])

    def along_x(n, source, target):
        x_copies[n] = send(source, target, others[4], xs.at[n], xr.at[n])

    along_y(0, p_ref, spot(mine, y, 0))
    along_x(0, p_ref, spot(mine, y, 0))
    to_core(p_ref, spot(mine, y, 0))
    swaps = [
        send(source, target, others[3], ws.at[n], wr.at[n])
        for n, (source, target) in enumerate(zip(away, came))
    ]
    for j in range(1, 4):
        z_copies[j - 1].wait_recv()
        piece = spot(mine, y, j)
        along_y(j, piece, piece)
        along_x(j, piece, piece)
        to_core(piece, piece)
    for j in range(4):
        y_copies[j].wait_recv()
        piece = spot(mine, 1 - y, j)
        if j < 2:
            along_x(4 + j, piece, piece)
        to_core(piece, piece)
        x_copies[j].wait_recv()
        piece = spot(theirs, y, j)
        if j >= 2:
            along_y(2 + j, piece, piece)
        to_core(piece, piece)
    for j in range(4):
        (x_copies[4 + j] if j < 2 else y_copies[2 + j]).wait_recv()
        piece = spot(theirs, 1 - y, j)
        to_core(piece, piece)
    for copy in core_copies + swaps:
        copy.wait_recv()
    own.wait()
    for copy in started:
        copy.wait_send()


def usual():
    return tuple(lax.axis_size(name) for name in AXES) == (2, 2, 2, 2, 2)


def gather_shared(qkv, output, away=()):
    rows_here = qkv.shape[0]
    parts = jnp.concatenate([qkv.reshape(rows_here, 3, D).transpose(1, 0, 2), output[None]])
    if not usual():
        return [lax.all_gather(parts, SHARD, axis=1, tiled=True)]
    quarter = 2 * lax.axis_index("x") + lax.axis_index("c")
    piece = lax.dynamic_index_in_dim(parts, quarter, axis=0, keepdims=False)
    return comm_call(
        lambda far, near, outs, near_outs, scratch, ready, done: shared_body(
            len(away), *far, *outs, *scratch
        ),
        [piece, *away],
        [jax.ShapeDtypeStruct(v.shape, v.dtype) for v in (out((4, D, D), BF), *away)],
        [DMA((n,)) for n in (1, 3, 3, 6, 6, 6, 6, 16, 16, 2, 2)],
        "gather_shared",
        5 if away else 0,
        0,
        5e7,
    )


SPAN = 96
UNIT = LAYERS * 2 * 4 * R


def adapters_body(*refs):
    id_ref, parts = refs[0], refs[1 : 1 + 4 * LAYERS]
    o_ref = refs[1 + 4 * LAYERS]
    sbuf, rbuf, tbuf, ubuf, ibuf, jbuf, asend, arecv, bsend, brecv, isend, irecv = refs[2 + 4 * LAYERS :]
    x, c, y = (lax.axis_index(name) for name in ("x", "c", "y"))
    z = 2 * lax.axis_index("zh") + lax.axis_index("zl")
    mates = []
    for dz in range(4):
        for dy in range(2):
            mates.append(((z + dz) % 4, flip(y, dy)))
    groups = [(flip(x, dx), flip(c, dc)) for dx in range(2) for dc in range(2)]
    barrier = pltpu.get_barrier_semaphore()
    peers = [{"zh": a // 2, "zl": a % 2, "y": b} for a, b in mates[1:]]
    peers += [{"x": a, "c": b} for a, b in groups[1:]]
    for who in peers:
        pl.semaphore_signal(barrier, inc=1, device_id=who, device_id_type=pl.DeviceIdType.MESH)
    for layer in range(LAYERS):
        gd_in, gd_out, gu_in, gu_out = parts[4 * layer : 4 * layer + 4]
        pieces = [gd_in[p * R : (p + 1) * R, :] for p in range(3)] + [gd_out[:R, :]]
        pieces += [gu_in[p * R : (p + 1) * R, p * D : (p + 1) * D] for p in range(3)] + [gu_out[:R, :]]
        sbuf[:, layer * 128 : (layer + 1) * 128] = jnp.concatenate(pieces).T.astype(BF)
    ibuf[...] = jnp.broadcast_to(id_ref[0].astype(F32).astype(BF), (16, 128))

    def share(k):
        return sbuf.at[pl.ds(pl.multiple_of(k * SPAN, SPAN), SPAN), :]

    pl.semaphore_wait(barrier, len(peers))
    me = 2 * z + y
    copies = []
    for n, (a, b) in enumerate(mates):
        if n == 0:
            rbuf[0] = share(me)[...]
            jbuf[0] = ibuf[...]
            continue
        at = (4 - n // 2) % 4 * 2 + n % 2
        copy = pltpu.make_async_remote_copy(
            src_ref=ibuf,
            dst_ref=jbuf.at[at],
            send_sem=isend.at[n],
            recv_sem=irecv.at[at],
            device_id={"zh": a // 2, "zl": a % 2, "y": b},
            device_id_type=pl.DeviceIdType.MESH,
        )
        copy.start()
        copies.append(copy)
        copy = pltpu.make_async_remote_copy(
            src_ref=share(2 * a + b),
            dst_ref=rbuf.at[at],
            send_sem=asend.at[n],
            recv_sem=arecv.at[at],
            device_id={"zh": a // 2, "zl": a % 2, "y": b},
            device_id_type=pl.DeviceIdType.MESH,
        )
        copy.start()
        copies.append(copy)
    for copy in copies:
        copy.wait()
    masks = []
    for n in range(8):
        own = jbuf[n][0:1, 0:1].astype(F32)
        masks.append([(own == k).astype(F32) for k in range(NA)])

    def add(i, carry):
        at = pl.ds(pl.multiple_of(i * 16, 16), 16)
        sums = [jnp.zeros((16, UNIT), F32) for _ in range(NA)]
        for n in range(8):
            values = rbuf[n, at, :].astype(F32)
            for k in range(NA):
                sums[k] = sums[k] + values * masks[n][k]
        for k in range(NA):
            tbuf[k, at, :] = sums[k].astype(BF)
        return carry

    lax.fori_loop(0, SPAN // 16, add, 0)
    copies = []
    ubuf[0] = tbuf[pl.ds(2 * (2 * x + c), 2)]
    for n, (a, b) in enumerate(groups):
        if n == 0:
            continue
        copy = pltpu.make_async_remote_copy(
            src_ref=tbuf.at[pl.ds(2 * (2 * a + b), 2)],
            dst_ref=ubuf.at[n],
            send_sem=bsend.at[n],
            recv_sem=brecv.at[n],
            device_id={"x": a, "c": b},
            device_id_type=pl.DeviceIdType.MESH,
        )
        copy.start()
        copies.append(copy)
    for copy in copies:
        copy.wait()
    total = ubuf[0].astype(F32)
    for n in range(1, 4):
        total = total + ubuf[n].astype(F32)
    o_ref[...] = total


def adapters(own, parts):
    specs = [pl.BlockSpec(memory_space=pltpu.SMEM)]
    specs += [pl.BlockSpec(memory_space=pltpu.VMEM)] * len(parts)
    return pl.pallas_call(
        adapters_body,
        in_specs=specs,
        out_specs=pl.BlockSpec(memory_space=pltpu.VMEM),
        out_shape=jax.ShapeDtypeStruct((2, SPAN, UNIT), F32),
        scratch_shapes=[
            pltpu.VMEM((D, UNIT), BF),
            pltpu.VMEM((8, SPAN, UNIT), BF),
            pltpu.VMEM((NA, SPAN, UNIT), BF),
            pltpu.VMEM((4, 2, SPAN, UNIT), BF),
            pltpu.VMEM((16, 128), BF),
            pltpu.VMEM((8, 16, 128), BF),
            DMA((8,)),
            DMA((8,)),
            DMA((4,)),
            DMA((4,)),
            DMA((8,)),
            DMA((8,)),
        ],
        compiler_params=pltpu.CompilerParams(
            vmem_limit_bytes=VMEM_BYTES, collective_id=4, has_side_effects=True
        ),
        name="adapters",
    )(own, *parts)


def both_rows(mine, other):
    y = lax.axis_index("y")
    return jnp.where(y == 0, jnp.stack([mine, other]), jnp.stack([other, mine]))


def own_and_other(w):
    y = lax.axis_index("y")
    return [lax.dynamic_index_in_dim(w, e, axis=0, keepdims=False) for e in (y, 1 - y)]


def across_y(v):
    return lax.ppermute(v, "y", [(0, 1), (1, 0)])


def swapped(w):
    mine, other = own_and_other(w)
    return both_rows(mine, across_y(other))


def gathered(w, axes):
    return lax.all_gather(w, axes, axis=0, tiled=True).reshape(-1, w.shape[-1])


def exchange(v, kind):
    return lax.all_to_all(v, OWNERS[kind], split_axis=0, concat_axis=0, tiled=True)


def pad_to(v, shape):
    return jnp.pad(v, [(0, n - m) for m, n in zip(v.shape, shape)])


def adapters_plain(owners, parts):
    layers = []
    for gd_in, gd_out, gu_in, gu_out in parts:
        downs = [gd_in[p * R : (p + 1) * R] for p in range(3)] + [gd_out[:R]]
        ups = [gu_in[p * R : (p + 1) * R, p * D : (p + 1) * D] for p in range(3)] + [gu_out[:R]]
        layers.append(jnp.concatenate(downs + ups))
    compact = jnp.concatenate(layers).astype(BF)
    ranks = lax.axis_size(SHARD)
    pieces = compact.reshape(UNIT, ranks, D // ranks).transpose(1, 0, 2)
    pieces = lax.all_to_all(pieces, SHARD, split_axis=0, concat_axis=0, tiled=True)
    pick = (owners[None, :] == jnp.arange(NA, dtype=jnp.int32)[:, None]).astype(F32)
    summed = jnp.dot(pick, pieces.reshape(ranks, -1).astype(F32), precision=HIGHEST).astype(BF)
    groups = lax.axis_size(EXPERT)
    summed = lax.all_to_all(
        summed.reshape(groups, NA // groups, -1), EXPERT, split_axis=0, concat_axis=0, tiled=True
    )
    summed = jnp.sum(summed.astype(F32), axis=0)
    return summed.reshape(summed.shape[0], UNIT, -1).transpose(0, 2, 1)


def per_device(
    tokens,
    segments,
    parents,
    adapter_of,
    routes,
    norm_gain,
    query_key_value_weight,
    output_weight,
    adapter_down,
    adapter_up,
    router,
    router_residual,
    const_proj,
    const_vec,
    w_gate_up,
    w_down,
    out_grad,
):
    fast = w_gate_up.shape[1] == 2
    kind = PLANE if fast else WIDE_SLICE
    barrier = lax.optimization_barrier
    if fast:
        mine, other = own_and_other(w_gate_up[0])
        parts = [lax.all_gather(mine, ("zh", "zl"), axis=0)]
        down_mine, down_other = own_and_other(w_down[0])
        first, other, down_other = gather_shared(
            query_key_value_weight[0], output_weight[0], (other, down_other)
        )
        shared = [first]
        parts.append(lax.all_gather(other, ("zh", "zl"), axis=0))
        gate_up_full = [parts]
        down_full = [gathered(both_rows(down_mine, down_other), ("zh", "zl"))]
    else:
        shared = gather_shared(query_key_value_weight[0], output_weight[0])
        gate_up_full = [[gathered(w_gate_up[layer, 0], SHARD)] for layer in range(LAYERS)]
        down_full = [gathered(w_down[layer, 0], SHARD) for layer in range(LAYERS)]

    which = adapter_of[0]
    down_sel = lax.dynamic_index_in_dim(adapter_down, which, axis=2, keepdims=False)
    up_sel = lax.dynamic_index_in_dim(adapter_up, which, axis=2, keepdims=False)
    down_in = jnp.pad(
        down_sel[:, :3].transpose(0, 2, 1, 3).reshape(LAYERS, D, 3 * R), ((0, 0), (0, 0), (0, 80))
    )
    down_out = jnp.pad(down_sel[:, 3], ((0, 0), (0, 0), (0, 112)))
    up_t = 2.0 * up_sel.transpose(0, 1, 3, 2)
    up_in = jnp.zeros((LAYERS, 128, 3 * D), BF)
    for p in range(3):
        up_in = up_in.at[:, p * R : (p + 1) * R, p * D : (p + 1) * D].set(up_t[:, p])
    up_out = jnp.pad(up_t[:, 3], ((0, 0), (0, 112), (0, 0)))
    rcat = jnp.concatenate([router, const_proj[:, 0], const_proj[:, 1]], axis=2)
    rcat = jnp.pad(rcat, ((0, 0), (0, 0), (0, 112)))
    rcat_t = rcat[:, :, :16].transpose(0, 2, 1)
    residual = pad_to(router_residual, (16, 128))
    residual_t = pad_to(router_residual.T, (16, 128))

    qf, kf, cos, sin, tcol, trow, router_s, router_ts, residual_s, residual_ts = prep(
        parents, segments.reshape(T, 1), routes, rcat, rcat_t, residual, residual_t
    )

    stream = tokens
    earlier = jnp.zeros((T, 128), F32)
    saved = []
    for layer in range(LAYERS):
        gain0 = norm_gain[layer, 0:1]
        gain1 = norm_gain[layer, 1:2]
        normed, narrow, qkv = project(
            stream, gain0, shared[layer], down_in[layer], up_in[layer], cos, sin
        )
        mixed, aug = attend(qkv, qf, kf)
        mid, sent, logits, narrow_out = settle(
            stream, mixed, shared[layer], down_out[layer], up_out[layer], gain1, router_s[layer],
            earlier, residual_s,
        )
        buffer = dispatch(trow, sent)
        received = exchange(buffer, kind)
        if layer == 0:
            if fast:
                later = barrier((w_gate_up[1], w_down[1], logits))
                gate_up_next, down_next = barrier((swapped(later[0]), later[1]))
                gate_up_full.append([gathered(gate_up_next, ("zh", "zl"))])
                down_full.append(gathered(swapped(down_next), ("zh", "zl")))
            later = lax.optimization_barrier(
                (query_key_value_weight[1], output_weight[1], logits)
            )
            shared += gather_shared(later[0], later[1])
            returned, gate, up = expert_forward(received, gate_up_full[0], down_full[0], kind)
        else:
            slot_grads = exchange(dispatch_grad(trow, out_grad, logits, routes), kind)
            grad_mixed, following, grad_mid, grad_logits, gu_out, gd_out = expert_both(
                *expert_parts(received, gate_up_full[1][0], kind), slot_grads, gate_up_full[1][0], down_full[1], mid, out_grad, mixed,
                shared[1], tcol, logits, routes, gain1, const_vec[1], router_ts[1], residual_ts,
                narrow_out, down_out[1], up_out[1], kind,
            )
            c0 = c1 = None
        if layer == 0:
            following, c0, c1 = combine(
                tcol, returned.reshape(SLOTS, D), mid, logits, routes, gain1, const_vec[0]
            )
        saved.append((stream, normed, narrow, qkv, mixed, aug, mid, logits, narrow_out, c0, c1))
        stream = following
        earlier = logits

    grad = out_grad
    parts = [None] * LAYERS
    for layer in reversed(range(LAYERS)):
        x_in, normed, narrow, qkv, mixed, aug, mid, logits, narrow_out, c0, c1 = saved[layer]
        gain0 = norm_gain[layer, 0:1]
        gain1 = norm_gain[layer, 1:2]
        if layer == 0:
            grad_mid, grad_mixed, gu_out, gd_out = expert_backward(
                gate, up, gate_up_full[0], down_full[0], grad, mid, c0, c1, mixed, shared[0], trow,
                tcol, logits, routes, grad_logits, gain1, const_vec[0], router_ts[0], narrow_out,
                down_out[0], up_out[0], kind,
            )
        grad, gu_in, gd_in = layer_back(
            grad_mid, grad_mixed, mixed, shared[layer], qkv, aug, normed, x_in, gain0, narrow,
            down_in[layer], up_in[layer], kf, cos, sin,
        )
        parts[layer] = (gd_in, gd_out, gu_in, gu_out)

    if usual():
        final = adapters(adapter_of, [v for layer in parts for v in layer])
    else:
        final = adapters_plain(lax.all_gather(adapter_of, SHARD, axis=0, tiled=True), parts)
    final = final.reshape(*final.shape[:2], LAYERS, 2, 4, R).transpose(3, 2, 4, 0, 1, 5)
    return (stream, grad, final[0], final[1])


def solution(mesh):
    owners, shards = mesh.shape["expert"], mesh.shape["shard"]
    each = NFFN // owners
    fine = jax.sharding.Mesh(
        mesh.devices.reshape(owners // 2, 2, shards // each**2, each, each), AXES
    )
    expert, shard, both = EXPERT, SHARD, AXES
    in_specs = (
        P(both, None),
        P(both, None),
        P(both, None),
        P(both),
        P(both, None),
        P(),
        P(None, shard, None),
        P(None, shard, None),
        P(),
        P(),
        P(),
        P(),
        P(),
        P(),
        P(None, expert, shard, None),
        P(None, expert, shard, None),
        P(both, None),
    )
    out_specs = (
        P(both, None),
        P(both, None),
        P(None, None, expert, shard, None),
        P(None, None, expert, shard, None),
    )
    return jax.shard_map(
        per_device, mesh=fine, in_specs=in_specs, out_specs=out_specs, check_vma=False
    )
```
